32 devices in a mesh: ctx: 8 (over y, x, core), fsdp: 4 (over z).
Axes of the slice: x: 2, y: 2, z: 4, core: 2. Of those that a mesh axis runs over, the one named last changes fastest.
Arguments:
- inputs: bfloat16 [4, 1024, 1600], P('fsdp', 'ctx'), may hold values from -6 to 6
- cotangent: bfloat16 [4, 1024, 1600], P('fsdp', 'ctx'), may hold values from -6 to 6
- norm_gain: float32 [1600], replicated, may hold values from 0.1 to 1.9
- query_proj: bfloat16 [1600, 1600], P('fsdp'), may hold values from -0.15625 to 0.15625
- key_proj: bfloat16 [1600, 320], P('fsdp'), may hold values from -0.15625 to 0.15625
- value_proj: bfloat16 [1600, 320], P('fsdp'), may hold values from -0.15625 to 0.15625
- attn_proj: bfloat16 [1600, 1600], P('fsdp'), may hold values from -0.15625 to 0.15625
- attn_gain: float32 [1600], replicated, may hold values from 0.1 to 1.9
- mixer_in: bfloat16 [1600, 6400], P('fsdp'), may hold values from -0.15625 to 0.15625
- conv_taps: float32 [4, 3200], replicated, may hold values from -3 to 3
- conv_bias: float32 [3200], replicated, may hold values from -3 to 3
- state_proj: bfloat16 [3200, 132], P('fsdp'), may hold values from -0.109375 to 0.109375
- step_proj: bfloat16 [100, 3200], P('fsdp'), may hold values from -0.625 to 0.625
- step_bias: float32 [3200], replicated, may hold values from -4 to 0
- decay_rate: float32 [3200, 16], replicated, may hold values from 9.765625e-05 to 0.5, as said below
- skip_gain: float32 [3200], replicated, may hold values from -6 to 6
- mixer_out: bfloat16 [3200, 1600], P('fsdp'), may hold values from -0.109375 to 0.109375
- ssm_gain: float32 [3200], replicated, may hold values from 0.1 to 1.9
- ffn_gain: float32 [1600], replicated, may hold values from 0.1 to 1.9
- gate_proj: bfloat16 [1600, 5504], P('fsdp'), may hold values from -0.15625 to 0.15625
- up_proj: bfloat16 [1600, 5504], P('fsdp'), may hold values from -0.15625 to 0.15625
- down_proj: bfloat16 [5504, 1600], P('fsdp'), may hold values from -0.078125 to 0.078125
Outputs:
- output: float32 [4, 1024, 1600], P('fsdp', 'ctx')
- input_grad: float32 [4, 1024, 1600], P('fsdp', 'ctx')
- norm_gain_grad: float32 [1600], replicated
- query_proj_grad: float32 [1600, 1600], P('fsdp', 'ctx')
- key_proj_grad: float32 [1600, 320], P('fsdp', 'ctx')
- value_proj_grad: float32 [1600, 320], P('fsdp', 'ctx')
- attn_proj_grad: float32 [1600, 1600], P('fsdp', 'ctx')
- attn_gain_grad: float32 [1600], replicated
- mixer_in_grad: float32 [1600, 6400], P('fsdp', 'ctx')
- conv_taps_grad: float32 [4, 3200], replicated
- conv_bias_grad: float32 [3200], replicated
- state_proj_grad: float32 [3200, 132], replicated
- step_proj_grad: float32 [100, 3200], P('fsdp', 'ctx')
- step_bias_grad: float32 [3200], replicated
- decay_rate_grad: float32 [3200, 16], replicated
- skip_gain_grad: float32 [3200], replicated
- mixer_out_grad: float32 [3200, 1600], P('fsdp', 'ctx')
- ssm_gain_grad: float32 [3200], replicated
- ffn_gain_grad: float32 [1600], replicated
- gate_proj_grad: float32 [1600, 5504], P('fsdp', 'ctx')
- up_proj_grad: float32 [1600, 5504], P('fsdp', 'ctx')
- down_proj_grad: float32 [5504, 1600], P('fsdp', 'ctx')
The draws below stay inside these ranges and needn't reach their ends.
Inputs may be any that keep to these rules, and one draw needn't show every extreme that they name: `decay_rate`: decay rates, all positive.
All inputs are finite; a program needn't handle non-finite values.
Results may differ from the reference program's by a relative error of at most 0.028.
Values may be sent and summed in bfloat16 or wider, within the bound.
A program may use at most 384 MiB of HBM per device.

```python
import math
import jax
import jax.numpy as jnp
from jax import lax

D = 1600
HEADS = 25
KV_HEADS = 5
HEAD = 64
INNER = 3200
STATE = 16
CONV = 4
DT_RANK = 100
FF = 5504
WINDOW = 1024
LENGTH = 1024
SEQS = 4
KVW = 320
XW = 132


def draw_decay_rate(key, part):
    key = jax.random.fold_in(key, 7)
    pick_key, slow_key, fast_key = jax.random.split(key, 3)
    slow_share = 0.5
    slow_rates = jnp.exp(jax.random.uniform(slow_key, (INNER, STATE), jnp.float32, jnp.log(0.1 / LENGTH), jnp.log(5.0 / LENGTH)))
    fast_rates = jnp.exp(jax.random.uniform(fast_key, (INNER, STATE), jnp.float32, jnp.log(0.01), jnp.log(0.5)))
    chosen = jax.random.uniform(pick_key, (INNER, STATE), jnp.float32) < slow_share
    return jnp.where(chosen, slow_rates, fast_rates).astype(jnp.float32)


def level_of(rng, dims, cuts, least, high):
    def one(dim, blocks):
        steps = jax.random.uniform(jax.random.fold_in(jax.random.fold_in(rng, 6), dim), (blocks,), jnp.float32, least / len(cuts), high / len(cuts))
        return jnp.repeat(jnp.exp(steps), dims[dim] // blocks).reshape((-1,) + (1,) * (len(dims) - dim - 1))

    loudness = one(*cuts[0])
    for cut in cuts[1:]:
        loudness = loudness * one(*cut)
    return loudness


def gaussian(rng, extent, spread, reach, shards=(), dtype=jnp.bfloat16):
    entries = jax.random.normal(rng, extent, jnp.float32) * spread
    if len(shards) > 0:
        entries = level_of(rng, extent, shards, -0.22, 0.18) * entries
    return jnp.clip(entries, min=-reach, max=reach).astype(dtype)


def setup_inputs(seed: int = 0) -> dict:
    seeds = jax.random.split(jax.random.key(seed), 23)
    inputs = gaussian(seeds[0], (SEQS, LENGTH, D), 1.0, 6.0, ((0, 4), (1, 8)))
    cotangent = gaussian(seeds[1], (SEQS, LENGTH, D), 1.0, 6.0, ((0, 4), (1, 8)))
    norm_gain = jnp.clip(1.0 + 0.18 * jax.random.normal(seeds[2], (D,), jnp.float32), 0.1, 1.9)
    query_proj = gaussian(seeds[3], (D, D), D ** -0.5, 0.15625, ((0, 4),))
    key_proj = gaussian(seeds[4], (D, KVW), D ** -0.5, 0.15625, ((0, 4),))
    value_proj = gaussian(seeds[5], (D, KVW), D ** -0.5, 0.15625, ((0, 4),))
    attn_proj = gaussian(seeds[6], (D, D), D ** -0.5, 0.15625, ((0, 4),))
    attn_gain = jnp.clip(1.0 + 0.18 * jax.random.normal(seeds[7], (D,), jnp.float32), 0.1, 1.9)
    mixer_in = gaussian(seeds[8], (D, 2 * INNER), D ** -0.5, 0.15625, ((0, 4),))
    conv_taps = gaussian(seeds[9], (CONV, INNER), 0.5, 3.0, (), jnp.float32)
    conv_bias = gaussian(seeds[10], (INNER,), 0.5, 3.0, (), jnp.float32)
    state_proj = gaussian(seeds[11], (INNER, XW), INNER ** -0.5, 0.109375, ((0, 4),))
    step_proj = gaussian(seeds[12], (DT_RANK, INNER), DT_RANK ** -0.5, 0.625, ((0, 4),))
    step_bias = jnp.clip(jax.random.uniform(seeds[13], (INNER,), jnp.float32, -4.0, 0.0), -4.0, 0.0)
    decay_rate = draw_decay_rate(jax.random.fold_in(seeds[22], 71), 0)
    skip_gain = gaussian(seeds[15], (INNER,), 1.0, 6.0, (), jnp.float32)
    mixer_out = gaussian(seeds[16], (INNER, D), INNER ** -0.5, 0.109375, ((0, 4),))
    ssm_gain = jnp.clip(1.0 + 0.18 * jax.random.normal(seeds[17], (INNER,), jnp.float32), 0.1, 1.9)
    ffn_gain = jnp.clip(1.0 + 0.18 * jax.random.normal(seeds[18], (D,), jnp.float32), 0.1, 1.9)
    gate_proj = gaussian(seeds[19], (D, FF), D ** -0.5, 0.15625, ((0, 4),))
    up_proj = gaussian(seeds[20], (D, FF), D ** -0.5, 0.15625, ((0, 4),))
    down_proj = gaussian(seeds[21], (FF, D), FF ** -0.5, 0.078125, ((0, 4),))
    return {"inputs": inputs, "cotangent": cotangent, "norm_gain": norm_gain, "query_proj": query_proj, "key_proj": key_proj, "value_proj": value_proj, "attn_proj": attn_proj, "attn_gain": attn_gain, "mixer_in": mixer_in, "conv_taps": conv_taps, "conv_bias": conv_bias, "state_proj": state_proj, "step_proj": step_proj, "step_bias": step_bias, "decay_rate": decay_rate, "skip_gain": skip_gain, "mixer_out": mixer_out, "ssm_gain": ssm_gain, "ffn_gain": ffn_gain, "gate_proj": gate_proj, "up_proj": up_proj, "down_proj": down_proj}


@jax.custom_vjp
def low(v):
    return lax.optimization_barrier(v.astype(jnp.bfloat16)).astype(jnp.float32)

@jax.custom_vjp
def low_back(v):
    return v

def low_keep(v):
    return (low(v), None)

def low_pass(kept, grad):
    return (grad,)

def back_keep(v):
    return (v, None)

def back_low(kept, grad):
    return (low(grad),)
low.defvjp(low_keep, low_pass)
low_back.defvjp(back_keep, back_low)
epsilon = 1e-06
highest = lax.Precision.HIGHEST

def rms_scale(values):
    return lax.rsqrt(lax.optimization_barrier(jnp.mean(values * values, axis=-1, keepdims=True)) + epsilon)

def matmul(left, right):
    return jnp.dot(left, right, precision=highest)

def attend(queries, keys_in, values_in):
    length = queries.shape[0]
    row_block = min(length, 512)
    key_span = WINDOW + row_block
    padding = jnp.zeros((WINDOW,) + keys_in.shape[1:], jnp.float32)
    keys_pad = jnp.concatenate([padding, keys_in], 0)
    vals_pad = jnp.concatenate([padding, values_in], 0)

    def one_block(row_start):
        q_rows = lax.dynamic_slice_in_dim(queries, row_start, row_block, 0)
        k_rows = lax.dynamic_slice_in_dim(keys_pad, row_start, key_span, 0)
        v_rows = lax.dynamic_slice_in_dim(vals_pad, row_start, key_span, 0)
        row_ids = lax.broadcasted_iota(jnp.int32, (row_block, key_span), 0)
        col_ids = lax.broadcasted_iota(jnp.int32, (row_block, key_span), 1)
        allowed = (col_ids > row_ids) & (col_ids <= row_ids + WINDOW) & (col_ids + row_start >= WINDOW)
        raw = low_back(jnp.einsum('qhgd,khd->hgqk', q_rows, k_rows, precision=highest) * HEAD ** (-0.5))
        scores = jnp.where(allowed, raw, -1e+30)
        attn_probs = low(jax.nn.softmax(scores, axis=-1))
        return jnp.einsum('hgqk,khd->qhgd', attn_probs, v_rows, precision=highest)
    starts = (jnp.arange(length // row_block) * row_block).astype(jnp.int32)
    blocks = lax.map(jax.checkpoint(one_block), starts)
    return blocks.reshape(length, HEADS * HEAD)

def selective_scan(steps, input_mat, output_mat, drive, decay_rate):
    length = steps.shape[0]
    block_len = math.gcd(length, 64)

    def one_block(state_in, pieces):

        def one_step(carried, step_item):
            step_i, input_i, output_i, drive_i = step_item
            carried = jnp.exp(-step_i[:, None] * decay_rate) * carried + (step_i * drive_i)[:, None] * input_i[None, :]
            return (carried, lax.optimization_barrier(jnp.sum(carried * output_i[None, :], axis=1)))
        return lax.scan(one_step, state_in, pieces)

    def blocked(values):
        return values.reshape((length // block_len, block_len) + values.shape[1:])
    start_state = jnp.zeros((INNER, STATE), jnp.float32)
    unused, scan_rows = lax.scan(jax.checkpoint(one_block), start_state, (blocked(steps), blocked(input_mat), blocked(output_mat), blocked(drive)))
    return scan_rows.reshape(length, INNER)

def layer(tokens, norm_gain, query_proj, key_proj, value_proj, attn_proj, attn_gain, mixer_in, conv_taps, conv_bias, state_proj, step_proj, step_bias, decay_rate, skip_gain, mixer_out, ssm_gain, ffn_gain, gate_proj, up_proj, down_proj):
    length = tokens.shape[0]
    group_size = HEADS // KV_HEADS
    normed = low(tokens * rms_scale(tokens) * norm_gain)
    queries = low(low_back(matmul(normed, query_proj)))
    keys_all = low(low_back(matmul(normed, key_proj)))
    vals_all = low(low_back(matmul(normed, value_proj)))
    attn_out = attend(queries.reshape(length, KV_HEADS, group_size, HEAD), keys_all.reshape(length, KV_HEADS, HEAD), vals_all.reshape(length, KV_HEADS, HEAD))
    attn_out = low_back(attn_out)
    branch_attn = low(attn_out * rms_scale(attn_out) * attn_gain)
    mixed_in = low(low_back(matmul(normed, mixer_in)))
    conv_src = mixed_in[:, :INNER]
    gate_z = mixed_in[:, INNER:]
    padded_src = jnp.concatenate([jnp.zeros((CONV - 1, INNER), jnp.float32), conv_src], 0)
    conv_pre = conv_bias + sum((conv_taps[tap_index] * padded_src[tap_index:tap_index + length] for tap_index in range(CONV)))
    conv_act = low(low_back(jax.nn.silu(conv_pre)))
    projected = low_back(matmul(conv_act, state_proj))
    step_low = low(projected[:, :DT_RANK])
    input_mat = projected[:, DT_RANK:DT_RANK + STATE]
    output_mat = projected[:, DT_RANK + STATE:]
    steps = jax.nn.softplus(low_back(matmul(step_low, step_proj)) + step_bias)
    scan_out = selective_scan(steps, input_mat, output_mat, conv_act, decay_rate)
    ssm_gated = (scan_out + skip_gain * conv_act) * jax.nn.silu(gate_z)
    branch_ssm = low(ssm_gated * rms_scale(ssm_gated) * ssm_gain)
    both_branches = low_back(matmul(branch_attn, attn_proj) + matmul(branch_ssm, mixer_out))
    middle = tokens + 0.5 * both_branches
    ffn_in = low(middle * rms_scale(middle) * ffn_gain)
    gate_pre = low_back(matmul(ffn_in, gate_proj))
    up_pre = low_back(matmul(ffn_in, up_proj))
    hidden = low(jax.nn.silu(gate_pre) * up_pre)
    return middle + low_back(matmul(hidden, down_proj))

def reference(inputs, cotangent, norm_gain, query_proj, key_proj, value_proj, attn_proj, attn_gain, mixer_in, conv_taps, conv_bias, state_proj, step_proj, step_bias, decay_rate, skip_gain, mixer_out, ssm_gain, ffn_gain, gate_proj, up_proj, down_proj):
    params = tuple((item.astype(jnp.float32) for item in (norm_gain, query_proj, key_proj, value_proj, attn_proj, attn_gain, mixer_in, conv_taps, conv_bias, state_proj, step_proj, step_bias, decay_rate, skip_gain, mixer_out, ssm_gain, ffn_gain, gate_proj, up_proj, down_proj)))

    def one_sequence(totals, pieces):
        seq_tokens, seq_cot = pieces
        result, pullback = jax.vjp(layer, seq_tokens.astype(jnp.float32), *params)
        grads = pullback(seq_cot.astype(jnp.float32))
        new_totals = tuple((total + grad_item for total, grad_item in zip(totals, grads[1:])))
        return (new_totals, (result, grads[0]))
    zeros_start = tuple((jnp.zeros_like(item) for item in params))
    totals, (outputs, input_grads) = lax.scan(one_sequence, zeros_start, (inputs, cotangent))
    return (outputs, input_grads) + totals
```

```python
import functools
import jax
import jax.numpy as jnp
from jax import lax
from jax.experimental import pallas as pl
from jax.experimental.pallas import tpu as pltpu
from jax.sharding import PartitionSpec as P

LANES = 128
STATE = 16
CHUNK = 128
HEAD = 64
KV_HEADS = 5
CONV = 4
DT_RANK = 100
WINDOW = 1024
EPSILON = 1e-06
LOG2_E = 1.4426950408889634
BF16 = jnp.bfloat16


MESH = pl.DeviceIdType.MESH
VMEM_LIMIT = 56 * 1024 * 1024
IN_VMEM = pl.BlockSpec(memory_space=pltpu.VMEM)


def flip(index, bit):
    return index + (1 - 2 * ((index // (1 << bit)) % 2)) * (1 << bit)


def greet(me, bits):
    barrier = pltpu.get_barrier_semaphore()
    for bit in range(bits):
        pl.semaphore_signal(
            barrier, inc=1, device_id={"ctx": flip(me, bit)}, device_id_type=MESH
        )
    pl.semaphore_wait(barrier, bits)


def halves_of(rows):
    half = rows // 2
    return (pl.ds(0, half), pl.ds(half, rows - half))


class Copies:
    def __init__(self, axis, send_sem, recv_sem):
        self.axis, self.send_sem, self.recv_sem = axis, send_sem, recv_sem
        self.started = []
        self.count = 0

    def make(self, source, target, device):
        copy = pltpu.make_async_remote_copy(
            src_ref=source,
            dst_ref=target,
            send_sem=self.send_sem.at[self.count],
            recv_sem=self.recv_sem.at[self.count],
            device_id={self.axis: device},
            device_id_type=MESH,
        )
        self.count += 1
        return copy

    def send(self, source, target, device):
        copy = self.make(source, target, device)
        copy.start()
        self.started.append(copy)
        return copy

    def finish(self):
        for copy in self.started:
            copy.wait_send()


def gather_sems(bits):
    return 1 + 2 * sum(1 << p for p in range(bits - 1)) + 2 * ((1 << (bits - 1)) - 1)


def gather_steps(copies, bits, out_ref):
    me = lax.axis_index("ctx")
    parts = halves_of(out_ref.shape[1])
    orders = (list(range(1, bits)), list(range(bits - 1, 0, -1)))

    def send(bit, shard, part):
        at = out_ref.at[shard] if part is None else out_ref.at[shard, part]
        return copies.send(at, at, flip(me, bit))

    known = ([me], [me])
    last, flying = [], [None, None]

    def begin():
        for h in range(2):
            flying[h] = [send(orders[h][0], shard, parts[h]) for shard in known[h]]
        last.append(send(0, me, None))

    def turn(phase, h):
        bit = orders[h][phase]
        for copy in flying[h]:
            copy.wait_recv()
        fresh = [flip(shard, bit) for shard in known[h]]
        known[h].extend(fresh)
        if phase + 1 < bits - 1:
            flying[h] = [send(orders[h][phase + 1], shard, parts[h]) for shard in known[h]]
        last.extend(send(0, shard, parts[h]) for shard in fresh)

    def end():
        for copy in last:
            copy.wait_recv()

    turns = [functools.partial(turn, p, h) for p in range(bits - 1) for h in range(2)]
    return [begin] + turns + [end]


def gather_kernel(bits, x_ref, out_ref, send_sem, recv_sem):
    me = lax.axis_index("ctx")
    greet(me, bits)
    out_ref[me] = x_ref[...]
    copies = Copies("ctx", send_sem, recv_sem)
    for step in gather_steps(copies, bits, out_ref):
        step()
    copies.finish()


def ctx_bits():
    return lax.axis_size("ctx").bit_length() - 1


def params(collective_id):
    return pltpu.CompilerParams(
        collective_id=collective_id, has_side_effects=True, vmem_limit_bytes=VMEM_LIMIT
    )


def gather_shards(x, collective_id):
    bits, ctx = ctx_bits(), lax.axis_size("ctx")
    sems = pltpu.SemaphoreType.DMA((gather_sems(bits),))
    return pl.pallas_call(
        functools.partial(gather_kernel, bits),
        out_shape=jax.ShapeDtypeStruct((ctx,) + x.shape, x.dtype),
        in_specs=[IN_VMEM],
        out_specs=IN_VMEM,
        scratch_shapes=[sems, sems],
        compiler_params=params(collective_id),
        name="gather_shards",
    )(x)


def gather_tokens(x, collective_id):
    return gather_shards(x, collective_id).reshape(-1, x.shape[1])


def row_parts(rows, count):
    tiles = rows // 16
    edges = [16 * (tiles * i // count) for i in range(count)] + [rows]
    return [pl.ds(a, b - a) for a, b in zip(edges[:-1], edges[1:]) if b > a]


def line_steps(copies, out_refs, pieces):
    me, size = lax.axis_index("fsdp"), lax.axis_size("fsdp")
    plans = []
    for way in (1, -1):
        for distance in range(size - 1):
            for ref, part in pieces:
                shard = me - way * distance
                inside = jnp.logical_and(shard >= 0, shard < size)
                held = jnp.where(inside, shard, me)
                to = me + way
                go = jnp.logical_and(inside, jnp.logical_and(to >= 0, to < size))
                target = jnp.where(jnp.logical_and(to >= 0, to < size), to, me - way)
                at = out_refs[ref].at[held, part]
                plans.append((way, distance, go, copies.make(at, at, target)))
    table = {}
    for way, distance, go, copy in plans:
        table.setdefault((way, distance), []).append((go, copy))

    def begin():
        for index in range(len(pieces)):
            for way in (1, -1):
                go, copy = table[way, 0][index]
                pl.when(go)(copy.start)

    def turn(distance, index):
        for way in (1, -1):
            _, came = table[way, distance - 1][index]
            origin = me - way * distance
            pl.when(jnp.logical_and(origin >= 0, origin < size))(came.wait_recv)
            if distance < size - 1:
                go, copy = table[way, distance][index]
                pl.when(go)(copy.start)

    def end():
        for way in (1, -1):
            for distance in range(size - 1):
                for go, copy in table[way, distance]:
                    pl.when(go)(copy.wait_send)

    turns = [
        functools.partial(turn, d, i) for d in range(1, size) for i in range(len(pieces))
    ]
    return [begin] + turns, end


def front_kernel(
    bits, count, x_ref, gain_ref, top_ref, in_ref, state_ref, step_ref,
    normed_ref, tops_ref, in_out, state_out, step_out,
    ctx_send, ctx_recv, line_send, line_recv,
):
    me, row, rows = lax.axis_index("ctx"), lax.axis_index("fsdp"), lax.axis_size("fsdp")
    barrier = pltpu.get_barrier_semaphore()
    for bit in range(bits):
        pl.semaphore_signal(
            barrier, inc=1, device_id={"ctx": flip(me, bit)}, device_id_type=MESH
        )
    for to in (row - 1, row + 1):
        there = jnp.logical_and(to >= 0, to < rows)

        @pl.when(there)
        def _():
            pl.semaphore_signal(
                barrier, inc=1, device_id={"fsdp": jnp.where(there, to, row)}, device_id_type=MESH
            )

    in_out[row] = in_ref[...]
    state_out[row] = state_ref[...]
    step_out[row] = step_ref[...]
    tokens = x_ref[...].astype(jnp.float32)
    scale = lax.rsqrt(jnp.mean(tokens * tokens, axis=-1, keepdims=True) + EPSILON)
    normed_ref[me] = (tokens * scale * gain_ref[...]).astype(normed_ref.dtype)
    tops_ref[me] = top_ref[...]
    neighbours = jnp.where(row > 0, 1, 0) + jnp.where(row < rows - 1, 1, 0)
    pl.semaphore_wait(barrier, bits + neighbours)

    line = Copies("fsdp", line_send, line_recv)
    across = Copies("ctx", ctx_send, ctx_recv)
    pieces = [(0, part) for part in row_parts(in_ref.shape[0], count)]
    pieces = [(1, pl.ds(0, state_ref.shape[0])), (2, pl.ds(0, step_ref.shape[0]))] + pieces
    line_list, line_end = line_steps(line, (in_out, state_out, step_out), pieces)
    first = gather_steps(across, bits, normed_ref)
    second = gather_steps(across, bits, tops_ref)
    token_list = first[:-1] + second[:-1] + [first[-1], second[-1]]
    line_list[0]()
    token_list[0]()
    line_rest, token_rest = line_list[1:], token_list[1:]
    done = 0
    for i, step in enumerate(line_rest):
        step()
        upto = len(token_rest) * (i + 1) // len(line_rest)
        for token_step in token_rest[done:upto]:
            token_step()
        done = upto
    across.finish()
    line_end()


def front(x, gain, top, in_part, state_part, step_part, collective_id):
    bits, ctx, fsdp = ctx_bits(), lax.axis_size("ctx"), lax.axis_size("fsdp")
    count = 4
    ctx_sems = pltpu.SemaphoreType.DMA((2 * gather_sems(bits),))
    line_sems = pltpu.SemaphoreType.DMA((2 * fsdp * (count + 2),))

    def stacked(array, size):
        return jax.ShapeDtypeStruct((size,) + array.shape, array.dtype)

    return pl.pallas_call(
        functools.partial(front_kernel, bits, count),
        out_shape=[
            stacked(x, ctx), stacked(top, ctx), stacked(in_part, fsdp), stacked(state_part, fsdp),
            stacked(step_part, fsdp),
        ],
        in_specs=[IN_VMEM] * 6,
        out_specs=[IN_VMEM] * 5,
        scratch_shapes=[ctx_sems, ctx_sems, line_sems, line_sems],
        compiler_params=params(collective_id),
        name="front",
    )(x, gain, top, in_part, state_part, step_part)


def product(x, weight, trans):
    dims = (((1,), (1 if trans else 0,)), ((), ()))
    return lax.dot_general(x, weight, dims, preferred_element_type=jnp.float32)


def subsets(chosen):
    out = [()]
    for bit in chosen:
        out = out + [s + (bit,) for s in out]
    return out


def flipped(shard, flips):
    for bit in flips:
        shard = flip(shard, bit)
    return shard


class Reducer:
    def __init__(self, copies, bits, part_ref, inbox, out_ref):
        self.copies, self.bits, self.part_ref = copies, bits, part_ref
        self.inbox, self.out_ref = inbox, out_ref
        self.me = lax.axis_index("ctx")
        self.parts = halves_of(out_ref.shape[0])
        self.orders = (list(range(1, bits)), list(range(bits - 1, 0, -1)))
        self.everyone = subsets(range(1, bits))[::-1]
        self.slots = {flips: slot for slot, flips in enumerate(self.everyone)}
        self.first = {}
        self.flying = [{}, {}]

    def to_sibling(self, flips, partial):
        slot = self.slots[flips]
        self.part_ref[slot] = partial.astype(self.part_ref.dtype)
        self.first[flips] = self.copies.send(
            self.part_ref.at[slot], self.inbox[0].at[slot], flip(self.me, 0)
        )

    def pass_on(self, h, phase, flips, following):
        bit = self.orders[h][phase]
        if bit in flips:
            kept = tuple(b for b in flips if b != bit)
            following[kept] = self.copies.send(
                self.inbox[0].at[self.slots[flips], self.parts[h]],
                self.inbox[1 + phase].at[len(following), self.parts[h]],
                flip(self.me, bit),
            )

    def own(self, flips, partial):
        self.first[flips].wait_recv()
        kept_ref, slot = self.inbox[0], self.slots[flips]
        kept_ref[slot] = (partial + kept_ref[slot].astype(jnp.float32)).astype(kept_ref.dtype)
        for h in range(2):
            self.pass_on(h, 0, flips, self.flying[h])

    def finish(self):
        kept_ref = self.inbox[0]
        for phase in range(self.bits - 1):
            for h in range(2):
                part, following = self.parts[h], {}
                for box, (flips, copy) in enumerate(list(self.flying[h].items())):
                    copy.wait_recv()
                    slot = self.slots[flips]
                    total = kept_ref[slot, part].astype(jnp.float32) + self.inbox[1 + phase][
                        box, part
                    ].astype(jnp.float32)
                    if phase == self.bits - 2:
                        self.out_ref[part] = total
                    else:
                        kept_ref[slot, part] = total.astype(kept_ref.dtype)
                        self.pass_on(h, phase + 1, flips, following)
                self.flying[h] = following


def reducer_boxes(ctx, bits, rows, columns):
    boxes = [ctx // 2, ctx // 2] + [ctx // 4 >> p for p in range(bits - 1)]
    sems = boxes[0] + 2 * sum(boxes[2:])
    return [pltpu.VMEM((box, rows, columns), BF16) for box in boxes], sems


def reduce_kernel(bits, trans, *refs):
    count = len(trans)
    x_refs, w_refs, out_ref = refs[:count], refs[count : 2 * count], refs[2 * count]
    part_ref, inbox = refs[2 * count + 1], refs[2 * count + 2 : -2]
    me = lax.axis_index("ctx")
    greet(me, bits)
    copies = Copies("ctx", *refs[-2:])
    reducer = Reducer(copies, bits, part_ref, inbox, out_ref)

    def partial(flips):
        shard = flipped(me, flips)
        return sum(
            product(x_ref[shard], w_ref[...], way)
            for x_ref, w_ref, way in zip(x_refs, w_refs, trans)
        )

    for flips in reducer.everyone:
        reducer.to_sibling(flips, partial(flips + (0,)))
    for flips in reducer.everyone:
        reducer.own(flips, partial(flips))
    reducer.finish()
    copies.finish()


def reduce_products(pairs, trans, collective_id):
    ctx, bits = lax.axis_size("ctx"), ctx_bits()
    rows = pairs[0][0].shape[0] // ctx
    columns = pairs[0][1].shape[0 if trans[0] else 1]
    boxes, count = reducer_boxes(ctx, bits, rows, columns)
    sems = pltpu.SemaphoreType.DMA((count,))
    return pl.pallas_call(
        functools.partial(reduce_kernel, bits, trans),
        out_shape=jax.ShapeDtypeStruct((rows, columns), jnp.float32),
        in_specs=[IN_VMEM] * (2 * len(pairs)),
        out_specs=IN_VMEM,
        scratch_shapes=boxes + [sems, sems],
        compiler_params=params(collective_id),
        name="reduce_products",
    )(*[x.reshape(ctx, rows, -1) for x, _ in pairs], *[w for _, w in pairs])


def greet_all(me, size):
    barrier = pltpu.get_barrier_semaphore()
    for turn in range(1, size):
        pl.semaphore_signal(
            barrier, inc=1, device_id={"ctx": (me + turn) % size}, device_id_type=MESH
        )
    pl.semaphore_wait(barrier, size - 1)


def sum_kernel(size, x_ref, out_ref, inbox, send_sem, recv_sem):
    me = lax.axis_index("ctx")
    greet_all(me, size)
    copies = Copies("ctx", send_sem, recv_sem)
    come = []
    for turn in range(1, size):
        to = (me + turn) % size
        come.append(copies.send(x_ref.at[to], inbox.at[turn - 1], to))
    total = x_ref[me].astype(jnp.float32)
    for turn in range(1, size):
        come[turn - 1].wait_recv()
        total = total + inbox[turn - 1].astype(jnp.float32)
    out_ref[me] = total.astype(out_ref.dtype)
    come = [
        copies.send(out_ref.at[me], out_ref.at[me], (me + turn) % size) for turn in range(1, size)
    ]
    for copy in come:
        copy.wait_recv()
    copies.finish()


def sum_everywhere(partial, collective_id):
    ctx = lax.axis_size("ctx")
    rows, columns = partial.shape[0] // ctx, partial.shape[1]
    sems = pltpu.SemaphoreType.DMA((2 * (ctx - 1),))
    return pl.pallas_call(
        functools.partial(sum_kernel, ctx),
        out_shape=jax.ShapeDtypeStruct((ctx, rows, columns), partial.dtype),
        in_specs=[IN_VMEM],
        out_specs=IN_VMEM,
        scratch_shapes=[pltpu.VMEM((ctx - 1, rows, columns), partial.dtype), sems, sems],
        compiler_params=params(collective_id),
        name="sum_everywhere",
    )(partial.reshape(ctx, rows, columns)).reshape(partial.shape)


def total_kernel(size, x_ref, out_ref, inbox, send_sem, recv_sem):
    me = lax.axis_index("ctx")
    greet_all(me, size)
    copies = Copies("ctx", send_sem, recv_sem)
    come = [
        copies.send(x_ref, inbox.at[turn - 1], (me + turn) % size) for turn in range(1, size)
    ]
    inbox_total = x_ref[...]
    for turn in range(1, size):
        come[turn - 1].wait_recv()
        inbox_total = inbox_total + inbox[turn - 1]
    out_ref[...] = inbox_total
    copies.finish()


def total_of(rows_sum, collective_id):
    ctx = lax.axis_size("ctx")
    flat = rows_sum.reshape(-1, LANES)
    sems = pltpu.SemaphoreType.DMA((ctx - 1,))
    return pl.pallas_call(
        functools.partial(total_kernel, ctx),
        out_shape=jax.ShapeDtypeStruct(flat.shape, flat.dtype),
        in_specs=[IN_VMEM],
        out_specs=IN_VMEM,
        scratch_shapes=[pltpu.VMEM((ctx - 1,) + flat.shape, flat.dtype), sems, sems],
        compiler_params=params(collective_id),
        name="total_of",
    )(flat).reshape(rows_sum.shape)


def settle_kernel(
    bits, size, count, channel_ref, gain_ref, all_ref, sums_ref,
    row_inbox, gain_inbox, line_inbox, ctx_send, ctx_recv, line_send, line_recv,
):
    me, row = lax.axis_index("ctx"), lax.axis_index("fsdp")
    barrier = pltpu.get_barrier_semaphore()
    for turn in range(1, size):
        pl.semaphore_signal(
            barrier, inc=1, device_id={"ctx": (me + turn) % size}, device_id_type=MESH
        )
    for turn in range(1, count):
        pl.semaphore_signal(
            barrier, inc=1, device_id={"fsdp": (row + turn) % count}, device_id_type=MESH
        )
    pl.semaphore_wait(barrier, size - 1 + count - 1)
    across, line = Copies("ctx", ctx_send, ctx_recv), Copies("fsdp", line_send, line_recv)
    band = channel_ref.shape[0] // count

    def band_of(index):
        return pl.ds(pl.multiple_of(index * band, 8), band)

    rows_come = []
    for turn in range(1, count):
        to = (row + turn) % count
        rows_come.append(line.send(channel_ref.at[band_of(to)], row_inbox.at[turn - 1], to))
    gains_come = [
        across.send(gain_ref, gain_inbox.at[turn - 1], (me + turn) % size)
        for turn in range(1, size)
    ]
    total = channel_ref[band_of(row)]
    for turn in range(1, count):
        rows_come[turn - 1].wait_recv()
        total = total + row_inbox[turn - 1]
    all_ref[me, band_of(row)] = total
    at = all_ref.at[me, band_of(row)]
    bands_come = [line.send(at, at, (row + turn) % count) for turn in range(1, count)]
    total = gain_ref[...]
    for turn in range(1, size):
        gains_come[turn - 1].wait_recv()
        total = total + gain_inbox[turn - 1]
    line_inbox[0] = total
    line_come = [
        line.send(line_inbox.at[0], line_inbox.at[turn], (row + turn) % count)
        for turn in range(1, count)
    ]
    for copy in bands_come:
        copy.wait_recv()
    for step in gather_steps(across, bits, all_ref):
        step()
    total = line_inbox[0]
    for turn in range(1, count):
        line_come[turn - 1].wait_recv()
        total = total + line_inbox[turn]
    sums_ref[...] = total
    across.finish()
    line.finish()


def settle_small(channel, gains, collective_id):
    ctx, fsdp, bits = lax.axis_size("ctx"), lax.axis_size("fsdp"), ctx_bits()
    ctx_sems = pltpu.SemaphoreType.DMA((ctx - 1 + gather_sems(bits),))
    line_sems = pltpu.SemaphoreType.DMA((3 * (fsdp - 1),))
    rows, columns = channel.shape
    return pl.pallas_call(
        functools.partial(settle_kernel, bits, ctx, fsdp),
        out_shape=[
            jax.ShapeDtypeStruct((ctx, rows, columns), jnp.float32),
            jax.ShapeDtypeStruct(gains.shape, jnp.float32),
        ],
        in_specs=[IN_VMEM] * 2,
        out_specs=[IN_VMEM] * 2,
        scratch_shapes=[
            pltpu.VMEM((fsdp - 1, rows // fsdp, columns), jnp.float32),
            pltpu.VMEM((ctx - 1,) + gains.shape, jnp.float32),
            pltpu.VMEM((fsdp,) + gains.shape, jnp.float32),
            ctx_sems, ctx_sems, line_sems, line_sems,
        ],
        compiler_params=params(collective_id),
        name="settle_small",
    )(channel, gains)


def plane_gather(copies, out_ref):
    me = lax.axis_index("ctx")
    parts = halves_of(out_ref.shape[1])
    held = {}

    def send(name, bit, flips, part=None):
        shard = flipped(me, flips)
        at = out_ref.at[shard] if part is None else out_ref.at[shard, part]
        held[name] = copies.send(at, at, flip(me, bit))

    def start():
        for bit in (1, 2, 0):
            send(("own", bit), bit, ())

    def forward():
        held["own", 1].wait_recv()
        send(("corner", 2), 2, (1,), parts[0])
        held["own", 2].wait_recv()
        send(("corner", 1), 1, (2,), parts[1])
        send(("core", (1,)), 0, (1,))
        send(("core", (2,)), 0, (2,))

    def corner():
        held["corner", 2].wait_recv()
        held["corner", 1].wait_recv()
        send(("core", (1, 2)), 0, (1, 2))

    def wait(flips):
        held["core", flips].wait_recv() if flips else held["own", 0].wait_recv()

    return start, forward, corner, wait


def ffn_kernel(
    x_ref, top_ref, pair_w, down_w,
    all_ref, hidden_ref, pair_ref, out_ref, grad_ref,
    own_ref, part_out, part_grad, *rest,
):
    bits = 3
    boxes = (len(rest) - 2) // 2
    inbox_out, inbox_grad = rest[:boxes], rest[boxes : 2 * boxes]
    me = lax.axis_index("ctx")
    greet(me, bits)
    all_ref[me] = x_ref[...]
    copies = Copies("ctx", *rest[-2:])
    start, forward, corner, wait = plane_gather(copies, all_ref)
    reducers = (
        Reducer(copies, bits, part_grad, inbox_grad, grad_ref),
        Reducer(copies, bits, part_out, inbox_out, out_ref),
    )
    rows, model = x_ref.shape
    hid = hidden_ref.shape[2]
    core = me % 2

    def work(slot, flips):
        first = 2 * (flipped(me, flips) // 2)
        pair = pl.ds(first, 2)
        x = all_ref[pair].reshape(2 * rows, model)
        pre = product(x, pair_w[...], False)
        gate, up = pre[:, :hid], pre[:, hid:]
        logistic = jax.nn.sigmoid(gate)
        gate_silu = gate * logistic
        hidden = (gate_silu * up).astype(BF16)
        hidden_ref[pair] = hidden.reshape(2, rows, hid)
        top = top_ref[pair].reshape(2 * rows, model)
        grad_hidden = product(top, down_w[...], True)
        slope = logistic * (1.0 + gate * (1.0 - logistic))
        pair_ref[pair, :, :hid] = (grad_hidden * up * slope).astype(BF16).reshape(2, rows, hid)
        pair_ref[pair, :, hid:] = (grad_hidden * gate_silu).astype(BF16).reshape(2, rows, hid)
        grads = pair_ref[pair].reshape(2 * rows, 2 * hid)
        for index, value in enumerate(
            (product(grads, pair_w[...], True), product(hidden, down_w[...], False))
        ):
            low, high = value[:rows], value[rows:]
            own_ref[index, slot] = jnp.where(core == 0, low, high)
            reducers[index].to_sibling(flips, jnp.where(core == 0, high, low))

    def settle(slot, flips):
        for index, reducer in enumerate(reducers):
            reducer.own(flips, own_ref[index, slot])

    start()
    wait(())
    work(0, ())
    forward()
    wait((1,))
    work(1, (1,))
    settle(0, ())
    corner()
    wait((2,))
    work(2, (2,))
    settle(1, (1,))
    wait((1, 2))
    work(3, (1, 2))
    settle(2, (2,))
    settle(3, (1, 2))
    for reducer in reducers:
        reducer.finish()
    copies.finish()


def ffn_both_ways(ffn_in, top, pair_full, down_full, collective_id):
    ctx, bits = lax.axis_size("ctx"), ctx_bits()
    rows, model = ffn_in.shape
    hid = down_full.shape[0]
    boxes, count = reducer_boxes(ctx, bits, rows, model)
    sems = pltpu.SemaphoreType.DMA((2 * count + 8,))
    all_rows, hidden, pair, out, grad = pl.pallas_call(
        ffn_kernel,
        out_shape=[
            jax.ShapeDtypeStruct((ctx, rows, model), BF16),
            jax.ShapeDtypeStruct((ctx, rows, hid), BF16),
            jax.ShapeDtypeStruct((ctx, rows, 2 * hid), BF16),
            jax.ShapeDtypeStruct((rows, model), jnp.float32),
            jax.ShapeDtypeStruct((rows, model), jnp.float32),
        ],
        in_specs=[IN_VMEM] * 4,
        out_specs=[IN_VMEM] * 5,
        scratch_shapes=[pltpu.VMEM((2, ctx // 2, rows, model), jnp.float32), boxes[0], boxes[0]]
        + boxes[1:]
        + boxes[1:]
        + [sems, sems],
        compiler_params=params(collective_id),
        name="ffn_both_ways",
    )(ffn_in, top.reshape(ctx, rows, model), pair_full, down_full)
    flat = [a.reshape(ctx * rows, -1) for a in (all_rows, hidden, pair)]
    return flat[0], flat[1], flat[2], out, grad


def scan_fwd_kernel(steps_ref, drive_ref, in_ref, out_ref, rate_ref, scan_ref, prev_ref, state_ref):
    tiles = steps_ref.shape[1] // LANES
    chunk = steps_ref.shape[0]

    @pl.when(pl.program_id(0) == 0)
    def _():
        state_ref[...] = jnp.zeros_like(state_ref)

    rates = [rate_ref[:, j * LANES : (j + 1) * LANES] for j in range(tiles)]

    def group(g, states):
        states = list(states)
        base = pl.multiple_of(g * 8, 8)
        for j in range(tiles):
            lanes = slice(j * LANES, (j + 1) * LANES)
            step_8 = steps_ref[pl.ds(base, 8), lanes]
            drive_8 = step_8 * drive_ref[pl.ds(base, 8), lanes]
            rows = []
            for t in range(8):
                in_t = in_ref[base + t]
                out_t = out_ref[base + t]
                decay = jnp.exp2(step_8[t : t + 1] * rates[j])
                prev_ref[base + t, :, lanes] = states[j]
                states[j] = decay * states[j] + drive_8[t : t + 1] * in_t
                rows.append(jnp.sum(states[j] * out_t, axis=0, keepdims=True))
            scan_ref[pl.ds(base, 8), lanes] = jnp.concatenate(rows, 0)
        return tuple(states)

    start = tuple(state_ref[:, j * LANES : (j + 1) * LANES] for j in range(tiles))
    final = lax.fori_loop(0, chunk // 8, group, start)
    for j in range(tiles):
        state_ref[:, j * LANES : (j + 1) * LANES] = final[j]


def scan_fwd(steps, drive, in_b, out_b, rates):
    length, width = steps.shape
    chunk = CHUNK
    row = pl.BlockSpec((chunk, width), lambda i: (i, 0))
    mat = pl.BlockSpec((chunk, STATE, LANES), lambda i: (i, 0, 0))
    rate = pl.BlockSpec((STATE, width), lambda i: (0, 0))
    return pl.pallas_call(
        scan_fwd_kernel,
        grid=(length // chunk,),
        in_specs=[row, row, mat, mat, rate],
        out_specs=[row, pl.BlockSpec((chunk, STATE, width), lambda i: (i, 0, 0))],
        out_shape=[
            jax.ShapeDtypeStruct((length, width), jnp.float32),
            jax.ShapeDtypeStruct((length, STATE, width), jnp.float32),
        ],
        scratch_shapes=[pltpu.VMEM((STATE, width), jnp.float32)],
        compiler_params=pltpu.CompilerParams(vmem_limit_bytes=48 * 1024 * 1024),
        name="scan_forward",
    )(steps, drive, in_b, out_b, rates)


def scan_bwd_kernel(
    steps_ref, drive_ref, grad_ref, in_ref, out_ref, rate_ref, prev_ref,
    gstep_ref, gdrive_ref, gin_ref, gout_ref, grate_ref,
    carry_ref, pin_ref, pout_ref,
):
    tiles = steps_ref.shape[1] // LANES
    chunk = steps_ref.shape[0]

    @pl.when(pl.program_id(0) == 0)
    def _():
        carry_ref[...] = jnp.zeros_like(carry_ref)
        grate_ref[...] = jnp.zeros_like(grate_ref)

    for j in range(tiles):
        lanes = slice(j * LANES, (j + 1) * LANES)
        rates = rate_ref[:, lanes]

        def group(k, kept):
            carry, acc = kept
            base = pl.multiple_of(chunk - 8 - k * 8, 8)
            step_8 = steps_ref[pl.ds(base, 8), lanes]
            x_8 = drive_ref[pl.ds(base, 8), lanes]
            drive_8 = step_8 * x_8
            grad_8 = grad_ref[pl.ds(base, 8), lanes]
            held_rows, dot_rows = [None] * 8, [None] * 8
            for t in range(7, -1, -1):
                in_t = in_ref[base + t]
                out_t = out_ref[base + t]
                previous = prev_ref[base + t, :, lanes]
                step_t = step_8[t : t + 1]
                drive_t = drive_8[t : t + 1]
                grad_t = grad_8[t : t + 1]
                decay = jnp.exp2(step_t * rates)
                adjoint = grad_t * out_t + carry
                carry = decay * adjoint
                held = carry * previous
                state = decay * previous + drive_t * in_t
                acc = acc + held * step_t
                held_rows[t] = jnp.sum(held * rates, axis=0, keepdims=True)
                dot_rows[t] = jnp.sum(adjoint * in_t, axis=0, keepdims=True)
                part_in = adjoint * drive_t
                part_out = state * grad_t
                at = pl.ds(pl.multiple_of((base + t) * STATE, STATE), STATE)
                if j == 0:
                    pin_ref[at] = part_in
                    pout_ref[at] = part_out
                else:
                    pin_ref[at] += part_in
                    pout_ref[at] += part_out
            held_8 = jnp.concatenate(held_rows, 0)
            dot_8 = jnp.concatenate(dot_rows, 0)
            gstep_ref[pl.ds(base, 8), lanes] = held_8 * 0.6931471805599453 + x_8 * dot_8
            gdrive_ref[pl.ds(base, 8), lanes] = step_8 * dot_8
            return carry, acc

        carry, acc = lax.fori_loop(
            0, chunk // 8, group, (carry_ref[:, lanes], grate_ref[:, lanes])
        )
        carry_ref[:, lanes] = carry
        grate_ref[:, lanes] = acc
    ones = jnp.ones((8, LANES), jnp.float32)
    dims = (((1,), (1,)), ((), ()))
    gin_ref[0] = lax.dot_general(ones, pin_ref[...], dims, preferred_element_type=jnp.float32)
    gout_ref[0] = lax.dot_general(ones, pout_ref[...], dims, preferred_element_type=jnp.float32)


def scan_bwd(steps, drive, grad, in_b, out_b, rates, previous):
    length, width = steps.shape
    chunk = CHUNK
    count = length // chunk
    row = pl.BlockSpec((chunk, width), lambda i: (count - 1 - i, 0))
    mat = pl.BlockSpec((chunk, STATE, LANES), lambda i: (count - 1 - i, 0, 0))
    rate = pl.BlockSpec((STATE, width), lambda i: (0, 0))
    red = pl.BlockSpec((1, 8, chunk * STATE), lambda i: (count - 1 - i, 0, 0))
    gstep, gdrive, gin, gout, grate = pl.pallas_call(
        scan_bwd_kernel,
        grid=(count,),
        in_specs=[row, row, row, mat, mat, rate,
                  pl.BlockSpec((chunk, STATE, width), lambda i: (count - 1 - i, 0, 0))],
        out_specs=[row, row, red, red, rate],
        out_shape=[
            jax.ShapeDtypeStruct((length, width), jnp.float32),
            jax.ShapeDtypeStruct((length, width), jnp.float32),
            jax.ShapeDtypeStruct((count, 8, chunk * STATE), jnp.float32),
            jax.ShapeDtypeStruct((count, 8, chunk * STATE), jnp.float32),
            jax.ShapeDtypeStruct((STATE, width), jnp.float32),
        ],
        scratch_shapes=[
            pltpu.VMEM((STATE, width), jnp.float32),
            pltpu.VMEM((chunk * STATE, LANES), jnp.float32),
            pltpu.VMEM((chunk * STATE, LANES), jnp.float32),
        ],
        compiler_params=pltpu.CompilerParams(vmem_limit_bytes=48 * 1024 * 1024),
        name="scan_backward",
    )(steps, drive, grad, in_b, out_b, rates, previous)
    return (gstep, gdrive, gin[:, 0].reshape(length, STATE), gout[:, 0].reshape(length, STATE), grate)


def matmul(left, right):
    return jnp.dot(left, right, preferred_element_type=jnp.float32)


def left_trans(left, right):
    return lax.dot_general(
        left, right, (((0,), (0,)), ((), ())), preferred_element_type=jnp.float32
    )


def right_trans(left, right):
    return lax.dot_general(
        left, right, (((1,), (1,)), ((), ())), preferred_element_type=jnp.float32
    )


def rms_scale(values):
    return lax.rsqrt(jnp.mean(values * values, axis=-1, keepdims=True) + EPSILON)


def norm_back(grad_out, values, scale_in, gain_in):
    scaled = grad_out * gain_in
    grad_in = scale_in * scaled - values * scale_in**3 * jnp.mean(
        scaled * values, axis=-1, keepdims=True
    )
    return (grad_in, jnp.sum(grad_out * values * scale_in, axis=0))


def silu_slope(values):
    logistic = jax.nn.sigmoid(values)
    return logistic * (1.0 + values * (1.0 - logistic))


def unit_count(width, ctx, fsdp):
    return ctx if width % (ctx * ctx) == 0 and ctx % fsdp == 0 else fsdp


def my_columns(array, units):
    span = array.shape[1] // units
    width = span // lax.axis_size("ctx")
    start = lax.axis_index("ctx") * width
    return [
        lax.dynamic_slice_in_dim(array, unit * span + start, width, 1) for unit in range(units)
    ]


def my_rows(array, units):
    span = array.shape[0] // units
    width = span // lax.axis_size("ctx")
    start = lax.axis_index("ctx") * width
    return [
        lax.dynamic_slice_in_dim(array, unit * span + start, width, 0) for unit in range(units)
    ]


def block_columns(array):
    width = array.shape[1] // lax.axis_size("ctx")
    return lax.dynamic_slice_in_dim(array, lax.axis_index("ctx") * width, width, 1)


def over_fsdp(array):
    return lax.all_gather(array, "fsdp", axis=0, tiled=True)


def to_blocks(array, units):
    ctx = lax.axis_size("ctx")
    rows = array.shape[0]
    width = array.shape[1] // units
    repeat = ctx // units
    pieces = array.reshape(rows, units, width).transpose(1, 0, 2)
    slots = jnp.repeat(pieces, repeat, axis=0) if repeat > 1 else pieces
    got = lax.all_to_all(slots, "ctx", 0, 0, tiled=True)
    if repeat > 1:
        first = units * lax.rem(lax.axis_index("ctx"), repeat)
        got = lax.dynamic_slice_in_dim(got, first, units, 0)
    return got.transpose(1, 0, 2).reshape(rows, units * width).astype(jnp.float32)


def rows_to_blocks(array, units):
    ctx = lax.axis_size("ctx")
    rows, columns = array.shape
    pieces = array.reshape(rows, ctx, columns // ctx).transpose(1, 0, 2)
    got = lax.all_to_all(pieces, "ctx", 0, 0, tiled=True)
    got = got.reshape(ctx, units, rows // units, columns // ctx).transpose(1, 0, 2, 3)
    return got.reshape(ctx * rows, columns // ctx).astype(jnp.float32)


def scatter_fsdp(*gradients):
    fsdp = lax.axis_size("fsdp")
    parts = [g.astype(BF16).reshape(fsdp, -1, g.shape[1]) for g in gradients]
    sizes = [part.shape[1] for part in parts]
    pad = -sum(sizes) % 16
    if pad:
        parts.append(jnp.zeros((fsdp, pad, gradients[0].shape[1]), BF16))
    joined = jnp.concatenate(parts, 1) if len(parts) > 1 else parts[0]
    joined = joined.reshape(-1, joined.shape[2])
    out = lax.psum_scatter(joined, "fsdp", scatter_dimension=0, tiled=True)
    starts = [sum(sizes[:i]) for i in range(len(sizes))]
    return [out[start : start + size] for start, size in zip(starts, sizes)]


def body(
    inputs,
    cotangent,
    norm_gain,
    query_proj,
    key_proj,
    value_proj,
    attn_proj,
    attn_gain,
    mixer_in,
    conv_taps,
    conv_bias,
    state_proj,
    step_proj,
    step_bias,
    decay_rate,
    skip_gain,
    mixer_out,
    ssm_gain,
    ffn_gain,
    gate_proj,
    up_proj,
    down_proj,
):
    ctx, fsdp = lax.axis_size("ctx"), lax.axis_size("fsdp")
    place = lax.axis_index("ctx")
    tokens = inputs[0].astype(jnp.float32)
    own, model = tokens.shape
    length = own * ctx
    inner = conv_bias.shape[0]
    mine = inner // ctx
    kv_mine = key_proj.shape[1] // ctx
    q_mine = query_proj.shape[1] // ctx
    hidden_units = unit_count(gate_proj.shape[1], ctx, fsdp)
    hidden_rows = hidden_units // fsdp
    hid = gate_proj.shape[1] // ctx
    group_size = query_proj.shape[1] // key_proj.shape[1]
    score_scale = HEAD ** (-0.5)

    src_part = jnp.concatenate(my_columns(mixer_in[:, :inner], fsdp), 1)
    state_part = my_rows(state_proj, 1)[0]
    step_part = jnp.concatenate(my_columns(step_proj, fsdp), 1)
    state_rows, step_rows = state_part.shape[0], step_part.shape[0]
    normed_all, grad_top, src_full, state_full, step_full = front(
        inputs[0],
        norm_gain[None],
        cotangent[0],
        src_part,
        jnp.pad(state_part, ((0, -state_rows % 16), (0, 0))),
        jnp.pad(step_part, ((0, -step_rows % 16), (0, 0))),
        0,
    )
    normed_all = normed_all.reshape(length, model)
    grad_top = grad_top.reshape(length, model)
    src_full = src_full.reshape(model, -1)
    state_full = state_full[:, :state_rows].reshape(-1, state_proj.shape[1])
    step_full = step_full[:, :step_rows].reshape(-1, mine)
    norm_scale = rms_scale(tokens)

    attn_pad = -attn_proj.shape[0] % ctx
    attn_rows_mine = (attn_proj.shape[0] + attn_pad) // ctx
    (
        query_proj, key_proj, value_proj, mixer_late, attn_proj, mixer_out, down_proj, gate_proj,
        up_proj, normed_all,
    ) = lax.optimization_barrier(
        (
            query_proj, key_proj, value_proj, mixer_in, attn_proj, mixer_out, down_proj, gate_proj,
            up_proj, normed_all,
        )
    )
    early_part = jnp.concatenate(
        [block_columns(query_proj), block_columns(key_proj), block_columns(value_proj)]
        + my_columns(mixer_late[:, inner:], fsdp),
        1,
    )
    out_part = jnp.concatenate(
        my_rows(jnp.pad(attn_proj, ((0, attn_pad), (0, 0))), 1) + my_rows(mixer_out, 1), 0
    )
    down_part = jnp.concatenate(my_rows(down_proj, hidden_rows), 0)
    ffn_part = jnp.concatenate(
        my_columns(gate_proj, hidden_units) + my_columns(up_proj, hidden_units), 1
    )
    rows_part = jnp.concatenate([out_part, down_part], 0)
    early_full = over_fsdp(early_part)
    rows_full = lax.all_gather(rows_part, "fsdp", axis=0)
    ffn_full = over_fsdp(ffn_part)
    attn_full = rows_full[:, :attn_rows_mine].reshape(-1, model)
    mixout_full = rows_full[:, attn_rows_mine : out_part.shape[0]].reshape(-1, model)
    down_full = rows_full[:, out_part.shape[0] :].reshape(-1, model)
    attn_width = attn_full.shape[0]

    def mine_of(vector):
        return jnp.concatenate(my_columns(vector.reshape(-1, inner), fsdp), 1)

    taps, bias, skip, gain_ssm, bias_step = (
        mine_of(conv_taps),
        mine_of(conv_bias),
        mine_of(skip_gain),
        mine_of(ssm_gain),
        mine_of(step_bias),
    )
    rates = jnp.concatenate(
        [
            lax.dynamic_slice_in_dim(
                decay_rate, unit * (inner // fsdp) + place * (mine // fsdp), mine // fsdp, 0
            )
            for unit in range(fsdp)
        ],
        0,
    ).T
    pad = -mine % LANES

    def padded(values):
        return jnp.pad(values, ((0, 0), (0, pad)))

    conv_src = matmul(normed_all, src_full).astype(BF16)

    padded_src = jnp.concatenate(
        [jnp.zeros((CONV - 1, mine), jnp.float32), conv_src.astype(jnp.float32)], 0
    )
    conv_pre = bias + sum(taps[tap][None] * padded_src[tap : tap + length] for tap in range(CONV))
    conv_act = jax.nn.silu(conv_pre).astype(BF16)
    conv_vals = conv_act.astype(jnp.float32)
    projected = sum_everywhere(matmul(conv_act, state_full).astype(BF16), 2).astype(jnp.float32)
    step_low = projected[:, :DT_RANK].astype(BF16)
    input_mat = projected[:, DT_RANK : DT_RANK + STATE]
    output_mat = projected[:, DT_RANK + STATE :]
    step_pre = matmul(step_low, step_full) + bias_step
    steps_dt = jax.nn.softplus(step_pre)
    in_b = jnp.broadcast_to(input_mat[:, :, None], (length, STATE, LANES))
    out_b = jnp.broadcast_to(output_mat[:, :, None], (length, STATE, LANES))
    rates_log2 = padded(-LOG2_E * rates)
    steps_pad, vals_pad = padded(steps_dt), padded(conv_vals)
    scan_out, states = scan_fwd(steps_pad, vals_pad, in_b, out_b, rates_log2)
    scan_out = scan_out[:, :mine]

    projected_in = matmul(normed_all, early_full).astype(BF16)
    queries = lax.all_to_all(projected_in[:, :q_mine], "ctx", 0, 1, tiled=True)
    keyvals = gather_shards(projected_in[:, q_mine : q_mine + 2 * kv_mine], 1)
    keys_all = keyvals[:, :, :kv_mine].transpose(1, 0, 2).reshape(length, KV_HEADS, HEAD)
    vals_all = keyvals[:, :, kv_mine:].transpose(1, 0, 2).reshape(length, KV_HEADS, HEAD)
    gate_z = projected_in[:, q_mine + 2 * kv_mine :].astype(jnp.float32)
    heads_q = queries.reshape(own, KV_HEADS, group_size, HEAD)
    row_ids = place * own + lax.broadcasted_iota(jnp.int32, (own, length), 0)
    col_ids = lax.broadcasted_iota(jnp.int32, (own, length), 1)
    allowed = (col_ids <= row_ids) & (col_ids > row_ids - WINDOW)

    def scores_of():
        raw = jnp.einsum("qhgd,khd->hgqk", heads_q, keys_all, preferred_element_type=jnp.float32)
        return jnp.where(allowed, raw * score_scale, -1e30)

    scores = scores_of()
    row_top = jnp.max(scores, axis=-1, keepdims=True)
    log_total = row_top + jnp.log(jnp.sum(jnp.exp(scores - row_top), axis=-1, keepdims=True))
    probs = jnp.exp(scores - log_total)
    probs_bf = probs.astype(BF16)
    attn_rows = jnp.einsum(
        "hgqk,khd->qhgd", probs_bf, vals_all, preferred_element_type=jnp.float32
    ).reshape(own, -1)
    attn_scale = rms_scale(attn_rows)
    branch_attn = (attn_rows * attn_scale * attn_gain).astype(BF16)

    def attn_to_channels(values):
        parts = jnp.pad(values.reshape(own, fsdp, -1), ((0, 0), (0, 0), (0, attn_pad)))
        parts = parts.reshape(own, fsdp, ctx, -1).transpose(2, 0, 1, 3).reshape(ctx, own, -1)
        return lax.all_to_all(parts, "ctx", 0, 0, tiled=True).reshape(length, -1)

    def attn_to_tokens(values):
        parts = values.reshape(ctx, own, -1)
        got = lax.all_to_all(parts, "ctx", 0, 0, tiled=True)
        got = got.reshape(ctx, own, fsdp, -1).transpose(1, 2, 0, 3).reshape(own, fsdp, -1)
        return got[:, :, : attn_proj.shape[0]].reshape(own, -1)

    branch_attn_c = attn_to_channels(branch_attn)

    ssm_raw = scan_out + skip * conv_vals
    gate_act = jax.nn.silu(gate_z)
    ssm_gated = ssm_raw * gate_act
    square = total_of(jnp.sum(ssm_gated * ssm_gated, axis=-1), 3)
    ssm_scale = lax.rsqrt(square / inner + EPSILON)[:, None]
    branch_ssm = (ssm_gated * ssm_scale * gain_ssm).astype(BF16)
    middle = tokens + 0.5 * reduce_products(
        [(branch_attn_c, attn_full), (branch_ssm, mixout_full)], (False, False), 4
    )
    ffn_scale = rms_scale(middle)
    ffn_in = (middle * ffn_scale * ffn_gain).astype(BF16)
    if ctx == 8:
        ffn_all, hidden, grad_pair, ffn_out, grad_ffn_in = ffn_both_ways(
            ffn_in, grad_top, ffn_full, down_full, 5
        )
    else:
        ffn_all = gather_tokens(ffn_in, 5)
        pre = matmul(ffn_all, ffn_full)
        gate_pre, up_pre = pre[:, :hid], pre[:, hid:]
        gate_silu = jax.nn.silu(gate_pre)
        hidden = (gate_silu * up_pre).astype(BF16)
        ffn_out = reduce_products([(hidden, down_full)], (False,), 6)
        grad_hidden = right_trans(grad_top, down_full)
        grad_gate = (grad_hidden * up_pre * silu_slope(gate_pre)).astype(BF16)
        grad_up = (grad_hidden * gate_silu).astype(BF16)
        grad_pair = jnp.concatenate([grad_gate, grad_up], 1)
        grad_ffn_in = reduce_products([(grad_pair, ffn_full)], (True,), 7)
    output = middle + ffn_out

    down_dw = left_trans(hidden, grad_top).astype(BF16)
    pair_dw = left_trans(ffn_all, grad_pair).astype(BF16)
    grad_ffn_in, down_dw, pair_dw = lax.optimization_barrier((grad_ffn_in, down_dw, pair_dw))
    (down_grad,) = scatter_fsdp(down_dw)
    (pair_grad,) = scatter_fsdp(pair_dw)
    grad_middle, grad_ffn_gain = norm_back(grad_ffn_in, middle, ffn_scale, ffn_gain)
    grad_middle = grad_middle + cotangent[0].astype(jnp.float32)
    grad_branch = (0.5 * grad_middle).astype(BF16)
    branch_all = gather_tokens(grad_branch, 8)
    branch_all, down_grad = lax.optimization_barrier((branch_all, down_grad))
    attn_grad, mixout_grad = scatter_fsdp(
        left_trans(branch_attn_c, branch_all), left_trans(branch_ssm, branch_all)
    )

    grad_attn = attn_to_tokens(right_trans(branch_all, attn_full).astype(BF16)).astype(jnp.float32)
    grad_attn_raw, grad_attn_gain = norm_back(grad_attn, attn_rows, attn_scale, attn_gain)
    grad_heads = grad_attn_raw.astype(BF16).reshape(own, KV_HEADS, group_size, HEAD)
    grad_probs = jnp.einsum(
        "qhgd,khd->hgqk", grad_heads, vals_all, preferred_element_type=jnp.float32
    )
    row_dot = jnp.sum(probs * grad_probs, axis=-1, keepdims=True)
    grad_scores = (probs * (grad_probs - row_dot)).astype(BF16)
    grad_queries = score_scale * jnp.einsum(
        "hgqk,khd->qhgd", grad_scores, keys_all, preferred_element_type=jnp.float32
    ).reshape(own, -1)
    grad_keys = score_scale * jnp.einsum(
        "hgqk,qhgd->khd", grad_scores, heads_q, preferred_element_type=jnp.float32
    )
    grad_vals = jnp.einsum(
        "hgqk,qhgd->khd", probs_bf, grad_heads, preferred_element_type=jnp.float32
    )
    grad_queries = lax.all_to_all(
        grad_queries.astype(BF16).reshape(own, ctx, -1).transpose(1, 0, 2), "ctx", 0, 0, tiled=True
    ).reshape(length, -1)
    grad_kv = jnp.concatenate(
        [
            grad_keys.reshape(length, ctx, kv_mine).transpose(1, 0, 2),
            grad_vals.reshape(length, ctx, kv_mine).transpose(1, 0, 2),
        ],
        2,
    ).astype(BF16)
    grad_kv = jnp.sum(
        lax.all_to_all(grad_kv, "ctx", 0, 0, tiled=True).astype(jnp.float32), axis=0
    ).astype(BF16)

    grad_norm = right_trans(branch_all, mixout_full)
    grad_ssm_gain = jnp.sum(grad_norm * ssm_gated * ssm_scale, axis=0)
    grad_norm, pair_grad = lax.optimization_barrier((grad_norm, pair_grad))
    scaled = grad_norm * gain_ssm
    mean_dot = total_of(jnp.sum(scaled * ssm_gated, axis=-1), 9)[:, None] / inner
    grad_gated = ssm_scale * scaled - ssm_gated * ssm_scale**3 * mean_dot
    grad_scan = grad_gated * gate_act
    grad_gate_z = grad_gated * ssm_raw * silu_slope(gate_z)
    grad_skip = jnp.sum(grad_scan * conv_vals, axis=0)
    grad_gate_bf = grad_gate_z.astype(BF16)
    grad_early = jnp.concatenate([grad_queries, grad_kv, grad_gate_bf], 1)
    (early_grad,) = scatter_fsdp(left_trans(normed_all, grad_early))
    grad_steps, grad_drive, grad_input_mat, grad_output_mat, grad_rate = scan_bwd(
        steps_pad, vals_pad, padded(grad_scan), in_b, out_b, rates_log2, states
    )
    grad_steps, attn_grad, mixout_grad = lax.optimization_barrier(
        (grad_steps, attn_grad, mixout_grad)
    )
    grad_steps, grad_drive, grad_rate = (
        grad_steps[:, :mine],
        grad_drive[:, :mine],
        -grad_rate[:, :mine],
    )
    grad_pre_full = grad_steps * jax.nn.sigmoid(step_pre)
    grad_step_bias = jnp.sum(grad_pre_full, axis=0)
    grad_pre = grad_pre_full.astype(BF16)
    step_dw = left_trans(step_low, grad_pre)
    grad_projected = sum_everywhere(
        jnp.concatenate(
            [right_trans(grad_pre, step_full), grad_input_mat, grad_output_mat], 1
        ).astype(BF16),
        10,
    )
    grad_state_proj = left_trans(conv_act, grad_projected)
    grad_conv_act = (
        right_trans(grad_projected, state_full) + grad_scan * skip + grad_drive
    ).astype(BF16)
    grad_conv_act, early_grad = lax.optimization_barrier((grad_conv_act, early_grad))
    grad_conv = grad_conv_act.astype(jnp.float32) * silu_slope(conv_pre)
    grad_conv_bias = jnp.sum(grad_conv, axis=0)
    grad_taps = jnp.stack(
        [jnp.sum(grad_conv * padded_src[tap : tap + length], axis=0) for tap in range(CONV)]
    )
    conv_tail = jnp.concatenate([grad_conv, jnp.zeros((CONV - 1, mine), jnp.float32)], 0)
    grad_src = sum(
        taps[tap][None] * conv_tail[CONV - 1 - tap : CONV - 1 - tap + length]
        for tap in range(CONV)
    )
    grad_src = grad_src.astype(BF16)
    src_grad, step_grad = scatter_fsdp(left_trans(normed_all, grad_src), step_dw)
    grad_normed = reduce_products(
        [(grad_early, early_full), (grad_src, src_full)], (True, True), 11
    )
    grad_tokens, grad_norm_gain = norm_back(grad_normed, tokens, norm_scale, norm_gain)
    grad_tokens = grad_tokens + grad_middle

    channel = jnp.concatenate(
        [
            grad_taps,
            jnp.stack([grad_conv_bias, grad_step_bias, grad_skip, grad_ssm_gain]),
            grad_rate,
            grad_state_proj.T,
        ],
        0,
    )
    gains = jnp.stack([grad_norm_gain, grad_attn_gain, grad_ffn_gain])
    channel, gains = settle_small(
        jnp.pad(channel, ((0, -channel.shape[0] % (8 * fsdp)), (0, 0))),
        jnp.pad(gains, ((0, 5), (0, 0))),
        12,
    )
    channel = channel.reshape(ctx, -1, fsdp, mine // fsdp).transpose(1, 2, 0, 3)
    channel = channel.reshape(-1, inner)
    sum_norm_gain, sum_attn_gain, sum_ffn_gain = gains[0], gains[1], gains[2]
    pair_blocks = to_blocks(
        jnp.concatenate(
            [
                pair_grad[:, :hid].reshape(-1, hidden_units, hid // hidden_units),
                pair_grad[:, hid:].reshape(-1, hidden_units, hid // hidden_units),
            ],
            0,
        ).reshape(-1, hid),
        hidden_units,
    )
    half = pair_grad.shape[0]
    return (
        output[None],
        grad_tokens[None],
        sum_norm_gain,
        early_grad[:, :q_mine].astype(jnp.float32),
        early_grad[:, q_mine : q_mine + kv_mine].astype(jnp.float32),
        early_grad[:, q_mine + kv_mine : q_mine + 2 * kv_mine].astype(jnp.float32),
        rows_to_blocks(attn_grad, 1)[: attn_proj.shape[0]],
        sum_attn_gain,
        to_blocks(jnp.concatenate([src_grad, early_grad[:, q_mine + 2 * kv_mine :]], 1), 2 * fsdp),
        channel[:CONV],
        channel[CONV],
        channel[CONV + 4 + STATE : CONV + 4 + STATE + state_proj.shape[1]].T,
        to_blocks(step_grad, fsdp),
        channel[CONV + 1],
        channel[CONV + 4 : CONV + 4 + STATE].T,
        channel[CONV + 2],
        rows_to_blocks(mixout_grad, 1),
        channel[CONV + 3],
        sum_ffn_gain,
        pair_blocks[:half],
        pair_blocks[half:],
        rows_to_blocks(down_grad, hidden_rows),
    )


def solution(mesh):
    rows, whole = P("fsdp", None), P()
    blocks, sequence = P("fsdp", "ctx"), P("fsdp", "ctx", None)
    return jax.shard_map(
        body,
        mesh=mesh,
        in_specs=(
            sequence, sequence, whole, rows, rows, rows, rows, whole, rows, whole, whole,
            rows, rows, whole, whole, whole, rows, whole, whole, rows, rows, rows,
        ),
        out_specs=(
            sequence, sequence, whole, blocks, blocks, blocks, blocks, whole, blocks, whole, whole,
            whole, blocks, whole, whole, whole, blocks, whole, whole, blocks, blocks, blocks,
        ),
        check_vma=False,
    )
```

```python
import functools
import jax
import jax.numpy as jnp
from jax import lax
from jax.experimental import pallas as pl
from jax.experimental.pallas import tpu as pltpu
from jax.sharding import PartitionSpec as P

LANES = 128
STATE = 16
CHUNK = 128
HEAD = 64
KV_HEADS = 5
CONV = 4
DT_RANK = 100
WINDOW = 1024
EPSILON = 1e-06
LOG2_E = 1.4426950408889634
BF16 = jnp.bfloat16


MESH = pl.DeviceIdType.MESH
VMEM_LIMIT = 56 * 1024 * 1024
IN_VMEM = pl.BlockSpec(memory_space=pltpu.VMEM)


def flip(index, bit):
    return index + (1 - 2 * ((index // (1 << bit)) % 2)) * (1 << bit)


def greet(me, bits):
    barrier = pltpu.get_barrier_semaphore()
    for bit in range(bits):
        pl.semaphore_signal(
            barrier, inc=1, device_id={"ctx": flip(me, bit)}, device_id_type=MESH
        )
    pl.semaphore_wait(barrier, bits)


def halves_of(rows):
    half = rows // 2 if rows % 32 == 0 else rows // 32 * 16
    return (pl.ds(0, half), pl.ds(half, rows - half))


class Copies:
    def __init__(self, axis, send_sem, recv_sem):
        self.axis, self.send_sem, self.recv_sem = axis, send_sem, recv_sem
        self.started = []
        self.count = 0

    def make(self, source, target, device):
        copy = pltpu.make_async_remote_copy(
            src_ref=source,
            dst_ref=target,
            send_sem=self.send_sem.at[self.count],
            recv_sem=self.recv_sem.at[self.count],
            device_id={self.axis: device},
            device_id_type=MESH,
        )
        self.count += 1
        return copy

    def send(self, source, target, device):
        copy = self.make(source, target, device)
        copy.start()
        self.started.append(copy)
        return copy

    def finish(self):
        for copy in self.started:
            copy.wait_send()


def gather_sems(bits):
    return 1 + 2 * sum(1 << p for p in range(bits - 1)) + 2 * ((1 << (bits - 1)) - 1)


def gather_steps(copies, bits, out_ref):
    me = lax.axis_index("ctx")
    parts = halves_of(out_ref.shape[1])
    orders = (list(range(1, bits)), list(range(bits - 1, 0, -1)))

    def send(bit, shard, part):
        at = out_ref.at[shard] if part is None else out_ref.at[shard, part]
        return copies.send(at, at, flip(me, bit))

    known = ([me], [me])
    last, flying = [], [None, None]

    def begin():
        for h in range(2):
            flying[h] = [send(orders[h][0], shard, parts[h]) for shard in known[h]]
        last.append(send(0, me, None))

    def turn(phase, h):
        bit = orders[h][phase]
        for copy in flying[h]:
            copy.wait_recv()
        fresh = [flip(shard, bit) for shard in known[h]]
        known[h].extend(fresh)
        if phase + 1 < bits - 1:
            flying[h] = [send(orders[h][phase + 1], shard, parts[h]) for shard in known[h]]
        last.extend(send(0, shard, parts[h]) for shard in fresh)

    def end():
        for copy in last:
            copy.wait_recv()

    turns = [functools.partial(turn, p, h) for p in range(bits - 1) for h in range(2)]
    return [begin] + turns + [end]


def gather_kernel(bits, x_ref, out_ref, send_sem, recv_sem):
    me = lax.axis_index("ctx")
    greet(me, bits)
    out_ref[me] = x_ref[...]
    copies = Copies("ctx", send_sem, recv_sem)
    for step in gather_steps(copies, bits, out_ref):
        step()
    copies.finish()


def ctx_bits():
    return lax.axis_size("ctx").bit_length() - 1


def params(collective_id):
    return pltpu.CompilerParams(
        collective_id=collective_id, has_side_effects=True, vmem_limit_bytes=VMEM_LIMIT
    )


def gather_shards(x, collective_id):
    bits, ctx = ctx_bits(), lax.axis_size("ctx")
    sems = pltpu.SemaphoreType.DMA((gather_sems(bits),))
    return pl.pallas_call(
        functools.partial(gather_kernel, bits),
        out_shape=jax.ShapeDtypeStruct((ctx,) + x.shape, x.dtype),
        in_specs=[IN_VMEM],
        out_specs=IN_VMEM,
        scratch_shapes=[sems, sems],
        compiler_params=params(collective_id),
        name="gather_shards",
    )(x)


def gather_tokens(x, collective_id):
    return gather_shards(x, collective_id).reshape(-1, x.shape[1])


def row_parts(rows, count):
    tiles = rows // 16
    edges = [16 * (tiles * i // count) for i in range(count)] + [rows]
    return [pl.ds(a, b - a) for a, b in zip(edges[:-1], edges[1:]) if b > a]


def line_steps(copies, out_refs, pieces):
    me, size = lax.axis_index("fsdp"), lax.axis_size("fsdp")
    plans = []
    for way in (1, -1):
        for distance in range(size - 1):
            for ref, part in pieces:
                shard = me - way * distance
                inside = jnp.logical_and(shard >= 0, shard < size)
                held = jnp.where(inside, shard, me)
                to = me + way
                go = jnp.logical_and(inside, jnp.logical_and(to >= 0, to < size))
                target = jnp.where(jnp.logical_and(to >= 0, to < size), to, me - way)
                at = out_refs[ref].at[held, part]
                plans.append((way, distance, go, copies.make(at, at, target)))
    table = {}
    for way, distance, go, copy in plans:
        table.setdefault((way, distance), []).append((go, copy))

    def begin():
        for index in range(len(pieces)):
            for way in (1, -1):
                go, copy = table[way, 0][index]
                pl.when(go)(copy.start)

    def turn(distance, index):
        for way in (1, -1):
            _, came = table[way, distance - 1][index]
            origin = me - way * distance
            pl.when(jnp.logical_and(origin >= 0, origin < size))(came.wait_recv)
            if distance < size - 1:
                go, copy = table[way, distance][index]
                pl.when(go)(copy.start)

    def end():
        for way in (1, -1):
            for distance in range(size - 1):
                for go, copy in table[way, distance]:
                    pl.when(go)(copy.wait_send)

    turns = [
        functools.partial(turn, d, i) for d in range(1, size) for i in range(len(pieces))
    ]
    return [begin] + turns, end


def front_kernel(
    bits, count, pack, x_ref, gain_ref, top_ref, in_ref, state_ref, step_ref, *rest,
):
    weights, rest = rest[: pack["inputs"]], rest[pack["inputs"] :]
    normed_ref, tops_ref, in_out, state_out, step_out = rest[:5]
    packed, rest = rest[5 : 5 + pack["outputs"]], rest[5 + pack["outputs"] :]
    ctx_send, ctx_recv, line_send, line_recv = rest[:4]
    me, row, rows = lax.axis_index("ctx"), lax.axis_index("fsdp"), lax.axis_size("fsdp")
    barrier = pltpu.get_barrier_semaphore()
    for bit in range(bits):
        pl.semaphore_signal(
            barrier, inc=1, device_id={"ctx": flip(me, bit)}, device_id_type=MESH
        )
    for to in (row - 1, row + 1):
        there = jnp.logical_and(to >= 0, to < rows)

        @pl.when(there)
        def _():
            pl.semaphore_signal(
                barrier, inc=1, device_id={"fsdp": jnp.where(there, to, row)}, device_id_type=MESH
            )

    in_out[row] = in_ref[...]
    state_out[row] = state_ref[...]
    step_out[row] = step_ref[...]
    neighbours = jnp.where(row > 0, 1, 0) + jnp.where(row < rows - 1, 1, 0)
    pl.semaphore_wait(barrier, bits + neighbours)

    line = Copies("fsdp", line_send, line_recv)
    across = Copies("ctx", ctx_send, ctx_recv)
    pieces = [(0, part) for part in row_parts(in_ref.shape[0], count)]
    pieces = [(1, pl.ds(0, state_ref.shape[0])), (2, pl.ds(0, step_ref.shape[0]))] + pieces
    line_list, line_end = line_steps(line, (in_out, state_out, step_out), pieces)
    line_list[0]()
    tokens = x_ref[...].astype(jnp.float32)
    scale = lax.rsqrt(jnp.mean(tokens * tokens, axis=-1, keepdims=True) + EPSILON)
    normed_ref[me] = (tokens * scale * gain_ref[...]).astype(normed_ref.dtype)
    first = gather_steps(across, bits, normed_ref)
    first[0]()
    tops_ref[me] = top_ref[...]
    second = gather_steps(across, bits, tops_ref)
    steps = list(pack["steps"](me, weights, packed, rest[4:])) if weights else []
    token_rest = first[1:-1] + [second[0]] + second[1:-1] + [first[-1], second[-1]]
    line_rest = line_list[1:]
    tokens_done = packs_done = 0
    spread = len(line_rest) * 3 // 4
    for i, step in enumerate(line_rest):
        upto = min(len(steps), len(steps) * (i + 1) // max(1, spread))
        for pack_step in steps[packs_done:upto]:
            pack_step()
        packs_done = max(packs_done, upto)
        step()
        upto = min(len(token_rest), len(token_rest) * (i + 1) // spread)
        for token_step in token_rest[tokens_done:upto]:
            token_step()
        tokens_done = max(tokens_done, upto)
    across.finish()
    line_end()


def front(x, gain, top, in_part, state_part, step_part, later, hidden_units, collective_id):
    bits, ctx, fsdp = ctx_bits(), lax.axis_size("ctx"), lax.axis_size("fsdp")
    count = 5
    ctx_sems = pltpu.SemaphoreType.DMA((2 * gather_sems(bits),))
    line_sems = pltpu.SemaphoreType.DMA((2 * fsdp * (count + 2),))
    pack = pack_out_plan(later, hidden_units)

    def stacked(array, size):
        return jax.ShapeDtypeStruct((size,) + array.shape, array.dtype)

    return pl.pallas_call(
        functools.partial(front_kernel, bits, count, pack),
        out_shape=[
            stacked(x, ctx), stacked(top, ctx), stacked(in_part, fsdp),
            stacked(state_part, fsdp), stacked(step_part, fsdp),
        ]
        + pack["shapes"],
        in_specs=[IN_VMEM] * 6 + [pl.BlockSpec(memory_space=pl.ANY)] * len(later),
        out_specs=[IN_VMEM] * (5 + pack["outputs"]),
        scratch_shapes=[ctx_sems, ctx_sems, line_sems, line_sems] + pack["scratch"],
        compiler_params=params(collective_id),
        name="front",
    )(x, gain, top, in_part, state_part, step_part, *later)


def product(x, weight, trans):
    dims = (((1,), (1 if trans else 0,)), ((), ()))
    return lax.dot_general(x, weight, dims, preferred_element_type=jnp.float32)


def subsets(chosen):
    out = [()]
    for bit in chosen:
        out = out + [s + (bit,) for s in out]
    return out


def flipped(shard, flips):
    for bit in flips:
        shard = flip(shard, bit)
    return shard


class Reducer:
    def __init__(self, copies, bits, part_ref, inbox, out_ref):
        self.copies, self.bits, self.part_ref = copies, bits, part_ref
        self.inbox, self.out_ref = inbox, out_ref
        self.me = lax.axis_index("ctx")
        self.parts = halves_of(out_ref.shape[0])
        self.orders = (list(range(1, bits)), list(range(bits - 1, 0, -1)))
        self.everyone = subsets(range(1, bits))[::-1]
        self.slots = {flips: slot for slot, flips in enumerate(self.everyone)}
        self.first = {}
        self.flying = [{}, {}]

    def to_sibling(self, flips, partial):
        slot = self.slots[flips]
        self.part_ref[slot] = partial.astype(self.part_ref.dtype)
        self.first[flips] = self.copies.send(
            self.part_ref.at[slot], self.inbox[0].at[slot], flip(self.me, 0)
        )

    def pass_on(self, h, phase, flips, following):
        bit = self.orders[h][phase]
        if bit in flips:
            kept = tuple(b for b in flips if b != bit)
            following[kept] = self.copies.send(
                self.inbox[0].at[self.slots[flips], self.parts[h]],
                self.inbox[1 + phase].at[len(following), self.parts[h]],
                flip(self.me, bit),
            )

    def own(self, flips, partial):
        self.first[flips].wait_recv()
        kept_ref, slot = self.inbox[0], self.slots[flips]
        kept_ref[slot] = (partial + kept_ref[slot].astype(jnp.float32)).astype(kept_ref.dtype)
        for h in range(2):
            self.pass_on(h, 0, flips, self.flying[h])

    def turn(self, phase, h):
        kept_ref = self.inbox[0]
        part, following = self.parts[h], {}
        for box, (flips, copy) in enumerate(list(self.flying[h].items())):
            copy.wait_recv()
            slot = self.slots[flips]
            total = kept_ref[slot, part].astype(jnp.float32) + self.inbox[1 + phase][
                box, part
            ].astype(jnp.float32)
            if phase == self.bits - 2:
                self.out_ref[part] = total
            else:
                kept_ref[slot, part] = total.astype(kept_ref.dtype)
                self.pass_on(h, phase + 1, flips, following)
        self.flying[h] = following

    def turns(self):
        return [functools.partial(self.turn, p, h) for p in range(self.bits - 1) for h in range(2)]

    def finish(self):
        for turn in self.turns():
            turn()


def reducer_boxes(ctx, bits, rows, columns):
    boxes = [ctx // 2, ctx // 2] + [ctx // 4 >> p for p in range(bits - 1)]
    sems = boxes[0] + 2 * sum(boxes[2:])
    return [pltpu.VMEM((box, rows, columns), BF16) for box in boxes], sems


def reduce_kernel(bits, trans, joint, *refs):
    count = len(trans)
    weights = 1 if joint else count
    x_refs, w_refs, out_ref = refs[:count], refs[count : count + weights], refs[count + weights]
    part_ref, inbox = refs[count + weights + 1], refs[count + weights + 2 : -2]
    me = lax.axis_index("ctx")
    greet(me, bits)
    if joint:
        whole, w_refs, inbox = w_refs[0], inbox[-count:], inbox[:-count]
        at = 0
        for w_ref in w_refs:
            wide = w_ref.shape[1]
            w_ref[...] = whole[:, at : at + wide]
            at += wide
    copies = Copies("ctx", *refs[-2:])
    reducer = Reducer(copies, bits, part_ref, inbox, out_ref)

    def partial(flips):
        shard = flipped(me, flips)
        return sum(
            product(x_ref[shard], w_ref[...], way)
            for x_ref, w_ref, way in zip(x_refs, w_refs, trans)
        )

    for flips in reducer.everyone:
        reducer.to_sibling(flips, partial(flips + (0,)))
    for flips in reducer.everyone:
        reducer.own(flips, partial(flips))
    reducer.finish()
    copies.finish()


def reduce_products(lefts, weights, trans, collective_id):
    ctx, bits = lax.axis_size("ctx"), ctx_bits()
    rows = lefts[0].shape[0] // ctx
    columns = weights[0].shape[0 if trans else 1]
    joint = len(weights) < len(lefts)
    boxes, count = reducer_boxes(ctx, bits, rows, columns)
    if joint:
        boxes = boxes + [pltpu.VMEM((columns, x.shape[1]), BF16) for x in lefts]
    sems = pltpu.SemaphoreType.DMA((count,))
    return pl.pallas_call(
        functools.partial(reduce_kernel, bits, (trans,) * len(lefts), joint),
        out_shape=jax.ShapeDtypeStruct((rows, columns), jnp.float32),
        in_specs=[IN_VMEM] * (len(lefts) + len(weights)),
        out_specs=IN_VMEM,
        scratch_shapes=boxes + [sems, sems],
        compiler_params=params(collective_id),
        name="reduce_products",
    )(*[x.reshape(ctx, rows, -1) for x in lefts], *weights)


def greet_all(me, size):
    barrier = pltpu.get_barrier_semaphore()
    for turn in range(1, size):
        pl.semaphore_signal(
            barrier, inc=1, device_id={"ctx": (me + turn) % size}, device_id_type=MESH
        )
    pl.semaphore_wait(barrier, size - 1)


def sum_kernel(size, x_ref, out_ref, inbox, send_sem, recv_sem):
    me = lax.axis_index("ctx")
    greet_all(me, size)
    copies = Copies("ctx", send_sem, recv_sem)
    come = []
    for turn in range(1, size):
        to = (me + turn) % size
        come.append(copies.send(x_ref.at[to], inbox.at[turn - 1], to))
    total = x_ref[me].astype(jnp.float32)
    for turn in range(1, size):
        come[turn - 1].wait_recv()
        total = total + inbox[turn - 1].astype(jnp.float32)
    out_ref[me] = total.astype(out_ref.dtype)
    come = [
        copies.send(out_ref.at[me], out_ref.at[me], (me + turn) % size) for turn in range(1, size)
    ]
    for copy in come:
        copy.wait_recv()
    copies.finish()


def sum_everywhere(partial, collective_id):
    ctx = lax.axis_size("ctx")
    rows, columns = partial.shape[0] // ctx, partial.shape[1]
    sems = pltpu.SemaphoreType.DMA((2 * (ctx - 1),))
    return pl.pallas_call(
        functools.partial(sum_kernel, ctx),
        out_shape=jax.ShapeDtypeStruct((ctx, rows, columns), partial.dtype),
        in_specs=[IN_VMEM],
        out_specs=IN_VMEM,
        scratch_shapes=[pltpu.VMEM((ctx - 1, rows, columns), partial.dtype), sems, sems],
        compiler_params=params(collective_id),
        name="sum_everywhere",
    )(partial.reshape(ctx, rows, columns)).reshape(partial.shape)


def total_kernel(size, x_ref, out_ref, inbox, send_sem, recv_sem):
    me = lax.axis_index("ctx")
    greet_all(me, size)
    copies = Copies("ctx", send_sem, recv_sem)
    come = [
        copies.send(x_ref, inbox.at[turn - 1], (me + turn) % size) for turn in range(1, size)
    ]
    inbox_total = x_ref[...]
    for turn in range(1, size):
        come[turn - 1].wait_recv()
        inbox_total = inbox_total + inbox[turn - 1]
    out_ref[...] = inbox_total
    copies.finish()


def total_of(rows_sum, collective_id):
    ctx = lax.axis_size("ctx")
    flat = rows_sum.reshape(-1, LANES)
    sems = pltpu.SemaphoreType.DMA((ctx - 1,))
    return pl.pallas_call(
        functools.partial(total_kernel, ctx),
        out_shape=jax.ShapeDtypeStruct(flat.shape, flat.dtype),
        in_specs=[IN_VMEM],
        out_specs=IN_VMEM,
        scratch_shapes=[pltpu.VMEM((ctx - 1,) + flat.shape, flat.dtype), sems, sems],
        compiler_params=params(collective_id),
        name="total_of",
    )(flat).reshape(rows_sum.shape)


def settle_kernel(
    bits, size, count, channel_ref, gain_ref, all_ref, sums_ref,
    row_inbox, gain_inbox, line_inbox, ctx_send, ctx_recv, line_send, line_recv,
):
    me, row = lax.axis_index("ctx"), lax.axis_index("fsdp")
    barrier = pltpu.get_barrier_semaphore()
    for turn in range(1, size):
        pl.semaphore_signal(
            barrier, inc=1, device_id={"ctx": (me + turn) % size}, device_id_type=MESH
        )
    for turn in range(1, count):
        pl.semaphore_signal(
            barrier, inc=1, device_id={"fsdp": (row + turn) % count}, device_id_type=MESH
        )
    pl.semaphore_wait(barrier, size - 1 + count - 1)
    across, line = Copies("ctx", ctx_send, ctx_recv), Copies("fsdp", line_send, line_recv)
    band = channel_ref.shape[0] // count

    def band_of(index):
        return pl.ds(pl.multiple_of(index * band, 8), band)

    rows_come = []
    for turn in range(1, count):
        to = (row + turn) % count
        rows_come.append(line.send(channel_ref.at[band_of(to)], row_inbox.at[turn - 1], to))
    gains_come = [
        across.send(gain_ref, gain_inbox.at[turn - 1], (me + turn) % size)
        for turn in range(1, size)
    ]
    total = channel_ref[band_of(row)]
    for turn in range(1, count):
        rows_come[turn - 1].wait_recv()
        total = total + row_inbox[turn - 1]
    all_ref[me, band_of(row)] = total
    at = all_ref.at[me, band_of(row)]
    bands_come = [line.send(at, at, (row + turn) % count) for turn in range(1, count)]
    total = gain_ref[...]
    for turn in range(1, size):
        gains_come[turn - 1].wait_recv()
        total = total + gain_inbox[turn - 1]
    line_inbox[0] = total
    line_come = [
        line.send(line_inbox.at[0], line_inbox.at[turn], (row + turn) % count)
        for turn in range(1, count)
    ]
    for copy in bands_come:
        copy.wait_recv()
    for step in gather_steps(across, bits, all_ref):
        step()
    total = line_inbox[0]
    for turn in range(1, count):
        line_come[turn - 1].wait_recv()
        total = total + line_inbox[turn]
    sums_ref[...] = total
    across.finish()
    line.finish()


def settle_small(channel, gains, collective_id):
    ctx, fsdp, bits = lax.axis_size("ctx"), lax.axis_size("fsdp"), ctx_bits()
    ctx_sems = pltpu.SemaphoreType.DMA((ctx - 1 + gather_sems(bits),))
    line_sems = pltpu.SemaphoreType.DMA((3 * (fsdp - 1),))
    rows, columns = channel.shape
    return pl.pallas_call(
        functools.partial(settle_kernel, bits, ctx, fsdp),
        out_shape=[
            jax.ShapeDtypeStruct((ctx, rows, columns), jnp.float32),
            jax.ShapeDtypeStruct(gains.shape, jnp.float32),
        ],
        in_specs=[IN_VMEM] * 2,
        out_specs=[IN_VMEM] * 2,
        scratch_shapes=[
            pltpu.VMEM((fsdp - 1, rows // fsdp, columns), jnp.float32),
            pltpu.VMEM((ctx - 1,) + gains.shape, jnp.float32),
            pltpu.VMEM((fsdp,) + gains.shape, jnp.float32),
            ctx_sems, ctx_sems, line_sems, line_sems,
        ],
        compiler_params=params(collective_id),
        name="settle_small",
    )(channel, gains)


def plane_gather(copies, out_ref):
    me = lax.axis_index("ctx")
    parts = halves_of(out_ref.shape[1])
    held = {}

    def send(name, bit, flips, part=None):
        shard = flipped(me, flips)
        at = out_ref.at[shard] if part is None else out_ref.at[shard, part]
        held[name] = copies.send(at, at, flip(me, bit))

    def start():
        for bit in (1, 2, 0):
            send(("own", bit), bit, ())

    def forward():
        held["own", 1].wait_recv()
        send(("corner", 2), 2, (1,), parts[0])
        held["own", 2].wait_recv()
        send(("corner", 1), 1, (2,), parts[1])
        send(("core", (1,)), 0, (1,))
        send(("core", (2,)), 0, (2,))

    def corner():
        held["corner", 2].wait_recv()
        held["corner", 1].wait_recv()
        send(("core", (1, 2)), 0, (1, 2))

    def wait(flips):
        held["core", flips].wait_recv() if flips else held["own", 0].wait_recv()

    return start, forward, corner, wait


def ffn_kernel(
    x_ref, top_ref, pair_w, down_w,
    pair_dw, down_dw, out_ref, grad_ref,
    all_ref, hidden_ref, pair_ref, own_ref, part_out, part_grad, *rest,
):
    bits = 3
    boxes = (len(rest) - 2) // 2
    inbox_out, inbox_grad = rest[:boxes], rest[boxes : 2 * boxes]
    me = lax.axis_index("ctx")
    greet(me, bits)
    all_ref[me] = x_ref[...]
    copies = Copies("ctx", *rest[-2:])
    start, forward, corner, wait = plane_gather(copies, all_ref)
    reducers = (
        Reducer(copies, bits, part_grad, inbox_grad, grad_ref),
        Reducer(copies, bits, part_out, inbox_out, out_ref),
    )
    rows, model = x_ref.shape
    hid = hidden_ref.shape[2]
    core = me % 2

    def work(slot, flips):
        first = 2 * (flipped(me, flips) // 2)
        pair = pl.ds(first, 2)
        x = all_ref[pair].reshape(2 * rows, model)
        pre = product(x, pair_w[...], False)
        gate, up = pre[:, :hid], pre[:, hid:]
        logistic = jax.nn.sigmoid(gate)
        gate_silu = gate * logistic
        hidden = (gate_silu * up).astype(BF16)
        hidden_ref[pair] = hidden.reshape(2, rows, hid)
        top = top_ref[pair].reshape(2 * rows, model)
        grad_hidden = product(top, down_w[...], True)
        slope = logistic * (1.0 + gate * (1.0 - logistic))
        pair_ref[pair, :, :hid] = (grad_hidden * up * slope).astype(BF16).reshape(2, rows, hid)
        pair_ref[pair, :, hid:] = (grad_hidden * gate_silu).astype(BF16).reshape(2, rows, hid)
        grads = pair_ref[pair].reshape(2 * rows, 2 * hid)
        for index, value in enumerate(
            (product(grads, pair_w[...], True), product(hidden, down_w[...], False))
        ):
            low, high = value[:rows], value[rows:]
            own_ref[index, slot] = jnp.where(core == 0, low, high)
            reducers[index].to_sibling(flips, jnp.where(core == 0, high, low))

    def settle(slot, flips):
        for index, reducer in enumerate(reducers):
            reducer.own(flips, own_ref[index, slot])

    start()
    wait(())
    work(0, ())
    forward()
    wait((1,))
    work(1, (1,))
    settle(0, ())
    corner()
    wait((2,))
    work(2, (2,))
    settle(1, (1,))
    wait((1, 2))
    work(3, (1, 2))
    settle(2, (2,))
    settle(3, (1, 2))

    def band(out, left_ref, right_ref, low, high):
        left = left_ref[:, :, low:high].reshape(size * rows, high - low)
        right = right_ref[...].reshape(size * rows, right_ref.shape[2])
        out[low:high] = lax.dot_general(
            left, right, (((0,), (0,)), ((), ())), preferred_element_type=jnp.float32
        ).astype(out.dtype)

    def bands(out, left_ref, right_ref, count):
        wide = left_ref.shape[2]
        tiles = -(-wide // 128)
        edges = [min(wide, 128 * (tiles * i // count)) for i in range(count + 1)]
        return [
            functools.partial(band, out, left_ref, right_ref, low, high)
            for low, high in zip(edges[:-1], edges[1:])
        ]

    size = all_ref.shape[0]
    work_left = bands(down_dw, hidden_ref, top_ref, 2) + bands(pair_dw, all_ref, pair_ref, 4)
    turns = [turn for pair in zip(*(reducer.turns() for reducer in reducers)) for turn in pair]
    done = 0
    for i, turn in enumerate(turns):
        upto = len(work_left) * (i + 1) // len(turns)
        for item in work_left[done:upto]:
            item()
        done = upto
        turn()
    copies.finish()


def ffn_both_ways(ffn_in, top, pair_full, down_full, collective_id):
    ctx, bits = lax.axis_size("ctx"), ctx_bits()
    rows, model = ffn_in.shape
    hid = down_full.shape[0]
    boxes, count = reducer_boxes(ctx, bits, rows, model)
    sems = pltpu.SemaphoreType.DMA((2 * count + 8,))
    return pl.pallas_call(
        ffn_kernel,
        out_shape=[
            jax.ShapeDtypeStruct((model, 2 * hid), BF16),
            jax.ShapeDtypeStruct((hid, model), BF16),
            jax.ShapeDtypeStruct((rows, model), jnp.float32),
            jax.ShapeDtypeStruct((rows, model), jnp.float32),
        ],
        in_specs=[IN_VMEM] * 4,
        out_specs=[IN_VMEM] * 4,
        scratch_shapes=[
            pltpu.VMEM((ctx, rows, model), BF16),
            pltpu.VMEM((ctx, rows, hid), BF16),
            pltpu.VMEM((ctx, rows, 2 * hid), BF16),
            pltpu.VMEM((2, ctx // 2, rows, model), jnp.float32),
            boxes[0],
            boxes[0],
        ]
        + boxes[1:]
        + boxes[1:]
        + [sems, sems],
        compiler_params=params(collective_id),
        name="ffn_both_ways",
    )(ffn_in, top.reshape(ctx, rows, model), pair_full, down_full)


def pieces_of(start, width, span):
    out = []
    at = start
    while at < start + width:
        block = at // span
        end = min(start + width, (block + 1) * span)
        out.append((block, at - start, end - start, at - block * span))
        at = end
    return out


def exchange(copies, send_ref, recv_ref, me, size):
    recv_ref[me] = send_ref[me]
    return [
        copies.send(send_ref.at[(me + turn) % size], recv_ref.at[me], (me + turn) % size)
        for turn in range(1, size)
    ]


def attention_kernel(
    size, fsdp, proj_ref, gain_ref,
    branch_ref, rows_ref, prob_ref, inverse_ref, q_ref, k_ref, v_ref,
    q_send, q_recv, kv_all, score_ref, attn_send, send_sem, recv_sem,
):
    bits = size.bit_length() - 1
    me = lax.axis_index("ctx")
    own, q_mine = q_send.shape[1], q_send.shape[2]
    kv_mine = kv_all.shape[2] // 2
    groups, keys, _ = k_ref.shape
    heads = q_ref.shape[1] // own
    queries = heads * own
    chunk = 128
    greet_all(me, size)
    copies = Copies("ctx", send_sem, recv_sem)
    for s in range(size):
        q_send[s] = proj_ref[s * own : (s + 1) * own, :q_mine]
    kv_all[me] = proj_ref[:, q_mine : q_mine + 2 * kv_mine]
    steps = gather_steps(copies, bits, kv_all)
    steps[0]()
    come = exchange(copies, q_send, q_recv, me, size)
    for step in steps[1:]:
        step()
    for copy in come:
        copy.wait_recv()

    for g in range(groups):
        for s, low, high, at in pieces_of(g * HEAD, HEAD, kv_mine):
            k_ref[g, :, low:high] = kv_all[s, :, at : at + high - low]
            v_ref[g, :, low:high] = kv_all[s, :, kv_mine + at : kv_mine + at + high - low]
        for h in range(heads):
            for s, low, high, at in pieces_of((g * heads + h) * HEAD, HEAD, q_mine):
                q_ref[g, h * own : (h + 1) * own, low:high] = q_recv[s, :, at : at + high - low]

    query_ids = me * own + lax.broadcasted_iota(jnp.int32, (chunk, queries), 1) % own
    key_ids = lax.broadcasted_iota(jnp.int32, (chunk, queries), 0)
    for g in range(groups):
        q_g = q_ref[g]

        def scores(i, top):
            at = pl.ds(pl.multiple_of(i * chunk, chunk), chunk)
            raw = product(k_ref[g, at], q_g, True) * (HEAD**-0.5)
            ids = key_ids + i * chunk
            kept = jnp.logical_and(ids <= query_ids, ids > query_ids - WINDOW)
            raw = jnp.where(kept, raw, -1e30)
            score_ref[at] = raw
            return jnp.maximum(top, jnp.max(raw, axis=0, keepdims=True))

        top = lax.fori_loop(
            0, keys // chunk, scores, jnp.full((1, queries), -1e30, jnp.float32)
        )

        def weights(i, total):
            at = pl.ds(pl.multiple_of(i * chunk, chunk), chunk)
            value = jnp.exp(score_ref[at] - top)
            prob_ref[g, at] = value.astype(BF16)
            return total + jnp.sum(value, axis=0, keepdims=True)

        total = lax.fori_loop(
            0, keys // chunk, weights, jnp.zeros((1, queries), jnp.float32)
        )
        inverse = 1.0 / total
        inverse_ref[g] = inverse
        out = lax.dot_general(
            v_ref[g], prob_ref[g], (((0,), (0,)), ((), ())), preferred_element_type=jnp.float32
        )
        out = (out * inverse).T
        for h in range(heads):
            at = (g * heads + h) * HEAD
            rows_ref[:, at : at + HEAD] = out[h * own : (h + 1) * own]

    values = rows_ref[...]
    scale = lax.rsqrt(jnp.mean(values * values, axis=-1, keepdims=True) + EPSILON)
    branch = (values * scale * gain_ref[...]).astype(BF16)
    part = values.shape[1] // fsdp
    width = part // size
    for d in range(size):
        for f in range(fsdp):
            at = f * part + d * width
            attn_send[d, :, f * width : (f + 1) * width] = branch[:, at : at + width]
    for copy in exchange(copies, attn_send, branch_ref, me, size):
        copy.wait_recv()
    copies.finish()


def attention_forward(projected, gain, kv_width, collective_id):
    ctx, fsdp, bits = lax.axis_size("ctx"), lax.axis_size("fsdp"), ctx_bits()
    length, model = projected.shape[0], gain.shape[0]
    own, q_mine, kv_mine = length // ctx, model // ctx, kv_width // ctx
    heads = model // kv_width
    sems = pltpu.SemaphoreType.DMA((2 * (ctx - 1) + gather_sems(bits),))
    shape = jax.ShapeDtypeStruct
    return pl.pallas_call(
        functools.partial(attention_kernel, ctx, fsdp),
        out_shape=[
            shape((ctx, own, q_mine), BF16),
            shape((own, model), jnp.float32),
            shape((KV_HEADS, length, heads * own), BF16),
            shape((KV_HEADS, 1, heads * own), jnp.float32),
            shape((KV_HEADS, heads * own, HEAD), BF16),
            shape((KV_HEADS, length, HEAD), BF16),
            shape((KV_HEADS, length, HEAD), BF16),
        ],
        in_specs=[IN_VMEM] * 2,
        out_specs=[IN_VMEM] * 7,
        scratch_shapes=[
            pltpu.VMEM((ctx, own, q_mine), BF16),
            pltpu.VMEM((ctx, own, q_mine), BF16),
            pltpu.VMEM((ctx, length, 2 * kv_mine), BF16),
            pltpu.VMEM((length, heads * own), jnp.float32),
            pltpu.VMEM((ctx, own, q_mine), BF16),
            sems, sems,
        ],
        compiler_params=params(collective_id),
        name="attention_forward",
    )(projected, gain[None])


def attention_back_kernel(
    size, fsdp, grad_ref, rows_ref, gain_ref, prob_ref, inverse_ref, q_ref, k_ref, v_ref,
    early_ref, gain_grad_ref,
    recv_ref, heads_ref, dp_ref, dq_ref, dkv_ref, dq_send, dq_recv, kv_part, kv_sum, *rest,
):
    bits = size.bit_length() - 1
    me = lax.axis_index("ctx")
    own, model = rows_ref.shape
    q_mine = model // size
    groups, keys, queries = prob_ref.shape
    heads = queries // own
    kv_mine = groups * HEAD // size
    chunk = 128
    scale_qk = HEAD**-0.5
    inbox = rest[:-2]
    greet_all(me, size)
    copies = Copies("ctx", *rest[-2:])
    come = exchange(copies, grad_ref, recv_ref, me, size)
    values = rows_ref[...]
    scale = lax.rsqrt(jnp.mean(values * values, axis=-1, keepdims=True) + EPSILON)
    for copy in come:
        copy.wait_recv()
    part = model // fsdp
    width = part // size
    for s in range(size):
        for f in range(fsdp):
            at = f * part + s * width
            dq_ref[:, at : at + width] = recv_ref[s, :, f * width : (f + 1) * width].astype(
                jnp.float32
            )
    grad = dq_ref[...]
    gain_grad_ref[...] = jnp.sum(grad * values * scale, axis=0, keepdims=True)
    scaled = grad * gain_ref[...]
    grad = scale * scaled - values * (scale * scale * scale) * jnp.mean(
        scaled * values, axis=-1, keepdims=True
    )
    grad = grad.astype(BF16)
    for h in range(groups * heads):
        at = (h % heads) * own
        heads_ref[h // heads, at : at + own] = grad[:, h * HEAD : (h + 1) * HEAD]

    for g in range(groups):
        q_g, do_g, inverse = q_ref[g], heads_ref[g], inverse_ref[g]
        q_t = q_g.astype(jnp.float32).T.astype(BF16)
        do_t = do_g.astype(jnp.float32).T.astype(BF16)

        def first(i, row_dot):
            at = pl.ds(pl.multiple_of(i * chunk, chunk), chunk)
            prob = prob_ref[g, at].astype(jnp.float32) * inverse
            grad_prob = product(v_ref[g, at], do_g, True)
            dp_ref[at] = grad_prob
            dkv_ref[groups + g, :, at] = product(do_t, prob.astype(BF16), True)
            return row_dot + jnp.sum(prob * grad_prob, axis=0, keepdims=True)

        row_dot = lax.fori_loop(
            0, keys // chunk, first, jnp.zeros((1, queries), jnp.float32)
        )

        def second(i, dq_t):
            at = pl.ds(pl.multiple_of(i * chunk, chunk), chunk)
            prob = prob_ref[g, at].astype(jnp.float32) * inverse
            grad_score = (prob * (dp_ref[at] - row_dot)).astype(BF16)
            dkv_ref[g, :, at] = scale_qk * product(q_t, grad_score, True)
            return dq_t + lax.dot_general(
                k_ref[g, at], grad_score, (((0,), (0,)), ((), ())),
                preferred_element_type=jnp.float32,
            )

        dq_t = lax.fori_loop(
            0, keys // chunk, second, jnp.zeros((HEAD, queries), jnp.float32)
        )
        dq_g = (scale_qk * dq_t).T
        for h in range(heads):
            at = (g * heads + h) * HEAD
            dq_ref[:, at : at + HEAD] = dq_g[h * own : (h + 1) * own]

    for d in range(size):
        dq_send[d] = dq_ref[:, d * q_mine : (d + 1) * q_mine].astype(BF16)
    come = exchange(copies, dq_send, dq_recv, me, size)
    flat = dkv_ref.reshape(2 * groups * HEAD, keys)
    for d in range(size):
        kv_part[d, :kv_mine] = flat[d * kv_mine : (d + 1) * kv_mine].astype(BF16)
        at = groups * HEAD + d * kv_mine
        kv_part[d, kv_mine:] = flat[at : at + kv_mine].astype(BF16)
    reducer = Reducer(copies, bits, None, inbox, kv_sum)
    for flips in reducer.everyone:
        reducer.first[flips] = copies.send(
            kv_part.at[flipped(me, flips + (0,))],
            inbox[0].at[reducer.slots[flips]],
            flip(me, 0),
        )
    for flips in reducer.everyone:
        reducer.own(flips, kv_part[flipped(me, flips)].astype(jnp.float32))
    for copy in come:
        copy.wait_recv()
    for s in range(size):
        early_ref[s * own : (s + 1) * own, :q_mine] = dq_recv[s]
    reducer.finish()
    early_ref[:, q_mine:] = kv_sum[...].T.astype(BF16)
    copies.finish()


def attention_backward(grad_c, rows, gain, kept, collective_id):
    ctx, fsdp, bits = lax.axis_size("ctx"), lax.axis_size("fsdp"), ctx_bits()
    prob = kept[0]
    own, model = rows.shape
    length = own * ctx
    q_mine, kv_mine = model // ctx, KV_HEADS * HEAD // ctx
    boxes, count = reducer_boxes(ctx, bits, 2 * kv_mine, length)
    sems = pltpu.SemaphoreType.DMA((2 * (ctx - 1) + count,))
    shape = jax.ShapeDtypeStruct
    return pl.pallas_call(
        functools.partial(attention_back_kernel, ctx, fsdp),
        out_shape=[
            shape((length, q_mine + 2 * kv_mine), BF16),
            shape((1, model), jnp.float32),
        ],
        in_specs=[IN_VMEM] * (3 + len(kept)),
        out_specs=[IN_VMEM] * 2,
        scratch_shapes=[
            pltpu.VMEM((ctx, own, q_mine), BF16),
            pltpu.VMEM(kept[2].shape, BF16),
            pltpu.VMEM((length, prob.shape[2]), jnp.float32),
            pltpu.VMEM((own, model), jnp.float32),
            pltpu.VMEM((2 * KV_HEADS, HEAD, length), jnp.float32),
            pltpu.VMEM((ctx, own, q_mine), BF16),
            pltpu.VMEM((ctx, own, q_mine), BF16),
            pltpu.VMEM((ctx, 2 * kv_mine, length), BF16),
            pltpu.VMEM((2 * kv_mine, length), jnp.float32),
        ]
        + boxes[1:]
        + [sems, sems],
        compiler_params=params(collective_id),
        name="attention_backward",
    )(grad_c.reshape(ctx, own, q_mine), rows, gain[None], *kept)


def finish_kernel(
    size, fsdp, early_ref, src_ref, step_ref, attn_ref, mix_ref, channel_ref, gain_ref,
    query_out, key_out, value_out, mixer_out, step_out, attn_out, mix_out, channel_out, sums_ref,
    all_ref, row_inbox, gain_inbox, line_inbox, c_send, c_recv, r_send, r_recv,
    ctx_send, ctx_recv, line_send, line_recv,
):
    bits = size.bit_length() - 1
    me, row = lax.axis_index("ctx"), lax.axis_index("fsdp")
    barrier = pltpu.get_barrier_semaphore()
    for turn in range(1, size):
        pl.semaphore_signal(
            barrier, inc=1, device_id={"ctx": (me + turn) % size}, device_id_type=MESH
        )
    for turn in range(1, fsdp):
        pl.semaphore_signal(
            barrier, inc=1, device_id={"fsdp": (row + turn) % fsdp}, device_id_type=MESH
        )
    q_mine, kv_mine = query_out.shape[1], key_out.shape[1]
    late = q_mine + 2 * kv_mine
    rows, width = src_ref.shape[0], src_ref.shape[1] // fsdp
    low, high = step_ref.shape[0], mix_ref.shape[0]
    attn_at = -(-high // 16) * 16
    block = mix_out.shape[1]
    repeat = size // fsdp
    pl.semaphore_wait(barrier, size - 1 + fsdp - 1)
    across, line = Copies("ctx", ctx_send, ctx_recv), Copies("fsdp", line_send, line_recv)
    band = channel_ref.shape[0] // fsdp

    def band_of(index):
        return pl.ds(pl.multiple_of(index * band, 8), band)

    bands = []
    for turn in range(1, fsdp):
        to = (row + turn) % fsdp
        bands.append(line.send(channel_ref.at[band_of(to)], row_inbox.at[turn - 1], to))
    gains = [
        across.send(gain_ref, gain_inbox.at[turn - 1], (me + turn) % size)
        for turn in range(1, size)
    ]
    c_send[:, rows:] = jnp.zeros((size, c_send.shape[1] - rows, width), BF16)
    r_send[...] = jnp.zeros(r_send.shape, BF16)
    for d in range(size):
        unit = d % fsdp
        if d < fsdp:
            c_send[d, :rows] = src_ref[:, unit * width : (unit + 1) * width]
        else:
            at = late + unit * width
            c_send[d, :rows] = early_ref[:, at : at + width]
        at = d // repeat * width
        c_send[d, rows : rows + low] = step_ref[:, at : at + width]
        r_send[d, :high] = mix_ref[:, d * block : (d + 1) * block]
        r_send[d, attn_at : attn_at + attn_ref.shape[0]] = attn_ref[:, d * block : (d + 1) * block]
    moved = exchange(across, c_send, c_recv, me, size) + exchange(across, r_send, r_recv, me, size)
    query_out[...] = early_ref[:, :q_mine].astype(jnp.float32)
    key_out[...] = early_ref[:, q_mine : q_mine + kv_mine].astype(jnp.float32)
    value_out[...] = early_ref[:, q_mine + kv_mine : late].astype(jnp.float32)

    total = channel_ref[band_of(row)]
    for turn in range(1, fsdp):
        bands[turn - 1].wait_recv()
        total = total + row_inbox[turn - 1]
    all_ref[me, band_of(row)] = total
    at = all_ref.at[me, band_of(row)]
    bands = [line.send(at, at, (row + turn) % fsdp) for turn in range(1, fsdp)]
    total = gain_ref[...]
    for turn in range(1, size):
        gains[turn - 1].wait_recv()
        total = total + gain_inbox[turn - 1]
    line_inbox[0] = total
    gains = [
        line.send(line_inbox.at[0], line_inbox.at[turn], (row + turn) % fsdp)
        for turn in range(1, fsdp)
    ]
    for copy in bands:
        copy.wait_recv()
    steps = gather_steps(across, bits, all_ref)
    steps[0]()
    for copy in moved:
        copy.wait_recv()
    for step in steps[1:-1]:
        step()
    for s in range(size):
        mixer_out[:, s * width : (s + 1) * width] = c_recv[s, :rows].astype(jnp.float32)
        mix_out[s * high : (s + 1) * high] = r_recv[s, :high].astype(jnp.float32)
        count = attn_ref.shape[0]
        attn_out[s * count : (s + 1) * count] = r_recv[s, attn_at : attn_at + count].astype(
            jnp.float32
        )
    for j in range(fsdp):
        source = fsdp * (me % repeat) + j
        step_out[:, j * width : (j + 1) * width] = c_recv[source, rows : rows + low].astype(
            jnp.float32
        )
    steps[-1]()
    part = channel_out.shape[1] // fsdp
    for s in range(size):
        for f in range(fsdp):
            at = f * part + s * width
            channel_out[:, at : at + width] = all_ref[s, :, f * width : (f + 1) * width]
    total = line_inbox[0]
    for turn in range(1, fsdp):
        gains[turn - 1].wait_recv()
        total = total + line_inbox[turn]
    sums_ref[...] = total
    across.finish()
    line.finish()


def finish(early, src, step, attn, mix, channel, gains, q_mine, kv_mine, collective_id):
    ctx, fsdp, bits = lax.axis_size("ctx"), lax.axis_size("fsdp"), ctx_bits()
    rows, mine = src.shape
    model = attn.shape[1]
    width, block = mine // fsdp, model // ctx
    pad_rows = rows + -(-step.shape[0] // 16) * 16
    stack_rows = -(-mix.shape[0] // 16) * 16 + -(-attn.shape[0] // 16) * 16
    ctx_sems = pltpu.SemaphoreType.DMA((3 * (ctx - 1) + gather_sems(bits),))
    line_sems = pltpu.SemaphoreType.DMA((3 * (fsdp - 1),))

    def shape(*sizes):
        return jax.ShapeDtypeStruct(sizes, jnp.float32)

    return pl.pallas_call(
        functools.partial(finish_kernel, ctx, fsdp),
        out_shape=[
            shape(rows, q_mine), shape(rows, kv_mine), shape(rows, kv_mine),
            shape(rows, ctx * width), shape(step.shape[0], mine),
            shape(ctx * attn.shape[0], block), shape(ctx * mix.shape[0], block),
            shape(channel.shape[0], ctx * mine), shape(*gains.shape),
        ],
        in_specs=[IN_VMEM] * 7,
        out_specs=[IN_VMEM] * 9,
        scratch_shapes=[
            pltpu.VMEM((ctx,) + channel.shape, jnp.float32),
            pltpu.VMEM((fsdp - 1, channel.shape[0] // fsdp, mine), jnp.float32),
            pltpu.VMEM((ctx - 1,) + gains.shape, jnp.float32),
            pltpu.VMEM((fsdp,) + gains.shape, jnp.float32),
            pltpu.VMEM((ctx, pad_rows, width), BF16),
            pltpu.VMEM((ctx, pad_rows, width), BF16),
            pltpu.VMEM((ctx, stack_rows, block), BF16),
            pltpu.VMEM((ctx, stack_rows, block), BF16),
            ctx_sems, ctx_sems, line_sems, line_sems,
        ],
        compiler_params=params(collective_id),
        name="finish",
    )(early, src, step, attn, mix, channel, gains)


def window(start, size, total, step):
    return pl.multiple_of(jnp.minimum(start // step * step, total - size), step)


def shifted(values, offset, axis):
    size = values.shape[axis]
    return pltpu.roll(values.astype(jnp.float32), lax.rem(size - offset, size), axis)


def pack_in_kernel(
    size, query_ref, key_ref, value_ref, mixer_ref, state_ref, step_ref,
    in_out, state_out, step_out, inbox, sems,
):
    me = lax.axis_index("ctx")
    units, _, span = inbox.shape
    total = mixer_ref.shape[1]
    width = total // units // size
    copies = []
    for u in range(units):
        at = window(u * (total // units) + me * width, span, total, 128)
        copy = pltpu.make_async_copy(mixer_ref.at[:, pl.ds(at, span)], inbox.at[u], sems.at[u])
        copy.start()
        copies.append(copy)
    at = 0
    for ref in (query_ref, key_ref, value_ref):
        wide = ref.shape[1] // size
        in_out[:, at : at + wide] = shifted(ref[...], me * wide, 1)[:, :wide].astype(BF16)
        at += wide
    high = state_ref.shape[0] // size
    first = window(me * high, 128, state_ref.shape[0], 16)
    rows = shifted(state_ref[pl.ds(first, 128)], me * high - first, 0)
    state_out[...] = rows[: state_out.shape[0]].astype(BF16)
    part = step_ref.shape[1] * 2 // units
    step_out[...] = jnp.zeros(step_out.shape, BF16)
    for f in range(units // 2):
        band = shifted(step_ref[:, f * part : (f + 1) * part], me * width, 1)
        step_out[: step_ref.shape[0], f * width : (f + 1) * width] = band[:, :width].astype(BF16)
    for u in range(units):
        copies[u].wait()
        start = u * (total // units) + me * width
        piece = shifted(inbox[u], start - window(start, span, total, 128), 1)[:, :width]
        to = at + (u + units // 2) % units * width
        in_out[:, to : to + width] = piece.astype(BF16)


def pack_in(query, key, value, mixer, state, step):
    ctx, fsdp = lax.axis_size("ctx"), lax.axis_size("fsdp")
    rows = mixer.shape[0]
    mine = mixer.shape[1] // 2 // ctx
    qkv = (query.shape[1] + key.shape[1] + value.shape[1]) // ctx
    state_rows = state.shape[0] // ctx
    shape = jax.ShapeDtypeStruct
    return pl.pallas_call(
        functools.partial(pack_in_kernel, ctx),
        out_shape=[
            shape((rows, qkv + 2 * mine), BF16),
            shape((state_rows + -state_rows % 16, state.shape[1]), BF16),
            shape((step.shape[0] + -step.shape[0] % 16, mine), BF16),
        ],
        in_specs=[IN_VMEM] * 3 + [pl.BlockSpec(memory_space=pl.ANY)] + [IN_VMEM] * 2,
        out_specs=[IN_VMEM] * 3,
        scratch_shapes=[
            pltpu.VMEM((2 * fsdp, rows, 256), BF16), pltpu.SemaphoreType.DMA((2 * fsdp,))
        ],
        compiler_params=pltpu.CompilerParams(vmem_limit_bytes=VMEM_LIMIT),
        name="pack_in",
    )(query, key, value, mixer, state, step)


def pack_out_plan(later, hidden_units):
    if not later:
        return {"inputs": 0, "outputs": 0, "shapes": [], "scratch": [], "steps": None}
    ctx, fsdp = lax.axis_size("ctx"), lax.axis_size("fsdp")
    gate, _, down, mix, attn = later
    rows, model, total = gate.shape[0], down.shape[0], gate.shape[1]
    hid_part = total // ctx // fsdp
    pad = -hid_part % 16
    units = hidden_units // fsdp
    width = hid_part // units
    high = (hid_part + pad) + (mix.shape[0] + attn.shape[0]) // ctx
    span = 256

    def box_rows(array):
        need = array.shape[0] // ctx
        return need + 15 + -(need + 15) % 16

    def steps(me, weights, outs, scratch):
        gate_ref, up_ref, down_ref, mix_ref, attn_ref = weights
        pair_out, rows_out = outs
        inbox, down_box, tail_box, mix_box, attn_box, sems = scratch
        copies = []

        def start_copy(source, target):
            copy = pltpu.make_async_copy(source, target, sems.at[len(copies)])
            copy.start()
            copies.append(copy)

        plans = []
        half = pair_out.shape[1] // 2
        for index, ref in enumerate((gate_ref, up_ref)):
            for u in range(hidden_units):
                start = u * (total // hidden_units) + me * width
                at = window(start, span, total, 128)
                start_copy(ref.at[:, pl.ds(at, span)], inbox.at[index, u])
                to = index * half + u * width + u // units * pad
                plans.append(("columns", inbox, (index, u), start - at, to, width))
        to = 0
        down_at = to
        to += units * width + pad
        for ref, box in ((mix_ref, mix_box), (attn_ref, attn_box)):
            tall = ref.shape[0] // size
            at = window(me * tall, box.shape[1], ref.shape[0], 16)
            start_copy(ref.at[pl.ds(at, box.shape[1])], box.at[0])
            plans.append(("rows", box, (0,), me * tall - at, to, tall))
            to += tall
        start_copy(down_ref, down_box)
        full = down.shape[1] // 128
        tail = down.shape[1] % 128

        def tile_of(index):
            at = pl.multiple_of(jnp.minimum(index, full - 1) * 128, 128)
            whole = down_box[:, pl.ds(at, 128)].astype(jnp.float32)
            return jnp.where(index >= full, tail_box[...], whole) if tail else whole

        def begin_down():
            copies[-1].wait()
            if tail:
                tail_box[...] = jnp.zeros(tail_box.shape, jnp.float32)
                tail_box[:, :tail] = down_box[:, full * 128 :].astype(jnp.float32)

        def place_down(u):
            start = u * (down.shape[1] // units) + me * width
            first = start // 128
            pair = jnp.concatenate([tile_of(first), tile_of(first + 1)], 1)
            turned = shifted(pair, start - first * 128, 1)[:, :128].T
            at = down_at + u * width
            rows_out[at : at + width] = turned[:width].astype(BF16)

        def clear():
            pair_out[...] = jnp.zeros(pair_out.shape, BF16)
            rows_out[...] = jnp.zeros(rows_out.shape, BF16)

        def place(copy, kind, box, index, offset, to, extent):
            copy.wait()
            values = box[index]
            if kind == "columns":
                pair_out[:, to : to + extent] = shifted(values, offset, 1)[:, :extent].astype(BF16)
            else:
                rows_out[to : to + extent] = shifted(values, offset, 0)[:extent].astype(BF16)

        placed = [functools.partial(place, copy, *plan) for copy, plan in zip(copies, plans)]
        downs = [functools.partial(place_down, u) for u in range(units)]
        return [clear] + placed + [begin_down] + downs

    size = ctx
    shape = jax.ShapeDtypeStruct
    return {
        "inputs": 5,
        "outputs": 2,
        "shapes": [
            shape((rows, 2 * fsdp * (hid_part + pad)), BF16),
            shape((high + -high % 16, model), BF16),
        ],
        "scratch": [
            pltpu.VMEM((2, hidden_units, rows, span), BF16),
            pltpu.VMEM(down.shape, BF16),
            pltpu.VMEM((model, 128), jnp.float32),
            pltpu.VMEM((1, box_rows(mix), model), BF16),
            pltpu.VMEM((1, box_rows(attn), model), BF16),
            pltpu.SemaphoreType.DMA((2 * hidden_units + 3,)),
        ],
        "steps": steps,
    }


def scan_fwd_kernel(steps_ref, drive_ref, in_ref, out_ref, rate_ref, scan_ref, prev_ref, state_ref):
    tiles = steps_ref.shape[1] // LANES
    chunk = steps_ref.shape[0]

    @pl.when(pl.program_id(0) == 0)
    def _():
        state_ref[...] = jnp.zeros_like(state_ref)

    rates = [rate_ref[:, j * LANES : (j + 1) * LANES] for j in range(tiles)]

    def group(g, states):
        states = list(states)
        base = pl.multiple_of(g * 8, 8)
        for j in range(tiles):
            lanes = slice(j * LANES, (j + 1) * LANES)
            step_8 = steps_ref[pl.ds(base, 8), lanes]
            drive_8 = step_8 * drive_ref[pl.ds(base, 8), lanes]
            rows = []
            for t in range(8):
                in_t = in_ref[base + t].astype(jnp.float32)
                out_t = out_ref[base + t].astype(jnp.float32)
                decay = jnp.exp2(step_8[t : t + 1] * rates[j])
                prev_ref[base + t, :, lanes] = states[j]
                states[j] = decay * states[j] + drive_8[t : t + 1] * in_t
                rows.append(jnp.sum(states[j] * out_t, axis=0, keepdims=True))
            scan_ref[pl.ds(base, 8), lanes] = jnp.concatenate(rows, 0)
        return tuple(states)

    start = tuple(state_ref[:, j * LANES : (j + 1) * LANES] for j in range(tiles))
    final = lax.fori_loop(0, chunk // 8, group, start)
    for j in range(tiles):
        state_ref[:, j * LANES : (j + 1) * LANES] = final[j]


def scan_fwd(steps, drive, in_b, out_b, rates):
    length, width = steps.shape
    chunk = CHUNK
    row = pl.BlockSpec((chunk, width), lambda i: (i, 0))
    mat = pl.BlockSpec((chunk, STATE, LANES), lambda i: (i, 0, 0))
    rate = pl.BlockSpec((STATE, width), lambda i: (0, 0))
    return pl.pallas_call(
        scan_fwd_kernel,
        grid=(length // chunk,),
        in_specs=[row, row, mat, mat, rate],
        out_specs=[row, pl.BlockSpec((chunk, STATE, width), lambda i: (i, 0, 0))],
        out_shape=[
            jax.ShapeDtypeStruct((length, width), jnp.float32),
            jax.ShapeDtypeStruct((length, STATE, width), jnp.float32),
        ],
        scratch_shapes=[pltpu.VMEM((STATE, width), jnp.float32)],
        compiler_params=pltpu.CompilerParams(vmem_limit_bytes=48 * 1024 * 1024),
        name="scan_forward",
    )(steps, drive, in_b, out_b, rates)


def scan_bwd_kernel(
    steps_ref, drive_ref, grad_ref, in_ref, out_ref, rate_ref, prev_ref,
    gstep_ref, gdrive_ref, gin_ref, gout_ref, grate_ref,
    carry_ref, pin_ref, pout_ref,
):
    tiles = steps_ref.shape[1] // LANES
    chunk = steps_ref.shape[0]

    @pl.when(pl.program_id(0) == 0)
    def _():
        carry_ref[...] = jnp.zeros_like(carry_ref)
        grate_ref[...] = jnp.zeros_like(grate_ref)

    for j in range(tiles):
        lanes = slice(j * LANES, (j + 1) * LANES)
        rates = rate_ref[:, lanes]

        def group(k, kept):
            carry, acc = kept
            base = pl.multiple_of(chunk - 8 - k * 8, 8)
            step_8 = steps_ref[pl.ds(base, 8), lanes]
            x_8 = drive_ref[pl.ds(base, 8), lanes]
            drive_8 = step_8 * x_8
            grad_8 = grad_ref[pl.ds(base, 8), lanes]
            held_rows, dot_rows = [None] * 8, [None] * 8
            for t in range(7, -1, -1):
                in_t = in_ref[base + t].astype(jnp.float32)
                out_t = out_ref[base + t].astype(jnp.float32)
                previous = prev_ref[base + t, :, lanes]
                step_t = step_8[t : t + 1]
                drive_t = drive_8[t : t + 1]
                grad_t = grad_8[t : t + 1]
                decay = jnp.exp2(step_t * rates)
                adjoint = grad_t * out_t + carry
                carry = decay * adjoint
                held = carry * previous
                state = decay * previous + drive_t * in_t
                acc = acc + held * step_t
                held_rows[t] = jnp.sum(held * rates, axis=0, keepdims=True)
                dot_rows[t] = jnp.sum(adjoint * in_t, axis=0, keepdims=True)
                part_in = adjoint * drive_t
                part_out = state * grad_t
                at = pl.ds(pl.multiple_of((base + t) * STATE, STATE), STATE)
                if j == 0:
                    pin_ref[at] = part_in
                    pout_ref[at] = part_out
                else:
                    pin_ref[at] += part_in
                    pout_ref[at] += part_out
            held_8 = jnp.concatenate(held_rows, 0)
            dot_8 = jnp.concatenate(dot_rows, 0)
            gstep_ref[pl.ds(base, 8), lanes] = held_8 * 0.6931471805599453 + x_8 * dot_8
            gdrive_ref[pl.ds(base, 8), lanes] = step_8 * dot_8
            return carry, acc

        carry, acc = lax.fori_loop(
            0, chunk // 8, group, (carry_ref[:, lanes], grate_ref[:, lanes])
        )
        carry_ref[:, lanes] = carry
        grate_ref[:, lanes] = acc
    ones = jnp.ones((8, LANES), jnp.float32)
    dims = (((1,), (1,)), ((), ()))
    gin_ref[0] = lax.dot_general(ones, pin_ref[...], dims, preferred_element_type=jnp.float32)
    gout_ref[0] = lax.dot_general(ones, pout_ref[...], dims, preferred_element_type=jnp.float32)


def scan_bwd(steps, drive, grad, in_b, out_b, rates, previous):
    length, width = steps.shape
    chunk = CHUNK
    count = length // chunk
    row = pl.BlockSpec((chunk, width), lambda i: (count - 1 - i, 0))
    mat = pl.BlockSpec((chunk, STATE, LANES), lambda i: (count - 1 - i, 0, 0))
    rate = pl.BlockSpec((STATE, width), lambda i: (0, 0))
    red = pl.BlockSpec((1, 8, chunk * STATE), lambda i: (count - 1 - i, 0, 0))
    gstep, gdrive, gin, gout, grate = pl.pallas_call(
        scan_bwd_kernel,
        grid=(count,),
        in_specs=[row, row, row, mat, mat, rate,
                  pl.BlockSpec((chunk, STATE, width), lambda i: (count - 1 - i, 0, 0))],
        out_specs=[row, row, red, red, rate],
        out_shape=[
            jax.ShapeDtypeStruct((length, width), jnp.float32),
            jax.ShapeDtypeStruct((length, width), jnp.float32),
            jax.ShapeDtypeStruct((count, 8, chunk * STATE), jnp.float32),
            jax.ShapeDtypeStruct((count, 8, chunk * STATE), jnp.float32),
            jax.ShapeDtypeStruct((STATE, width), jnp.float32),
        ],
        scratch_shapes=[
            pltpu.VMEM((STATE, width), jnp.float32),
            pltpu.VMEM((chunk * STATE, LANES), jnp.float32),
            pltpu.VMEM((chunk * STATE, LANES), jnp.float32),
        ],
        compiler_params=pltpu.CompilerParams(vmem_limit_bytes=48 * 1024 * 1024),
        name="scan_backward",
    )(steps, drive, grad, in_b, out_b, rates, previous)
    return (gstep, gdrive, gin[:, 0].reshape(length, STATE), gout[:, 0].reshape(length, STATE), grate)


def matmul(left, right):
    return jnp.dot(left, right, preferred_element_type=jnp.float32)


def left_trans(left, right):
    return lax.dot_general(
        left, right, (((0,), (0,)), ((), ())), preferred_element_type=jnp.float32
    )


def right_trans(left, right):
    return lax.dot_general(
        left, right, (((1,), (1,)), ((), ())), preferred_element_type=jnp.float32
    )


def rms_scale(values):
    return lax.rsqrt(jnp.mean(values * values, axis=-1, keepdims=True) + EPSILON)


def norm_back(grad_out, values, scale_in, gain_in):
    scaled = grad_out * gain_in
    grad_in = scale_in * scaled - values * scale_in**3 * jnp.mean(
        scaled * values, axis=-1, keepdims=True
    )
    return (grad_in, jnp.sum(grad_out * values * scale_in, axis=0))


def silu_slope(values):
    logistic = jax.nn.sigmoid(values)
    return logistic * (1.0 + values * (1.0 - logistic))


def unit_count(width, ctx, fsdp):
    return ctx if width % (ctx * ctx) == 0 and ctx % fsdp == 0 else fsdp


def my_columns(array, units):
    span = array.shape[1] // units
    width = span // lax.axis_size("ctx")
    start = lax.axis_index("ctx") * width
    return [
        lax.dynamic_slice_in_dim(array, unit * span + start, width, 1) for unit in range(units)
    ]


def my_rows(array, units):
    span = array.shape[0] // units
    width = span // lax.axis_size("ctx")
    start = lax.axis_index("ctx") * width
    return [
        lax.dynamic_slice_in_dim(array, unit * span + start, width, 0) for unit in range(units)
    ]


def block_columns(array):
    width = array.shape[1] // lax.axis_size("ctx")
    return lax.dynamic_slice_in_dim(array, lax.axis_index("ctx") * width, width, 1)


def over_fsdp(array):
    return lax.all_gather(array, "fsdp", axis=0, tiled=True)


def to_slots(array, units):
    repeat = lax.axis_size("ctx") // units
    rows, width = array.shape[0], array.shape[1] // units
    pieces = array.reshape(rows, units, width).transpose(1, 0, 2)
    return jnp.repeat(pieces, repeat, axis=0) if repeat > 1 else pieces


def from_slots(got, units):
    repeat = lax.axis_size("ctx") // units
    if repeat > 1:
        first = units * lax.rem(lax.axis_index("ctx"), repeat)
        got = lax.dynamic_slice_in_dim(got, first, units, 0)
    rows, width = got.shape[1:]
    return got.transpose(1, 0, 2).reshape(rows, units * width).astype(jnp.float32)


def to_blocks(array, units):
    got = lax.all_to_all(to_slots(array, units), "ctx", 0, 0, tiled=True)
    return from_slots(got, units)


def rows_to_slots(array):
    ctx = lax.axis_size("ctx")
    rows, columns = array.shape
    return array.reshape(rows, ctx, columns // ctx).transpose(1, 0, 2)


def rows_from_slots(got, units):
    ctx, rows, columns = got.shape
    got = got.reshape(ctx, units, rows // units, columns).transpose(1, 0, 2, 3)
    return got.reshape(ctx * rows, columns).astype(jnp.float32)


def rows_to_blocks(array, units):
    got = lax.all_to_all(rows_to_slots(array), "ctx", 0, 0, tiled=True)
    return rows_from_slots(got, units)


def scatter_fsdp(*gradients):
    fsdp = lax.axis_size("fsdp")
    parts = [g.astype(BF16).reshape(fsdp, -1, g.shape[1]) for g in gradients]
    sizes = [part.shape[1] for part in parts]
    pad = -sum(sizes) % 16
    if pad:
        parts.append(jnp.zeros((fsdp, pad, gradients[0].shape[1]), BF16))
    joined = jnp.concatenate(parts, 1) if len(parts) > 1 else parts[0]
    joined = joined.reshape(-1, joined.shape[2])
    out = lax.psum_scatter(joined, "fsdp", scatter_dimension=0, tiled=True)
    starts = [sum(sizes[:i]) for i in range(len(sizes))]
    return [out[start : start + size] for start, size in zip(starts, sizes)]


def body(
    inputs,
    cotangent,
    norm_gain,
    query_proj,
    key_proj,
    value_proj,
    attn_proj,
    attn_gain,
    mixer_in,
    conv_taps,
    conv_bias,
    state_proj,
    step_proj,
    step_bias,
    decay_rate,
    skip_gain,
    mixer_out,
    ssm_gain,
    ffn_gain,
    gate_proj,
    up_proj,
    down_proj,
):
    ctx, fsdp = lax.axis_size("ctx"), lax.axis_size("fsdp")
    place = lax.axis_index("ctx")
    tokens = inputs[0].astype(jnp.float32)
    own, model = tokens.shape
    length = own * ctx
    inner = conv_bias.shape[0]
    mine = inner // ctx
    kv_mine = key_proj.shape[1] // ctx
    q_mine = query_proj.shape[1] // ctx
    hidden_units = unit_count(gate_proj.shape[1], ctx, fsdp)
    hidden_rows = hidden_units // fsdp
    hid = gate_proj.shape[1] // ctx
    group_size = query_proj.shape[1] // key_proj.shape[1]
    score_scale = HEAD ** (-0.5)

    hid_part = hid // fsdp
    hid_pad = -hid_part % 16
    hid_all = hid + fsdp * hid_pad
    attn_pad = -attn_proj.shape[0] % ctx
    attn_rows_mine = (attn_proj.shape[0] + attn_pad) // ctx
    state_rows, step_rows = state_proj.shape[0] // ctx, step_proj.shape[0]
    if ctx == 8:
        in_part, state_part, step_part = pack_in(
            query_proj, key_proj, value_proj, mixer_in, state_proj, step_proj
        )
        later = (gate_proj, up_proj, down_proj.T, mixer_out, attn_proj)
    else:
        in_part = jnp.concatenate(
            [block_columns(array) for array in (query_proj, key_proj, value_proj)]
            + my_columns(mixer_in[:, inner:], fsdp)
            + my_columns(mixer_in[:, :inner], fsdp),
            1,
        )
        later = ()
        state_part = jnp.pad(my_rows(state_proj, 1)[0], ((0, -state_rows % 16), (0, 0)))
        step_part = jnp.pad(
            jnp.concatenate(my_columns(step_proj, fsdp), 1), ((0, -step_rows % 16), (0, 0))
        )

        def hidden_columns(array):
            pieces = my_columns(array, hidden_units)
            if hid_pad:
                for f in range(fsdp, 0, -1):
                    pieces.insert(f * hidden_rows, jnp.zeros((array.shape[0], hid_pad), BF16))
            return pieces

        ffn_part = jnp.concatenate(hidden_columns(gate_proj) + hidden_columns(up_proj), 1)
        rows_part = jnp.concatenate(
            my_rows(down_proj, hidden_rows)
            + [jnp.zeros((hid_pad, model), BF16)]
            + my_rows(mixer_out, 1)
            + my_rows(jnp.pad(attn_proj, ((0, attn_pad), (0, 0))), 1),
            0,
        )
    mix_rows = mixer_out.shape[0] // ctx
    normed_all, grad_top, in_full, state_full, step_full, *parts = front(
        inputs[0], norm_gain[None], cotangent[0], in_part, state_part, step_part, later,
        hidden_units, 0,
    )
    if parts:
        ffn_part, rows_part = parts
    normed_all = normed_all.reshape(length, model)
    grad_top = grad_top.reshape(length, model)
    in_full = in_full.reshape(model, -1)
    state_full = state_full[:, :state_rows].reshape(-1, state_proj.shape[1])
    step_full = step_full[:, :step_rows].reshape(-1, mine)
    norm_scale = rms_scale(tokens)
    rows_full = lax.all_gather(rows_part, "fsdp", axis=0)
    ffn_full = over_fsdp(ffn_part)
    down_at = hid_part + hid_pad
    down_full = rows_full[:, :down_at].reshape(-1, model)
    mixout_full = rows_full[:, down_at : down_at + mix_rows].reshape(-1, model)
    attn_at = down_at + mix_rows
    attn_full = rows_full[:, attn_at : attn_at + attn_rows_mine].reshape(-1, model)
    attn_width = attn_full.shape[0]

    def mine_of(vector):
        return jnp.concatenate(my_columns(vector.reshape(-1, inner), fsdp), 1)

    taps, bias, skip, gain_ssm, bias_step = (
        mine_of(conv_taps),
        mine_of(conv_bias),
        mine_of(skip_gain),
        mine_of(ssm_gain),
        mine_of(step_bias),
    )
    rates = jnp.concatenate(
        [
            lax.dynamic_slice_in_dim(
                decay_rate, unit * (inner // fsdp) + place * (mine // fsdp), mine // fsdp, 0
            )
            for unit in range(fsdp)
        ],
        0,
    ).T
    pad = -mine % LANES

    def padded(values):
        return jnp.pad(values, ((0, 0), (0, pad)))

    projected_in = matmul(normed_all, in_full).astype(BF16)
    conv_src = projected_in[:, q_mine + 2 * kv_mine + mine :]

    padded_src = jnp.concatenate(
        [jnp.zeros((CONV - 1, mine), jnp.float32), conv_src.astype(jnp.float32)], 0
    )
    conv_pre = bias + sum(taps[tap][None] * padded_src[tap : tap + length] for tap in range(CONV))
    conv_act = jax.nn.silu(conv_pre).astype(BF16)
    conv_vals = conv_act.astype(jnp.float32)
    projected = sum_everywhere(matmul(conv_act, state_full).astype(BF16), 2).astype(jnp.float32)
    step_low = projected[:, :DT_RANK].astype(BF16)
    input_mat = projected[:, DT_RANK : DT_RANK + STATE]
    output_mat = projected[:, DT_RANK + STATE :]
    step_pre = matmul(step_low, step_full) + bias_step
    steps_dt = jax.nn.softplus(step_pre)
    in_b = jnp.broadcast_to(input_mat.astype(BF16)[:, :, None], (length, STATE, LANES))
    out_b = jnp.broadcast_to(output_mat.astype(BF16)[:, :, None], (length, STATE, LANES))
    rates_log2 = padded(-LOG2_E * rates)
    steps_pad, vals_pad = padded(steps_dt), padded(conv_vals)
    scan_out, states = scan_fwd(steps_pad, vals_pad, in_b, out_b, rates_log2)
    scan_out = scan_out[:, :mine]

    gate_z = projected_in[:, q_mine + 2 * kv_mine : q_mine + 2 * kv_mine + mine].astype(jnp.float32)
    def attn_to_channels(values):
        parts = jnp.pad(values.reshape(own, fsdp, -1), ((0, 0), (0, 0), (0, attn_pad)))
        parts = parts.reshape(own, fsdp, ctx, -1).transpose(2, 0, 1, 3).reshape(ctx, own, -1)
        return lax.all_to_all(parts, "ctx", 0, 0, tiled=True).reshape(length, -1)

    def attn_to_tokens(values):
        parts = values.reshape(ctx, own, -1)
        got = lax.all_to_all(parts, "ctx", 0, 0, tiled=True)
        got = got.reshape(ctx, own, fsdp, -1).transpose(1, 2, 0, 3).reshape(own, fsdp, -1)
        return got[:, :, : attn_proj.shape[0]].reshape(own, -1)

    if ctx == 8:
        branch_attn_c, attn_rows, *attn_kept = attention_forward(
            projected_in, attn_gain, key_proj.shape[1], 1
        )
        branch_attn_c = branch_attn_c.reshape(length, -1)
    else:
        queries = lax.all_to_all(projected_in[:, :q_mine], "ctx", 0, 1, tiled=True)
        keyvals = gather_shards(projected_in[:, q_mine : q_mine + 2 * kv_mine], 1)
        keys_all = keyvals[:, :, :kv_mine].transpose(1, 0, 2).reshape(length, KV_HEADS, HEAD)
        vals_all = keyvals[:, :, kv_mine:].transpose(1, 0, 2).reshape(length, KV_HEADS, HEAD)
        heads_q = queries.reshape(own, KV_HEADS, group_size, HEAD)
        row_ids = place * own + lax.broadcasted_iota(jnp.int32, (own, length), 0)
        col_ids = lax.broadcasted_iota(jnp.int32, (own, length), 1)
        allowed = (col_ids <= row_ids) & (col_ids > row_ids - WINDOW)

        def scores_of():
            raw = jnp.einsum("qhgd,khd->hgqk", heads_q, keys_all, preferred_element_type=jnp.float32)
            return jnp.where(allowed, raw * score_scale, -1e30)

        scores = scores_of()
        row_top = jnp.max(scores, axis=-1, keepdims=True)
        log_total = row_top + jnp.log(jnp.sum(jnp.exp(scores - row_top), axis=-1, keepdims=True))
        probs = jnp.exp(scores - log_total)
        probs_bf = probs.astype(BF16)
        attn_rows = jnp.einsum(
            "hgqk,khd->qhgd", probs_bf, vals_all, preferred_element_type=jnp.float32
        ).reshape(own, -1)
        attn_scale = rms_scale(attn_rows)
        branch_attn = (attn_rows * attn_scale * attn_gain).astype(BF16)
        branch_attn_c = attn_to_channels(branch_attn)

    ssm_raw = scan_out + skip * conv_vals
    gate_act = jax.nn.silu(gate_z)
    ssm_gated = ssm_raw * gate_act
    square = total_of(jnp.sum(ssm_gated * ssm_gated, axis=-1), 3)
    ssm_scale = lax.rsqrt(square / inner + EPSILON)[:, None]
    branch_ssm = (ssm_gated * ssm_scale * gain_ssm).astype(BF16)
    middle = tokens + 0.5 * reduce_products(
        [branch_attn_c, branch_ssm], [attn_full, mixout_full], False, 4
    )
    ffn_scale = rms_scale(middle)
    ffn_in = (middle * ffn_scale * ffn_gain).astype(BF16)
    if ctx == 8:
        pair_dw, down_dw, ffn_out, grad_ffn_in = ffn_both_ways(
            ffn_in, grad_top, ffn_full, down_full, 5
        )
    else:
        ffn_all = gather_tokens(ffn_in, 5)
        pre = matmul(ffn_all, ffn_full)
        gate_pre, up_pre = pre[:, :hid_all], pre[:, hid_all:]
        gate_silu = jax.nn.silu(gate_pre)
        hidden = (gate_silu * up_pre).astype(BF16)
        ffn_out = reduce_products([hidden], [down_full], False, 6)
        grad_hidden = right_trans(grad_top, down_full)
        grad_gate = (grad_hidden * up_pre * silu_slope(gate_pre)).astype(BF16)
        grad_up = (grad_hidden * gate_silu).astype(BF16)
        grad_pair = jnp.concatenate([grad_gate, grad_up], 1)
        grad_ffn_in = reduce_products([grad_pair], [ffn_full], True, 7)
        down_dw = left_trans(hidden, grad_top).astype(BF16)
        pair_dw = left_trans(ffn_all, grad_pair).astype(BF16)
    output = middle + ffn_out

    grad_ffn_in, down_dw, pair_dw = lax.optimization_barrier((grad_ffn_in, down_dw, pair_dw))
    (down_grad,) = scatter_fsdp(down_dw)
    (pair_grad,) = scatter_fsdp(pair_dw)
    grad_middle, grad_ffn_gain = norm_back(grad_ffn_in, middle, ffn_scale, ffn_gain)
    grad_middle = grad_middle + cotangent[0].astype(jnp.float32)
    grad_branch = (0.5 * grad_middle).astype(BF16)
    branch_all = gather_tokens(grad_branch, 8)
    attn_dw, mixout_dw = left_trans(branch_attn_c, branch_all), left_trans(branch_ssm, branch_all)
    grad_attn_c = right_trans(branch_all, attn_full).astype(BF16)
    if ctx == 8:
        grad_early, grad_attn_gain = attention_backward(
            grad_attn_c, attn_rows, attn_gain, attn_kept, 13
        )
        grad_attn_gain = grad_attn_gain[0]
    else:
        grad_attn = attn_to_tokens(grad_attn_c).astype(jnp.float32)
        grad_attn_raw, grad_attn_gain = norm_back(grad_attn, attn_rows, attn_scale, attn_gain)
        grad_heads = grad_attn_raw.astype(BF16).reshape(own, KV_HEADS, group_size, HEAD)
        grad_probs = jnp.einsum(
            "qhgd,khd->hgqk", grad_heads, vals_all, preferred_element_type=jnp.float32
        )
        row_dot = jnp.sum(probs * grad_probs, axis=-1, keepdims=True)
        grad_scores = (probs * (grad_probs - row_dot)).astype(BF16)
        grad_queries = score_scale * jnp.einsum(
            "hgqk,khd->qhgd", grad_scores, keys_all, preferred_element_type=jnp.float32
        ).reshape(own, -1)
        grad_keys = score_scale * jnp.einsum(
            "hgqk,qhgd->khd", grad_scores, heads_q, preferred_element_type=jnp.float32
        )
        grad_vals = jnp.einsum(
            "hgqk,qhgd->khd", probs_bf, grad_heads, preferred_element_type=jnp.float32
        )
        grad_queries = lax.all_to_all(
            grad_queries.astype(BF16).reshape(own, ctx, -1).transpose(1, 0, 2), "ctx", 0, 0, tiled=True
        ).reshape(length, -1)
        grad_kv = jnp.concatenate(
            [
                grad_keys.reshape(length, ctx, kv_mine).transpose(1, 0, 2),
                grad_vals.reshape(length, ctx, kv_mine).transpose(1, 0, 2),
            ],
            2,
        ).astype(BF16)
        grad_kv = jnp.sum(
            lax.all_to_all(grad_kv, "ctx", 0, 0, tiled=True).astype(jnp.float32), axis=0
        ).astype(BF16)
        grad_early = jnp.concatenate([grad_queries, grad_kv], 1)

    grad_early, attn_dw, mixout_dw, pair_grad = lax.optimization_barrier(
        (grad_early, attn_dw.astype(BF16), mixout_dw.astype(BF16), pair_grad)
    )
    attn_grad, mixout_grad = scatter_fsdp(attn_dw, mixout_dw)

    grad_norm = right_trans(branch_all, mixout_full)
    grad_ssm_gain = jnp.sum(grad_norm * ssm_gated * ssm_scale, axis=0)
    scaled = grad_norm * gain_ssm
    mean_dot = total_of(jnp.sum(scaled * ssm_gated, axis=-1), 9)[:, None] / inner
    grad_gated = ssm_scale * scaled - ssm_gated * ssm_scale**3 * mean_dot
    grad_scan = grad_gated * gate_act
    grad_gate_z = grad_gated * ssm_raw * silu_slope(gate_z)
    grad_skip = jnp.sum(grad_scan * conv_vals, axis=0)
    grad_gate_bf = grad_gate_z.astype(BF16)
    grad_early = jnp.concatenate([grad_early, grad_gate_bf], 1)
    (early_grad,) = scatter_fsdp(left_trans(normed_all, grad_early))
    pair_grad = pair_grad.reshape(-1, 2, fsdp, down_at)[..., :hid_part]
    pair_slots = to_slots(pair_grad.transpose(1, 0, 2, 3).reshape(-1, hid), hidden_units)
    down_slots = rows_to_slots(down_grad[:hid_part])
    pair_slots = lax.all_to_all(pair_slots, "ctx", 0, 0, tiled=True)
    down_slots = lax.all_to_all(down_slots, "ctx", 0, 0, tiled=True)
    grad_steps, grad_drive, grad_input_mat, grad_output_mat, grad_rate = scan_bwd(
        steps_pad, vals_pad, padded(grad_scan), in_b, out_b, rates_log2, states
    )
    grad_steps, pair_slots, down_slots, attn_grad, mixout_grad = lax.optimization_barrier(
        (grad_steps, pair_slots, down_slots, attn_grad, mixout_grad)
    )
    pair_blocks = from_slots(pair_slots, hidden_units)
    down_blocks = rows_from_slots(down_slots, hidden_rows)
    grad_steps, grad_drive, grad_rate = (
        grad_steps[:, :mine],
        grad_drive[:, :mine],
        -grad_rate[:, :mine],
    )
    grad_pre_full = grad_steps * jax.nn.sigmoid(step_pre)
    grad_step_bias = jnp.sum(grad_pre_full, axis=0)
    grad_pre = grad_pre_full.astype(BF16)
    step_dw = left_trans(step_low, grad_pre)
    grad_projected = sum_everywhere(
        jnp.concatenate(
            [right_trans(grad_pre, step_full), grad_input_mat, grad_output_mat], 1
        ).astype(BF16),
        10,
    )
    grad_state_proj = left_trans(conv_act, grad_projected)
    grad_conv_act = (
        right_trans(grad_projected, state_full) + grad_scan * skip + grad_drive
    ).astype(BF16)
    grad_conv_act, early_grad = lax.optimization_barrier((grad_conv_act, early_grad))
    grad_conv = grad_conv_act.astype(jnp.float32) * silu_slope(conv_pre)
    grad_conv_bias = jnp.sum(grad_conv, axis=0)
    grad_taps = jnp.stack(
        [jnp.sum(grad_conv * padded_src[tap : tap + length], axis=0) for tap in range(CONV)]
    )
    conv_tail = jnp.concatenate([grad_conv, jnp.zeros((CONV - 1, mine), jnp.float32)], 0)
    grad_src = sum(
        taps[tap][None] * conv_tail[CONV - 1 - tap : CONV - 1 - tap + length]
        for tap in range(CONV)
    )
    grad_src = grad_src.astype(BF16)
    src_grad, step_grad = scatter_fsdp(left_trans(normed_all, grad_src), step_dw)
    grad_normed = reduce_products([grad_early, grad_src], [in_full], True, 11)
    grad_tokens, grad_norm_gain = norm_back(grad_normed, tokens, norm_scale, norm_gain)
    grad_tokens = grad_tokens + grad_middle

    channel = jnp.concatenate(
        [
            grad_taps,
            jnp.stack([grad_conv_bias, grad_step_bias, grad_skip, grad_ssm_gain]),
            grad_rate,
            grad_state_proj.T,
        ],
        0,
    )
    gains = jnp.stack([grad_norm_gain, grad_attn_gain, grad_ffn_gain])
    channel = jnp.pad(channel, ((0, -channel.shape[0] % (8 * fsdp)), (0, 0)))
    gains = jnp.pad(gains, ((0, 5), (0, 0)))
    if ctx == 8 and ctx == 2 * fsdp and not attn_pad:
        (
            query_grad, key_grad, value_grad, mixer_grad, step_grad, attn_grad, mixout_grad, channel, gains,
        ) = finish(
            early_grad, src_grad, step_grad, attn_grad, mixout_grad, channel, gains,
            q_mine, kv_mine, 12,
        )
    else:
        channel, gains = settle_small(channel, gains, 12)
        channel = channel.reshape(ctx, -1, fsdp, mine // fsdp).transpose(1, 2, 0, 3)
        channel = channel.reshape(-1, inner)
        late_at = q_mine + 2 * kv_mine
        query_grad = early_grad[:, :q_mine].astype(jnp.float32)
        key_grad = early_grad[:, q_mine : q_mine + kv_mine].astype(jnp.float32)
        value_grad = early_grad[:, q_mine + kv_mine : late_at].astype(jnp.float32)
        mixer_grad = to_blocks(
            jnp.concatenate([src_grad, early_grad[:, late_at:]], 1), 2 * fsdp
        )
        step_grad = to_blocks(step_grad, fsdp)
        attn_grad = rows_to_blocks(attn_grad, 1)[: attn_proj.shape[0]]
        mixout_grad = rows_to_blocks(mixout_grad, 1)
    sum_norm_gain, sum_attn_gain, sum_ffn_gain = gains[0], gains[1], gains[2]
    half = pair_blocks.shape[0] // 2
    return (
        output[None],
        grad_tokens[None],
        sum_norm_gain,
        query_grad,
        key_grad,
        value_grad,
        attn_grad,
        sum_attn_gain,
        mixer_grad,
        channel[:CONV],
        channel[CONV],
        channel[CONV + 4 + STATE : CONV + 4 + STATE + state_proj.shape[1]].T,
        step_grad,
        channel[CONV + 1],
        channel[CONV + 4 : CONV + 4 + STATE].T,
        channel[CONV + 2],
        mixout_grad,
        channel[CONV + 3],
        sum_ffn_gain,
        pair_blocks[:half],
        pair_blocks[half:],
        down_blocks,
    )


def solution(mesh):
    rows, whole = P("fsdp", None), P()
    blocks, sequence = P("fsdp", "ctx"), P("fsdp", "ctx", None)
    return jax.shard_map(
        body,
        mesh=mesh,
        in_specs=(
            sequence, sequence, whole, rows, rows, rows, rows, whole, rows, whole, whole,
            rows, rows, whole, whole, whole, rows, whole, whole, rows, rows, rows,
        ),
        out_specs=(
            sequence, sequence, whole, blocks, blocks, blocks, blocks, whole, blocks, whole, whole,
            whole, blocks, whole, whole, whole, blocks, whole, whole, blocks, blocks, blocks,
        ),
        check_vma=False,
    )
```

```python
import functools
import jax
import jax.numpy as jnp
from jax import lax
from jax.experimental import pallas as pl
from jax.experimental.pallas import tpu as pltpu
from jax.sharding import PartitionSpec as P

LANES = 128
STATE = 16
CHUNK = 128
HEAD = 64
KV_HEADS = 5
CONV = 4
DT_RANK = 100
WINDOW = 1024
EPSILON = 1e-06
LOG2_E = 1.4426950408889634
BF16 = jnp.bfloat16


MESH = pl.DeviceIdType.MESH
VMEM_LIMIT = 56 * 1024 * 1024
IN_VMEM = pl.BlockSpec(memory_space=pltpu.VMEM)


def flip(index, bit):
    return index + (1 - 2 * ((index // (1 << bit)) % 2)) * (1 << bit)


def greet(me, bits):
    barrier = pltpu.get_barrier_semaphore()
    for bit in range(bits):
        pl.semaphore_signal(
            barrier, inc=1, device_id={"ctx": flip(me, bit)}, device_id_type=MESH
        )
    pl.semaphore_wait(barrier, bits)


def halves_of(rows):
    half = rows // 2 if rows % 32 == 0 else rows // 32 * 16
    return (pl.ds(0, half), pl.ds(half, rows - half))


class Copies:
    def __init__(self, axis, send_sem, recv_sem):
        self.axis, self.send_sem, self.recv_sem = axis, send_sem, recv_sem
        self.started = []
        self.count = 0

    def make(self, source, target, device):
        copy = pltpu.make_async_remote_copy(
            src_ref=source,
            dst_ref=target,
            send_sem=self.send_sem.at[self.count],
            recv_sem=self.recv_sem.at[self.count],
            device_id={self.axis: device},
            device_id_type=MESH,
        )
        self.count += 1
        return copy

    def send(self, source, target, device):
        copy = self.make(source, target, device)
        copy.start()
        self.started.append(copy)
        return copy

    def finish(self):
        for copy in self.started:
            copy.wait_send()


def gather_sems(bits):
    return 1 + 2 * sum(1 << p for p in range(bits - 1)) + 2 * ((1 << (bits - 1)) - 1)


def gather_steps(copies, bits, out_ref):
    me = lax.axis_index("ctx")
    parts = halves_of(out_ref.shape[1])
    orders = (list(range(1, bits)), list(range(bits - 1, 0, -1)))

    def send(bit, shard, part):
        at = out_ref.at[shard] if part is None else out_ref.at[shard, part]
        return copies.send(at, at, flip(me, bit))

    known = ([me], [me])
    last, flying = [], [None, None]

    def begin():
        for h in range(2):
            flying[h] = [send(orders[h][0], shard, parts[h]) for shard in known[h]]
        last.append(send(0, me, None))

    def turn(phase, h):
        bit = orders[h][phase]
        for copy in flying[h]:
            copy.wait_recv()
        fresh = [flip(shard, bit) for shard in known[h]]
        known[h].extend(fresh)
        if phase + 1 < bits - 1:
            flying[h] = [send(orders[h][phase + 1], shard, parts[h]) for shard in known[h]]
        last.extend(send(0, shard, parts[h]) for shard in fresh)

    def end():
        for copy in last:
            copy.wait_recv()

    turns = [functools.partial(turn, p, h) for p in range(bits - 1) for h in range(2)]
    return [begin] + turns + [end]


def gather_kernel(bits, x_ref, out_ref, send_sem, recv_sem):
    me = lax.axis_index("ctx")
    greet(me, bits)
    out_ref[me] = x_ref[...]
    copies = Copies("ctx", send_sem, recv_sem)
    for step in gather_steps(copies, bits, out_ref):
        step()
    copies.finish()


def ctx_bits():
    return lax.axis_size("ctx").bit_length() - 1


def params(collective_id):
    return pltpu.CompilerParams(
        collective_id=collective_id, has_side_effects=True, vmem_limit_bytes=VMEM_LIMIT
    )


def gather_shards(x, collective_id):
    bits, ctx = ctx_bits(), lax.axis_size("ctx")
    sems = pltpu.SemaphoreType.DMA((gather_sems(bits),))
    return pl.pallas_call(
        functools.partial(gather_kernel, bits),
        out_shape=jax.ShapeDtypeStruct((ctx,) + x.shape, x.dtype),
        in_specs=[IN_VMEM],
        out_specs=IN_VMEM,
        scratch_shapes=[sems, sems],
        compiler_params=params(collective_id),
        name="gather_shards",
    )(x)


def gather_tokens(x, collective_id):
    return gather_shards(x, collective_id).reshape(-1, x.shape[1])


def row_parts(rows, count):
    tiles = rows // 16
    edges = [16 * (tiles * i // count) for i in range(count)] + [rows]
    return [pl.ds(a, b - a) for a, b in zip(edges[:-1], edges[1:]) if b > a]


def line_steps(copies, out_refs, pieces):
    me, size = lax.axis_index("fsdp"), lax.axis_size("fsdp")
    plans = []
    for way in (1, -1):
        for distance in range(size - 1):
            for ref, part in pieces:
                shard = me - way * distance
                inside = jnp.logical_and(shard >= 0, shard < size)
                held = jnp.where(inside, shard, me)
                to = me + way
                go = jnp.logical_and(inside, jnp.logical_and(to >= 0, to < size))
                target = jnp.where(jnp.logical_and(to >= 0, to < size), to, me - way)
                at = out_refs[ref].at[held, part]
                plans.append((way, distance, go, copies.make(at, at, target)))
    table = {}
    for way, distance, go, copy in plans:
        table.setdefault((way, distance), []).append((go, copy))

    def begin():
        for index in range(len(pieces)):
            for way in (1, -1):
                go, copy = table[way, 0][index]
                pl.when(go)(copy.start)

    def turn(distance, index):
        for way in (1, -1):
            _, came = table[way, distance - 1][index]
            origin = me - way * distance
            pl.when(jnp.logical_and(origin >= 0, origin < size))(came.wait_recv)
            if distance < size - 1:
                go, copy = table[way, distance][index]
                pl.when(go)(copy.start)

    def end():
        for way in (1, -1):
            for distance in range(size - 1):
                for go, copy in table[way, distance]:
                    pl.when(go)(copy.wait_send)

    turns = [
        functools.partial(turn, d, i) for d in range(1, size) for i in range(len(pieces))
    ]
    return [begin] + turns, end


def front_kernel(
    bits, count, turned, pack_first, pack, x_ref, gain_ref, top_ref, *rest,
):
    number = 6 if pack_first["scratch"] else 3
    first_refs, rest = rest[:number], rest[number:]
    weights, rest = rest[: pack["inputs"]], rest[pack["inputs"] :]
    normed_ref, tops_ref, in_out, state_out, step_out = rest[:5]
    packed, rest = rest[5 : 5 + pack["outputs"]], rest[5 + pack["outputs"] :]
    ctx_send, ctx_recv, line_send, line_recv = rest[:4]
    first_scratch, rest = rest[4 : 4 + len(pack_first["scratch"])], rest[4 + len(pack_first["scratch"]) :]
    me, row, rows = lax.axis_index("ctx"), lax.axis_index("fsdp"), lax.axis_size("fsdp")
    barrier = pltpu.get_barrier_semaphore()
    for bit in range(bits):
        pl.semaphore_signal(
            barrier, inc=1, device_id={"ctx": flip(me, bit)}, device_id_type=MESH
        )
    for to in (row - 1, row + 1):
        there = jnp.logical_and(to >= 0, to < rows)

        @pl.when(there)
        def _():
            pl.semaphore_signal(
                barrier, inc=1, device_id={"fsdp": jnp.where(there, to, row)}, device_id_type=MESH
            )

    if first_scratch:
        copies = pack_in_begin(first_refs, first_scratch)
        pack_in(row, copies, first_refs, first_scratch, in_out, state_out, step_out)
    else:
        for out, ref in zip((in_out, state_out, step_out), first_refs):
            out[row] = ref[...]
    neighbours = jnp.where(row > 0, 1, 0) + jnp.where(row < rows - 1, 1, 0)
    pl.semaphore_wait(barrier, bits + neighbours)

    line = Copies("fsdp", line_send, line_recv)
    across = Copies("ctx", ctx_send, ctx_recv)
    pieces = [(0, part) for part in row_parts(in_out.shape[1], count)]
    pieces = [(1, pl.ds(0, state_out.shape[1])), (2, pl.ds(0, step_out.shape[1]))] + pieces
    line_list, line_end = line_steps(line, (in_out, state_out, step_out), pieces)
    line_list[0]()
    tokens = x_ref[...].astype(jnp.float32)
    if turned:
        tokens = tokens.T
    scale = lax.rsqrt(jnp.mean(tokens * tokens, axis=-1, keepdims=True) + EPSILON)
    normed_ref[me] = (tokens * scale * gain_ref[...]).astype(normed_ref.dtype)
    first = gather_steps(across, bits, normed_ref)
    first[0]()
    tops = top_ref[...].astype(jnp.float32)
    tops_ref[me] = (tops.T if turned else tops).astype(tops_ref.dtype)
    second = gather_steps(across, bits, tops_ref)
    steps = list(pack["steps"](me, weights, packed, rest)) if weights else []
    token_rest = first[1:-1] + [second[0]] + second[1:-1] + [first[-1], second[-1]]
    line_rest = line_list[1:]
    tokens_done = packs_done = 0
    spread = len(line_rest) * 3 // 4
    for i, step in enumerate(line_rest):
        upto = min(len(steps), len(steps) * (i + 1) // max(1, spread))
        for pack_step in steps[packs_done:upto]:
            pack_step()
        packs_done = max(packs_done, upto)
        step()
        upto = min(len(token_rest), len(token_rest) * (i + 1) // spread)
        for token_step in token_rest[tokens_done:upto]:
            token_step()
        tokens_done = max(tokens_done, upto)
    across.finish()
    line_end()


def front(x, gain, top, first, later, hidden_units, collective_id):
    bits, ctx, fsdp = ctx_bits(), lax.axis_size("ctx"), lax.axis_size("fsdp")
    count = 5
    ctx_sems = pltpu.SemaphoreType.DMA((2 * gather_sems(bits),))
    line_sems = pltpu.SemaphoreType.DMA((2 * fsdp * (count + 2),))
    pack_first, pack = pack_in_plan(first), pack_out_plan(later, hidden_units)
    turned = bool(later)
    tokens = jax.ShapeDtypeStruct(x.shape[::-1] if turned else x.shape, x.dtype)
    in_any = pl.BlockSpec(memory_space=pl.ANY)

    def stacked(array, size):
        return jax.ShapeDtypeStruct((size,) + array.shape, array.dtype)

    return pl.pallas_call(
        functools.partial(front_kernel, bits, count, turned, pack_first, pack),
        out_shape=[stacked(tokens, ctx), stacked(tokens, ctx)]
        + [stacked(part, fsdp) for part in pack_first["shapes"]]
        + pack["shapes"],
        in_specs=[IN_VMEM] * 3
        + [in_any if i in pack_first["any"] else IN_VMEM for i in range(len(first))]
        + [in_any] * len(later),
        out_specs=[IN_VMEM] * (5 + pack["outputs"]),
        scratch_shapes=[ctx_sems, ctx_sems, line_sems, line_sems]
        + pack_first["scratch"]
        + pack["scratch"],
        compiler_params=params(collective_id),
        name="front",
    )(x, gain, top, *first, *later)


def product(x, weight, trans):
    dims = (((1,), (1 if trans else 0,)), ((), ()))
    return lax.dot_general(x, weight, dims, preferred_element_type=jnp.float32)


def subsets(chosen):
    out = [()]
    for bit in chosen:
        out = out + [s + (bit,) for s in out]
    return out


def flipped(shard, flips):
    for bit in flips:
        shard = flip(shard, bit)
    return shard


class Reducer:
    def __init__(self, copies, bits, part_ref, inbox, out_ref):
        self.copies, self.bits, self.part_ref = copies, bits, part_ref
        self.inbox, self.out_ref = inbox, out_ref
        self.me = lax.axis_index("ctx")
        self.parts = halves_of(out_ref.shape[0])
        self.orders = (list(range(1, bits)), list(range(bits - 1, 0, -1)))
        self.everyone = subsets(range(1, bits))[::-1]
        self.slots = {flips: slot for slot, flips in enumerate(self.everyone)}
        self.first = {}
        self.flying = [{}, {}]

    def to_sibling(self, flips, partial):
        slot = self.slots[flips]
        self.part_ref[slot] = partial.astype(self.part_ref.dtype)
        self.first[flips] = self.copies.send(
            self.part_ref.at[slot], self.inbox[0].at[slot], flip(self.me, 0)
        )

    def pass_on(self, h, phase, flips, following):
        bit = self.orders[h][phase]
        if bit in flips:
            kept = tuple(b for b in flips if b != bit)
            following[kept] = self.copies.send(
                self.inbox[0].at[self.slots[flips], self.parts[h]],
                self.inbox[1 + phase].at[len(following), self.parts[h]],
                flip(self.me, bit),
            )

    def send_parts(self, parts_ref):
        for flips in self.everyone:
            self.first[flips] = self.copies.send(
                parts_ref.at[flipped(self.me, flips + (0,))],
                self.inbox[0].at[self.slots[flips]],
                flip(self.me, 0),
            )

    def own(self, flips, partial):
        self.first[flips].wait_recv()
        kept_ref, slot = self.inbox[0], self.slots[flips]
        kept_ref[slot] = (partial + kept_ref[slot].astype(jnp.float32)).astype(kept_ref.dtype)
        for h in range(2):
            self.pass_on(h, 0, flips, self.flying[h])

    def turn(self, phase, h):
        kept_ref = self.inbox[0]
        part, following = self.parts[h], {}
        for box, (flips, copy) in enumerate(list(self.flying[h].items())):
            copy.wait_recv()
            slot = self.slots[flips]
            total = kept_ref[slot, part].astype(jnp.float32) + self.inbox[1 + phase][
                box, part
            ].astype(jnp.float32)
            if phase == self.bits - 2:
                self.out_ref[part] = total
            else:
                kept_ref[slot, part] = total.astype(kept_ref.dtype)
                self.pass_on(h, phase + 1, flips, following)
        self.flying[h] = following

    def turns(self):
        return [functools.partial(self.turn, p, h) for p in range(self.bits - 1) for h in range(2)]

    def finish(self):
        for turn in self.turns():
            turn()


def reducer_boxes(ctx, bits, rows, columns):
    boxes = [ctx // 2, ctx // 2] + [ctx // 4 >> p for p in range(bits - 1)]
    sems = boxes[0] + 2 * sum(boxes[2:])
    return [pltpu.VMEM((box, rows, columns), BF16) for box in boxes], sems


def reduce_kernel(bits, trans, joint, *refs):
    count = len(trans)
    weights = 1 if joint else count
    x_refs, w_refs, out_ref = refs[:count], refs[count : count + weights], refs[count + weights]
    part_ref, inbox = refs[count + weights + 1], refs[count + weights + 2 : -2]
    me = lax.axis_index("ctx")
    greet(me, bits)
    if joint:
        whole, w_refs, inbox = w_refs[0], inbox[-count:], inbox[:-count]
        at = 0
        for w_ref in w_refs:
            wide = w_ref.shape[1]
            w_ref[...] = whole[:, at : at + wide]
            at += wide
    copies = Copies("ctx", *refs[-2:])
    reducer = Reducer(copies, bits, part_ref, inbox, out_ref)

    def partial(flips):
        shard = flipped(me, flips)
        return sum(
            product(x_ref[shard], w_ref[...], way)
            for x_ref, w_ref, way in zip(x_refs, w_refs, trans)
        )

    for flips in reducer.everyone:
        reducer.to_sibling(flips, partial(flips + (0,)))
    for flips in reducer.everyone:
        reducer.own(flips, partial(flips))
    reducer.finish()
    copies.finish()


def reduce_products(lefts, weights, trans, collective_id):
    ctx, bits = lax.axis_size("ctx"), ctx_bits()
    rows = lefts[0].shape[0] // ctx
    columns = weights[0].shape[0 if trans else 1]
    joint = len(weights) < len(lefts)
    boxes, count = reducer_boxes(ctx, bits, rows, columns)
    if joint:
        boxes = boxes + [pltpu.VMEM((columns, x.shape[1]), BF16) for x in lefts]
    sems = pltpu.SemaphoreType.DMA((count,))
    return pl.pallas_call(
        functools.partial(reduce_kernel, bits, (trans,) * len(lefts), joint),
        out_shape=jax.ShapeDtypeStruct((rows, columns), jnp.float32),
        in_specs=[IN_VMEM] * (len(lefts) + len(weights)),
        out_specs=IN_VMEM,
        scratch_shapes=boxes + [sems, sems],
        compiler_params=params(collective_id),
        name="reduce_products",
    )(*[x.reshape(ctx, rows, -1) for x in lefts], *weights)


def relay_copies(pair_send, pair_recv, down_send, down_recv, send_sem, recv_sem):
    size = pair_send.shape[0]
    me = lax.axis_index("ctx")
    copies = Copies("ctx", send_sem, recv_sem)
    return [
        copies.make(send.at[(me + turn) % size], recv.at[me], (me + turn) % size)
        for send, recv in ((pair_send, pair_recv), (down_send, down_recv))
        for turn in range(1, size)
    ]


def relay_begin(units, pair_ref, down_ref, pair_send, pair_recv, down_send, down_recv, *sems):
    size = pair_send.shape[0]
    me = lax.axis_index("ctx")
    greet_all(me, size)
    wide, block = pair_send.shape[2] // 2, down_send.shape[2]
    half, part = pair_ref.shape[1] // 2, down_ref.shape[0]
    for d in range(size):
        at = d // units * part + d % units * wide
        pair_send[d, :, :wide] = pair_ref[:, at : at + wide]
        pair_send[d, :, wide:] = pair_ref[:, half + at : half + at + wide]
        down_send[d] = down_ref[:, d * block : (d + 1) * block]
    for copy in relay_copies(pair_send, pair_recv, down_send, down_recv, *sems):
        copy.start()
    pair_recv[me] = pair_send[me]
    down_recv[me] = down_send[me]


def relay_end(units, gate_out, up_out, down_out, pair_send, pair_recv, down_send, down_recv, *sems):
    size, wide = pair_send.shape[0], pair_send.shape[2] // 2
    for copy in relay_copies(pair_send, pair_recv, down_send, down_recv, *sems):
        copy.wait()
    for s in range(size):
        at = s * wide
        gate_out[:, at : at + wide] = pair_recv[s, :, :wide].astype(jnp.float32)
        up_out[:, at : at + wide] = pair_recv[s, :, wide:].astype(jnp.float32)
        for u in range(units):
            to = u * size * wide + at
            down_out[to : to + wide] = down_recv[s, u * wide : (u + 1) * wide].astype(jnp.float32)


def greet_all(me, size):
    barrier = pltpu.get_barrier_semaphore()
    for turn in range(1, size):
        pl.semaphore_signal(
            barrier, inc=1, device_id={"ctx": (me + turn) % size}, device_id_type=MESH
        )
    pl.semaphore_wait(barrier, size - 1)


def sum_kernel(size, x_ref, out_ref, send_ref, inbox, all_ref, send_sem, recv_sem):
    me = lax.axis_index("ctx")
    greet_all(me, size)
    columns = x_ref.shape[2]
    copies = Copies("ctx", send_sem, recv_sem)
    send_ref[:, columns:] = jnp.zeros((size, send_ref.shape[1] - columns, x_ref.shape[1]), BF16)
    for e in range(size):
        send_ref[e, :columns] = x_ref[e].astype(jnp.float32).T.astype(BF16)
    come = []
    for turn in range(1, size):
        to = (me + turn) % size
        come.append(copies.send(send_ref.at[to], inbox.at[turn - 1], to))
    total = send_ref[me].astype(jnp.float32)
    for turn in range(1, size):
        come[turn - 1].wait_recv()
        total = total + inbox[turn - 1].astype(jnp.float32)
    all_ref[me] = total.astype(BF16)
    come = [
        copies.send(all_ref.at[me], all_ref.at[me], (me + turn) % size) for turn in range(1, size)
    ]
    for copy in come:
        copy.wait_recv()
    for e in range(size):
        out_ref[e] = all_ref[e].astype(jnp.float32).T[:, :columns].astype(out_ref.dtype)
    copies.finish()


def sum_everywhere(partial, collective_id):
    ctx = lax.axis_size("ctx")
    rows, columns = partial.shape[0] // ctx, partial.shape[1]
    high = columns + -columns % 16
    sems = pltpu.SemaphoreType.DMA((2 * (ctx - 1),))
    return pl.pallas_call(
        functools.partial(sum_kernel, ctx),
        out_shape=jax.ShapeDtypeStruct((ctx, rows, columns), partial.dtype),
        in_specs=[IN_VMEM],
        out_specs=IN_VMEM,
        scratch_shapes=[
            pltpu.VMEM((ctx, high, rows), BF16),
            pltpu.VMEM((ctx - 1, high, rows), BF16),
            pltpu.VMEM((ctx, high, rows), BF16),
            sems, sems,
        ],
        compiler_params=params(collective_id),
        name="sum_everywhere",
    )(partial.reshape(ctx, rows, columns)).reshape(partial.shape)


def total_kernel(size, x_ref, out_ref, inbox, send_sem, recv_sem):
    me = lax.axis_index("ctx")
    greet_all(me, size)
    copies = Copies("ctx", send_sem, recv_sem)
    come = [
        copies.send(x_ref, inbox.at[turn - 1], (me + turn) % size) for turn in range(1, size)
    ]
    inbox_total = x_ref[...]
    for turn in range(1, size):
        come[turn - 1].wait_recv()
        inbox_total = inbox_total + inbox[turn - 1]
    out_ref[...] = inbox_total
    copies.finish()


def total_of(rows_sum, collective_id):
    ctx = lax.axis_size("ctx")
    flat = rows_sum.reshape(-1, LANES)
    sems = pltpu.SemaphoreType.DMA((ctx - 1,))
    return pl.pallas_call(
        functools.partial(total_kernel, ctx),
        out_shape=jax.ShapeDtypeStruct(flat.shape, flat.dtype),
        in_specs=[IN_VMEM],
        out_specs=IN_VMEM,
        scratch_shapes=[pltpu.VMEM((ctx - 1,) + flat.shape, flat.dtype), sems, sems],
        compiler_params=params(collective_id),
        name="total_of",
    )(flat).reshape(rows_sum.shape)


def settle_kernel(
    bits, size, count, channel_ref, gain_ref, all_ref, sums_ref,
    row_inbox, gain_inbox, line_inbox, ctx_send, ctx_recv, line_send, line_recv,
):
    me, row = lax.axis_index("ctx"), lax.axis_index("fsdp")
    barrier = pltpu.get_barrier_semaphore()
    for turn in range(1, size):
        pl.semaphore_signal(
            barrier, inc=1, device_id={"ctx": (me + turn) % size}, device_id_type=MESH
        )
    for turn in range(1, count):
        pl.semaphore_signal(
            barrier, inc=1, device_id={"fsdp": (row + turn) % count}, device_id_type=MESH
        )
    pl.semaphore_wait(barrier, size - 1 + count - 1)
    across, line = Copies("ctx", ctx_send, ctx_recv), Copies("fsdp", line_send, line_recv)
    band = channel_ref.shape[0] // count

    def band_of(index):
        return pl.ds(pl.multiple_of(index * band, 8), band)

    rows_come = []
    for turn in range(1, count):
        to = (row + turn) % count
        rows_come.append(line.send(channel_ref.at[band_of(to)], row_inbox.at[turn - 1], to))
    gains_come = [
        across.send(gain_ref, gain_inbox.at[turn - 1], (me + turn) % size)
        for turn in range(1, size)
    ]
    total = channel_ref[band_of(row)]
    for turn in range(1, count):
        rows_come[turn - 1].wait_recv()
        total = total + row_inbox[turn - 1]
    all_ref[me, band_of(row)] = total
    at = all_ref.at[me, band_of(row)]
    bands_come = [line.send(at, at, (row + turn) % count) for turn in range(1, count)]
    total = gain_ref[...]
    for turn in range(1, size):
        gains_come[turn - 1].wait_recv()
        total = total + gain_inbox[turn - 1]
    line_inbox[0] = total
    line_come = [
        line.send(line_inbox.at[0], line_inbox.at[turn], (row + turn) % count)
        for turn in range(1, count)
    ]
    for copy in bands_come:
        copy.wait_recv()
    for step in gather_steps(across, bits, all_ref):
        step()
    total = line_inbox[0]
    for turn in range(1, count):
        line_come[turn - 1].wait_recv()
        total = total + line_inbox[turn]
    sums_ref[...] = total
    across.finish()
    line.finish()


def settle_small(channel, gains, collective_id):
    ctx, fsdp, bits = lax.axis_size("ctx"), lax.axis_size("fsdp"), ctx_bits()
    ctx_sems = pltpu.SemaphoreType.DMA((ctx - 1 + gather_sems(bits),))
    line_sems = pltpu.SemaphoreType.DMA((3 * (fsdp - 1),))
    rows, columns = channel.shape
    return pl.pallas_call(
        functools.partial(settle_kernel, bits, ctx, fsdp),
        out_shape=[
            jax.ShapeDtypeStruct((ctx, rows, columns), jnp.float32),
            jax.ShapeDtypeStruct(gains.shape, jnp.float32),
        ],
        in_specs=[IN_VMEM] * 2,
        out_specs=[IN_VMEM] * 2,
        scratch_shapes=[
            pltpu.VMEM((fsdp - 1, rows // fsdp, columns), jnp.float32),
            pltpu.VMEM((ctx - 1,) + gains.shape, jnp.float32),
            pltpu.VMEM((fsdp,) + gains.shape, jnp.float32),
            ctx_sems, ctx_sems, line_sems, line_sems,
        ],
        compiler_params=params(collective_id),
        name="settle_small",
    )(channel, gains)


def plane_gather(copies, out_ref):
    me = lax.axis_index("ctx")
    parts = halves_of(out_ref.shape[1])
    held = {}

    def send(name, bit, flips, part=None):
        shard = flipped(me, flips)
        at = out_ref.at[shard] if part is None else out_ref.at[shard, part]
        held[name] = copies.send(at, at, flip(me, bit))

    def start():
        for bit in (1, 2, 0):
            send(("own", bit), bit, ())

    def forward():
        held["own", 1].wait_recv()
        send(("corner", 2), 2, (1,), parts[0])
        held["own", 2].wait_recv()
        send(("corner", 1), 1, (2,), parts[1])
        send(("core", (1,)), 0, (1,))
        send(("core", (2,)), 0, (2,))

    def corner():
        held["corner", 2].wait_recv()
        held["corner", 1].wait_recv()
        send(("core", (1, 2)), 0, (1, 2))

    def wait(flips):
        held["core", flips].wait_recv() if flips else held["own", 0].wait_recv()

    return start, forward, corner, wait


def ffn_kernel(
    x_ref, top_ref, pair_w, down_w,
    pair_dw, down_dw, out_ref, grad_ref,
    all_ref, hidden_ref, pair_ref, own_ref, part_grad, *rest,
):
    bits = 3
    me = lax.axis_index("ctx")
    greet(me, bits)
    all_ref[me] = x_ref[...]
    copies = Copies("ctx", *rest[-2:])
    start, forward, corner, wait = plane_gather(copies, all_ref)
    reducer = Reducer(copies, bits, part_grad, rest[:-2], grad_ref)
    rows, model = x_ref.shape
    hid = hidden_ref.shape[2]
    core = me % 2

    def work(slot, flips):
        first = 2 * (flipped(me, flips) // 2)
        pair = pl.ds(first, 2)
        x = all_ref[pair].reshape(2 * rows, model)
        pre = product(x, pair_w[...], False)
        gate, up = pre[:, :hid], pre[:, hid:]
        logistic = jax.nn.sigmoid(gate)
        gate_silu = gate * logistic
        hidden = (gate_silu * up).astype(BF16)
        hidden_ref[pair] = hidden.reshape(2, rows, hid)
        top = top_ref[pair].reshape(2 * rows, model)
        grad_hidden = product(top, down_w[...], True)
        slope = logistic * (1.0 + gate * (1.0 - logistic))
        pair_ref[pair, :, :hid] = (grad_hidden * up * slope).astype(BF16).reshape(2, rows, hid)
        pair_ref[pair, :, hid:] = (grad_hidden * gate_silu).astype(BF16).reshape(2, rows, hid)
        grads = pair_ref[pair].reshape(2 * rows, 2 * hid)
        value = product(grads, pair_w[...], True)
        low, high = value[:rows], value[rows:]
        own_ref[slot] = jnp.where(core == 0, low, high)
        reducer.to_sibling(flips, jnp.where(core == 0, high, low))
        value = product(hidden, down_w[...], False)
        out_ref[pair] = value.astype(BF16).reshape(2, rows, model)

    def settle(slot, flips):
        reducer.own(flips, own_ref[slot])

    start()
    wait(())
    work(0, ())
    forward()
    wait((1,))
    work(1, (1,))
    settle(0, ())
    corner()
    wait((2,))
    work(2, (2,))
    settle(1, (1,))
    wait((1, 2))
    work(3, (1, 2))
    settle(2, (2,))
    settle(3, (1, 2))

    def band(out, left_ref, right_ref, low, high):
        left = left_ref[:, :, low:high].reshape(size * rows, high - low)
        right = right_ref[...].reshape(size * rows, right_ref.shape[2])
        out[low:high] = lax.dot_general(
            left, right, (((0,), (0,)), ((), ())), preferred_element_type=jnp.float32
        ).astype(out.dtype)

    def bands(out, left_ref, right_ref, count):
        wide = left_ref.shape[2]
        tiles = -(-wide // 128)
        edges = [min(wide, 128 * (tiles * i // count)) for i in range(count + 1)]
        return [
            functools.partial(band, out, left_ref, right_ref, low, high)
            for low, high in zip(edges[:-1], edges[1:])
        ]

    size = all_ref.shape[0]
    work_left = bands(down_dw, hidden_ref, top_ref, 2) + bands(pair_dw, all_ref, pair_ref, 4)
    turns = reducer.turns()
    done = 0
    for i, turn in enumerate(turns):
        upto = len(work_left) * (i + 1) // len(turns)
        for item in work_left[done:upto]:
            item()
        done = upto
        turn()
    copies.finish()


def ffn_both_ways(ffn_in, top, pair_full, down_full, collective_id):
    ctx, bits = lax.axis_size("ctx"), ctx_bits()
    rows, model = ffn_in.shape
    hid = down_full.shape[0]
    boxes, count = reducer_boxes(ctx, bits, rows, model)
    sems = pltpu.SemaphoreType.DMA((count + 8,))
    return pl.pallas_call(
        ffn_kernel,
        out_shape=[
            jax.ShapeDtypeStruct((model, 2 * hid), BF16),
            jax.ShapeDtypeStruct((hid, model), BF16),
            jax.ShapeDtypeStruct((ctx, rows, model), BF16),
            jax.ShapeDtypeStruct((rows, model), jnp.float32),
        ],
        in_specs=[IN_VMEM] * 4,
        out_specs=[IN_VMEM] * 4,
        scratch_shapes=[
            pltpu.VMEM((ctx, rows, model), BF16),
            pltpu.VMEM((ctx, rows, hid), BF16),
            pltpu.VMEM((ctx, rows, 2 * hid), BF16),
            pltpu.VMEM((ctx // 2, rows, model), jnp.float32),
        ]
        + boxes
        + [sems, sems],
        compiler_params=params(collective_id),
        name="ffn_both_ways",
    )(ffn_in, top.reshape(ctx, rows, model), pair_full, down_full)


def pieces_of(start, width, span):
    out = []
    at = start
    while at < start + width:
        block = at // span
        end = min(start + width, (block + 1) * span)
        out.append((block, at - start, end - start, at - block * span))
        at = end
    return out


def exchange(copies, send_ref, recv_ref, me, size):
    recv_ref[me] = send_ref[me]
    return [
        copies.send(send_ref.at[(me + turn) % size], recv_ref.at[me], (me + turn) % size)
        for turn in range(1, size)
    ]


def attention_kernel(
    size, fsdp, proj_ref, gain_ref,
    branch_ref, rows_ref, prob_ref, inverse_ref, q_ref, k_ref, v_ref,
    q_send, q_recv, kv_all, score_ref, attn_send, send_sem, recv_sem,
):
    bits = size.bit_length() - 1
    me = lax.axis_index("ctx")
    own, q_mine = q_send.shape[1], q_send.shape[2]
    kv_mine = kv_all.shape[2] // 2
    groups, keys, _ = k_ref.shape
    heads = q_ref.shape[1] // own
    queries = heads * own
    chunk = 128
    greet_all(me, size)
    copies = Copies("ctx", send_sem, recv_sem)
    for s in range(size):
        q_send[s] = proj_ref[s * own : (s + 1) * own, :q_mine]
    kv_all[me] = proj_ref[:, q_mine : q_mine + 2 * kv_mine]
    steps = gather_steps(copies, bits, kv_all)
    steps[0]()
    come = exchange(copies, q_send, q_recv, me, size)
    for step in steps[1:]:
        step()
    for copy in come:
        copy.wait_recv()

    for g in range(groups):
        for s, low, high, at in pieces_of(g * HEAD, HEAD, kv_mine):
            k_ref[g, :, low:high] = kv_all[s, :, at : at + high - low]
            v_ref[g, :, low:high] = kv_all[s, :, kv_mine + at : kv_mine + at + high - low]
        for h in range(heads):
            for s, low, high, at in pieces_of((g * heads + h) * HEAD, HEAD, q_mine):
                q_ref[g, h * own : (h + 1) * own, low:high] = q_recv[s, :, at : at + high - low]

    query_ids = me * own + lax.broadcasted_iota(jnp.int32, (chunk, queries), 1) % own
    key_ids = lax.broadcasted_iota(jnp.int32, (chunk, queries), 0)
    for g in range(groups):
        q_g = q_ref[g]

        def scores(i, top):
            at = pl.ds(pl.multiple_of(i * chunk, chunk), chunk)
            raw = product(k_ref[g, at], q_g, True) * (HEAD**-0.5)
            ids = key_ids + i * chunk
            kept = jnp.logical_and(ids <= query_ids, ids > query_ids - WINDOW)
            raw = jnp.where(kept, raw, -1e30)
            score_ref[at] = raw
            return jnp.maximum(top, jnp.max(raw, axis=0, keepdims=True))

        top = lax.fori_loop(
            0, keys // chunk, scores, jnp.full((1, queries), -1e30, jnp.float32)
        )

        def weights(i, total):
            at = pl.ds(pl.multiple_of(i * chunk, chunk), chunk)
            value = jnp.exp(score_ref[at] - top)
            prob_ref[g, at] = value.astype(BF16)
            return total + jnp.sum(value, axis=0, keepdims=True)

        total = lax.fori_loop(
            0, keys // chunk, weights, jnp.zeros((1, queries), jnp.float32)
        )
        inverse = 1.0 / total
        inverse_ref[g] = inverse
        out = lax.dot_general(
            v_ref[g], prob_ref[g], (((0,), (0,)), ((), ())), preferred_element_type=jnp.float32
        )
        out = (out * inverse).T
        for h in range(heads):
            at = (g * heads + h) * HEAD
            rows_ref[:, at : at + HEAD] = out[h * own : (h + 1) * own]

    values = rows_ref[...]
    scale = lax.rsqrt(jnp.mean(values * values, axis=-1, keepdims=True) + EPSILON)
    branch = (values * scale * gain_ref[...]).astype(BF16)
    part = values.shape[1] // fsdp
    width = part // size
    for d in range(size):
        for f in range(fsdp):
            at = f * part + d * width
            attn_send[d, :, f * width : (f + 1) * width] = branch[:, at : at + width]
    for copy in exchange(copies, attn_send, branch_ref, me, size):
        copy.wait_recv()
    copies.finish()


def attention_forward(projected, gain, kv_width, collective_id):
    ctx, fsdp, bits = lax.axis_size("ctx"), lax.axis_size("fsdp"), ctx_bits()
    length, model = projected.shape[0], gain.shape[0]
    own, q_mine, kv_mine = length // ctx, model // ctx, kv_width // ctx
    heads = model // kv_width
    sems = pltpu.SemaphoreType.DMA((2 * (ctx - 1) + gather_sems(bits),))
    shape = jax.ShapeDtypeStruct
    return pl.pallas_call(
        functools.partial(attention_kernel, ctx, fsdp),
        out_shape=[
            shape((ctx, own, q_mine), BF16),
            shape((own, model), jnp.float32),
            shape((KV_HEADS, length, heads * own), BF16),
            shape((KV_HEADS, 1, heads * own), jnp.float32),
            shape((KV_HEADS, heads * own, HEAD), BF16),
            shape((KV_HEADS, length, HEAD), BF16),
            shape((KV_HEADS, length, HEAD), BF16),
        ],
        in_specs=[IN_VMEM] * 2,
        out_specs=[IN_VMEM] * 7,
        scratch_shapes=[
            pltpu.VMEM((ctx, own, q_mine), BF16),
            pltpu.VMEM((ctx, own, q_mine), BF16),
            pltpu.VMEM((ctx, length, 2 * kv_mine), BF16),
            pltpu.VMEM((length, heads * own), jnp.float32),
            pltpu.VMEM((ctx, own, q_mine), BF16),
            sems, sems,
        ],
        compiler_params=params(collective_id),
        name="attention_forward",
    )(projected, gain[None])


def attention_back_kernel(
    size, fsdp, grad_ref, rows_ref, gain_ref, parts_ref, branch_ref, ssm_ref, top_ref,
    prob_ref, inverse_ref, q_ref, k_ref, v_ref,
    early_ref, gain_grad_ref, ffn_ref, dw_ref,
    recv_ref, heads_ref, dp_ref, dq_ref, dkv_ref, dq_send, dq_recv, kv_part, kv_sum, *rest,
):
    bits = size.bit_length() - 1
    me = lax.axis_index("ctx")
    own, model = rows_ref.shape
    q_mine = model // size
    groups, keys, queries = prob_ref.shape
    heads = queries // own
    kv_mine = groups * HEAD // size
    chunk = 128
    scale_qk = HEAD**-0.5
    boxes = (len(rest) - 2) // 2
    inbox, ffn_inbox = rest[:boxes], rest[boxes : 2 * boxes]
    greet_all(me, size)
    copies = Copies("ctx", *rest[-2:])
    come = exchange(copies, grad_ref, recv_ref, me, size)
    ffn_sum = Reducer(copies, bits, None, ffn_inbox, ffn_ref)
    ffn_sum.send_parts(parts_ref)

    def add_parts():
        for flips in ffn_sum.everyone:
            ffn_sum.own(flips, parts_ref[flipped(me, flips)].astype(jnp.float32))

    beside = [add_parts] + ffn_sum.turns()
    values = rows_ref[...]
    scale = lax.rsqrt(jnp.mean(values * values, axis=-1, keepdims=True) + EPSILON)
    at = 0
    for ref in (ssm_ref, branch_ref):
        wide = ref.shape[1] // fsdp
        weights = lax.dot_general(
            ref[...], top_ref[...], (((0,), (0,)), ((), ())), preferred_element_type=jnp.float32
        ).astype(BF16)
        for f in range(fsdp):
            dw_ref[f, at : at + wide] = weights[f * wide : (f + 1) * wide]
        at += wide
    dw_ref[:, at:] = jnp.zeros((fsdp, dw_ref.shape[1] - at, model), BF16)
    for copy in come:
        copy.wait_recv()
    part = model // fsdp
    width = part // size
    for s in range(size):
        for f in range(fsdp):
            at = f * part + s * width
            dq_ref[:, at : at + width] = recv_ref[s, :, f * width : (f + 1) * width].astype(
                jnp.float32
            )
    grad = dq_ref[...]
    gain_grad_ref[...] = jnp.sum(grad * values * scale, axis=0, keepdims=True)
    scaled = grad * gain_ref[...]
    grad = scale * scaled - values * (scale * scale * scale) * jnp.mean(
        scaled * values, axis=-1, keepdims=True
    )
    grad = grad.astype(BF16)
    for h in range(groups * heads):
        at = (h % heads) * own
        heads_ref[h // heads, at : at + own] = grad[:, h * HEAD : (h + 1) * HEAD]

    for g in range(groups):
        q_g, do_g, inverse = q_ref[g], heads_ref[g], inverse_ref[g]
        q_t = q_g.astype(jnp.float32).T.astype(BF16)
        do_t = do_g.astype(jnp.float32).T.astype(BF16)

        def first(i, row_dot):
            at = pl.ds(pl.multiple_of(i * chunk, chunk), chunk)
            prob = prob_ref[g, at].astype(jnp.float32) * inverse
            grad_prob = product(v_ref[g, at], do_g, True)
            dp_ref[at] = grad_prob
            dkv_ref[groups + g, :, at] = product(do_t, prob.astype(BF16), True)
            return row_dot + jnp.sum(prob * grad_prob, axis=0, keepdims=True)

        row_dot = lax.fori_loop(
            0, keys // chunk, first, jnp.zeros((1, queries), jnp.float32)
        )

        def second(i, dq_t):
            at = pl.ds(pl.multiple_of(i * chunk, chunk), chunk)
            prob = prob_ref[g, at].astype(jnp.float32) * inverse
            grad_score = (prob * (dp_ref[at] - row_dot)).astype(BF16)
            dkv_ref[g, :, at] = scale_qk * product(q_t, grad_score, True)
            return dq_t + lax.dot_general(
                k_ref[g, at], grad_score, (((0,), (0,)), ((), ())),
                preferred_element_type=jnp.float32,
            )

        dq_t = lax.fori_loop(
            0, keys // chunk, second, jnp.zeros((HEAD, queries), jnp.float32)
        )
        dq_g = (scale_qk * dq_t).T
        for h in range(heads):
            at = (g * heads + h) * HEAD
            dq_ref[:, at : at + HEAD] = dq_g[h * own : (h + 1) * own]
        if beside:
            beside.pop(0)()

    for step in beside:
        step()
    for d in range(size):
        dq_send[d] = dq_ref[:, d * q_mine : (d + 1) * q_mine].astype(BF16)
    come = exchange(copies, dq_send, dq_recv, me, size)
    flat = dkv_ref.reshape(2 * groups * HEAD, keys)
    for d in range(size):
        kv_part[d, :kv_mine] = flat[d * kv_mine : (d + 1) * kv_mine].astype(BF16)
        at = groups * HEAD + d * kv_mine
        kv_part[d, kv_mine:] = flat[at : at + kv_mine].astype(BF16)
    reducer = Reducer(copies, bits, None, inbox, kv_sum)
    reducer.send_parts(kv_part)
    for flips in reducer.everyone:
        reducer.own(flips, kv_part[flipped(me, flips)].astype(jnp.float32))
    for copy in come:
        copy.wait_recv()
    for s in range(size):
        early_ref[s * own : (s + 1) * own, :q_mine] = dq_recv[s]
    reducer.finish()
    early_ref[:, q_mine:] = kv_sum[...].T.astype(BF16)
    copies.finish()


def attention_backward(grad_c, rows, gain, parts, branches, top, kept, collective_id):
    ctx, fsdp, bits = lax.axis_size("ctx"), lax.axis_size("fsdp"), ctx_bits()
    prob = kept[0]
    own, model = rows.shape
    length = own * ctx
    q_mine, kv_mine = model // ctx, KV_HEADS * HEAD // ctx
    boxes, count = reducer_boxes(ctx, bits, 2 * kv_mine, length)
    ffn_boxes, ffn_count = reducer_boxes(ctx, bits, own, model)
    dw_rows = sum(branch.shape[1] for branch in branches) // fsdp
    sems = pltpu.SemaphoreType.DMA((2 * (ctx - 1) + count + ffn_count,))
    shape = jax.ShapeDtypeStruct
    return pl.pallas_call(
        functools.partial(attention_back_kernel, ctx, fsdp),
        out_shape=[
            shape((length, q_mine + 2 * kv_mine), BF16),
            shape((1, model), jnp.float32),
            shape((own, model), jnp.float32),
            shape((fsdp, dw_rows + -dw_rows % 16, model), BF16),
        ],
        in_specs=[IN_VMEM] * (7 + len(kept)),
        out_specs=[IN_VMEM] * 4,
        scratch_shapes=[
            pltpu.VMEM((ctx, own, q_mine), BF16),
            pltpu.VMEM(kept[2].shape, BF16),
            pltpu.VMEM((length, prob.shape[2]), jnp.float32),
            pltpu.VMEM((own, model), jnp.float32),
            pltpu.VMEM((2 * KV_HEADS, HEAD, length), jnp.float32),
            pltpu.VMEM((ctx, own, q_mine), BF16),
            pltpu.VMEM((ctx, own, q_mine), BF16),
            pltpu.VMEM((ctx, 2 * kv_mine, length), BF16),
            pltpu.VMEM((2 * kv_mine, length), jnp.float32),
        ]
        + boxes[1:]
        + ffn_boxes[1:]
        + [sems, sems],
        compiler_params=params(collective_id),
        name="attention_backward",
    )(grad_c.reshape(ctx, own, q_mine), rows, gain[None], parts, *branches, top, *kept)


def finish_kernel(
    size, fsdp, early_ref, src_ref, stack_ref, channel_ref, gain_ref,
    query_out, key_out, value_out, mixer_out, step_out, attn_out, mix_out, channel_out, sums_ref,
    all_ref, row_inbox, gain_inbox, line_inbox, c_send, c_recv, r_send, r_recv,
    ctx_send, ctx_recv, line_send, line_recv,
):
    bits = size.bit_length() - 1
    me, row = lax.axis_index("ctx"), lax.axis_index("fsdp")
    barrier = pltpu.get_barrier_semaphore()
    for turn in range(1, size):
        pl.semaphore_signal(
            barrier, inc=1, device_id={"ctx": (me + turn) % size}, device_id_type=MESH
        )
    for turn in range(1, fsdp):
        pl.semaphore_signal(
            barrier, inc=1, device_id={"fsdp": (row + turn) % fsdp}, device_id_type=MESH
        )
    q_mine, kv_mine = query_out.shape[1], key_out.shape[1]
    late = q_mine + 2 * kv_mine
    rows, width = early_ref.shape[0], src_ref.shape[1] // fsdp
    low, high = step_out.shape[0], mix_out.shape[0] // size
    block = mix_out.shape[1]
    repeat = size // fsdp
    pl.semaphore_wait(barrier, size - 1 + fsdp - 1)
    across, line = Copies("ctx", ctx_send, ctx_recv), Copies("fsdp", line_send, line_recv)
    band = channel_ref.shape[0] // fsdp

    def band_of(index):
        return pl.ds(pl.multiple_of(index * band, 8), band)

    bands = []
    for turn in range(1, fsdp):
        to = (row + turn) % fsdp
        bands.append(line.send(channel_ref.at[band_of(to)], row_inbox.at[turn - 1], to))
    gains = [
        across.send(gain_ref, gain_inbox.at[turn - 1], (me + turn) % size)
        for turn in range(1, size)
    ]
    for d in range(size):
        unit = d % fsdp
        if d < fsdp:
            c_send[d, :rows] = src_ref[:rows, unit * width : (unit + 1) * width]
        else:
            at = late + unit * width
            c_send[d, :rows] = early_ref[:, at : at + width]
        at = d // repeat * width
        c_send[d, rows:] = src_ref[rows:, at : at + width]
        r_send[d] = stack_ref[:, d * block : (d + 1) * block]
    moved = exchange(across, c_send, c_recv, me, size) + exchange(across, r_send, r_recv, me, size)
    query_out[...] = early_ref[:, :q_mine].astype(jnp.float32)
    key_out[...] = early_ref[:, q_mine : q_mine + kv_mine].astype(jnp.float32)
    value_out[...] = early_ref[:, q_mine + kv_mine : late].astype(jnp.float32)

    total = channel_ref[band_of(row)]
    for turn in range(1, fsdp):
        bands[turn - 1].wait_recv()
        total = total + row_inbox[turn - 1]
    all_ref[me, band_of(row)] = total
    at = all_ref.at[me, band_of(row)]
    bands = [line.send(at, at, (row + turn) % fsdp) for turn in range(1, fsdp)]
    total = gain_ref[...]
    for turn in range(1, size):
        gains[turn - 1].wait_recv()
        total = total + gain_inbox[turn - 1]
    line_inbox[0] = total
    gains = [
        line.send(line_inbox.at[0], line_inbox.at[turn], (row + turn) % fsdp)
        for turn in range(1, fsdp)
    ]
    for copy in bands:
        copy.wait_recv()
    steps = gather_steps(across, bits, all_ref)
    steps[0]()
    for copy in moved:
        copy.wait_recv()
    for step in steps[1:-1]:
        step()
    for s in range(size):
        mixer_out[:, s * width : (s + 1) * width] = c_recv[s, :rows].astype(jnp.float32)
        mix_out[s * high : (s + 1) * high] = r_recv[s, :high].astype(jnp.float32)
        count = attn_out.shape[0] // size
        attn_out[s * count : (s + 1) * count] = r_recv[s, high : high + count].astype(jnp.float32)
    for j in range(fsdp):
        source = fsdp * (me % repeat) + j
        step_out[:, j * width : (j + 1) * width] = c_recv[source, rows : rows + low].astype(
            jnp.float32
        )
    steps[-1]()
    part = channel_out.shape[1] // fsdp
    for s in range(size):
        for f in range(fsdp):
            at = f * part + s * width
            channel_out[:, at : at + width] = all_ref[s, :, f * width : (f + 1) * width]
    total = line_inbox[0]
    for turn in range(1, fsdp):
        gains[turn - 1].wait_recv()
        total = total + line_inbox[turn]
    sums_ref[...] = total
    across.finish()
    line.finish()


def finish(early, src, stack, channel, gains, sizes, collective_id):
    ctx, fsdp, bits = lax.axis_size("ctx"), lax.axis_size("fsdp"), ctx_bits()
    q_mine, kv_mine, step_rows, mix_rows, attn_rows = sizes
    rows, mine = early.shape[0], src.shape[1]
    width, block = mine // fsdp, stack.shape[1] // ctx
    ctx_sems = pltpu.SemaphoreType.DMA((3 * (ctx - 1) + gather_sems(bits),))
    line_sems = pltpu.SemaphoreType.DMA((3 * (fsdp - 1),))

    def shape(*sizes):
        return jax.ShapeDtypeStruct(sizes, jnp.float32)

    return pl.pallas_call(
        functools.partial(finish_kernel, ctx, fsdp),
        out_shape=[
            shape(rows, q_mine), shape(rows, kv_mine), shape(rows, kv_mine),
            shape(rows, ctx * width), shape(step_rows, mine),
            shape(ctx * attn_rows, block), shape(ctx * mix_rows, block),
            shape(channel.shape[0], ctx * mine), shape(*gains.shape),
        ],
        in_specs=[IN_VMEM] * 5,
        out_specs=[IN_VMEM] * 9,
        scratch_shapes=[
            pltpu.VMEM((ctx,) + channel.shape, jnp.float32),
            pltpu.VMEM((fsdp - 1, channel.shape[0] // fsdp, mine), jnp.float32),
            pltpu.VMEM((ctx - 1,) + gains.shape, jnp.float32),
            pltpu.VMEM((fsdp,) + gains.shape, jnp.float32),
            pltpu.VMEM((ctx, src.shape[0], width), BF16),
            pltpu.VMEM((ctx, src.shape[0], width), BF16),
            pltpu.VMEM((ctx, stack.shape[0], block), BF16),
            pltpu.VMEM((ctx, stack.shape[0], block), BF16),
            ctx_sems, ctx_sems, line_sems, line_sems,
        ],
        compiler_params=params(collective_id),
        name="finish",
    )(early, src, stack, channel, gains)


def window(start, size, total, step):
    return pl.multiple_of(jnp.minimum(start // step * step, total - size), step)


def shifted(values, offset, axis):
    size = values.shape[axis]
    return pltpu.roll(values.astype(jnp.float32), lax.rem(size - offset, size), axis)


def pack_in_begin(weights, scratch):
    mixer_ref, (inbox, sems) = weights[3], scratch
    me, size = lax.axis_index("ctx"), lax.axis_size("ctx")
    units, _, span = inbox.shape
    total = mixer_ref.shape[1]
    width = total // units // size
    copies = []
    for u in range(units):
        at = window(u * (total // units) + me * width, span, total, 128)
        copy = pltpu.make_async_copy(mixer_ref.at[:, pl.ds(at, span)], inbox.at[u], sems.at[u])
        copy.start()
        copies.append(copy)
    return copies


def pack_in(row, copies, weights, scratch, in_out, state_out, step_out):
    query_ref, key_ref, value_ref, mixer_ref, state_ref, step_ref = weights
    inbox = scratch[0]
    me, size = lax.axis_index("ctx"), lax.axis_size("ctx")
    units, _, span = inbox.shape
    total = mixer_ref.shape[1]
    width = total // units // size
    at = 0
    for ref in (query_ref, key_ref, value_ref):
        wide = ref.shape[1] // size
        in_out[row, :, at : at + wide] = shifted(ref[...], me * wide, 1)[:, :wide].astype(BF16)
        at += wide
    high = state_ref.shape[1] // size
    turned = shifted(state_ref[...], me * high, 1)[:, :128].T
    state_out[row] = turned[: state_out.shape[1]].astype(BF16)
    part = step_ref.shape[1] * 2 // units
    step_out[row] = jnp.zeros(step_out.shape[1:], BF16)
    for f in range(units // 2):
        band = shifted(step_ref[:, f * part : (f + 1) * part], me * width, 1)[:, :width]
        step_out[row, : step_ref.shape[0], f * width : (f + 1) * width] = band.astype(BF16)
    for u in range(units):
        copies[u].wait()
        start = u * (total // units) + me * width
        piece = shifted(inbox[u], start - window(start, span, total, 128), 1)[:, :width]
        to = at + (u + units // 2) % units * width
        in_out[row, :, to : to + width] = piece.astype(BF16)


def pack_in_plan(first):
    shape = jax.ShapeDtypeStruct
    if len(first) == 3:
        return {"shapes": [shape(a.shape, a.dtype) for a in first], "scratch": [], "any": ()}
    query, key, value, mixer, state, step = first
    ctx, fsdp = lax.axis_size("ctx"), lax.axis_size("fsdp")
    rows = mixer.shape[0]
    mine = mixer.shape[1] // 2 // ctx
    qkv = (query.shape[1] + key.shape[1] + value.shape[1]) // ctx
    state_rows = state.shape[1] // ctx
    return {
        "shapes": [
            shape((rows, qkv + 2 * mine), BF16),
            shape((state_rows + -state_rows % 16, state.shape[0]), BF16),
            shape((step.shape[0] + -step.shape[0] % 16, mine), BF16),
        ],
        "scratch": [
            pltpu.VMEM((2 * fsdp, rows, 256), BF16), pltpu.SemaphoreType.DMA((2 * fsdp,))
        ],
        "any": (3,),
    }


def pack_out_plan(later, hidden_units):
    if not later:
        return {"inputs": 0, "outputs": 0, "shapes": [], "scratch": [], "steps": None}
    ctx, fsdp = lax.axis_size("ctx"), lax.axis_size("fsdp")
    gate, _, down, mix, attn = later
    rows, model, total = gate.shape[0], down.shape[0], gate.shape[1]
    hid_part = total // ctx // fsdp
    pad = -hid_part % 16
    units = hidden_units // fsdp
    width = hid_part // units
    high = (hid_part + pad) + (mix.shape[0] + attn.shape[0]) // ctx
    span = 256

    def box_rows(array):
        need = array.shape[0] // ctx
        return need + 15 + -(need + 15) % 16

    def steps(me, weights, outs, scratch):
        gate_ref, up_ref, down_ref, mix_ref, attn_ref = weights
        pair_out, rows_out = outs
        inbox, down_box, tail_box, mix_box, attn_box, sems = scratch
        copies = []

        def start_copy(source, target):
            copy = pltpu.make_async_copy(source, target, sems.at[len(copies)])
            copy.start()
            copies.append(copy)

        plans = []
        half = pair_out.shape[1] // 2
        for index, ref in enumerate((gate_ref, up_ref)):
            for u in range(hidden_units):
                start = u * (total // hidden_units) + me * width
                at = window(start, span, total, 128)
                start_copy(ref.at[:, pl.ds(at, span)], inbox.at[index, u])
                to = index * half + u * width + u // units * pad
                plans.append(("columns", inbox, (index, u), start - at, to, width))
        to = 0
        down_at = to
        to += units * width + pad
        for ref, box in ((mix_ref, mix_box), (attn_ref, attn_box)):
            tall = ref.shape[0] // size
            at = window(me * tall, box.shape[1], ref.shape[0], 16)
            start_copy(ref.at[pl.ds(at, box.shape[1])], box.at[0])
            plans.append(("rows", box, (0,), me * tall - at, to, tall))
            to += tall
        start_copy(down_ref, down_box)
        full = down.shape[1] // 128
        tail = down.shape[1] % 128

        def tile_of(index):
            at = pl.multiple_of(jnp.minimum(index, full - 1) * 128, 128)
            whole = down_box[:, pl.ds(at, 128)].astype(jnp.float32)
            return jnp.where(index >= full, tail_box[...], whole) if tail else whole

        def begin_down():
            copies[-1].wait()
            if tail:
                tail_box[...] = jnp.zeros(tail_box.shape, jnp.float32)
                tail_box[:, :tail] = down_box[:, full * 128 :].astype(jnp.float32)

        def place_down(u):
            start = u * (down.shape[1] // units) + me * width
            first = start // 128
            pair = jnp.concatenate([tile_of(first), tile_of(first + 1)], 1)
            turned = shifted(pair, start - first * 128, 1)[:, :128].T
            at = down_at + u * width
            rows_out[at : at + width] = turned[:width].astype(BF16)

        def clear():
            pair_out[...] = jnp.zeros(pair_out.shape, BF16)
            rows_out[...] = jnp.zeros(rows_out.shape, BF16)

        def place(copy, kind, box, index, offset, to, extent):
            copy.wait()
            values = box[index]
            if kind == "columns":
                pair_out[:, to : to + extent] = shifted(values, offset, 1)[:, :extent].astype(BF16)
            else:
                rows_out[to : to + extent] = shifted(values, offset, 0)[:extent].astype(BF16)

        placed = [functools.partial(place, copy, *plan) for copy, plan in zip(copies, plans)]
        downs = [functools.partial(place_down, u) for u in range(units)]
        return [clear] + placed + [begin_down] + downs

    size = ctx
    shape = jax.ShapeDtypeStruct
    return {
        "inputs": 5,
        "outputs": 2,
        "shapes": [
            shape((rows, 2 * fsdp * (hid_part + pad)), BF16),
            shape((high + -high % 16, model), BF16),
        ],
        "scratch": [
            pltpu.VMEM((2, hidden_units, rows, span), BF16),
            pltpu.VMEM(down.shape, BF16),
            pltpu.VMEM((model, 128), jnp.float32),
            pltpu.VMEM((1, box_rows(mix), model), BF16),
            pltpu.VMEM((1, box_rows(attn), model), BF16),
            pltpu.SemaphoreType.DMA((2 * hidden_units + 3,)),
        ],
        "steps": steps,
    }


def scan_fwd_kernel(steps_ref, drive_ref, in_ref, out_ref, rate_ref, scan_ref, prev_ref, state_ref):
    tiles = steps_ref.shape[1] // LANES
    chunk = steps_ref.shape[0]

    @pl.when(pl.program_id(0) == 0)
    def _():
        state_ref[...] = jnp.zeros_like(state_ref)

    rates = [rate_ref[:, j * LANES : (j + 1) * LANES] for j in range(tiles)]

    def group(g, states):
        states = list(states)
        base = pl.multiple_of(g * 8, 8)
        for j in range(tiles):
            lanes = slice(j * LANES, (j + 1) * LANES)
            step_8 = steps_ref[pl.ds(base, 8), lanes]
            drive_8 = step_8 * drive_ref[pl.ds(base, 8), lanes]
            rows = []
            for t in range(8):
                in_t = in_ref[base + t].astype(jnp.float32)
                out_t = out_ref[base + t].astype(jnp.float32)
                decay = jnp.exp2(step_8[t : t + 1] * rates[j])
                prev_ref[base + t, :, lanes] = states[j]
                states[j] = decay * states[j] + drive_8[t : t + 1] * in_t
                rows.append(jnp.sum(states[j] * out_t, axis=0, keepdims=True))
            scan_ref[pl.ds(base, 8), lanes] = jnp.concatenate(rows, 0)
        return tuple(states)

    start = tuple(state_ref[:, j * LANES : (j + 1) * LANES] for j in range(tiles))
    final = lax.fori_loop(0, chunk // 8, group, start)
    for j in range(tiles):
        state_ref[:, j * LANES : (j + 1) * LANES] = final[j]


def scan_fwd(steps, drive, in_b, out_b, rates):
    length, width = steps.shape
    chunk = CHUNK
    row = pl.BlockSpec((chunk, width), lambda i: (i, 0))
    mat = pl.BlockSpec((chunk, STATE, LANES), lambda i: (i, 0, 0))
    rate = pl.BlockSpec((STATE, width), lambda i: (0, 0))
    return pl.pallas_call(
        scan_fwd_kernel,
        grid=(length // chunk,),
        in_specs=[row, row, mat, mat, rate],
        out_specs=[row, pl.BlockSpec((chunk, STATE, width), lambda i: (i, 0, 0))],
        out_shape=[
            jax.ShapeDtypeStruct((length, width), jnp.float32),
            jax.ShapeDtypeStruct((length, STATE, width), jnp.float32),
        ],
        scratch_shapes=[pltpu.VMEM((STATE, width), jnp.float32)],
        compiler_params=pltpu.CompilerParams(vmem_limit_bytes=48 * 1024 * 1024),
        name="scan_forward",
    )(steps, drive, in_b, out_b, rates)


def scan_bwd_kernel(
    units, steps_ref, drive_ref, grad_ref, in_ref, out_ref, rate_ref, prev_ref, *refs
):
    exchanged, refs = refs[: 2 if units else 0], refs[2 if units else 0 :]
    gstep_ref, gdrive_ref, gin_ref, gout_ref, grate_ref = refs[:5]
    received, refs = refs[5 : 8 if units else 5], refs[8 if units else 5 :]
    carry_ref, pin_ref, pout_ref = refs[:3]
    slots = refs[3:]
    tiles = steps_ref.shape[1] // LANES
    chunk = steps_ref.shape[0]
    if units:
        pl.when(pl.program_id(0) == 0)(functools.partial(relay_begin, units, *exchanged, *slots))

    @pl.when(pl.program_id(0) == 0)
    def _():
        carry_ref[...] = jnp.zeros_like(carry_ref)
        grate_ref[...] = jnp.zeros_like(grate_ref)

    for j in range(tiles):
        lanes = slice(j * LANES, (j + 1) * LANES)
        rates = rate_ref[:, lanes]

        def group(k, kept):
            carry, acc = kept
            base = pl.multiple_of(chunk - 8 - k * 8, 8)
            step_8 = steps_ref[pl.ds(base, 8), lanes]
            x_8 = drive_ref[pl.ds(base, 8), lanes]
            drive_8 = step_8 * x_8
            grad_8 = grad_ref[pl.ds(base, 8), lanes]
            held_rows, dot_rows = [None] * 8, [None] * 8
            for t in range(7, -1, -1):
                in_t = in_ref[base + t].astype(jnp.float32)
                out_t = out_ref[base + t].astype(jnp.float32)
                previous = prev_ref[base + t, :, lanes]
                step_t = step_8[t : t + 1]
                drive_t = drive_8[t : t + 1]
                grad_t = grad_8[t : t + 1]
                decay = jnp.exp2(step_t * rates)
                adjoint = grad_t * out_t + carry
                carry = decay * adjoint
                held = carry * previous
                state = decay * previous + drive_t * in_t
                acc = acc + held * step_t
                held_rows[t] = jnp.sum(held * rates, axis=0, keepdims=True)
                dot_rows[t] = jnp.sum(adjoint * in_t, axis=0, keepdims=True)
                part_in = adjoint * drive_t
                part_out = state * grad_t
                at = pl.ds(pl.multiple_of((base + t) * STATE, STATE), STATE)
                if j == 0:
                    pin_ref[at] = part_in
                    pout_ref[at] = part_out
                else:
                    pin_ref[at] += part_in
                    pout_ref[at] += part_out
            held_8 = jnp.concatenate(held_rows, 0)
            dot_8 = jnp.concatenate(dot_rows, 0)
            gstep_ref[pl.ds(base, 8), lanes] = held_8 * 0.6931471805599453 + x_8 * dot_8
            gdrive_ref[pl.ds(base, 8), lanes] = step_8 * dot_8
            return carry, acc

        carry, acc = lax.fori_loop(
            0, chunk // 8, group, (carry_ref[:, lanes], grate_ref[:, lanes])
        )
        carry_ref[:, lanes] = carry
        grate_ref[:, lanes] = acc
    ones = jnp.ones((8, LANES), jnp.float32)
    dims = (((1,), (1,)), ((), ()))
    gin_ref[0] = lax.dot_general(ones, pin_ref[...], dims, preferred_element_type=jnp.float32)
    gout_ref[0] = lax.dot_general(ones, pout_ref[...], dims, preferred_element_type=jnp.float32)
    if units:
        last = pl.num_programs(0) - 1
        pl.when(pl.program_id(0) == last)(functools.partial(relay_end, units, *received, *slots))


def scan_bwd(steps, drive, grad, in_b, out_b, rates, previous, relay=(), units=0, hidden=0, collective_id=None):
    length, width = steps.shape
    chunk = CHUNK
    count = length // chunk
    row = pl.BlockSpec((chunk, width), lambda i: (count - 1 - i, 0))
    mat = pl.BlockSpec((chunk, STATE, LANES), lambda i: (count - 1 - i, 0, 0))
    rate = pl.BlockSpec((STATE, width), lambda i: (0, 0))
    red = pl.BlockSpec((1, 8, chunk * STATE), lambda i: (count - 1 - i, 0, 0))
    shape = jax.ShapeDtypeStruct
    relay_out, slots = [], []
    settings = dict(vmem_limit_bytes=56 * 1024 * 1024)
    if relay:
        ctx = lax.axis_size("ctx")
        pair, down = relay
        wide, block = hidden // ctx, down.shape[1] // ctx
        relay_out = [
            shape((pair.shape[0], ctx * wide), jnp.float32),
            shape((pair.shape[0], ctx * wide), jnp.float32),
            shape((units * ctx * wide, block), jnp.float32),
        ]
        slots = [
            pltpu.VMEM((ctx, pair.shape[0], 2 * wide), BF16),
            pltpu.VMEM((ctx, pair.shape[0], 2 * wide), BF16),
            pltpu.VMEM((ctx, down.shape[0], block), BF16),
            pltpu.VMEM((ctx, down.shape[0], block), BF16),
            pltpu.SemaphoreType.DMA((2 * (ctx - 1),)),
            pltpu.SemaphoreType.DMA((2 * (ctx - 1),)),
        ]
        settings.update(collective_id=collective_id, has_side_effects=True)
    gstep, gdrive, gin, gout, grate, *relayed = pl.pallas_call(
        functools.partial(scan_bwd_kernel, units),
        grid=(count,),
        in_specs=[row, row, row, mat, mat, rate,
                  pl.BlockSpec((chunk, STATE, width), lambda i: (count - 1 - i, 0, 0))]
        + [pl.BlockSpec(a.shape, lambda i: (0, 0)) for a in relay],
        out_specs=[row, row, red, red, rate]
        + [pl.BlockSpec(a.shape, lambda i: (0, 0)) for a in relay_out],
        out_shape=[
            shape((length, width), jnp.float32),
            shape((length, width), jnp.float32),
            shape((count, 8, chunk * STATE), jnp.float32),
            shape((count, 8, chunk * STATE), jnp.float32),
            shape((STATE, width), jnp.float32),
        ]
        + relay_out,
        scratch_shapes=[
            pltpu.VMEM((STATE, width), jnp.float32),
            pltpu.VMEM((chunk * STATE, LANES), jnp.float32),
            pltpu.VMEM((chunk * STATE, LANES), jnp.float32),
        ]
        + slots,
        compiler_params=pltpu.CompilerParams(**settings),
        name="scan_backward",
    )(steps, drive, grad, in_b, out_b, rates, previous, *relay)
    return (
        gstep, gdrive, gin[:, 0].reshape(length, STATE), gout[:, 0].reshape(length, STATE), grate,
        relayed,
    )


def matmul(left, right):
    return jnp.dot(left, right, preferred_element_type=jnp.float32)


def left_trans(left, right):
    return lax.dot_general(
        left, right, (((0,), (0,)), ((), ())), preferred_element_type=jnp.float32
    )


def right_trans(left, right):
    return lax.dot_general(
        left, right, (((1,), (1,)), ((), ())), preferred_element_type=jnp.float32
    )


def rms_scale(values):
    return lax.rsqrt(jnp.mean(values * values, axis=-1, keepdims=True) + EPSILON)


def norm_back(grad_out, values, scale_in, gain_in):
    scaled = grad_out * gain_in
    grad_in = scale_in * scaled - values * scale_in**3 * jnp.mean(
        scaled * values, axis=-1, keepdims=True
    )
    return (grad_in, jnp.sum(grad_out * values * scale_in, axis=0))


def silu_slope(values):
    logistic = jax.nn.sigmoid(values)
    return logistic * (1.0 + values * (1.0 - logistic))


def unit_count(width, ctx, fsdp):
    return ctx if width % (ctx * ctx) == 0 and ctx % fsdp == 0 else fsdp


def my_columns(array, units):
    span = array.shape[1] // units
    width = span // lax.axis_size("ctx")
    start = lax.axis_index("ctx") * width
    return [
        lax.dynamic_slice_in_dim(array, unit * span + start, width, 1) for unit in range(units)
    ]


def my_rows(array, units):
    span = array.shape[0] // units
    width = span // lax.axis_size("ctx")
    start = lax.axis_index("ctx") * width
    return [
        lax.dynamic_slice_in_dim(array, unit * span + start, width, 0) for unit in range(units)
    ]


def block_columns(array):
    width = array.shape[1] // lax.axis_size("ctx")
    return lax.dynamic_slice_in_dim(array, lax.axis_index("ctx") * width, width, 1)


def over_fsdp(array):
    return lax.all_gather(array, "fsdp", axis=0, tiled=True)


def to_slots(array, units):
    repeat = lax.axis_size("ctx") // units
    rows, width = array.shape[0], array.shape[1] // units
    pieces = array.reshape(rows, units, width).transpose(1, 0, 2)
    return jnp.repeat(pieces, repeat, axis=0) if repeat > 1 else pieces


def from_slots(got, units):
    repeat = lax.axis_size("ctx") // units
    if repeat > 1:
        first = units * lax.rem(lax.axis_index("ctx"), repeat)
        got = lax.dynamic_slice_in_dim(got, first, units, 0)
    rows, width = got.shape[1:]
    return got.transpose(1, 0, 2).reshape(rows, units * width).astype(jnp.float32)


def to_blocks(array, units):
    got = lax.all_to_all(to_slots(array, units), "ctx", 0, 0, tiled=True)
    return from_slots(got, units)


def rows_to_slots(array):
    ctx = lax.axis_size("ctx")
    rows, columns = array.shape
    return array.reshape(rows, ctx, columns // ctx).transpose(1, 0, 2)


def rows_from_slots(got, units):
    ctx, rows, columns = got.shape
    got = got.reshape(ctx, units, rows // units, columns).transpose(1, 0, 2, 3)
    return got.reshape(ctx * rows, columns).astype(jnp.float32)


def rows_to_blocks(array, units):
    got = lax.all_to_all(rows_to_slots(array), "ctx", 0, 0, tiled=True)
    return rows_from_slots(got, units)


def scatter_fsdp(*gradients):
    fsdp = lax.axis_size("fsdp")
    parts = [g.astype(BF16).reshape(fsdp, -1, g.shape[1]) for g in gradients]
    pad = -sum(part.shape[1] for part in parts) % 16
    if pad:
        parts.append(jnp.zeros((fsdp, pad, gradients[0].shape[1]), BF16))
    joined = jnp.concatenate(parts, 1) if len(parts) > 1 else parts[0]
    joined = joined.reshape(-1, joined.shape[2])
    return lax.psum_scatter(joined, "fsdp", scatter_dimension=0, tiled=True)


def body(
    inputs,
    cotangent,
    norm_gain,
    query_proj,
    key_proj,
    value_proj,
    attn_proj,
    attn_gain,
    mixer_in,
    conv_taps,
    conv_bias,
    state_proj,
    step_proj,
    step_bias,
    decay_rate,
    skip_gain,
    mixer_out,
    ssm_gain,
    ffn_gain,
    gate_proj,
    up_proj,
    down_proj,
):
    ctx, fsdp = lax.axis_size("ctx"), lax.axis_size("fsdp")
    place = lax.axis_index("ctx")
    tokens = inputs[0].astype(jnp.float32)
    own, model = tokens.shape
    length = own * ctx
    inner = conv_bias.shape[0]
    mine = inner // ctx
    kv_mine = key_proj.shape[1] // ctx
    q_mine = query_proj.shape[1] // ctx
    hidden_units = unit_count(gate_proj.shape[1], ctx, fsdp)
    hidden_rows = hidden_units // fsdp
    hid = gate_proj.shape[1] // ctx
    group_size = query_proj.shape[1] // key_proj.shape[1]
    score_scale = HEAD ** (-0.5)

    hid_part = hid // fsdp
    hid_pad = -hid_part % 16
    hid_all = hid + fsdp * hid_pad
    attn_pad = -attn_proj.shape[0] % ctx
    attn_rows_mine = (attn_proj.shape[0] + attn_pad) // ctx
    state_rows, step_rows = state_proj.shape[0] // ctx, step_proj.shape[0]
    if ctx == 8:
        first = (query_proj, key_proj, value_proj, mixer_in, state_proj.T, step_proj)
        later = (gate_proj, up_proj, down_proj.T, mixer_out, attn_proj)
        x_in, top_in = inputs[0].T, cotangent[0].T
    else:
        in_part = jnp.concatenate(
            [block_columns(array) for array in (query_proj, key_proj, value_proj)]
            + my_columns(mixer_in[:, inner:], fsdp)
            + my_columns(mixer_in[:, :inner], fsdp),
            1,
        )
        later = ()
        x_in, top_in = inputs[0], cotangent[0]
        state_part = jnp.pad(my_rows(state_proj, 1)[0], ((0, -state_rows % 16), (0, 0)))
        step_part = jnp.pad(
            jnp.concatenate(my_columns(step_proj, fsdp), 1), ((0, -step_rows % 16), (0, 0))
        )

        first = (in_part, state_part, step_part)

        def hidden_columns(array):
            pieces = my_columns(array, hidden_units)
            if hid_pad:
                for f in range(fsdp, 0, -1):
                    pieces.insert(f * hidden_rows, jnp.zeros((array.shape[0], hid_pad), BF16))
            return pieces

        ffn_part = jnp.concatenate(hidden_columns(gate_proj) + hidden_columns(up_proj), 1)
        rows_part = jnp.concatenate(
            my_rows(down_proj, hidden_rows)
            + [jnp.zeros((hid_pad, model), BF16)]
            + my_rows(mixer_out, 1)
            + my_rows(jnp.pad(attn_proj, ((0, attn_pad), (0, 0))), 1),
            0,
        )
    mix_rows = mixer_out.shape[0] // ctx
    normed_all, grad_top, in_full, state_full, step_full, *parts = front(
        x_in, norm_gain[None], top_in, first, later, hidden_units, 0
    )
    if parts:
        ffn_part, rows_part = parts
    normed_all = normed_all.reshape(length, model)
    grad_top = grad_top.reshape(length, model)
    in_full = in_full.reshape(model, -1)
    state_full = state_full[:, :state_rows].reshape(-1, state_proj.shape[1])
    step_full = step_full[:, :step_rows].reshape(-1, mine)
    norm_scale = rms_scale(tokens)
    rows_full = lax.all_gather(rows_part, "fsdp", axis=0)
    ffn_full = over_fsdp(ffn_part)
    down_at = hid_part + hid_pad
    down_full = rows_full[:, :down_at].reshape(-1, model)
    mixout_full = rows_full[:, down_at : down_at + mix_rows].reshape(-1, model)
    attn_at = down_at + mix_rows
    attn_full = rows_full[:, attn_at : attn_at + attn_rows_mine].reshape(-1, model)
    attn_width = attn_full.shape[0]

    def mine_of(vector):
        return jnp.concatenate(my_columns(vector.reshape(-1, inner), fsdp), 1)

    taps, bias, skip, gain_ssm, bias_step = (
        mine_of(conv_taps),
        mine_of(conv_bias),
        mine_of(skip_gain),
        mine_of(ssm_gain),
        mine_of(step_bias),
    )
    rates = jnp.concatenate(
        [
            lax.dynamic_slice_in_dim(
                decay_rate, unit * (inner // fsdp) + place * (mine // fsdp), mine // fsdp, 0
            )
            for unit in range(fsdp)
        ],
        0,
    ).T
    pad = -mine % LANES

    def padded(values):
        return jnp.pad(values, ((0, 0), (0, pad)))

    projected_in = matmul(normed_all, in_full).astype(BF16)
    conv_src = projected_in[:, q_mine + 2 * kv_mine + mine :]

    padded_src = jnp.concatenate(
        [jnp.zeros((CONV - 1, mine), jnp.float32), conv_src.astype(jnp.float32)], 0
    )
    conv_pre = bias + sum(taps[tap][None] * padded_src[tap : tap + length] for tap in range(CONV))
    conv_act = jax.nn.silu(conv_pre).astype(BF16)
    conv_vals = conv_act.astype(jnp.float32)
    projected = sum_everywhere(matmul(conv_act, state_full).astype(BF16), 2).astype(jnp.float32)
    step_low = projected[:, :DT_RANK].astype(BF16)
    input_mat = projected[:, DT_RANK : DT_RANK + STATE]
    output_mat = projected[:, DT_RANK + STATE :]
    step_pre = matmul(step_low, step_full) + bias_step
    steps_dt = jax.nn.softplus(step_pre)
    in_b = jnp.broadcast_to(input_mat.astype(BF16)[:, :, None], (length, STATE, LANES))
    out_b = jnp.broadcast_to(output_mat.astype(BF16)[:, :, None], (length, STATE, LANES))
    rates_log2 = padded(-LOG2_E * rates)
    steps_pad, vals_pad = padded(steps_dt), padded(conv_vals)
    scan_out, states = scan_fwd(steps_pad, vals_pad, in_b, out_b, rates_log2)
    scan_out = scan_out[:, :mine]

    gate_z = projected_in[:, q_mine + 2 * kv_mine : q_mine + 2 * kv_mine + mine].astype(jnp.float32)
    def attn_to_channels(values):
        parts = jnp.pad(values.reshape(own, fsdp, -1), ((0, 0), (0, 0), (0, attn_pad)))
        parts = parts.reshape(own, fsdp, ctx, -1).transpose(2, 0, 1, 3).reshape(ctx, own, -1)
        return lax.all_to_all(parts, "ctx", 0, 0, tiled=True).reshape(length, -1)

    def attn_to_tokens(values):
        parts = values.reshape(ctx, own, -1)
        got = lax.all_to_all(parts, "ctx", 0, 0, tiled=True)
        got = got.reshape(ctx, own, fsdp, -1).transpose(1, 2, 0, 3).reshape(own, fsdp, -1)
        return got[:, :, : attn_proj.shape[0]].reshape(own, -1)

    if ctx == 8:
        branch_attn_c, attn_rows, *attn_kept = attention_forward(
            projected_in, attn_gain, key_proj.shape[1], 1
        )
        branch_attn_c = branch_attn_c.reshape(length, -1)
    else:
        queries = lax.all_to_all(projected_in[:, :q_mine], "ctx", 0, 1, tiled=True)
        keyvals = gather_shards(projected_in[:, q_mine : q_mine + 2 * kv_mine], 1)
        keys_all = keyvals[:, :, :kv_mine].transpose(1, 0, 2).reshape(length, KV_HEADS, HEAD)
        vals_all = keyvals[:, :, kv_mine:].transpose(1, 0, 2).reshape(length, KV_HEADS, HEAD)
        heads_q = queries.reshape(own, KV_HEADS, group_size, HEAD)
        row_ids = place * own + lax.broadcasted_iota(jnp.int32, (own, length), 0)
        col_ids = lax.broadcasted_iota(jnp.int32, (own, length), 1)
        allowed = (col_ids <= row_ids) & (col_ids > row_ids - WINDOW)

        def scores_of():
            raw = jnp.einsum("qhgd,khd->hgqk", heads_q, keys_all, preferred_element_type=jnp.float32)
            return jnp.where(allowed, raw * score_scale, -1e30)

        scores = scores_of()
        row_top = jnp.max(scores, axis=-1, keepdims=True)
        log_total = row_top + jnp.log(jnp.sum(jnp.exp(scores - row_top), axis=-1, keepdims=True))
        probs = jnp.exp(scores - log_total)
        probs_bf = probs.astype(BF16)
        attn_rows = jnp.einsum(
            "hgqk,khd->qhgd", probs_bf, vals_all, preferred_element_type=jnp.float32
        ).reshape(own, -1)
        attn_scale = rms_scale(attn_rows)
        branch_attn = (attn_rows * attn_scale * attn_gain).astype(BF16)
        branch_attn_c = attn_to_channels(branch_attn)

    ssm_raw = scan_out + skip * conv_vals
    gate_act = jax.nn.silu(gate_z)
    ssm_gated = ssm_raw * gate_act
    square = total_of(jnp.sum(ssm_gated * ssm_gated, axis=-1), 3)
    ssm_scale = lax.rsqrt(square / inner + EPSILON)[:, None]
    branch_ssm = (ssm_gated * ssm_scale * gain_ssm).astype(BF16)
    middle = tokens + 0.5 * reduce_products(
        [branch_attn_c, branch_ssm], [attn_full, mixout_full], False, 4
    )
    ffn_scale = rms_scale(middle)
    ffn_in = (middle * ffn_scale * ffn_gain).astype(BF16)
    if ctx == 8:
        pair_dw, down_dw, ffn_out, grad_ffn_in = ffn_both_ways(
            ffn_in, grad_top, ffn_full, down_full, 5
        )
    else:
        ffn_all = gather_tokens(ffn_in, 5)
        pre = matmul(ffn_all, ffn_full)
        gate_pre, up_pre = pre[:, :hid_all], pre[:, hid_all:]
        gate_silu = jax.nn.silu(gate_pre)
        hidden = (gate_silu * up_pre).astype(BF16)
        ffn_out = reduce_products([hidden], [down_full], False, 6)
        grad_hidden = right_trans(grad_top, down_full)
        grad_gate = (grad_hidden * up_pre * silu_slope(gate_pre)).astype(BF16)
        grad_up = (grad_hidden * gate_silu).astype(BF16)
        grad_pair = jnp.concatenate([grad_gate, grad_up], 1)
        grad_ffn_in = reduce_products([grad_pair], [ffn_full], True, 7)
        down_dw = left_trans(hidden, grad_top).astype(BF16)
        pair_dw = left_trans(ffn_all, grad_pair).astype(BF16)
    grad_ffn_in, down_dw, pair_dw = lax.optimization_barrier((grad_ffn_in, down_dw, pair_dw))
    down_grad = scatter_fsdp(down_dw)
    pair_grad = scatter_fsdp(pair_dw)
    grad_middle, grad_ffn_gain = norm_back(grad_ffn_in, middle, ffn_scale, ffn_gain)
    grad_middle = grad_middle + cotangent[0].astype(jnp.float32)
    grad_branch = (0.5 * grad_middle).astype(BF16)
    branch_all = gather_tokens(grad_branch, 8)
    grad_attn_c = right_trans(branch_all, attn_full).astype(BF16)
    if ctx == 8:
        grad_early, grad_attn_gain, ffn_out, out_dw = attention_backward(
            grad_attn_c, attn_rows, attn_gain, ffn_out, (branch_attn_c, branch_ssm), branch_all,
            attn_kept, 13,
        )
        out_dw = [out_dw.reshape(-1, model)]
        grad_attn_gain = grad_attn_gain[0]
    else:
        grad_attn = attn_to_tokens(grad_attn_c).astype(jnp.float32)
        grad_attn_raw, grad_attn_gain = norm_back(grad_attn, attn_rows, attn_scale, attn_gain)
        grad_heads = grad_attn_raw.astype(BF16).reshape(own, KV_HEADS, group_size, HEAD)
        grad_probs = jnp.einsum(
            "qhgd,khd->hgqk", grad_heads, vals_all, preferred_element_type=jnp.float32
        )
        row_dot = jnp.sum(probs * grad_probs, axis=-1, keepdims=True)
        grad_scores = (probs * (grad_probs - row_dot)).astype(BF16)
        grad_queries = score_scale * jnp.einsum(
            "hgqk,khd->qhgd", grad_scores, keys_all, preferred_element_type=jnp.float32
        ).reshape(own, -1)
        grad_keys = score_scale * jnp.einsum(
            "hgqk,qhgd->khd", grad_scores, heads_q, preferred_element_type=jnp.float32
        )
        grad_vals = jnp.einsum(
            "hgqk,qhgd->khd", probs_bf, grad_heads, preferred_element_type=jnp.float32
        )
        grad_queries = lax.all_to_all(
            grad_queries.astype(BF16).reshape(own, ctx, -1).transpose(1, 0, 2), "ctx", 0, 0, tiled=True
        ).reshape(length, -1)
        grad_kv = jnp.concatenate(
            [
                grad_keys.reshape(length, ctx, kv_mine).transpose(1, 0, 2),
                grad_vals.reshape(length, ctx, kv_mine).transpose(1, 0, 2),
            ],
            2,
        ).astype(BF16)
        grad_kv = jnp.sum(
            lax.all_to_all(grad_kv, "ctx", 0, 0, tiled=True).astype(jnp.float32), axis=0
        ).astype(BF16)
        grad_early = jnp.concatenate([grad_queries, grad_kv], 1)
        out_dw = [
            left_trans(branch_ssm, branch_all).astype(BF16),
            left_trans(branch_attn_c, branch_all).astype(BF16),
        ]

    grad_early, out_dw, pair_grad = lax.optimization_barrier((grad_early, out_dw, pair_grad))
    out_grad = scatter_fsdp(*out_dw)

    output = middle + ffn_out

    grad_norm = right_trans(branch_all, mixout_full)
    grad_ssm_gain = jnp.sum(grad_norm * ssm_gated * ssm_scale, axis=0)
    scaled = grad_norm * gain_ssm
    mean_dot = total_of(jnp.sum(scaled * ssm_gated, axis=-1), 9)[:, None] / inner
    grad_gated = ssm_scale * scaled - ssm_gated * ssm_scale**3 * mean_dot
    grad_scan = grad_gated * gate_act
    grad_gate_z = grad_gated * ssm_raw * silu_slope(gate_z)
    grad_skip = jnp.sum(grad_scan * conv_vals, axis=0)
    grad_gate_bf = grad_gate_z.astype(BF16)
    grad_early = jnp.concatenate([grad_early, grad_gate_bf], 1)
    early_grad = scatter_fsdp(left_trans(normed_all, grad_early))
    with_relay = ctx == 8 and hidden_units == ctx
    grad_steps, grad_drive, grad_input_mat, grad_output_mat, grad_rate, relayed = scan_bwd(
        steps_pad, vals_pad, padded(grad_scan), in_b, out_b, rates_log2, states,
        *(((pair_grad, down_grad), hidden_rows, hid, 14) if with_relay else ()),
    )
    grad_steps, out_grad = lax.optimization_barrier((grad_steps, out_grad))
    grad_steps, grad_drive, grad_rate = (
        grad_steps[:, :mine],
        grad_drive[:, :mine],
        -grad_rate[:, :mine],
    )
    grad_pre_full = grad_steps * jax.nn.sigmoid(step_pre)
    grad_step_bias = jnp.sum(grad_pre_full, axis=0)
    grad_pre = grad_pre_full.astype(BF16)
    step_dw = left_trans(step_low, grad_pre)
    grad_projected = sum_everywhere(
        jnp.concatenate(
            [right_trans(grad_pre, step_full), grad_input_mat, grad_output_mat], 1
        ).astype(BF16),
        10,
    )
    grad_state_proj = left_trans(conv_act, grad_projected)
    grad_conv_act = (
        right_trans(grad_projected, state_full) + grad_scan * skip + grad_drive
    ).astype(BF16)
    grad_conv = grad_conv_act.astype(jnp.float32) * silu_slope(conv_pre)
    grad_conv_bias = jnp.sum(grad_conv, axis=0)
    grad_taps = jnp.stack(
        [jnp.sum(grad_conv * padded_src[tap : tap + length], axis=0) for tap in range(CONV)]
    )
    conv_tail = jnp.concatenate([grad_conv, jnp.zeros((CONV - 1, mine), jnp.float32)], 0)
    grad_src = sum(
        taps[tap][None] * conv_tail[CONV - 1 - tap : CONV - 1 - tap + length]
        for tap in range(CONV)
    )
    grad_src = grad_src.astype(BF16)
    src_grad = scatter_fsdp(left_trans(normed_all, grad_src), step_dw)
    grad_normed = reduce_products([grad_early, grad_src], [in_full], True, 11)
    if with_relay:
        gate_blocks, up_blocks, down_blocks = relayed
    else:
        pair_grad = pair_grad.reshape(-1, 2, fsdp, down_at)[..., :hid_part]
        gate_blocks = to_blocks(pair_grad[:, 0].reshape(-1, hid), hidden_units)
        up_blocks = to_blocks(pair_grad[:, 1].reshape(-1, hid), hidden_units)
        down_blocks = rows_to_blocks(down_grad[:hid_part], hidden_rows)
    grad_tokens, grad_norm_gain = norm_back(grad_normed, tokens, norm_scale, norm_gain)
    grad_tokens = grad_tokens + grad_middle

    channel = jnp.concatenate(
        [
            grad_taps,
            jnp.stack([grad_conv_bias, grad_step_bias, grad_skip, grad_ssm_gain]),
            grad_rate,
            grad_state_proj.T,
        ],
        0,
    )
    gains = jnp.stack([grad_norm_gain, grad_attn_gain, grad_ffn_gain])
    channel = jnp.pad(channel, ((0, -channel.shape[0] % (8 * fsdp)), (0, 0)))
    gains = jnp.pad(gains, ((0, 5), (0, 0)))
    if ctx == 8 and ctx == 2 * fsdp and not attn_pad:
        (
            query_grad, key_grad, value_grad, mixer_grad, step_grad, attn_grad, mixout_grad, channel, gains,
        ) = finish(
            early_grad, src_grad, out_grad, channel, gains,
            (q_mine, kv_mine, step_rows, mix_rows, attn_rows_mine), 12,
        )
    else:
        channel, gains = settle_small(channel, gains, 12)
        channel = channel.reshape(ctx, -1, fsdp, mine // fsdp).transpose(1, 2, 0, 3)
        channel = channel.reshape(-1, inner)
        late_at = q_mine + 2 * kv_mine
        step_grad = src_grad[early_grad.shape[0] :][:step_rows]
        src_grad = src_grad[: early_grad.shape[0]]
        mixout_grad = out_grad[:mix_rows]
        attn_grad = out_grad[mix_rows : mix_rows + attn_rows_mine]
        query_grad = early_grad[:, :q_mine].astype(jnp.float32)
        key_grad = early_grad[:, q_mine : q_mine + kv_mine].astype(jnp.float32)
        value_grad = early_grad[:, q_mine + kv_mine : late_at].astype(jnp.float32)
        mixer_grad = to_blocks(
            jnp.concatenate([src_grad, early_grad[:, late_at:]], 1), 2 * fsdp
        )
        step_grad = to_blocks(step_grad, fsdp)
        attn_grad = rows_to_blocks(attn_grad, 1)[: attn_proj.shape[0]]
        mixout_grad = rows_to_blocks(mixout_grad, 1)
    sum_norm_gain, sum_attn_gain, sum_ffn_gain = gains[0], gains[1], gains[2]
    return (
        output[None],
        grad_tokens[None],
        sum_norm_gain,
        query_grad,
        key_grad,
        value_grad,
        attn_grad,
        sum_attn_gain,
        mixer_grad,
        channel[:CONV],
        channel[CONV],
        channel[CONV + 4 + STATE : CONV + 4 + STATE + state_proj.shape[1]].T,
        step_grad,
        channel[CONV + 1],
        channel[CONV + 4 : CONV + 4 + STATE].T,
        channel[CONV + 2],
        mixout_grad,
        channel[CONV + 3],
        sum_ffn_gain,
        gate_blocks,
        up_blocks,
        down_blocks,
    )


def solution(mesh):
    rows, whole = P("fsdp", None), P()
    blocks, sequence = P("fsdp", "ctx"), P("fsdp", "ctx", None)
    return jax.shard_map(
        body,
        mesh=mesh,
        in_specs=(
            sequence, sequence, whole, rows, rows, rows, rows, whole, rows, whole, whole,
            rows, rows, whole, whole, whole, rows, whole, whole, rows, rows, rows,
        ),
        out_specs=(
            sequence, sequence, whole, blocks, blocks, blocks, blocks, whole, blocks, whole, whole,
            whole, blocks, whole, whole, whole, blocks, whole, whole, blocks, blocks, blocks,
        ),
        check_vma=False,
    )
```

```python
import functools
import jax
import jax.numpy as jnp
from jax import lax
from jax.experimental import pallas as pl
from jax.experimental.pallas import tpu as pltpu
from jax.sharding import PartitionSpec as P

LANES = 128
STATE = 16
CHUNK = 128
HEAD = 64
KV_HEADS = 5
CONV = 4
DT_RANK = 100
WINDOW = 1024
EPSILON = 1e-06
LOG2_E = 1.4426950408889634
BF16 = jnp.bfloat16


MESH = pl.DeviceIdType.MESH
VMEM_LIMIT = 56 * 1024 * 1024
IN_VMEM = pl.BlockSpec(memory_space=pltpu.VMEM)


def flip(index, bit):
    return index + (1 - 2 * ((index // (1 << bit)) % 2)) * (1 << bit)


def greet(me, bits):
    barrier = pltpu.get_barrier_semaphore()
    for bit in range(bits):
        pl.semaphore_signal(
            barrier, inc=1, device_id={"ctx": flip(me, bit)}, device_id_type=MESH
        )
    pl.semaphore_wait(barrier, bits)


def halves_of(rows):
    half = rows // 2 if rows % 32 == 0 else rows // 32 * 16
    return (pl.ds(0, half), pl.ds(half, rows - half))


class Copies:
    def __init__(self, axis, send_sem, recv_sem):
        self.axis, self.send_sem, self.recv_sem = axis, send_sem, recv_sem
        self.started = []
        self.count = 0

    def make(self, source, target, device):
        copy = pltpu.make_async_remote_copy(
            src_ref=source,
            dst_ref=target,
            send_sem=self.send_sem.at[self.count],
            recv_sem=self.recv_sem.at[self.count],
            device_id={self.axis: device},
            device_id_type=MESH,
        )
        self.count += 1
        return copy

    def send(self, source, target, device):
        copy = self.make(source, target, device)
        copy.start()
        self.started.append(copy)
        return copy

    def finish(self):
        for copy in self.started:
            copy.wait_send()


def gather_sems(bits):
    return 1 + 2 * sum(1 << p for p in range(bits - 1)) + 2 * ((1 << (bits - 1)) - 1)


def gather_steps(copies, bits, out_ref):
    me = lax.axis_index("ctx")
    parts = halves_of(out_ref.shape[1])
    orders = (list(range(1, bits)), list(range(bits - 1, 0, -1)))

    def send(bit, shard, part):
        at = out_ref.at[shard] if part is None else out_ref.at[shard, part]
        return copies.send(at, at, flip(me, bit))

    known = ([me], [me])
    last, flying = [], [None, None]

    def begin():
        for h in range(2):
            flying[h] = [send(orders[h][0], shard, parts[h]) for shard in known[h]]
        last.append(send(0, me, None))

    def turn(phase, h):
        bit = orders[h][phase]
        for copy in flying[h]:
            copy.wait_recv()
        fresh = [flip(shard, bit) for shard in known[h]]
        known[h].extend(fresh)
        if phase + 1 < bits - 1:
            flying[h] = [send(orders[h][phase + 1], shard, parts[h]) for shard in known[h]]
        last.extend(send(0, shard, parts[h]) for shard in fresh)

    def end():
        for copy in last:
            copy.wait_recv()

    turns = [functools.partial(turn, p, h) for p in range(bits - 1) for h in range(2)]
    return [begin] + turns + [end]


def gather_kernel(bits, x_ref, out_ref, send_sem, recv_sem):
    me = lax.axis_index("ctx")
    greet(me, bits)
    out_ref[me] = x_ref[...]
    copies = Copies("ctx", send_sem, recv_sem)
    for step in gather_steps(copies, bits, out_ref):
        step()
    copies.finish()


def ctx_bits():
    return lax.axis_size("ctx").bit_length() - 1


def params(collective_id):
    return pltpu.CompilerParams(
        collective_id=collective_id, has_side_effects=True, vmem_limit_bytes=VMEM_LIMIT
    )


def gather_shards(x, collective_id):
    bits, ctx = ctx_bits(), lax.axis_size("ctx")
    sems = pltpu.SemaphoreType.DMA((gather_sems(bits),))
    return pl.pallas_call(
        functools.partial(gather_kernel, bits),
        out_shape=jax.ShapeDtypeStruct((ctx,) + x.shape, x.dtype),
        in_specs=[IN_VMEM],
        out_specs=IN_VMEM,
        scratch_shapes=[sems, sems],
        compiler_params=params(collective_id),
        name="gather_shards",
    )(x)


def gather_tokens(x, collective_id):
    return gather_shards(x, collective_id).reshape(-1, x.shape[1])


def row_parts(rows, count):
    tiles = rows // 16
    edges = [16 * (tiles * i // count) for i in range(count)] + [rows]
    return [pl.ds(a, b - a) for a, b in zip(edges[:-1], edges[1:]) if b > a]


def line_steps(copies, out_refs, pieces):
    me, size = lax.axis_index("fsdp"), lax.axis_size("fsdp")
    plans = []
    for way in (1, -1):
        for distance in range(size - 1):
            for ref, part in pieces:
                shard = me - way * distance
                inside = jnp.logical_and(shard >= 0, shard < size)
                held = jnp.where(inside, shard, me)
                to = me + way
                go = jnp.logical_and(inside, jnp.logical_and(to >= 0, to < size))
                target = jnp.where(jnp.logical_and(to >= 0, to < size), to, me - way)
                at = out_refs[ref].at[held, part]
                plans.append((way, distance, go, copies.make(at, at, target)))
    table = {}
    for way, distance, go, copy in plans:
        table.setdefault((way, distance), []).append((go, copy))

    def begin():
        for index in range(len(pieces)):
            for way in (1, -1):
                go, copy = table[way, 0][index]
                pl.when(go)(copy.start)

    def turn(distance, index):
        for way in (1, -1):
            _, came = table[way, distance - 1][index]
            origin = me - way * distance
            pl.when(jnp.logical_and(origin >= 0, origin < size))(came.wait_recv)
            if distance < size - 1:
                go, copy = table[way, distance][index]
                pl.when(go)(copy.start)

    def end():
        for way in (1, -1):
            for distance in range(size - 1):
                for go, copy in table[way, distance]:
                    pl.when(go)(copy.wait_send)

    turns = [
        functools.partial(turn, d, i) for d in range(1, size) for i in range(len(pieces))
    ]
    return [begin] + turns, end


def front_kernel(
    bits, count, turned, pack_first, pack, x_ref, gain_ref, top_ref, *rest,
):
    number = 6 if pack_first["scratch"] else 3
    first_refs, rest = rest[:number], rest[number:]
    weights, rest = rest[: pack["inputs"]], rest[pack["inputs"] :]
    normed_ref, tops_ref, in_out, state_out, step_out = rest[:5]
    packed, rest = rest[5 : 5 + pack["outputs"]], rest[5 + pack["outputs"] :]
    ctx_send, ctx_recv, line_send, line_recv = rest[:4]
    first_scratch, rest = rest[4 : 4 + len(pack_first["scratch"])], rest[4 + len(pack_first["scratch"]) :]
    me, row, rows = lax.axis_index("ctx"), lax.axis_index("fsdp"), lax.axis_size("fsdp")
    barrier = pltpu.get_barrier_semaphore()
    for bit in range(bits):
        pl.semaphore_signal(
            barrier, inc=1, device_id={"ctx": flip(me, bit)}, device_id_type=MESH
        )
    for to in (row - 1, row + 1):
        there = jnp.logical_and(to >= 0, to < rows)

        @pl.when(there)
        def _():
            pl.semaphore_signal(
                barrier, inc=1, device_id={"fsdp": jnp.where(there, to, row)}, device_id_type=MESH
            )

    if first_scratch:
        copies = pack_in_begin(first_refs, first_scratch)
        pack_in(row, copies, first_refs, first_scratch, in_out, state_out, step_out)
    else:
        for out, ref in zip((in_out, state_out, step_out), first_refs):
            out[row] = ref[...]
    neighbours = jnp.where(row > 0, 1, 0) + jnp.where(row < rows - 1, 1, 0)
    pl.semaphore_wait(barrier, bits + neighbours)

    line = Copies("fsdp", line_send, line_recv)
    across = Copies("ctx", ctx_send, ctx_recv)
    pieces = [(0, part) for part in row_parts(in_out.shape[1], count)]
    pieces = [(1, pl.ds(0, state_out.shape[1])), (2, pl.ds(0, step_out.shape[1]))] + pieces
    line_list, line_end = line_steps(line, (in_out, state_out, step_out), pieces)
    line_list[0]()
    tokens = x_ref[...].astype(jnp.float32)
    if turned:
        tokens = tokens.T
    scale = lax.rsqrt(jnp.mean(tokens * tokens, axis=-1, keepdims=True) + EPSILON)
    normed_ref[me] = (tokens * scale * gain_ref[...]).astype(normed_ref.dtype)
    first = gather_steps(across, bits, normed_ref)
    first[0]()
    tops = top_ref[...].astype(jnp.float32)
    tops_ref[me] = (tops.T if turned else tops).astype(tops_ref.dtype)
    second = gather_steps(across, bits, tops_ref)
    steps = list(pack["steps"](me, weights, packed, rest)) if weights else []
    token_rest = first[1:-1] + [second[0]] + second[1:-1] + [first[-1], second[-1]]
    line_rest = line_list[1:]
    tokens_done = packs_done = 0
    spread = len(line_rest) * 3 // 4
    for i, step in enumerate(line_rest):
        upto = min(len(steps), len(steps) * (i + 1) // max(1, spread))
        for pack_step in steps[packs_done:upto]:
            pack_step()
        packs_done = max(packs_done, upto)
        step()
        upto = min(len(token_rest), len(token_rest) * (i + 1) // spread)
        for token_step in token_rest[tokens_done:upto]:
            token_step()
        tokens_done = max(tokens_done, upto)
    across.finish()
    line_end()


def front(x, gain, top, first, later, hidden_units, collective_id):
    bits, ctx, fsdp = ctx_bits(), lax.axis_size("ctx"), lax.axis_size("fsdp")
    count = 5
    ctx_sems = pltpu.SemaphoreType.DMA((2 * gather_sems(bits),))
    line_sems = pltpu.SemaphoreType.DMA((2 * fsdp * (count + 2),))
    pack_first, pack = pack_in_plan(first), pack_out_plan(later, hidden_units)
    turned = bool(later)
    tokens = jax.ShapeDtypeStruct(x.shape[::-1] if turned else x.shape, x.dtype)
    in_any = pl.BlockSpec(memory_space=pl.ANY)

    def stacked(array, size):
        return jax.ShapeDtypeStruct((size,) + array.shape, array.dtype)

    return pl.pallas_call(
        functools.partial(front_kernel, bits, count, turned, pack_first, pack),
        out_shape=[stacked(tokens, ctx), stacked(tokens, ctx)]
        + [stacked(part, fsdp) for part in pack_first["shapes"]]
        + pack["shapes"],
        in_specs=[IN_VMEM] * 3
        + [in_any if i in pack_first["any"] else IN_VMEM for i in range(len(first))]
        + [in_any] * len(later),
        out_specs=[IN_VMEM] * (5 + pack["outputs"]),
        scratch_shapes=[ctx_sems, ctx_sems, line_sems, line_sems]
        + pack_first["scratch"]
        + pack["scratch"],
        compiler_params=params(collective_id),
        name="front",
    )(x, gain, top, *first, *later)


def product(x, weight, trans):
    dims = (((1,), (1 if trans else 0,)), ((), ()))
    return lax.dot_general(x, weight, dims, preferred_element_type=jnp.float32)


def subsets(chosen):
    out = [()]
    for bit in chosen:
        out = out + [s + (bit,) for s in out]
    return out


def flipped(shard, flips):
    for bit in flips:
        shard = flip(shard, bit)
    return shard


class Reducer:
    def __init__(self, copies, bits, part_ref, inbox, out_ref):
        self.copies, self.bits, self.part_ref = copies, bits, part_ref
        self.inbox, self.out_ref = inbox, out_ref
        self.me = lax.axis_index("ctx")
        self.parts = halves_of(out_ref.shape[0])
        self.orders = (list(range(1, bits)), list(range(bits - 1, 0, -1)))
        self.everyone = subsets(range(1, bits))[::-1]
        self.slots = {flips: slot for slot, flips in enumerate(self.everyone)}
        self.first = {}
        self.flying = [{}, {}]

    def to_sibling(self, flips, partial):
        slot = self.slots[flips]
        self.part_ref[slot] = partial.astype(self.part_ref.dtype)
        self.first[flips] = self.copies.send(
            self.part_ref.at[slot], self.inbox[0].at[slot], flip(self.me, 0)
        )

    def pass_on(self, h, phase, flips, following):
        bit = self.orders[h][phase]
        if bit in flips:
            kept = tuple(b for b in flips if b != bit)
            following[kept] = self.copies.send(
                self.inbox[0].at[self.slots[flips], self.parts[h]],
                self.inbox[1 + phase].at[len(following), self.parts[h]],
                flip(self.me, bit),
            )

    def send_parts(self, parts_ref):
        for flips in self.everyone:
            self.first[flips] = self.copies.send(
                parts_ref.at[flipped(self.me, flips + (0,))],
                self.inbox[0].at[self.slots[flips]],
                flip(self.me, 0),
            )

    def own(self, flips, partial):
        self.first[flips].wait_recv()
        kept_ref, slot = self.inbox[0], self.slots[flips]
        kept_ref[slot] = (partial + kept_ref[slot].astype(jnp.float32)).astype(kept_ref.dtype)
        for h in range(2):
            self.pass_on(h, 0, flips, self.flying[h])

    def turn(self, phase, h):
        kept_ref = self.inbox[0]
        part, following = self.parts[h], {}
        for box, (flips, copy) in enumerate(list(self.flying[h].items())):
            copy.wait_recv()
            slot = self.slots[flips]
            total = kept_ref[slot, part].astype(jnp.float32) + self.inbox[1 + phase][
                box, part
            ].astype(jnp.float32)
            if phase == self.bits - 2:
                self.out_ref[part] = total
            else:
                kept_ref[slot, part] = total.astype(kept_ref.dtype)
                self.pass_on(h, phase + 1, flips, following)
        self.flying[h] = following

    def turns(self):
        return [functools.partial(self.turn, p, h) for p in range(self.bits - 1) for h in range(2)]

    def finish(self):
        for turn in self.turns():
            turn()


def reducer_boxes(ctx, bits, rows, columns):
    boxes = [ctx // 2, ctx // 2] + [ctx // 4 >> p for p in range(bits - 1)]
    sems = boxes[0] + 2 * sum(boxes[2:])
    return [pltpu.VMEM((box, rows, columns), BF16) for box in boxes], sems


def reduce_kernel(bits, trans, joint, *refs):
    count = len(trans)
    weights = 1 if joint else count
    x_refs, w_refs, out_ref = refs[:count], refs[count : count + weights], refs[count + weights]
    part_ref, inbox = refs[count + weights + 1], refs[count + weights + 2 : -2]
    me = lax.axis_index("ctx")
    greet(me, bits)
    if joint:
        whole, w_refs, inbox = w_refs[0], inbox[-count:], inbox[:-count]
        at = 0
        for w_ref in w_refs:
            wide = w_ref.shape[1]
            w_ref[...] = whole[:, at : at + wide]
            at += wide
    copies = Copies("ctx", *refs[-2:])
    reducer = Reducer(copies, bits, part_ref, inbox, out_ref)

    def partial(flips):
        shard = flipped(me, flips)
        return sum(
            product(x_ref[shard], w_ref[...], way)
            for x_ref, w_ref, way in zip(x_refs, w_refs, trans)
        )

    for flips in reducer.everyone:
        reducer.to_sibling(flips, partial(flips + (0,)))
    for flips in reducer.everyone:
        reducer.own(flips, partial(flips))
    reducer.finish()
    copies.finish()


def reduce_products(lefts, weights, trans, collective_id):
    ctx, bits = lax.axis_size("ctx"), ctx_bits()
    rows = lefts[0].shape[0] // ctx
    columns = weights[0].shape[0 if trans else 1]
    joint = len(weights) < len(lefts)
    boxes, count = reducer_boxes(ctx, bits, rows, columns)
    if joint:
        boxes = boxes + [pltpu.VMEM((columns, x.shape[1]), BF16) for x in lefts]
    sems = pltpu.SemaphoreType.DMA((count,))
    return pl.pallas_call(
        functools.partial(reduce_kernel, bits, (trans,) * len(lefts), joint),
        out_shape=jax.ShapeDtypeStruct((rows, columns), jnp.float32),
        in_specs=[IN_VMEM] * (len(lefts) + len(weights)),
        out_specs=IN_VMEM,
        scratch_shapes=boxes + [sems, sems],
        compiler_params=params(collective_id),
        name="reduce_products",
    )(*[x.reshape(ctx, rows, -1) for x in lefts], *weights)


def relay_copies(pair_send, pair_recv, down_send, down_recv, send_sem, recv_sem):
    size = pair_send.shape[0]
    me = lax.axis_index("ctx")
    copies = Copies("ctx", send_sem, recv_sem)
    return [
        copies.make(send.at[(me + turn) % size], recv.at[me], (me + turn) % size)
        for send, recv in ((pair_send, pair_recv), (down_send, down_recv))
        for turn in range(1, size)
    ]


def relay_begin(units, stack_ref, pair_send, pair_recv, down_send, down_recv, *sems):
    size = pair_send.shape[0]
    me = lax.axis_index("ctx")
    greet_all(me, size)
    wide, block = pair_send.shape[2] // 2, down_send.shape[2]
    high, part, span = pair_send.shape[1], down_send.shape[1], stack_ref.shape[1]
    half = span // 2
    model = size * block
    pieces, tall = spill_of(part, model, span)
    for d in range(size):
        at = d // units * part + d % units * wide
        pair_send[d, :, :wide] = stack_ref[:high, at : at + wide]
        pair_send[d, :, wide:] = stack_ref[:high, half + at : half + at + wide]
        low, up = d * block, (d + 1) * block
        if low < span:
            down_send[d, :, : min(up, span) - low] = stack_ref[high : high + part, low : min(up, span)]
        if up > span:
            first = max(low, span)
            for k in range(pieces):
                begin, end = k * tall, min(part, (k + 1) * tall)
                lane = k * (model - span) + first - span
                down_send[d, begin:end, first - low :] = stack_ref[
                    high + part : high + part + end - begin, lane : lane + up - first
                ]
    for copy in relay_copies(pair_send, pair_recv, down_send, down_recv, *sems):
        copy.start()
    pair_recv[me] = pair_send[me]
    down_recv[me] = down_send[me]


def relay_end(units, gate_out, up_out, down_out, pair_send, pair_recv, down_send, down_recv, *sems):
    size, wide = pair_send.shape[0], pair_send.shape[2] // 2
    for copy in relay_copies(pair_send, pair_recv, down_send, down_recv, *sems):
        copy.wait()
    for s in range(size):
        at = s * wide
        gate_out[:, at : at + wide] = pair_recv[s, :, :wide].astype(jnp.float32)
        up_out[:, at : at + wide] = pair_recv[s, :, wide:].astype(jnp.float32)
        for u in range(units):
            to = u * size * wide + at
            down_out[to : to + wide] = down_recv[s, u * wide : (u + 1) * wide].astype(jnp.float32)


def greet_all(me, size):
    barrier = pltpu.get_barrier_semaphore()
    for turn in range(1, size):
        pl.semaphore_signal(
            barrier, inc=1, device_id={"ctx": (me + turn) % size}, device_id_type=MESH
        )
    pl.semaphore_wait(barrier, size - 1)


def sum_kernel(size, x_ref, out_ref, send_ref, inbox, all_ref, send_sem, recv_sem):
    me = lax.axis_index("ctx")
    greet_all(me, size)
    columns = x_ref.shape[2]
    copies = Copies("ctx", send_sem, recv_sem)
    send_ref[:, columns:] = jnp.zeros((size, send_ref.shape[1] - columns, x_ref.shape[1]), BF16)
    for e in range(size):
        send_ref[e, :columns] = x_ref[e].astype(jnp.float32).T.astype(BF16)
    come = []
    for turn in range(1, size):
        to = (me + turn) % size
        come.append(copies.send(send_ref.at[to], inbox.at[turn - 1], to))
    total = send_ref[me].astype(jnp.float32)
    for turn in range(1, size):
        come[turn - 1].wait_recv()
        total = total + inbox[turn - 1].astype(jnp.float32)
    all_ref[me] = total.astype(BF16)
    come = [
        copies.send(all_ref.at[me], all_ref.at[me], (me + turn) % size) for turn in range(1, size)
    ]
    for copy in come:
        copy.wait_recv()
    for e in range(size):
        out_ref[e] = all_ref[e].astype(jnp.float32).T[:, :columns].astype(out_ref.dtype)
    copies.finish()


def sum_everywhere(partial, collective_id):
    ctx = lax.axis_size("ctx")
    rows, columns = partial.shape[0] // ctx, partial.shape[1]
    high = columns + -columns % 16
    sems = pltpu.SemaphoreType.DMA((2 * (ctx - 1),))
    return pl.pallas_call(
        functools.partial(sum_kernel, ctx),
        out_shape=jax.ShapeDtypeStruct((ctx, rows, columns), partial.dtype),
        in_specs=[IN_VMEM],
        out_specs=IN_VMEM,
        scratch_shapes=[
            pltpu.VMEM((ctx, high, rows), BF16),
            pltpu.VMEM((ctx - 1, high, rows), BF16),
            pltpu.VMEM((ctx, high, rows), BF16),
            sems, sems,
        ],
        compiler_params=params(collective_id),
        name="sum_everywhere",
    )(partial.reshape(ctx, rows, columns)).reshape(partial.shape)


def total_kernel(size, x_ref, out_ref, inbox, send_sem, recv_sem):
    me = lax.axis_index("ctx")
    greet_all(me, size)
    copies = Copies("ctx", send_sem, recv_sem)
    come = [
        copies.send(x_ref, inbox.at[turn - 1], (me + turn) % size) for turn in range(1, size)
    ]
    inbox_total = x_ref[...]
    for turn in range(1, size):
        come[turn - 1].wait_recv()
        inbox_total = inbox_total + inbox[turn - 1]
    out_ref[...] = inbox_total
    copies.finish()


def total_of(rows_sum, collective_id):
    ctx = lax.axis_size("ctx")
    flat = rows_sum.reshape(-1, LANES)
    sems = pltpu.SemaphoreType.DMA((ctx - 1,))
    return pl.pallas_call(
        functools.partial(total_kernel, ctx),
        out_shape=jax.ShapeDtypeStruct(flat.shape, flat.dtype),
        in_specs=[IN_VMEM],
        out_specs=IN_VMEM,
        scratch_shapes=[pltpu.VMEM((ctx - 1,) + flat.shape, flat.dtype), sems, sems],
        compiler_params=params(collective_id),
        name="total_of",
    )(flat).reshape(rows_sum.shape)


def settle_kernel(
    bits, size, count, channel_ref, gain_ref, all_ref, sums_ref,
    row_inbox, gain_inbox, line_inbox, ctx_send, ctx_recv, line_send, line_recv,
):
    me, row = lax.axis_index("ctx"), lax.axis_index("fsdp")
    barrier = pltpu.get_barrier_semaphore()
    for turn in range(1, size):
        pl.semaphore_signal(
            barrier, inc=1, device_id={"ctx": (me + turn) % size}, device_id_type=MESH
        )
    for turn in range(1, count):
        pl.semaphore_signal(
            barrier, inc=1, device_id={"fsdp": (row + turn) % count}, device_id_type=MESH
        )
    pl.semaphore_wait(barrier, size - 1 + count - 1)
    across, line = Copies("ctx", ctx_send, ctx_recv), Copies("fsdp", line_send, line_recv)
    band = channel_ref.shape[0] // count

    def band_of(index):
        return pl.ds(pl.multiple_of(index * band, 8), band)

    rows_come = []
    for turn in range(1, count):
        to = (row + turn) % count
        rows_come.append(line.send(channel_ref.at[band_of(to)], row_inbox.at[turn - 1], to))
    gains_come = [
        across.send(gain_ref, gain_inbox.at[turn - 1], (me + turn) % size)
        for turn in range(1, size)
    ]
    total = channel_ref[band_of(row)]
    for turn in range(1, count):
        rows_come[turn - 1].wait_recv()
        total = total + row_inbox[turn - 1]
    all_ref[me, band_of(row)] = total
    at = all_ref.at[me, band_of(row)]
    bands_come = [line.send(at, at, (row + turn) % count) for turn in range(1, count)]
    total = gain_ref[...]
    for turn in range(1, size):
        gains_come[turn - 1].wait_recv()
        total = total + gain_inbox[turn - 1]
    line_inbox[0] = total
    line_come = [
        line.send(line_inbox.at[0], line_inbox.at[turn], (row + turn) % count)
        for turn in range(1, count)
    ]
    for copy in bands_come:
        copy.wait_recv()
    for step in gather_steps(across, bits, all_ref):
        step()
    total = line_inbox[0]
    for turn in range(1, count):
        line_come[turn - 1].wait_recv()
        total = total + line_inbox[turn]
    sums_ref[...] = total
    across.finish()
    line.finish()


def settle_small(channel, gains, collective_id):
    ctx, fsdp, bits = lax.axis_size("ctx"), lax.axis_size("fsdp"), ctx_bits()
    ctx_sems = pltpu.SemaphoreType.DMA((ctx - 1 + gather_sems(bits),))
    line_sems = pltpu.SemaphoreType.DMA((3 * (fsdp - 1),))
    rows, columns = channel.shape
    return pl.pallas_call(
        functools.partial(settle_kernel, bits, ctx, fsdp),
        out_shape=[
            jax.ShapeDtypeStruct((ctx, rows, columns), jnp.float32),
            jax.ShapeDtypeStruct(gains.shape, jnp.float32),
        ],
        in_specs=[IN_VMEM] * 2,
        out_specs=[IN_VMEM] * 2,
        scratch_shapes=[
            pltpu.VMEM((fsdp - 1, rows // fsdp, columns), jnp.float32),
            pltpu.VMEM((ctx - 1,) + gains.shape, jnp.float32),
            pltpu.VMEM((fsdp,) + gains.shape, jnp.float32),
            ctx_sems, ctx_sems, line_sems, line_sems,
        ],
        compiler_params=params(collective_id),
        name="settle_small",
    )(channel, gains)


def plane_gather(copies, out_ref):
    me = lax.axis_index("ctx")
    parts = halves_of(out_ref.shape[1])
    held = {}

    def send(name, bit, flips, part=None):
        shard = flipped(me, flips)
        at = out_ref.at[shard] if part is None else out_ref.at[shard, part]
        held[name] = copies.send(at, at, flip(me, bit))

    def start():
        for bit in (1, 2, 0):
            send(("own", bit), bit, ())

    def forward():
        held["own", 1].wait_recv()
        send(("corner", 2), 2, (1,), parts[0])
        held["own", 2].wait_recv()
        send(("corner", 1), 1, (2,), parts[1])
        send(("core", (1,)), 0, (1,))
        send(("core", (2,)), 0, (2,))

    def corner():
        held["corner", 2].wait_recv()
        held["corner", 1].wait_recv()
        send(("core", (1, 2)), 0, (1, 2))

    def wait(flips):
        held["core", flips].wait_recv() if flips else held["own", 0].wait_recv()

    return start, forward, corner, wait


def ffn_kernel(
    x_ref, top_ref, pair_w, down_w,
    dw_ref, out_ref, grad_ref,
    all_ref, hidden_ref, pair_ref, own_ref, part_grad, *rest,
):
    bits = 3
    me = lax.axis_index("ctx")
    greet(me, bits)
    all_ref[me] = x_ref[...]
    copies = Copies("ctx", *rest[-2:])
    start, forward, corner, wait = plane_gather(copies, all_ref)
    reducer = Reducer(copies, bits, part_grad, rest[:-2], grad_ref)
    rows, model = x_ref.shape
    hid = hidden_ref.shape[2]
    core = me % 2

    def work(slot, flips):
        first = 2 * (flipped(me, flips) // 2)
        pair = pl.ds(first, 2)
        x = all_ref[pair].reshape(2 * rows, model)
        pre = product(x, pair_w[...], False)
        gate, up = pre[:, :hid], pre[:, hid:]
        logistic = jax.nn.sigmoid(gate)
        gate_silu = gate * logistic
        hidden = (gate_silu * up).astype(BF16)
        hidden_ref[pair] = hidden.reshape(2, rows, hid)
        top = top_ref[pair].reshape(2 * rows, model)
        grad_hidden = product(top, down_w[...], True)
        slope = logistic * (1.0 + gate * (1.0 - logistic))
        pair_ref[pair, :, :hid] = (grad_hidden * up * slope).astype(BF16).reshape(2, rows, hid)
        pair_ref[pair, :, hid:] = (grad_hidden * gate_silu).astype(BF16).reshape(2, rows, hid)
        grads = pair_ref[pair].reshape(2 * rows, 2 * hid)
        value = product(grads, pair_w[...], True)
        low, high = value[:rows], value[rows:]
        own_ref[slot] = jnp.where(core == 0, low, high)
        reducer.to_sibling(flips, jnp.where(core == 0, high, low))

    def project(first):
        pair = pl.ds(first, 2)
        hidden = hidden_ref[pair].reshape(2 * rows, hid)
        out_ref[pair] = product(hidden, down_w[...], False).astype(BF16).reshape(2, rows, model)

    def settle(slot, flips):
        reducer.own(flips, own_ref[slot])

    start()
    wait(())
    work(0, ())
    forward()
    wait((1,))
    work(1, (1,))
    settle(0, ())
    corner()
    wait((2,))
    work(2, (2,))
    settle(1, (1,))
    wait((1, 2))
    work(3, (1, 2))
    settle(2, (2,))
    settle(3, (1, 2))

    size, blocks = all_ref.shape[0], dw_ref.shape[0]
    high, part, wide = model // blocks, hid // blocks, 2 * hid
    pieces, tall = spill_of(part, model, wide)

    def over_tokens(left_ref, right_ref, low, count):
        left = left_ref[:, :, low : low + count].reshape(size * rows, count)
        right = right_ref[...].reshape(size * rows, right_ref.shape[2])
        return lax.dot_general(
            left, right, (((0,), (0,)), ((), ())), preferred_element_type=jnp.float32
        ).astype(BF16)

    def pair_band(f):
        dw_ref[f, :high] = over_tokens(all_ref, pair_ref, f * high, high)

    def down_band(f):
        values = over_tokens(hidden_ref, top_ref, f * part, part)
        dw_ref[f, high : high + part] = values[:, :wide]
        dw_ref[f, high + part :] = jnp.zeros((dw_ref.shape[1] - high - part, wide), BF16)
        spill = model - wide
        for k in range(pieces):
            low, up = k * tall, min(part, (k + 1) * tall)
            dw_ref[f, high + part : high + part + up - low, k * spill : (k + 1) * spill] = values[
                low:up, wide:
            ]

    work_left = [functools.partial(down_band, f) for f in range(blocks)]
    work_left += [functools.partial(pair_band, f) for f in range(blocks)]
    work_left += [functools.partial(project, first) for first in range(0, size, 2)]
    turns = reducer.turns()
    done = 0
    for i, turn in enumerate(turns):
        upto = len(work_left) * (i + 1) // len(turns)
        for item in work_left[done:upto]:
            item()
        done = upto
        turn()
    copies.finish()


def spill_of(part, model, wide):
    pieces = wide // (model - wide)
    return pieces, -(-part // pieces)


def stack_rows(model, hid, blocks):
    _, tall = spill_of(hid // blocks, model, 2 * hid)
    return model // blocks + hid // blocks + tall + -tall % 16


def ffn_both_ways(ffn_in, top, pair_full, down_full, collective_id):
    ctx, fsdp, bits = lax.axis_size("ctx"), lax.axis_size("fsdp"), ctx_bits()
    rows, model = ffn_in.shape
    hid = down_full.shape[0]
    boxes, count = reducer_boxes(ctx, bits, rows, model)
    sems = pltpu.SemaphoreType.DMA((count + 8,))
    return pl.pallas_call(
        ffn_kernel,
        out_shape=[
            jax.ShapeDtypeStruct((fsdp, stack_rows(model, hid, fsdp), 2 * hid), BF16),
            jax.ShapeDtypeStruct((ctx, rows, model), BF16),
            jax.ShapeDtypeStruct((rows, model), jnp.float32),
        ],
        in_specs=[IN_VMEM] * 4,
        out_specs=[IN_VMEM] * 3,
        scratch_shapes=[
            pltpu.VMEM((ctx, rows, model), BF16),
            pltpu.VMEM((ctx, rows, hid), BF16),
            pltpu.VMEM((ctx, rows, 2 * hid), BF16),
            pltpu.VMEM((ctx // 2, rows, model), jnp.float32),
        ]
        + boxes
        + [sems, sems],
        compiler_params=params(collective_id),
        name="ffn_both_ways",
    )(ffn_in, top.reshape(ctx, rows, model), pair_full, down_full)


def pieces_of(start, width, span):
    out = []
    at = start
    while at < start + width:
        block = at // span
        end = min(start + width, (block + 1) * span)
        out.append((block, at - start, end - start, at - block * span))
        at = end
    return out


def exchange(copies, send_ref, recv_ref, me, size):
    recv_ref[me] = send_ref[me]
    return [
        copies.send(send_ref.at[(me + turn) % size], recv_ref.at[me], (me + turn) % size)
        for turn in range(1, size)
    ]


def attention_kernel(
    size, fsdp, proj_ref, gain_ref,
    branch_ref, rows_ref, prob_ref, inverse_ref, q_ref, k_ref, v_ref,
    q_send, q_recv, kv_all, score_ref, attn_send, send_sem, recv_sem,
):
    bits = size.bit_length() - 1
    me = lax.axis_index("ctx")
    own, q_mine = q_send.shape[1], q_send.shape[2]
    kv_mine = kv_all.shape[2] // 2
    groups, keys, _ = k_ref.shape
    heads = q_ref.shape[1] // own
    queries = heads * own
    chunk = 128
    greet_all(me, size)
    copies = Copies("ctx", send_sem, recv_sem)
    for s in range(size):
        q_send[s] = proj_ref[s * own : (s + 1) * own, :q_mine]
    kv_all[me] = proj_ref[:, q_mine : q_mine + 2 * kv_mine]
    steps = gather_steps(copies, bits, kv_all)
    steps[0]()
    come = exchange(copies, q_send, q_recv, me, size)
    for step in steps[1:]:
        step()
    for copy in come:
        copy.wait_recv()

    for g in range(groups):
        for s, low, high, at in pieces_of(g * HEAD, HEAD, kv_mine):
            k_ref[g, :, low:high] = kv_all[s, :, at : at + high - low]
            v_ref[g, :, low:high] = kv_all[s, :, kv_mine + at : kv_mine + at + high - low]
        for h in range(heads):
            for s, low, high, at in pieces_of((g * heads + h) * HEAD, HEAD, q_mine):
                q_ref[g, h * own : (h + 1) * own, low:high] = q_recv[s, :, at : at + high - low]

    query_ids = me * own + lax.broadcasted_iota(jnp.int32, (chunk, queries), 1) % own
    key_ids = lax.broadcasted_iota(jnp.int32, (chunk, queries), 0)
    for g in range(groups):
        q_g = q_ref[g]

        def scores(i, top):
            at = pl.ds(pl.multiple_of(i * chunk, chunk), chunk)
            raw = product(k_ref[g, at], q_g, True) * (HEAD**-0.5)
            ids = key_ids + i * chunk
            kept = jnp.logical_and(ids <= query_ids, ids > query_ids - WINDOW)
            raw = jnp.where(kept, raw, -1e30)
            score_ref[at] = raw
            return jnp.maximum(top, jnp.max(raw, axis=0, keepdims=True))

        top = lax.fori_loop(
            0, keys // chunk, scores, jnp.full((1, queries), -1e30, jnp.float32)
        )

        def weights(i, total):
            at = pl.ds(pl.multiple_of(i * chunk, chunk), chunk)
            value = jnp.exp(score_ref[at] - top)
            prob_ref[g, at] = value.astype(BF16)
            return total + jnp.sum(value, axis=0, keepdims=True)

        total = lax.fori_loop(
            0, keys // chunk, weights, jnp.zeros((1, queries), jnp.float32)
        )
        inverse = 1.0 / total
        inverse_ref[g] = inverse
        out = lax.dot_general(
            v_ref[g], prob_ref[g], (((0,), (0,)), ((), ())), preferred_element_type=jnp.float32
        )
        out = (out * inverse).T
        for h in range(heads):
            at = (g * heads + h) * HEAD
            rows_ref[:, at : at + HEAD] = out[h * own : (h + 1) * own]

    values = rows_ref[...]
    scale = lax.rsqrt(jnp.mean(values * values, axis=-1, keepdims=True) + EPSILON)
    branch = (values * scale * gain_ref[...]).astype(BF16)
    part = values.shape[1] // fsdp
    width = part // size
    for d in range(size):
        for f in range(fsdp):
            at = f * part + d * width
            attn_send[d, :, f * width : (f + 1) * width] = branch[:, at : at + width]
    for copy in exchange(copies, attn_send, branch_ref, me, size):
        copy.wait_recv()
    copies.finish()


def attention_forward(projected, gain, kv_width, collective_id):
    ctx, fsdp, bits = lax.axis_size("ctx"), lax.axis_size("fsdp"), ctx_bits()
    length, model = projected.shape[0], gain.shape[0]
    own, q_mine, kv_mine = length // ctx, model // ctx, kv_width // ctx
    heads = model // kv_width
    sems = pltpu.SemaphoreType.DMA((2 * (ctx - 1) + gather_sems(bits),))
    shape = jax.ShapeDtypeStruct
    return pl.pallas_call(
        functools.partial(attention_kernel, ctx, fsdp),
        out_shape=[
            shape((ctx, own, q_mine), BF16),
            shape((own, model), jnp.float32),
            shape((KV_HEADS, length, heads * own), BF16),
            shape((KV_HEADS, 1, heads * own), jnp.float32),
            shape((KV_HEADS, heads * own, HEAD), BF16),
            shape((KV_HEADS, length, HEAD), BF16),
            shape((KV_HEADS, length, HEAD), BF16),
        ],
        in_specs=[IN_VMEM] * 2,
        out_specs=[IN_VMEM] * 7,
        scratch_shapes=[
            pltpu.VMEM((ctx, own, q_mine), BF16),
            pltpu.VMEM((ctx, own, q_mine), BF16),
            pltpu.VMEM((ctx, length, 2 * kv_mine), BF16),
            pltpu.VMEM((length, heads * own), jnp.float32),
            pltpu.VMEM((ctx, own, q_mine), BF16),
            sems, sems,
        ],
        compiler_params=params(collective_id),
        name="attention_forward",
    )(projected, gain[None])


def attention_back_kernel(
    size, fsdp, attn_w, mix_w, rows_ref, gain_ref, ssm_gain_ref, gated_ref,
    parts_ref, branch_ref, ssm_ref, top_ref,
    prob_ref, inverse_ref, q_ref, k_ref, v_ref,
    early_ref, gain_grad_ref, ffn_ref, dw_ref, norm_grad_ref, dot_ref,
    grad_ref, dot_part, dot_inbox, recv_ref, heads_ref, dp_ref, dq_ref, dkv_ref, dq_send, dq_recv, kv_part, kv_sum, *rest,
):
    bits = size.bit_length() - 1
    me = lax.axis_index("ctx")
    own, model = rows_ref.shape
    q_mine = model // size
    groups, keys, queries = prob_ref.shape
    heads = queries // own
    kv_mine = groups * HEAD // size
    chunk = 128
    scale_qk = HEAD**-0.5
    boxes = (len(rest) - 2) // 2
    inbox, ffn_inbox = rest[:boxes], rest[boxes : 2 * boxes]
    greet_all(me, size)
    copies = Copies("ctx", *rest[-2:])
    for s in range(size):
        grad_ref[s] = product(top_ref[s * own : (s + 1) * own], attn_w[...], True).astype(BF16)
    come = exchange(copies, grad_ref, recv_ref, me, size)
    norm_grad_ref[...] = product(top_ref[...], mix_w[...], True)
    scaled = norm_grad_ref[...] * ssm_gain_ref[...] * gated_ref[...]
    dot_part[...] = lax.dot_general(
        jnp.ones((dot_ref.shape[0], scaled.shape[1]), jnp.float32), scaled,
        (((1,), (1,)), ((), ())),
        precision=lax.Precision.HIGHEST, preferred_element_type=jnp.float32,
    )
    dots = [
        copies.send(dot_part, dot_inbox.at[turn - 1], (me + turn) % size)
        for turn in range(1, size)
    ]
    ffn_sum = Reducer(copies, bits, None, ffn_inbox, ffn_ref)
    ffn_sum.send_parts(parts_ref)

    def add_parts():
        for flips in ffn_sum.everyone:
            ffn_sum.own(flips, parts_ref[flipped(me, flips)].astype(jnp.float32))

    beside = [add_parts] + ffn_sum.turns()
    values = rows_ref[...]
    scale = lax.rsqrt(jnp.mean(values * values, axis=-1, keepdims=True) + EPSILON)
    at = 0
    for ref in (ssm_ref, branch_ref):
        wide = ref.shape[1] // fsdp
        weights = lax.dot_general(
            ref[...], top_ref[...], (((0,), (0,)), ((), ())), preferred_element_type=jnp.float32
        ).astype(BF16)
        for f in range(fsdp):
            dw_ref[f, at : at + wide] = weights[f * wide : (f + 1) * wide]
        at += wide
    dw_ref[:, at:] = jnp.zeros((fsdp, dw_ref.shape[1] - at, model), BF16)
    for copy in come:
        copy.wait_recv()
    part = model // fsdp
    width = part // size
    for s in range(size):
        for f in range(fsdp):
            at = f * part + s * width
            dq_ref[:, at : at + width] = recv_ref[s, :, f * width : (f + 1) * width].astype(
                jnp.float32
            )
    grad = dq_ref[...]
    gain_grad_ref[...] = jnp.sum(grad * values * scale, axis=0, keepdims=True)
    scaled = grad * gain_ref[...]
    grad = scale * scaled - values * (scale * scale * scale) * jnp.mean(
        scaled * values, axis=-1, keepdims=True
    )
    grad = grad.astype(BF16)
    for h in range(groups * heads):
        at = (h % heads) * own
        heads_ref[h // heads, at : at + own] = grad[:, h * HEAD : (h + 1) * HEAD]

    for g in range(groups):
        q_g, do_g, inverse = q_ref[g], heads_ref[g], inverse_ref[g]
        q_t = q_g.astype(jnp.float32).T.astype(BF16)
        do_t = do_g.astype(jnp.float32).T.astype(BF16)

        def first(i, row_dot):
            at = pl.ds(pl.multiple_of(i * chunk, chunk), chunk)
            prob = prob_ref[g, at].astype(jnp.float32) * inverse
            grad_prob = product(v_ref[g, at], do_g, True)
            dp_ref[at] = grad_prob
            dkv_ref[groups + g, :, at] = product(do_t, prob.astype(BF16), True)
            return row_dot + jnp.sum(prob * grad_prob, axis=0, keepdims=True)

        row_dot = lax.fori_loop(
            0, keys // chunk, first, jnp.zeros((1, queries), jnp.float32)
        )

        def second(i, dq_t):
            at = pl.ds(pl.multiple_of(i * chunk, chunk), chunk)
            prob = prob_ref[g, at].astype(jnp.float32) * inverse
            grad_score = (prob * (dp_ref[at] - row_dot)).astype(BF16)
            dkv_ref[g, :, at] = scale_qk * product(q_t, grad_score, True)
            return dq_t + lax.dot_general(
                k_ref[g, at], grad_score, (((0,), (0,)), ((), ())),
                preferred_element_type=jnp.float32,
            )

        dq_t = lax.fori_loop(
            0, keys // chunk, second, jnp.zeros((HEAD, queries), jnp.float32)
        )
        dq_g = (scale_qk * dq_t).T
        for h in range(heads):
            at = (g * heads + h) * HEAD
            dq_ref[:, at : at + HEAD] = dq_g[h * own : (h + 1) * own]
        if beside:
            beside.pop(0)()

    for step in beside:
        step()
    for copy in dots:
        copy.wait_recv()
    total = dot_part[...]
    for turn in range(1, size):
        total = total + dot_inbox[turn - 1]
    dot_ref[...] = total
    for d in range(size):
        dq_send[d] = dq_ref[:, d * q_mine : (d + 1) * q_mine].astype(BF16)
    come = exchange(copies, dq_send, dq_recv, me, size)
    flat = dkv_ref.reshape(2 * groups * HEAD, keys)
    for d in range(size):
        kv_part[d, :kv_mine] = flat[d * kv_mine : (d + 1) * kv_mine].astype(BF16)
        at = groups * HEAD + d * kv_mine
        kv_part[d, kv_mine:] = flat[at : at + kv_mine].astype(BF16)
    reducer = Reducer(copies, bits, None, inbox, kv_sum)
    reducer.send_parts(kv_part)
    for flips in reducer.everyone:
        reducer.own(flips, kv_part[flipped(me, flips)].astype(jnp.float32))
    for copy in come:
        copy.wait_recv()
    for s in range(size):
        early_ref[s * own : (s + 1) * own, :q_mine] = dq_recv[s]
    reducer.finish()
    early_ref[:, q_mine:] = kv_sum[...].T.astype(BF16)
    copies.finish()


def attention_backward(weights, rows, gains, gated, parts, branches, top, kept, collective_id):
    ctx, fsdp, bits = lax.axis_size("ctx"), lax.axis_size("fsdp"), ctx_bits()
    prob = kept[0]
    own, model = rows.shape
    length = own * ctx
    q_mine, kv_mine = model // ctx, KV_HEADS * HEAD // ctx
    boxes, count = reducer_boxes(ctx, bits, 2 * kv_mine, length)
    ffn_boxes, ffn_count = reducer_boxes(ctx, bits, own, model)
    dw_rows = sum(branch.shape[1] for branch in branches) // fsdp
    sems = pltpu.SemaphoreType.DMA((3 * (ctx - 1) + count + ffn_count,))
    shape = jax.ShapeDtypeStruct
    return pl.pallas_call(
        functools.partial(attention_back_kernel, ctx, fsdp),
        out_shape=[
            shape((length, q_mine + 2 * kv_mine), BF16),
            shape((1, model), jnp.float32),
            shape((own, model), jnp.float32),
            shape((fsdp, dw_rows + -dw_rows % 16, model), BF16),
            shape(gated.shape, jnp.float32),
            shape((8, length), jnp.float32),
        ],
        in_specs=[IN_VMEM] * (10 + len(kept)),
        out_specs=[IN_VMEM] * 6,
        scratch_shapes=[
            pltpu.VMEM((ctx, own, q_mine), BF16),
            pltpu.VMEM((8, length), jnp.float32),
            pltpu.VMEM((ctx - 1, 8, length), jnp.float32),
            pltpu.VMEM((ctx, own, q_mine), BF16),
            pltpu.VMEM(kept[2].shape, BF16),
            pltpu.VMEM((length, prob.shape[2]), jnp.float32),
            pltpu.VMEM((own, model), jnp.float32),
            pltpu.VMEM((2 * KV_HEADS, HEAD, length), jnp.float32),
            pltpu.VMEM((ctx, own, q_mine), BF16),
            pltpu.VMEM((ctx, own, q_mine), BF16),
            pltpu.VMEM((ctx, 2 * kv_mine, length), BF16),
            pltpu.VMEM((2 * kv_mine, length), jnp.float32),
        ]
        + boxes[1:]
        + ffn_boxes[1:]
        + [sems, sems],
        compiler_params=params(collective_id),
        name="attention_backward",
    )(*weights, rows, *[gain.reshape(1, -1) for gain in gains], gated, parts, *branches, top, *kept)


def greet_planes(me, size, row, rows):
    barrier = pltpu.get_barrier_semaphore()
    for turn in range(1, size):
        pl.semaphore_signal(
            barrier, inc=1, device_id={"ctx": (me + turn) % size}, device_id_type=MESH
        )
    for turn in range(1, rows):
        pl.semaphore_signal(
            barrier, inc=1, device_id={"fsdp": (row + turn) % rows}, device_id_type=MESH
        )
    pl.semaphore_wait(barrier, size - 1 + rows - 1)


class SomeExchange:
    def __init__(self, copies, send_ref, recv_ref, me, size, chosen):
        self.send_ref, self.recv_ref, self.me, self.mine = send_ref, recv_ref, me, chosen(me)
        self.plans = []
        for turn in range(1, size):
            to = (me + turn) % size
            self.plans.append((chosen(to), copies.make(send_ref.at[to], recv_ref.at[me], to)))

    def start(self):
        for chosen, copy in self.plans:
            pl.when(chosen)(copy.start)

        @pl.when(self.mine)
        def _():
            self.recv_ref[self.me] = self.send_ref[self.me]

    def wait(self):
        for _, copy in self.plans:
            pl.when(self.mine)(copy.wait_recv)

    def finish(self):
        for chosen, copy in self.plans:
            pl.when(chosen)(copy.wait_send)


def back_kernel(
    size, fsdp, first_ref, second_ref, weight_ref, early_ref, stack_ref, head_ref, state_ref,
    sum_ref, query_out, key_out, value_out, gate_recv, attn_out, mix_out, head_sum, state_sum,
    first_w, second_w, head_inbox, state_inbox, c_send, r_send, r_recv,
    ctx_send, ctx_recv, line_send, line_recv, part_ref, *inbox,
):
    bits = size.bit_length() - 1
    me, row = lax.axis_index("ctx"), lax.axis_index("fsdp")
    greet_planes(me, size, row, fsdp)
    q_mine, kv_mine = query_out.shape[1], key_out.shape[1]
    late = q_mine + 2 * kv_mine
    rows, width = c_send.shape[1], c_send.shape[2]
    high, block = mix_out.shape[0] // size, mix_out.shape[1]
    across, line = Copies("ctx", ctx_send, ctx_recv), Copies("fsdp", line_send, line_recv)
    small = ((head_ref, head_inbox, head_sum), (state_ref, state_inbox, state_sum))

    def band_of(ref, index):
        band = ref.shape[0] // fsdp
        return pl.ds(pl.multiple_of(index * band, band), band)

    bands = []
    for turn in range(1, fsdp):
        to = (row + turn) % fsdp
        for ref, box, _ in small:
            bands.append(line.send(ref.at[band_of(ref, to)], box.at[turn - 1], to))
    for d in range(size):
        r_send[d] = stack_ref[:, d * block : (d + 1) * block]
        if d >= fsdp:
            at = late + (d - fsdp) * width
            c_send[d] = early_ref[:, at : at + width]
    gates = SomeExchange(across, c_send, gate_recv, me, size, lambda d: d >= fsdp)
    gates.start()
    moved = exchange(across, r_send, r_recv, me, size)
    cut = first_w.shape[1]
    first_w[...] = weight_ref[:, :cut]
    second_w[...] = weight_ref[:, cut:]
    reducer = Reducer(across, bits, part_ref, inbox, sum_ref)

    def partial(flips):
        shard = flipped(me, flips)
        return product(first_ref[shard], first_w[...], True) + product(
            second_ref[shard], second_w[...], True
        )

    for flips in reducer.everyone:
        reducer.to_sibling(flips, partial(flips + (0,)))
    for flips in reducer.everyone:
        reducer.own(flips, partial(flips))
    for copy in bands:
        copy.wait_recv()
    bands = []
    for ref, box, sum_of in small:
        total = ref[band_of(ref, row)].astype(jnp.float32)
        for turn in range(1, fsdp):
            total = total + box[turn - 1].astype(jnp.float32)
        sum_of[band_of(ref, row)] = total.astype(sum_of.dtype)
        at = sum_of.at[band_of(ref, row)]
        bands += [line.send(at, at, (row + turn) % fsdp) for turn in range(1, fsdp)]
    turns = reducer.turns()
    for turn in turns[:2]:
        turn()

    @pl.when(me < fsdp)
    def _():
        gate_recv[...] = jnp.zeros(gate_recv.shape, BF16)

    query_out[...] = early_ref[:, :q_mine].astype(jnp.float32)
    key_out[...] = early_ref[:, q_mine : q_mine + kv_mine].astype(jnp.float32)
    value_out[...] = early_ref[:, q_mine + kv_mine : late].astype(jnp.float32)
    for turn in turns[2:]:
        turn()
    for copy in moved:
        copy.wait_recv()
    count = attn_out.shape[0] // size
    for s in range(size):
        mix_out[s * high : (s + 1) * high] = r_recv[s, :high].astype(jnp.float32)
        attn_out[s * count : (s + 1) * count] = r_recv[s, high : high + count].astype(jnp.float32)
    gates.wait()
    gates.finish()
    for copy in bands:
        copy.wait_recv()
    across.finish()
    line.finish()


def reduce_and_place(first, second, weight, early, stack, head, state, sizes, collective_id):
    ctx, fsdp, bits = lax.axis_size("ctx"), lax.axis_size("fsdp"), ctx_bits()
    q_mine, kv_mine, mix_rows, attn_rows = sizes
    own, columns = first.shape[0] // ctx, weight.shape[0]
    rows, mine = early.shape[0], second.shape[1]
    width, block = mine // fsdp, stack.shape[1] // ctx
    boxes, count = reducer_boxes(ctx, bits, own, columns)
    ctx_sems = pltpu.SemaphoreType.DMA((count + 2 * (ctx - 1),))
    line_sems = pltpu.SemaphoreType.DMA((4 * (fsdp - 1),))

    def shape(*sizes):
        return jax.ShapeDtypeStruct(sizes, jnp.float32)

    return pl.pallas_call(
        functools.partial(back_kernel, ctx, fsdp),
        out_shape=[
            shape(own, columns), shape(rows, q_mine), shape(rows, kv_mine), shape(rows, kv_mine),
            jax.ShapeDtypeStruct((ctx, rows, width), BF16),
            shape(ctx * attn_rows, block), shape(ctx * mix_rows, block),
            shape(*head.shape),
            jax.ShapeDtypeStruct(state.shape, BF16),
        ],
        in_specs=[IN_VMEM] * 7,
        out_specs=[IN_VMEM] * 9,
        scratch_shapes=[
            pltpu.VMEM((columns, first.shape[1]), BF16),
            pltpu.VMEM((columns, second.shape[1]), BF16),
            pltpu.VMEM((fsdp - 1, head.shape[0] // fsdp, mine), jnp.float32),
            pltpu.VMEM((fsdp - 1, state.shape[0] // fsdp, mine), BF16),
            pltpu.VMEM((ctx, rows, width), BF16),
            pltpu.VMEM((ctx, stack.shape[0], block), BF16),
            pltpu.VMEM((ctx, stack.shape[0], block), BF16),
            ctx_sems, ctx_sems, line_sems, line_sems,
        ]
        + boxes,
        compiler_params=params(collective_id),
        name="reduce_and_place",
    )(
        first.reshape(ctx, own, -1), second.reshape(ctx, own, -1), weight, early, stack, head, state
    )


def finish_kernel(
    size, fsdp, src_ref, gate_ref, head_ref, state_ref, gain_ref,
    mixer_out, step_out, head_out, state_out, sums_ref,
    head_all, state_all, gain_inbox, line_inbox, c_send, c_recv, s_send, s_recv, ctx_send, ctx_recv, line_send, line_recv,
):
    me, row = lax.axis_index("ctx"), lax.axis_index("fsdp")
    greet_planes(me, size, row, fsdp)
    rows, width, low = c_send.shape[1], c_send.shape[2], step_out.shape[0]
    repeat = size // fsdp
    across, line = Copies("ctx", ctx_send, ctx_recv), Copies("fsdp", line_send, line_recv)
    head_all[me] = head_ref[...]
    state_all[me] = state_ref[...]
    lists = [gather_steps(across, size.bit_length() - 1, ref) for ref in (state_all, head_all)]
    steps = [step for pair in zip(*lists) for step in pair]
    steps[0]()
    steps[1]()
    gains = [
        across.send(gain_ref, gain_inbox.at[turn - 1], (me + turn) % size)
        for turn in range(1, size)
    ]
    for d in range(size):
        if d < fsdp:
            c_send[d] = src_ref[:rows, d * width : (d + 1) * width]
        at = d // repeat * width
        s_send[d] = src_ref[rows:, at : at + width]
    parts = SomeExchange(across, c_send, c_recv, me, size, lambda d: d < fsdp)
    parts.start()
    moved = exchange(across, s_send, s_recv, me, size)
    for step in steps[2:6]:
        step()
    total = gain_ref[...]
    for turn in range(1, size):
        gains[turn - 1].wait_recv()
        total = total + gain_inbox[turn - 1]
    line_inbox[0] = total
    gains = [
        line.send(line_inbox.at[0], line_inbox.at[turn], (row + turn) % fsdp)
        for turn in range(1, fsdp)
    ]

    @pl.when(me >= fsdp)
    def _():
        for s in range(size):
            mixer_out[:, s * width : (s + 1) * width] = gate_ref[s].astype(jnp.float32)

    for step in steps[6:-2]:
        step()
    parts.wait()

    @pl.when(me < fsdp)
    def _():
        for s in range(size):
            mixer_out[:, s * width : (s + 1) * width] = c_recv[s].astype(jnp.float32)

    steps[-2]()
    steps[-1]()
    part = head_out.shape[1] // fsdp
    for out, ref in ((state_out, state_all), (head_out, head_all)):
        for s in range(size):
            for f in range(fsdp):
                at = f * part + s * width
                out[:, at : at + width] = ref[s, :, f * width : (f + 1) * width].astype(out.dtype)

    for copy in moved:
        copy.wait_recv()
    for j in range(fsdp):
        source = fsdp * (me % repeat) + j
        step_out[:, j * width : (j + 1) * width] = s_recv[source, :low].astype(jnp.float32)
    total = line_inbox[0]
    for turn in range(1, fsdp):
        gains[turn - 1].wait_recv()
        total = total + line_inbox[turn]
    sums_ref[...] = total
    parts.finish()
    across.finish()
    line.finish()


def finish(src, gates, head, state, gains, step_rows, collective_id):
    ctx, fsdp = lax.axis_size("ctx"), lax.axis_size("fsdp")
    rows, width = gates.shape[1:]
    ctx_sems = pltpu.SemaphoreType.DMA((3 * (ctx - 1) + 2 * gather_sems(ctx_bits()),))
    line_sems = pltpu.SemaphoreType.DMA((fsdp - 1,))

    def shape(*sizes):
        return jax.ShapeDtypeStruct(sizes, jnp.float32)

    return pl.pallas_call(
        functools.partial(finish_kernel, ctx, fsdp),
        out_shape=[
            shape(rows, ctx * width), shape(step_rows, fsdp * width),
            shape(head.shape[0], ctx * head.shape[1]), shape(state.shape[0], ctx * head.shape[1]),
            shape(*gains.shape),
        ],
        in_specs=[IN_VMEM] * 5,
        out_specs=[IN_VMEM] * 5,
        scratch_shapes=[
            pltpu.VMEM((ctx,) + head.shape, jnp.float32),
            pltpu.VMEM((ctx,) + state.shape, BF16),
            pltpu.VMEM((ctx - 1,) + gains.shape, jnp.float32),
            pltpu.VMEM((fsdp,) + gains.shape, jnp.float32),
            pltpu.VMEM((ctx, rows, width), BF16),
            pltpu.VMEM((ctx, rows, width), BF16),
            pltpu.VMEM((ctx, src.shape[0] - rows, width), BF16),
            pltpu.VMEM((ctx, src.shape[0] - rows, width), BF16),
            ctx_sems, ctx_sems, line_sems, line_sems,
        ],
        compiler_params=params(collective_id),
        name="finish",
    )(src, gates, head, state, gains)


def window(start, size, total, step):
    return pl.multiple_of(jnp.minimum(start // step * step, total - size), step)


def shifted(values, offset, axis):
    size = values.shape[axis]
    return pltpu.roll(values.astype(jnp.float32), lax.rem(size - offset, size), axis)


def pack_in_begin(weights, scratch):
    mixer_ref, (inbox, sems) = weights[3], scratch
    me, size = lax.axis_index("ctx"), lax.axis_size("ctx")
    units, _, span = inbox.shape
    total = mixer_ref.shape[1]
    width = total // units // size
    copies = []
    for u in range(units):
        at = window(u * (total // units) + me * width, span, total, 128)
        copy = pltpu.make_async_copy(mixer_ref.at[:, pl.ds(at, span)], inbox.at[u], sems.at[u])
        copy.start()
        copies.append(copy)
    return copies


def pack_in(row, copies, weights, scratch, in_out, state_out, step_out):
    query_ref, key_ref, value_ref, mixer_ref, state_ref, step_ref = weights
    inbox = scratch[0]
    me, size = lax.axis_index("ctx"), lax.axis_size("ctx")
    units, _, span = inbox.shape
    total = mixer_ref.shape[1]
    width = total // units // size
    at = 0
    for ref in (query_ref, key_ref, value_ref):
        wide = ref.shape[1] // size
        in_out[row, :, at : at + wide] = shifted(ref[...], me * wide, 1)[:, :wide].astype(BF16)
        at += wide
    high = state_ref.shape[1] // size
    turned = shifted(state_ref[...], me * high, 1)[:, :128].T
    state_out[row] = turned[: state_out.shape[1]].astype(BF16)
    part = step_ref.shape[1] * 2 // units
    step_out[row] = jnp.zeros(step_out.shape[1:], BF16)
    for f in range(units // 2):
        band = shifted(step_ref[:, f * part : (f + 1) * part], me * width, 1)[:, :width]
        step_out[row, : step_ref.shape[0], f * width : (f + 1) * width] = band.astype(BF16)
    for u in range(units):
        copies[u].wait()
        start = u * (total // units) + me * width
        piece = shifted(inbox[u], start - window(start, span, total, 128), 1)[:, :width]
        to = at + (u + units // 2) % units * width
        in_out[row, :, to : to + width] = piece.astype(BF16)


def pack_in_plan(first):
    shape = jax.ShapeDtypeStruct
    if len(first) == 3:
        return {"shapes": [shape(a.shape, a.dtype) for a in first], "scratch": [], "any": ()}
    query, key, value, mixer, state, step = first
    ctx, fsdp = lax.axis_size("ctx"), lax.axis_size("fsdp")
    rows = mixer.shape[0]
    mine = mixer.shape[1] // 2 // ctx
    qkv = (query.shape[1] + key.shape[1] + value.shape[1]) // ctx
    state_rows = state.shape[1] // ctx
    return {
        "shapes": [
            shape((rows, qkv + 2 * mine), BF16),
            shape((state_rows + -state_rows % 16, state.shape[0]), BF16),
            shape((step.shape[0] + -step.shape[0] % 16, mine), BF16),
        ],
        "scratch": [
            pltpu.VMEM((2 * fsdp, rows, 256), BF16), pltpu.SemaphoreType.DMA((2 * fsdp,))
        ],
        "any": (3,),
    }


def pack_out_plan(later, hidden_units):
    if not later:
        return {"inputs": 0, "outputs": 0, "shapes": [], "scratch": [], "steps": None}
    ctx, fsdp = lax.axis_size("ctx"), lax.axis_size("fsdp")
    gate, _, down, mix, attn = later
    rows, model, total = gate.shape[0], down.shape[0], gate.shape[1]
    hid_part = total // ctx // fsdp
    pad = -hid_part % 16
    units = hidden_units // fsdp
    width = hid_part // units
    high = (hid_part + pad) + (mix.shape[0] + attn.shape[0]) // ctx
    span = 256

    def box_rows(array):
        need = array.shape[0] // ctx
        return need + 15 + -(need + 15) % 16

    def steps(me, weights, outs, scratch):
        gate_ref, up_ref, down_ref, mix_ref, attn_ref = weights
        pair_out, rows_out = outs
        inbox, down_box, tail_box, mix_box, attn_box, sems = scratch
        copies = []

        def start_copy(source, target):
            copy = pltpu.make_async_copy(source, target, sems.at[len(copies)])
            copy.start()
            copies.append(copy)

        plans = []
        half = pair_out.shape[1] // 2
        for index, ref in enumerate((gate_ref, up_ref)):
            for u in range(hidden_units):
                start = u * (total // hidden_units) + me * width
                at = window(start, span, total, 128)
                start_copy(ref.at[:, pl.ds(at, span)], inbox.at[index, u])
                to = index * half + u * width + u // units * pad
                plans.append(("columns", inbox, (index, u), start - at, to, width))
        to = 0
        down_at = to
        to += units * width + pad
        for ref, box in ((mix_ref, mix_box), (attn_ref, attn_box)):
            tall = ref.shape[0] // size
            at = window(me * tall, box.shape[1], ref.shape[0], 16)
            start_copy(ref.at[pl.ds(at, box.shape[1])], box.at[0])
            plans.append(("rows", box, (0,), me * tall - at, to, tall))
            to += tall
        start_copy(down_ref, down_box)
        full = down.shape[1] // 128
        tail = down.shape[1] % 128

        def tile_of(index):
            at = pl.multiple_of(jnp.minimum(index, full - 1) * 128, 128)
            whole = down_box[:, pl.ds(at, 128)].astype(jnp.float32)
            return jnp.where(index >= full, tail_box[...], whole) if tail else whole

        def begin_down():
            copies[-1].wait()
            if tail:
                tail_box[...] = jnp.zeros(tail_box.shape, jnp.float32)
                tail_box[:, :tail] = down_box[:, full * 128 :].astype(jnp.float32)

        def place_down(u):
            start = u * (down.shape[1] // units) + me * width
            first = start // 128
            pair = jnp.concatenate([tile_of(first), tile_of(first + 1)], 1)
            turned = shifted(pair, start - first * 128, 1)[:, :128].T
            at = down_at + u * width
            rows_out[at : at + width] = turned[:width].astype(BF16)

        def clear():
            pair_out[...] = jnp.zeros(pair_out.shape, BF16)
            rows_out[...] = jnp.zeros(rows_out.shape, BF16)

        def place(copy, kind, box, index, offset, to, extent):
            copy.wait()
            values = box[index]
            if kind == "columns":
                pair_out[:, to : to + extent] = shifted(values, offset, 1)[:, :extent].astype(BF16)
            else:
                rows_out[to : to + extent] = shifted(values, offset, 0)[:extent].astype(BF16)

        placed = [functools.partial(place, copy, *plan) for copy, plan in zip(copies, plans)]
        downs = [functools.partial(place_down, u) for u in range(units)]
        return [clear] + placed + [begin_down] + downs

    size = ctx
    shape = jax.ShapeDtypeStruct
    return {
        "inputs": 5,
        "outputs": 2,
        "shapes": [
            shape((rows, 2 * fsdp * (hid_part + pad)), BF16),
            shape((high + -high % 16, model), BF16),
        ],
        "scratch": [
            pltpu.VMEM((2, hidden_units, rows, span), BF16),
            pltpu.VMEM(down.shape, BF16),
            pltpu.VMEM((model, 128), jnp.float32),
            pltpu.VMEM((1, box_rows(mix), model), BF16),
            pltpu.VMEM((1, box_rows(attn), model), BF16),
            pltpu.SemaphoreType.DMA((2 * hidden_units + 3,)),
        ],
        "steps": steps,
    }


def scan_fwd_kernel(steps_ref, drive_ref, in_ref, out_ref, rate_ref, scan_ref, prev_ref, state_ref):
    tiles = steps_ref.shape[1] // LANES
    chunk = steps_ref.shape[0]

    @pl.when(pl.program_id(0) == 0)
    def _():
        state_ref[...] = jnp.zeros_like(state_ref)

    rates = [rate_ref[:, j * LANES : (j + 1) * LANES] for j in range(tiles)]

    def group(g, states):
        states = list(states)
        base = pl.multiple_of(g * 8, 8)
        for j in range(tiles):
            lanes = slice(j * LANES, (j + 1) * LANES)
            step_8 = steps_ref[pl.ds(base, 8), lanes]
            drive_8 = step_8 * drive_ref[pl.ds(base, 8), lanes]
            rows = []
            for t in range(8):
                in_t = in_ref[base + t].astype(jnp.float32)
                out_t = out_ref[base + t].astype(jnp.float32)
                decay = jnp.exp2(step_8[t : t + 1] * rates[j])
                prev_ref[base + t, :, lanes] = states[j]
                states[j] = decay * states[j] + drive_8[t : t + 1] * in_t
                rows.append(jnp.sum(states[j] * out_t, axis=0, keepdims=True))
            scan_ref[pl.ds(base, 8), lanes] = jnp.concatenate(rows, 0)
        return tuple(states)

    start = tuple(state_ref[:, j * LANES : (j + 1) * LANES] for j in range(tiles))
    final = lax.fori_loop(0, chunk // 8, group, start)
    for j in range(tiles):
        state_ref[:, j * LANES : (j + 1) * LANES] = final[j]


def scan_fwd(steps, drive, in_b, out_b, rates):
    length, width = steps.shape
    chunk = CHUNK
    row = pl.BlockSpec((chunk, width), lambda i: (i, 0))
    mat = pl.BlockSpec((chunk, STATE, LANES), lambda i: (i, 0, 0))
    rate = pl.BlockSpec((STATE, width), lambda i: (0, 0))
    return pl.pallas_call(
        scan_fwd_kernel,
        grid=(length // chunk,),
        in_specs=[row, row, mat, mat, rate],
        out_specs=[row, pl.BlockSpec((chunk, STATE, width), lambda i: (i, 0, 0))],
        out_shape=[
            jax.ShapeDtypeStruct((length, width), jnp.float32),
            jax.ShapeDtypeStruct((length, STATE, width), jnp.float32),
        ],
        scratch_shapes=[pltpu.VMEM((STATE, width), jnp.float32)],
        compiler_params=pltpu.CompilerParams(vmem_limit_bytes=48 * 1024 * 1024),
        name="scan_forward",
    )(steps, drive, in_b, out_b, rates)


def scan_bwd_kernel(
    units, steps_ref, drive_ref, grad_ref, in_ref, out_ref, rate_ref, prev_ref, *refs
):
    exchanged, refs = refs[: 1 if units else 0], refs[1 if units else 0 :]
    gstep_ref, gdrive_ref, gin_ref, gout_ref, grate_ref = refs[:5]
    received, refs = refs[5 : 8 if units else 5], refs[8 if units else 5 :]
    carry_ref, pin_ref, pout_ref = refs[:3]
    slots = refs[3:]
    tiles = steps_ref.shape[1] // LANES
    chunk = steps_ref.shape[0]
    if units:
        pl.when(pl.program_id(0) == 0)(functools.partial(relay_begin, units, *exchanged, *slots))

    @pl.when(pl.program_id(0) == 0)
    def _():
        carry_ref[...] = jnp.zeros_like(carry_ref)
        grate_ref[...] = jnp.zeros_like(grate_ref)

    for j in range(tiles):
        lanes = slice(j * LANES, (j + 1) * LANES)
        rates = rate_ref[:, lanes]

        def group(k, kept):
            carry, acc = kept
            base = pl.multiple_of(chunk - 8 - k * 8, 8)
            step_8 = steps_ref[pl.ds(base, 8), lanes]
            x_8 = drive_ref[pl.ds(base, 8), lanes]
            drive_8 = step_8 * x_8
            grad_8 = grad_ref[pl.ds(base, 8), lanes]
            held_rows, dot_rows = [None] * 8, [None] * 8
            for t in range(7, -1, -1):
                in_t = in_ref[base + t].astype(jnp.float32)
                out_t = out_ref[base + t].astype(jnp.float32)
                previous = prev_ref[base + t, :, lanes]
                step_t = step_8[t : t + 1]
                drive_t = drive_8[t : t + 1]
                grad_t = grad_8[t : t + 1]
                decay = jnp.exp2(step_t * rates)
                adjoint = grad_t * out_t + carry
                carry = decay * adjoint
                held = carry * previous
                state = decay * previous + drive_t * in_t
                acc = acc + held * step_t
                held_rows[t] = jnp.sum(held * rates, axis=0, keepdims=True)
                dot_rows[t] = jnp.sum(adjoint * in_t, axis=0, keepdims=True)
                part_in = adjoint * drive_t
                part_out = state * grad_t
                at = pl.ds(pl.multiple_of((base + t) * STATE, STATE), STATE)
                if j == 0:
                    pin_ref[at] = part_in
                    pout_ref[at] = part_out
                else:
                    pin_ref[at] += part_in
                    pout_ref[at] += part_out
            held_8 = jnp.concatenate(held_rows, 0)
            dot_8 = jnp.concatenate(dot_rows, 0)
            gstep_ref[pl.ds(base, 8), lanes] = held_8 * 0.6931471805599453 + x_8 * dot_8
            gdrive_ref[pl.ds(base, 8), lanes] = step_8 * dot_8
            return carry, acc

        carry, acc = lax.fori_loop(
            0, chunk // 8, group, (carry_ref[:, lanes], grate_ref[:, lanes])
        )
        carry_ref[:, lanes] = carry
        grate_ref[:, lanes] = acc
    ones = jnp.ones((8, LANES), jnp.float32)
    dims = (((1,), (1,)), ((), ()))
    gin_ref[0] = lax.dot_general(ones, pin_ref[...], dims, preferred_element_type=jnp.float32)
    gout_ref[0] = lax.dot_general(ones, pout_ref[...], dims, preferred_element_type=jnp.float32)
    if units:
        last = pl.num_programs(0) - 1
        pl.when(pl.program_id(0) == last)(functools.partial(relay_end, units, *received, *slots))


def scan_bwd(steps, drive, grad, in_b, out_b, rates, previous, relay=None, units=0, hidden=0, part=0, model=0, collective_id=None):
    length, width = steps.shape
    chunk = CHUNK
    count = length // chunk
    row = pl.BlockSpec((chunk, width), lambda i: (count - 1 - i, 0))
    mat = pl.BlockSpec((chunk, STATE, LANES), lambda i: (count - 1 - i, 0, 0))
    rate = pl.BlockSpec((STATE, width), lambda i: (0, 0))
    red = pl.BlockSpec((1, 8, chunk * STATE), lambda i: (count - 1 - i, 0, 0))
    shape = jax.ShapeDtypeStruct
    relay_out, slots = [], []
    extra = [] if relay is None else [relay]
    settings = dict(vmem_limit_bytes=56 * 1024 * 1024)
    if relay is not None:
        ctx, fsdp = lax.axis_size("ctx"), lax.axis_size("fsdp")
        wide, block, high = hidden // ctx, model // ctx, model // fsdp
        relay_out = [
            shape((high, ctx * wide), jnp.float32),
            shape((high, ctx * wide), jnp.float32),
            shape((units * ctx * wide, block), jnp.float32),
        ]
        slots = [
            pltpu.VMEM((ctx, high, 2 * wide), BF16),
            pltpu.VMEM((ctx, high, 2 * wide), BF16),
            pltpu.VMEM((ctx, part, block), BF16),
            pltpu.VMEM((ctx, part, block), BF16),
            pltpu.SemaphoreType.DMA((2 * (ctx - 1),)),
            pltpu.SemaphoreType.DMA((2 * (ctx - 1),)),
        ]
        settings.update(collective_id=collective_id, has_side_effects=True)
    gstep, gdrive, gin, gout, grate, *relayed = pl.pallas_call(
        functools.partial(scan_bwd_kernel, units),
        grid=(count,),
        in_specs=[row, row, row, mat, mat, rate,
                  pl.BlockSpec((chunk, STATE, width), lambda i: (count - 1 - i, 0, 0))]
        + [pl.BlockSpec(a.shape, lambda i: (0, 0)) for a in extra],
        out_specs=[row, row, red, red, rate]
        + [pl.BlockSpec(a.shape, lambda i: (0, 0)) for a in relay_out],
        out_shape=[
            shape((length, width), jnp.float32),
            shape((length, width), jnp.float32),
            shape((count, 8, chunk * STATE), jnp.float32),
            shape((count, 8, chunk * STATE), jnp.float32),
            shape((STATE, width), jnp.float32),
        ]
        + relay_out,
        scratch_shapes=[
            pltpu.VMEM((STATE, width), jnp.float32),
            pltpu.VMEM((chunk * STATE, LANES), jnp.float32),
            pltpu.VMEM((chunk * STATE, LANES), jnp.float32),
        ]
        + slots,
        compiler_params=pltpu.CompilerParams(**settings),
        name="scan_backward",
    )(steps, drive, grad, in_b, out_b, rates, previous, *extra)
    return (
        gstep, gdrive, gin[:, 0].reshape(length, STATE), gout[:, 0].reshape(length, STATE), grate,
        relayed,
    )


def matmul(left, right):
    return jnp.dot(left, right, preferred_element_type=jnp.float32)


def left_trans(left, right):
    return lax.dot_general(
        left, right, (((0,), (0,)), ((), ())), preferred_element_type=jnp.float32
    )


def right_trans(left, right):
    return lax.dot_general(
        left, right, (((1,), (1,)), ((), ())), preferred_element_type=jnp.float32
    )


def rms_scale(values):
    return lax.rsqrt(jnp.mean(values * values, axis=-1, keepdims=True) + EPSILON)


def norm_back(grad_out, values, scale_in, gain_in):
    scaled = grad_out * gain_in
    grad_in = scale_in * scaled - values * scale_in**3 * jnp.mean(
        scaled * values, axis=-1, keepdims=True
    )
    return (grad_in, jnp.sum(grad_out * values * scale_in, axis=0))


def silu_slope(values):
    logistic = jax.nn.sigmoid(values)
    return logistic * (1.0 + values * (1.0 - logistic))


def unit_count(width, ctx, fsdp):
    return ctx if width % (ctx * ctx) == 0 and ctx % fsdp == 0 else fsdp


def my_columns(array, units):
    span = array.shape[1] // units
    width = span // lax.axis_size("ctx")
    start = lax.axis_index("ctx") * width
    return [
        lax.dynamic_slice_in_dim(array, unit * span + start, width, 1) for unit in range(units)
    ]


def my_rows(array, units):
    span = array.shape[0] // units
    width = span // lax.axis_size("ctx")
    start = lax.axis_index("ctx") * width
    return [
        lax.dynamic_slice_in_dim(array, unit * span + start, width, 0) for unit in range(units)
    ]


def block_columns(array):
    width = array.shape[1] // lax.axis_size("ctx")
    return lax.dynamic_slice_in_dim(array, lax.axis_index("ctx") * width, width, 1)


def over_fsdp(array):
    return lax.all_gather(array, "fsdp", axis=0, tiled=True)


def to_slots(array, units):
    repeat = lax.axis_size("ctx") // units
    rows, width = array.shape[0], array.shape[1] // units
    pieces = array.reshape(rows, units, width).transpose(1, 0, 2)
    return jnp.repeat(pieces, repeat, axis=0) if repeat > 1 else pieces


def from_slots(got, units):
    repeat = lax.axis_size("ctx") // units
    if repeat > 1:
        first = units * lax.rem(lax.axis_index("ctx"), repeat)
        got = lax.dynamic_slice_in_dim(got, first, units, 0)
    rows, width = got.shape[1:]
    return got.transpose(1, 0, 2).reshape(rows, units * width).astype(jnp.float32)


def to_blocks(array, units):
    got = lax.all_to_all(to_slots(array, units), "ctx", 0, 0, tiled=True)
    return from_slots(got, units)


def rows_to_slots(array):
    ctx = lax.axis_size("ctx")
    rows, columns = array.shape
    return array.reshape(rows, ctx, columns // ctx).transpose(1, 0, 2)


def rows_from_slots(got, units):
    ctx, rows, columns = got.shape
    got = got.reshape(ctx, units, rows // units, columns).transpose(1, 0, 2, 3)
    return got.reshape(ctx * rows, columns).astype(jnp.float32)


def rows_to_blocks(array, units):
    got = lax.all_to_all(rows_to_slots(array), "ctx", 0, 0, tiled=True)
    return rows_from_slots(got, units)


def scatter_fsdp(*gradients):
    fsdp = lax.axis_size("fsdp")
    parts = [g.astype(BF16).reshape(fsdp, -1, g.shape[1]) for g in gradients]
    pad = -sum(part.shape[1] for part in parts) % 16
    if pad:
        parts.append(jnp.zeros((fsdp, pad, gradients[0].shape[1]), BF16))
    joined = jnp.concatenate(parts, 1) if len(parts) > 1 else parts[0]
    joined = joined.reshape(-1, joined.shape[2])
    return lax.psum_scatter(joined, "fsdp", scatter_dimension=0, tiled=True)


def body(
    inputs,
    cotangent,
    norm_gain,
    query_proj,
    key_proj,
    value_proj,
    attn_proj,
    attn_gain,
    mixer_in,
    conv_taps,
    conv_bias,
    state_proj,
    step_proj,
    step_bias,
    decay_rate,
    skip_gain,
    mixer_out,
    ssm_gain,
    ffn_gain,
    gate_proj,
    up_proj,
    down_proj,
):
    ctx, fsdp = lax.axis_size("ctx"), lax.axis_size("fsdp")
    place = lax.axis_index("ctx")
    tokens = inputs[0].astype(jnp.float32)
    own, model = tokens.shape
    length = own * ctx
    inner = conv_bias.shape[0]
    mine = inner // ctx
    kv_mine = key_proj.shape[1] // ctx
    q_mine = query_proj.shape[1] // ctx
    hidden_units = unit_count(gate_proj.shape[1], ctx, fsdp)
    hidden_rows = hidden_units // fsdp
    hid = gate_proj.shape[1] // ctx
    group_size = query_proj.shape[1] // key_proj.shape[1]
    score_scale = HEAD ** (-0.5)

    hid_part = hid // fsdp
    hid_pad = -hid_part % 16
    hid_all = hid + fsdp * hid_pad
    attn_pad = -attn_proj.shape[0] % ctx
    attn_rows_mine = (attn_proj.shape[0] + attn_pad) // ctx
    state_rows, step_rows = state_proj.shape[0] // ctx, step_proj.shape[0]
    if ctx == 8:
        first = (query_proj, key_proj, value_proj, mixer_in, state_proj.T, step_proj)
        later = (gate_proj, up_proj, down_proj.T, mixer_out, attn_proj)
        x_in, top_in = inputs[0].T, cotangent[0].T
    else:
        in_part = jnp.concatenate(
            [block_columns(array) for array in (query_proj, key_proj, value_proj)]
            + my_columns(mixer_in[:, inner:], fsdp)
            + my_columns(mixer_in[:, :inner], fsdp),
            1,
        )
        later = ()
        x_in, top_in = inputs[0], cotangent[0]
        state_part = jnp.pad(my_rows(state_proj, 1)[0], ((0, -state_rows % 16), (0, 0)))
        step_part = jnp.pad(
            jnp.concatenate(my_columns(step_proj, fsdp), 1), ((0, -step_rows % 16), (0, 0))
        )

        first = (in_part, state_part, step_part)

        def hidden_columns(array):
            pieces = my_columns(array, hidden_units)
            if hid_pad:
                for f in range(fsdp, 0, -1):
                    pieces.insert(f * hidden_rows, jnp.zeros((array.shape[0], hid_pad), BF16))
            return pieces

        ffn_part = jnp.concatenate(hidden_columns(gate_proj) + hidden_columns(up_proj), 1)
        rows_part = jnp.concatenate(
            my_rows(down_proj, hidden_rows)
            + [jnp.zeros((hid_pad, model), BF16)]
            + my_rows(mixer_out, 1)
            + my_rows(jnp.pad(attn_proj, ((0, attn_pad), (0, 0))), 1),
            0,
        )
    mix_rows = mixer_out.shape[0] // ctx
    normed_all, grad_top, in_full, state_full, step_full, *parts = front(
        x_in, norm_gain[None], top_in, first, later, hidden_units, 0
    )
    if parts:
        ffn_part, rows_part = parts
    normed_all = normed_all.reshape(length, model)
    grad_top = grad_top.reshape(length, model)
    in_full = in_full.reshape(model, -1)
    state_full = state_full[:, :state_rows].reshape(-1, state_proj.shape[1])
    step_full = step_full[:, :step_rows].reshape(-1, mine)
    norm_scale = rms_scale(tokens)
    rows_full = lax.all_gather(rows_part, "fsdp", axis=0)
    ffn_full = over_fsdp(ffn_part)
    down_at = hid_part + hid_pad
    down_full = rows_full[:, :down_at].reshape(-1, model)
    mixout_full = rows_full[:, down_at : down_at + mix_rows].reshape(-1, model)
    attn_at = down_at + mix_rows
    attn_full = rows_full[:, attn_at : attn_at + attn_rows_mine].reshape(-1, model)
    attn_width = attn_full.shape[0]

    def mine_of(vector):
        return jnp.concatenate(my_columns(vector.reshape(-1, inner), fsdp), 1)

    taps, bias, skip, gain_ssm, bias_step = (
        mine_of(conv_taps),
        mine_of(conv_bias),
        mine_of(skip_gain),
        mine_of(ssm_gain),
        mine_of(step_bias),
    )
    rates = jnp.concatenate(
        [
            lax.dynamic_slice_in_dim(
                decay_rate, unit * (inner // fsdp) + place * (mine // fsdp), mine // fsdp, 0
            )
            for unit in range(fsdp)
        ],
        0,
    ).T
    pad = -mine % LANES

    def padded(values):
        return jnp.pad(values, ((0, 0), (0, pad)))

    projected_in = matmul(normed_all, in_full).astype(BF16)
    conv_src = projected_in[:, q_mine + 2 * kv_mine + mine :]

    padded_src = jnp.concatenate(
        [jnp.zeros((CONV - 1, mine), jnp.float32), conv_src.astype(jnp.float32)], 0
    )
    conv_pre = bias + sum(taps[tap][None] * padded_src[tap : tap + length] for tap in range(CONV))
    conv_act = jax.nn.silu(conv_pre).astype(BF16)
    conv_vals = conv_act.astype(jnp.float32)
    projected = sum_everywhere(matmul(conv_act, state_full).astype(BF16), 2).astype(jnp.float32)
    step_low = projected[:, :DT_RANK].astype(BF16)
    input_mat = projected[:, DT_RANK : DT_RANK + STATE]
    output_mat = projected[:, DT_RANK + STATE :]
    step_pre = matmul(step_low, step_full) + bias_step
    steps_dt = jax.nn.softplus(step_pre)
    in_b = jnp.broadcast_to(input_mat.astype(BF16)[:, :, None], (length, STATE, LANES))
    out_b = jnp.broadcast_to(output_mat.astype(BF16)[:, :, None], (length, STATE, LANES))
    rates_log2 = padded(-LOG2_E * rates)
    steps_pad, vals_pad = padded(steps_dt), padded(conv_vals)
    scan_out, states = scan_fwd(steps_pad, vals_pad, in_b, out_b, rates_log2)
    scan_out = scan_out[:, :mine]

    gate_z = projected_in[:, q_mine + 2 * kv_mine : q_mine + 2 * kv_mine + mine].astype(jnp.float32)
    def attn_to_channels(values):
        parts = jnp.pad(values.reshape(own, fsdp, -1), ((0, 0), (0, 0), (0, attn_pad)))
        parts = parts.reshape(own, fsdp, ctx, -1).transpose(2, 0, 1, 3).reshape(ctx, own, -1)
        return lax.all_to_all(parts, "ctx", 0, 0, tiled=True).reshape(length, -1)

    def attn_to_tokens(values):
        parts = values.reshape(ctx, own, -1)
        got = lax.all_to_all(parts, "ctx", 0, 0, tiled=True)
        got = got.reshape(ctx, own, fsdp, -1).transpose(1, 2, 0, 3).reshape(own, fsdp, -1)
        return got[:, :, : attn_proj.shape[0]].reshape(own, -1)

    if ctx == 8:
        branch_attn_c, attn_rows, *attn_kept = attention_forward(
            projected_in, attn_gain, key_proj.shape[1], 1
        )
        branch_attn_c = branch_attn_c.reshape(length, -1)
    else:
        queries = lax.all_to_all(projected_in[:, :q_mine], "ctx", 0, 1, tiled=True)
        keyvals = gather_shards(projected_in[:, q_mine : q_mine + 2 * kv_mine], 1)
        keys_all = keyvals[:, :, :kv_mine].transpose(1, 0, 2).reshape(length, KV_HEADS, HEAD)
        vals_all = keyvals[:, :, kv_mine:].transpose(1, 0, 2).reshape(length, KV_HEADS, HEAD)
        heads_q = queries.reshape(own, KV_HEADS, group_size, HEAD)
        row_ids = place * own + lax.broadcasted_iota(jnp.int32, (own, length), 0)
        col_ids = lax.broadcasted_iota(jnp.int32, (own, length), 1)
        allowed = (col_ids <= row_ids) & (col_ids > row_ids - WINDOW)

        def scores_of():
            raw = jnp.einsum("qhgd,khd->hgqk", heads_q, keys_all, preferred_element_type=jnp.float32)
            return jnp.where(allowed, raw * score_scale, -1e30)

        scores = scores_of()
        row_top = jnp.max(scores, axis=-1, keepdims=True)
        log_total = row_top + jnp.log(jnp.sum(jnp.exp(scores - row_top), axis=-1, keepdims=True))
        probs = jnp.exp(scores - log_total)
        probs_bf = probs.astype(BF16)
        attn_rows = jnp.einsum(
            "hgqk,khd->qhgd", probs_bf, vals_all, preferred_element_type=jnp.float32
        ).reshape(own, -1)
        attn_scale = rms_scale(attn_rows)
        branch_attn = (attn_rows * attn_scale * attn_gain).astype(BF16)
        branch_attn_c = attn_to_channels(branch_attn)

    ssm_raw = scan_out + skip * conv_vals
    gate_act = jax.nn.silu(gate_z)
    ssm_gated = ssm_raw * gate_act
    square = total_of(jnp.sum(ssm_gated * ssm_gated, axis=-1), 3)
    ssm_scale = lax.rsqrt(square / inner + EPSILON)[:, None]
    branch_ssm = (ssm_gated * ssm_scale * gain_ssm).astype(BF16)
    middle = tokens + 0.5 * reduce_products(
        [branch_attn_c, branch_ssm], [attn_full, mixout_full], False, 4
    )
    ffn_scale = rms_scale(middle)
    ffn_in = (middle * ffn_scale * ffn_gain).astype(BF16)
    if ctx == 8:
        ffn_dw, ffn_out, grad_ffn_in = ffn_both_ways(ffn_in, grad_top, ffn_full, down_full, 5)
        ffn_dw = [ffn_dw.reshape(-1, 2 * hid_all)]
    else:
        ffn_all = gather_tokens(ffn_in, 5)
        pre = matmul(ffn_all, ffn_full)
        gate_pre, up_pre = pre[:, :hid_all], pre[:, hid_all:]
        gate_silu = jax.nn.silu(gate_pre)
        hidden = (gate_silu * up_pre).astype(BF16)
        ffn_out = reduce_products([hidden], [down_full], False, 6)
        grad_hidden = right_trans(grad_top, down_full)
        grad_gate = (grad_hidden * up_pre * silu_slope(gate_pre)).astype(BF16)
        grad_up = (grad_hidden * gate_silu).astype(BF16)
        grad_pair = jnp.concatenate([grad_gate, grad_up], 1)
        grad_ffn_in = reduce_products([grad_pair], [ffn_full], True, 7)
        down_dw = left_trans(hidden, grad_top).astype(BF16)
        pair_dw = left_trans(ffn_all, grad_pair).astype(BF16)
        ffn_dw = [pair_dw, down_dw]
    grad_ffn_in, ffn_dw = lax.optimization_barrier((grad_ffn_in, ffn_dw))
    ffn_grad = [scatter_fsdp(dw) for dw in ffn_dw]
    grad_middle, grad_ffn_gain = norm_back(grad_ffn_in, middle, ffn_scale, ffn_gain)
    grad_middle = grad_middle + cotangent[0].astype(jnp.float32)
    grad_branch = (0.5 * grad_middle).astype(BF16)
    branch_all = gather_tokens(grad_branch, 8)
    if ctx == 8:
        grad_early, grad_attn_gain, ffn_out, out_dw, grad_norm, dots = attention_backward(
            (attn_full, mixout_full), attn_rows, (attn_gain, gain_ssm), ssm_gated, ffn_out,
            (branch_attn_c, branch_ssm), branch_all, attn_kept, 13,
        )
        dots = dots[0]
        out_dw = [out_dw.reshape(-1, model)]
        grad_attn_gain = grad_attn_gain[0]
    else:
        grad_attn_c = right_trans(branch_all, attn_full).astype(BF16)
        grad_norm = right_trans(branch_all, mixout_full)
        dots = total_of(jnp.sum(grad_norm * gain_ssm * ssm_gated, axis=-1), 9)
        grad_attn = attn_to_tokens(grad_attn_c).astype(jnp.float32)
        grad_attn_raw, grad_attn_gain = norm_back(grad_attn, attn_rows, attn_scale, attn_gain)
        grad_heads = grad_attn_raw.astype(BF16).reshape(own, KV_HEADS, group_size, HEAD)
        grad_probs = jnp.einsum(
            "qhgd,khd->hgqk", grad_heads, vals_all, preferred_element_type=jnp.float32
        )
        row_dot = jnp.sum(probs * grad_probs, axis=-1, keepdims=True)
        grad_scores = (probs * (grad_probs - row_dot)).astype(BF16)
        grad_queries = score_scale * jnp.einsum(
            "hgqk,khd->qhgd", grad_scores, keys_all, preferred_element_type=jnp.float32
        ).reshape(own, -1)
        grad_keys = score_scale * jnp.einsum(
            "hgqk,qhgd->khd", grad_scores, heads_q, preferred_element_type=jnp.float32
        )
        grad_vals = jnp.einsum(
            "hgqk,qhgd->khd", probs_bf, grad_heads, preferred_element_type=jnp.float32
        )
        grad_queries = lax.all_to_all(
            grad_queries.astype(BF16).reshape(own, ctx, -1).transpose(1, 0, 2), "ctx", 0, 0, tiled=True
        ).reshape(length, -1)
        grad_kv = jnp.concatenate(
            [
                grad_keys.reshape(length, ctx, kv_mine).transpose(1, 0, 2),
                grad_vals.reshape(length, ctx, kv_mine).transpose(1, 0, 2),
            ],
            2,
        ).astype(BF16)
        grad_kv = jnp.sum(
            lax.all_to_all(grad_kv, "ctx", 0, 0, tiled=True).astype(jnp.float32), axis=0
        ).astype(BF16)
        grad_early = jnp.concatenate([grad_queries, grad_kv], 1)
        out_dw = [
            left_trans(branch_ssm, branch_all).astype(BF16),
            left_trans(branch_attn_c, branch_all).astype(BF16),
        ]

    grad_early, out_dw = lax.optimization_barrier((grad_early, out_dw))
    out_grad = scatter_fsdp(*out_dw)

    output = middle + ffn_out

    grad_ssm_gain = jnp.sum(grad_norm * ssm_gated * ssm_scale, axis=0)
    scaled = grad_norm * gain_ssm
    mean_dot = dots[:, None] / inner
    grad_gated = ssm_scale * scaled - ssm_gated * ssm_scale**3 * mean_dot
    grad_scan = grad_gated * gate_act
    grad_gate_z = grad_gated * ssm_raw * silu_slope(gate_z)
    grad_skip = jnp.sum(grad_scan * conv_vals, axis=0)
    grad_gate_bf = grad_gate_z.astype(BF16)
    grad_early = jnp.concatenate([grad_early, grad_gate_bf], 1)
    early_grad = scatter_fsdp(left_trans(normed_all, grad_early))
    with_relay = ctx == 8
    grad_steps, grad_drive, grad_input_mat, grad_output_mat, grad_rate, relayed = scan_bwd(
        steps_pad, vals_pad, padded(grad_scan), in_b, out_b, rates_log2, states,
        *((ffn_grad[0], hidden_rows, hid, down_at, model, 14) if with_relay else ()),
    )
    grad_steps, out_grad = lax.optimization_barrier((grad_steps, out_grad))
    grad_steps, grad_drive, grad_rate = (
        grad_steps[:, :mine],
        grad_drive[:, :mine],
        -grad_rate[:, :mine],
    )
    grad_pre_full = grad_steps * jax.nn.sigmoid(step_pre)
    grad_step_bias = jnp.sum(grad_pre_full, axis=0)
    grad_pre = grad_pre_full.astype(BF16)
    step_dw = left_trans(step_low, grad_pre)
    grad_projected = sum_everywhere(
        jnp.concatenate(
            [right_trans(grad_pre, step_full), grad_input_mat, grad_output_mat], 1
        ).astype(BF16),
        10,
    )
    grad_state_proj = left_trans(conv_act, grad_projected)
    grad_conv_act = (
        right_trans(grad_projected, state_full) + grad_scan * skip + grad_drive
    ).astype(BF16)
    grad_conv = grad_conv_act.astype(jnp.float32) * silu_slope(conv_pre)
    grad_conv_bias = jnp.sum(grad_conv, axis=0)
    grad_taps = jnp.stack(
        [jnp.sum(grad_conv * padded_src[tap : tap + length], axis=0) for tap in range(CONV)]
    )
    conv_tail = jnp.concatenate([grad_conv, jnp.zeros((CONV - 1, mine), jnp.float32)], 0)
    grad_src = sum(
        taps[tap][None] * conv_tail[CONV - 1 - tap : CONV - 1 - tap + length]
        for tap in range(CONV)
    )
    grad_src = grad_src.astype(BF16)
    src_grad = scatter_fsdp(left_trans(normed_all, grad_src), step_dw)
    state_rows_all = grad_state_proj.shape[1]
    state_cut = state_rows_all // (16 * fsdp) * 16 * fsdp
    grad_state = grad_state_proj.T
    head = jnp.concatenate(
        [
            grad_taps,
            jnp.stack([grad_conv_bias, grad_step_bias, grad_skip, grad_ssm_gain]),
            grad_rate,
            grad_state[state_cut:],
        ],
        0,
    )
    head = jnp.pad(head, ((0, -head.shape[0] % (8 * fsdp)), (0, 0)))
    grad_state = grad_state[:state_cut].astype(BF16)
    placing = ctx == 8 and ctx == 2 * fsdp and not attn_pad
    if placing:
        (
            grad_normed, query_grad, key_grad, value_grad, gates, attn_grad, mixout_grad, head,
            grad_state,
        ) = reduce_and_place(
            grad_early, grad_src, in_full, early_grad, out_grad, head, grad_state,
            (q_mine, kv_mine, mix_rows, attn_rows_mine), 11,
        )
    else:
        grad_normed = reduce_products([grad_early, grad_src], [in_full], True, 11)
    if with_relay:
        gate_blocks, up_blocks, down_blocks = relayed
    else:
        pair_grad, down_grad = ffn_grad
        pair_grad = pair_grad.reshape(-1, 2, fsdp, down_at)[..., :hid_part]
        gate_blocks = to_blocks(pair_grad[:, 0].reshape(-1, hid), hidden_units)
        up_blocks = to_blocks(pair_grad[:, 1].reshape(-1, hid), hidden_units)
        down_blocks = rows_to_blocks(down_grad[:hid_part], hidden_rows)
    grad_tokens, grad_norm_gain = norm_back(grad_normed, tokens, norm_scale, norm_gain)
    grad_tokens = grad_tokens + grad_middle

    gains = jnp.stack([grad_norm_gain, grad_attn_gain, grad_ffn_gain])
    gains = jnp.pad(gains, ((0, 5), (0, 0)))
    if placing:
        mixer_grad, step_grad, head, grad_state, gains = finish(
            src_grad, gates, head, grad_state, gains, step_rows, 12
        )
    else:
        channel = jnp.concatenate([head, grad_state.astype(jnp.float32)], 0)
        channel, gains = settle_small(channel, gains, 12)
        channel = channel.reshape(ctx, -1, fsdp, mine // fsdp).transpose(1, 2, 0, 3)
        channel = channel.reshape(-1, inner)
        head, grad_state = channel[: head.shape[0]], channel[head.shape[0] :]
        late_at = q_mine + 2 * kv_mine
        step_grad = src_grad[early_grad.shape[0] :][:step_rows]
        src_grad = src_grad[: early_grad.shape[0]]
        mixout_grad = out_grad[:mix_rows]
        attn_grad = out_grad[mix_rows : mix_rows + attn_rows_mine]
        query_grad = early_grad[:, :q_mine].astype(jnp.float32)
        key_grad = early_grad[:, q_mine : q_mine + kv_mine].astype(jnp.float32)
        value_grad = early_grad[:, q_mine + kv_mine : late_at].astype(jnp.float32)
        mixer_grad = to_blocks(
            jnp.concatenate([src_grad, early_grad[:, late_at:]], 1), 2 * fsdp
        )
        step_grad = to_blocks(step_grad, fsdp)
        attn_grad = rows_to_blocks(attn_grad, 1)[: attn_proj.shape[0]]
        mixout_grad = rows_to_blocks(mixout_grad, 1)
    sum_norm_gain, sum_attn_gain, sum_ffn_gain = gains[0], gains[1], gains[2]
    return (
        output[None],
        grad_tokens[None],
        sum_norm_gain,
        query_grad,
        key_grad,
        value_grad,
        attn_grad,
        sum_attn_gain,
        mixer_grad,
        head[:CONV],
        head[CONV],
        jnp.concatenate(
            [grad_state, head[CONV + 4 + STATE :][: state_rows_all - state_cut]], 0
        ).T,
        step_grad,
        head[CONV + 1],
        head[CONV + 4 : CONV + 4 + STATE].T,
        head[CONV + 2],
        mixout_grad,
        head[CONV + 3],
        sum_ffn_gain,
        gate_blocks,
        up_blocks,
        down_blocks,
    )


def solution(mesh):
    rows, whole = P("fsdp", None), P()
    blocks, sequence = P("fsdp", "ctx"), P("fsdp", "ctx", None)
    return jax.shard_map(
        body,
        mesh=mesh,
        in_specs=(
            sequence, sequence, whole, rows, rows, rows, rows, whole, rows, whole, whole,
            rows, rows, whole, whole, whole, rows, whole, whole, rows, rows, rows,
        ),
        out_specs=(
            sequence, sequence, whole, blocks, blocks, blocks, blocks, whole, blocks, whole, whole,
            whole, blocks, whole, whole, whole, blocks, whole, whole, blocks, blocks, blocks,
        ),
        check_vma=False,
    )
```

```python
import functools
import jax
import jax.numpy as jnp
from jax import lax
from jax.experimental import pallas as pl
from jax.experimental.pallas import tpu as pltpu
from jax.sharding import PartitionSpec as P

LANES = 128
STATE = 16
CHUNK = 128
HEAD = 64
KV_HEADS = 5
CONV = 4
DT_RANK = 100
WINDOW = 1024
EPSILON = 1e-06
LOG2_E = 1.4426950408889634
BF16 = jnp.bfloat16


MESH = pl.DeviceIdType.MESH
VMEM_LIMIT = 56 * 1024 * 1024
IN_VMEM = pl.BlockSpec(memory_space=pltpu.VMEM)


def flip(index, bit):
    return index + (1 - 2 * ((index // (1 << bit)) % 2)) * (1 << bit)


def greet(me, bits):
    barrier = pltpu.get_barrier_semaphore()
    for bit in range(bits):
        pl.semaphore_signal(
            barrier, inc=1, device_id={"ctx": flip(me, bit)}, device_id_type=MESH
        )
    pl.semaphore_wait(barrier, bits)


def halves_of(rows):
    half = rows // 2 if rows % 32 == 0 else rows // 32 * 16
    return (pl.ds(0, half), pl.ds(half, rows - half))


class Copies:
    def __init__(self, axis, send_sem, recv_sem):
        self.axis, self.send_sem, self.recv_sem = axis, send_sem, recv_sem
        self.started = []
        self.count = 0

    def make(self, source, target, device):
        copy = pltpu.make_async_remote_copy(
            src_ref=source,
            dst_ref=target,
            send_sem=self.send_sem.at[self.count],
            recv_sem=self.recv_sem.at[self.count],
            device_id={self.axis: device},
            device_id_type=MESH,
        )
        self.count += 1
        return copy

    def send(self, source, target, device):
        copy = self.make(source, target, device)
        copy.start()
        self.started.append(copy)
        return copy

    def finish(self):
        for copy in self.started:
            copy.wait_send()


def gather_sems(bits):
    return 1 + 2 * sum(1 << p for p in range(bits - 1)) + 2 * ((1 << (bits - 1)) - 1)


def gather_steps(copies, bits, out_ref):
    me = lax.axis_index("ctx")
    parts = halves_of(out_ref.shape[1])
    orders = (list(range(1, bits)), list(range(bits - 1, 0, -1)))

    def send(bit, shard, part):
        at = out_ref.at[shard] if part is None else out_ref.at[shard, part]
        return copies.send(at, at, flip(me, bit))

    known = ([me], [me])
    last, flying = [], [None, None]

    def begin():
        for h in range(2):
            flying[h] = [send(orders[h][0], shard, parts[h]) for shard in known[h]]
        last.append(send(0, me, None))

    def turn(phase, h):
        bit = orders[h][phase]
        for copy in flying[h]:
            copy.wait_recv()
        fresh = [flip(shard, bit) for shard in known[h]]
        known[h].extend(fresh)
        if phase + 1 < bits - 1:
            flying[h] = [send(orders[h][phase + 1], shard, parts[h]) for shard in known[h]]
        last.extend(send(0, shard, parts[h]) for shard in fresh)

    def end():
        for copy in last:
            copy.wait_recv()

    turns = [functools.partial(turn, p, h) for p in range(bits - 1) for h in range(2)]
    return [begin] + turns + [end]


def gather_kernel(bits, x_ref, out_ref, send_sem, recv_sem):
    me = lax.axis_index("ctx")
    greet(me, bits)
    out_ref[me] = x_ref[...]
    copies = Copies("ctx", send_sem, recv_sem)
    for step in gather_steps(copies, bits, out_ref):
        step()
    copies.finish()


def ctx_bits():
    return lax.axis_size("ctx").bit_length() - 1


def params(collective_id):
    return pltpu.CompilerParams(
        collective_id=collective_id, has_side_effects=True, vmem_limit_bytes=VMEM_LIMIT
    )


def gather_shards(x, collective_id):
    bits, ctx = ctx_bits(), lax.axis_size("ctx")
    sems = pltpu.SemaphoreType.DMA((gather_sems(bits),))
    return pl.pallas_call(
        functools.partial(gather_kernel, bits),
        out_shape=jax.ShapeDtypeStruct((ctx,) + x.shape, x.dtype),
        in_specs=[IN_VMEM],
        out_specs=IN_VMEM,
        scratch_shapes=[sems, sems],
        compiler_params=params(collective_id),
        name="gather_shards",
    )(x)


def gather_tokens(x, collective_id):
    return gather_shards(x, collective_id).reshape(-1, x.shape[1])


def row_parts(rows, count):
    tiles = rows // 16
    edges = [16 * (tiles * i // count) for i in range(count)] + [rows]
    return [pl.ds(a, b - a) for a, b in zip(edges[:-1], edges[1:]) if b > a]


def line_steps(copies, out_refs, pieces):
    me, size = lax.axis_index("fsdp"), lax.axis_size("fsdp")
    plans = []
    for way in (1, -1):
        for distance in range(size - 1):
            for ref, part in pieces:
                shard = me - way * distance
                inside = jnp.logical_and(shard >= 0, shard < size)
                held = jnp.where(inside, shard, me)
                to = me + way
                go = jnp.logical_and(inside, jnp.logical_and(to >= 0, to < size))
                target = jnp.where(jnp.logical_and(to >= 0, to < size), to, me - way)
                at = out_refs[ref].at[held, part]
                plans.append((way, distance, go, copies.make(at, at, target)))
    table = {}
    for way, distance, go, copy in plans:
        table.setdefault((way, distance), []).append((go, copy))

    def begin():
        for index in range(len(pieces)):
            for way in (1, -1):
                go, copy = table[way, 0][index]
                pl.when(go)(copy.start)

    def turn(distance, index):
        for way in (1, -1):
            _, came = table[way, distance - 1][index]
            origin = me - way * distance
            pl.when(jnp.logical_and(origin >= 0, origin < size))(came.wait_recv)
            if distance < size - 1:
                go, copy = table[way, distance][index]
                pl.when(go)(copy.start)

    def end():
        for way in (1, -1):
            for distance in range(size - 1):
                for go, copy in table[way, distance]:
                    pl.when(go)(copy.wait_send)

    turns = [
        functools.partial(turn, d, i) for d in range(1, size) for i in range(len(pieces))
    ]
    return [begin] + turns, end


def front_kernel(
    bits, count, turned, pack_first, pack, x_ref, gain_ref, top_ref, *rest,
):
    number = 6 if pack_first["scratch"] else 3
    first_refs, rest = rest[:number], rest[number:]
    weights, rest = rest[: pack["inputs"]], rest[pack["inputs"] :]
    normed_ref, tops_ref, in_out, state_out, step_out = rest[:5]
    packed, rest = rest[5 : 5 + pack["outputs"]], rest[5 + pack["outputs"] :]
    ctx_send, ctx_recv, line_send, line_recv = rest[:4]
    first_scratch, rest = rest[4 : 4 + len(pack_first["scratch"])], rest[4 + len(pack_first["scratch"]) :]
    me, row, rows = lax.axis_index("ctx"), lax.axis_index("fsdp"), lax.axis_size("fsdp")
    barrier = pltpu.get_barrier_semaphore()
    for bit in range(bits):
        pl.semaphore_signal(
            barrier, inc=1, device_id={"ctx": flip(me, bit)}, device_id_type=MESH
        )
    for to in (row - 1, row + 1):
        there = jnp.logical_and(to >= 0, to < rows)

        @pl.when(there)
        def _():
            pl.semaphore_signal(
                barrier, inc=1, device_id={"fsdp": jnp.where(there, to, row)}, device_id_type=MESH
            )

    if first_scratch:
        copies = pack_in_begin(first_refs, first_scratch)
        pack_in(row, copies, first_refs, first_scratch, in_out, state_out, step_out)
    else:
        for out, ref in zip((in_out, state_out, step_out), first_refs):
            out[row] = ref[...]
    neighbours = jnp.where(row > 0, 1, 0) + jnp.where(row < rows - 1, 1, 0)
    pl.semaphore_wait(barrier, bits + neighbours)

    line = Copies("fsdp", line_send, line_recv)
    across = Copies("ctx", ctx_send, ctx_recv)
    pieces = [(0, part) for part in row_parts(in_out.shape[1], count)]
    pieces = [(1, pl.ds(0, state_out.shape[1])), (2, pl.ds(0, step_out.shape[1]))] + pieces
    line_list, line_end = line_steps(line, (in_out, state_out, step_out), pieces)
    line_list[0]()
    tokens = x_ref[...].astype(jnp.float32)
    if turned:
        tokens = tokens.T
    scale = lax.rsqrt(jnp.mean(tokens * tokens, axis=-1, keepdims=True) + EPSILON)
    normed_ref[me] = (tokens * scale * gain_ref[...]).astype(normed_ref.dtype)
    first = gather_steps(across, bits, normed_ref)
    first[0]()
    tops = top_ref[...].astype(jnp.float32)
    tops_ref[me] = (tops.T if turned else tops).astype(tops_ref.dtype)
    second = gather_steps(across, bits, tops_ref)
    steps = list(pack["steps"](me, weights, packed, rest)) if weights else []
    token_rest = first[1:-1] + [second[0]] + second[1:-1] + [first[-1], second[-1]]
    line_rest = line_list[1:]
    tokens_done = packs_done = 0
    spread = len(line_rest) * 3 // 4
    for i, step in enumerate(line_rest):
        upto = min(len(steps), len(steps) * (i + 1) // max(1, spread))
        for pack_step in steps[packs_done:upto]:
            pack_step()
        packs_done = max(packs_done, upto)
        step()
        upto = min(len(token_rest), len(token_rest) * (i + 1) // spread)
        for token_step in token_rest[tokens_done:upto]:
            token_step()
        tokens_done = max(tokens_done, upto)
    across.finish()
    line_end()


def front(x, gain, top, first, later, hidden_units, collective_id):
    bits, ctx, fsdp = ctx_bits(), lax.axis_size("ctx"), lax.axis_size("fsdp")
    count = 5
    ctx_sems = pltpu.SemaphoreType.DMA((2 * gather_sems(bits),))
    line_sems = pltpu.SemaphoreType.DMA((2 * fsdp * (count + 2),))
    pack_first, pack = pack_in_plan(first), pack_out_plan(later, hidden_units)
    turned = bool(later)
    tokens = jax.ShapeDtypeStruct(x.shape[::-1] if turned else x.shape, x.dtype)
    in_any = pl.BlockSpec(memory_space=pl.ANY)

    def stacked(array, size):
        return jax.ShapeDtypeStruct((size,) + array.shape, array.dtype)

    return pl.pallas_call(
        functools.partial(front_kernel, bits, count, turned, pack_first, pack),
        out_shape=[stacked(tokens, ctx), stacked(tokens, ctx)]
        + [stacked(part, fsdp) for part in pack_first["shapes"]]
        + pack["shapes"],
        in_specs=[IN_VMEM] * 3
        + [in_any if i in pack_first["any"] else IN_VMEM for i in range(len(first))]
        + [in_any] * len(later),
        out_specs=[IN_VMEM] * (5 + pack["outputs"]),
        scratch_shapes=[ctx_sems, ctx_sems, line_sems, line_sems]
        + pack_first["scratch"]
        + pack["scratch"],
        compiler_params=params(collective_id),
        name="front",
    )(x, gain, top, *first, *later)


def product(x, weight, trans):
    dims = (((1,), (1 if trans else 0,)), ((), ()))
    return lax.dot_general(x, weight, dims, preferred_element_type=jnp.float32)


def subsets(chosen):
    out = [()]
    for bit in chosen:
        out = out + [s + (bit,) for s in out]
    return out


def flipped(shard, flips):
    for bit in flips:
        shard = flip(shard, bit)
    return shard


class Reducer:
    def __init__(self, copies, bits, part_ref, inbox, out_ref):
        self.copies, self.bits, self.part_ref = copies, bits, part_ref
        self.inbox, self.out_ref = inbox, out_ref
        self.me = lax.axis_index("ctx")
        self.parts = halves_of(out_ref.shape[0])
        self.orders = (list(range(1, bits)), list(range(bits - 1, 0, -1)))
        self.everyone = subsets(range(1, bits))[::-1]
        self.slots = {flips: slot for slot, flips in enumerate(self.everyone)}
        self.first = {}
        self.flying = [{}, {}]

    def to_sibling(self, flips, partial):
        slot = self.slots[flips]
        self.part_ref[slot] = partial.astype(self.part_ref.dtype)
        self.first[flips] = self.copies.send(
            self.part_ref.at[slot], self.inbox[0].at[slot], flip(self.me, 0)
        )

    def pass_on(self, h, phase, flips, following):
        bit = self.orders[h][phase]
        if bit in flips:
            kept = tuple(b for b in flips if b != bit)
            following[kept] = self.copies.send(
                self.inbox[0].at[self.slots[flips], self.parts[h]],
                self.inbox[1 + phase].at[len(following), self.parts[h]],
                flip(self.me, bit),
            )

    def send_parts(self, parts_ref):
        for flips in self.everyone:
            self.first[flips] = self.copies.send(
                parts_ref.at[flipped(self.me, flips + (0,))],
                self.inbox[0].at[self.slots[flips]],
                flip(self.me, 0),
            )

    def own(self, flips, partial):
        self.first[flips].wait_recv()
        kept_ref, slot = self.inbox[0], self.slots[flips]
        kept_ref[slot] = (partial + kept_ref[slot].astype(jnp.float32)).astype(kept_ref.dtype)
        for h in range(2):
            self.pass_on(h, 0, flips, self.flying[h])

    def turn(self, phase, h):
        kept_ref = self.inbox[0]
        part, following = self.parts[h], {}
        for box, (flips, copy) in enumerate(list(self.flying[h].items())):
            copy.wait_recv()
            slot = self.slots[flips]
            total = kept_ref[slot, part].astype(jnp.float32) + self.inbox[1 + phase][
                box, part
            ].astype(jnp.float32)
            if phase == self.bits - 2:
                self.out_ref[part] = total
            else:
                kept_ref[slot, part] = total.astype(kept_ref.dtype)
                self.pass_on(h, phase + 1, flips, following)
        self.flying[h] = following

    def turns(self):
        return [functools.partial(self.turn, p, h) for p in range(self.bits - 1) for h in range(2)]

    def finish(self):
        for turn in self.turns():
            turn()


def reducer_boxes(ctx, bits, rows, columns):
    boxes = [ctx // 2, ctx // 2] + [ctx // 4 >> p for p in range(bits - 1)]
    sems = boxes[0] + 2 * sum(boxes[2:])
    return [pltpu.VMEM((box, rows, columns), BF16) for box in boxes], sems


def reduce_kernel(bits, trans, joint, *refs):
    count = len(trans)
    weights = 1 if joint else count
    x_refs, w_refs, out_ref = refs[:count], refs[count : count + weights], refs[count + weights]
    part_ref, inbox = refs[count + weights + 1], refs[count + weights + 2 : -2]
    me = lax.axis_index("ctx")
    greet(me, bits)
    if joint:
        whole, w_refs, inbox = w_refs[0], inbox[-count:], inbox[:-count]
        at = 0
        for w_ref in w_refs:
            wide = w_ref.shape[1]
            w_ref[...] = whole[:, at : at + wide]
            at += wide
    copies = Copies("ctx", *refs[-2:])
    reducer = Reducer(copies, bits, part_ref, inbox, out_ref)

    def partial(flips):
        shard = flipped(me, flips)
        return sum(
            product(x_ref[shard], w_ref[...], way)
            for x_ref, w_ref, way in zip(x_refs, w_refs, trans)
        )

    for flips in reducer.everyone:
        reducer.to_sibling(flips, partial(flips + (0,)))
    for flips in reducer.everyone:
        reducer.own(flips, partial(flips))
    reducer.finish()
    copies.finish()


def reduce_products(lefts, weights, trans, collective_id):
    ctx, bits = lax.axis_size("ctx"), ctx_bits()
    rows = lefts[0].shape[0] // ctx
    columns = weights[0].shape[0 if trans else 1]
    joint = len(weights) < len(lefts)
    boxes, count = reducer_boxes(ctx, bits, rows, columns)
    if joint:
        boxes = boxes + [pltpu.VMEM((columns, x.shape[1]), BF16) for x in lefts]
    sems = pltpu.SemaphoreType.DMA((count,))
    return pl.pallas_call(
        functools.partial(reduce_kernel, bits, (trans,) * len(lefts), joint),
        out_shape=jax.ShapeDtypeStruct((rows, columns), jnp.float32),
        in_specs=[IN_VMEM] * (len(lefts) + len(weights)),
        out_specs=IN_VMEM,
        scratch_shapes=boxes + [sems, sems],
        compiler_params=params(collective_id),
        name="reduce_products",
    )(*[x.reshape(ctx, rows, -1) for x in lefts], *weights)


def relay_copies(pair_send, pair_recv, down_send, down_recv, send_sem, recv_sem):
    size = pair_send.shape[0]
    me = lax.axis_index("ctx")
    copies = Copies("ctx", send_sem, recv_sem)
    return [
        copies.make(send.at[(me + turn) % size], recv.at[me], (me + turn) % size)
        for send, recv in ((pair_send, pair_recv), (down_send, down_recv))
        for turn in range(1, size)
    ]


def relay_begin(units, stack_ref, pair_send, pair_recv, down_send, down_recv, *sems):
    size = pair_send.shape[0]
    me = lax.axis_index("ctx")
    greet_all(me, size)
    wide, block = pair_send.shape[2] // 2, down_send.shape[2]
    high, part, span = pair_send.shape[1], down_send.shape[1], stack_ref.shape[1]
    half = span // 2
    model = size * block
    pieces, tall = spill_of(part, model, span)
    for d in range(size):
        at = d // units * part + d % units * wide
        pair_send[d, :, :wide] = stack_ref[:high, at : at + wide]
        pair_send[d, :, wide:] = stack_ref[:high, half + at : half + at + wide]
        low, up = d * block, (d + 1) * block
        if low < span:
            down_send[d, :, : min(up, span) - low] = stack_ref[high : high + part, low : min(up, span)]
        if up > span:
            first = max(low, span)
            for k in range(pieces):
                begin, end = k * tall, min(part, (k + 1) * tall)
                lane = k * (model - span) + first - span
                down_send[d, begin:end, first - low :] = stack_ref[
                    high + part : high + part + end - begin, lane : lane + up - first
                ]
    for copy in relay_copies(pair_send, pair_recv, down_send, down_recv, *sems):
        copy.start()
    pair_recv[me] = pair_send[me]
    down_recv[me] = down_send[me]


def relay_end(units, gate_out, up_out, down_out, pair_send, pair_recv, down_send, down_recv, *sems):
    size, wide = pair_send.shape[0], pair_send.shape[2] // 2
    for copy in relay_copies(pair_send, pair_recv, down_send, down_recv, *sems):
        copy.wait()
    for s in range(size):
        at = s * wide
        gate_out[:, at : at + wide] = pair_recv[s, :, :wide].astype(jnp.float32)
        up_out[:, at : at + wide] = pair_recv[s, :, wide:].astype(jnp.float32)
        for u in range(units):
            to = u * size * wide + at
            down_out[to : to + wide] = down_recv[s, u * wide : (u + 1) * wide].astype(jnp.float32)


def greet_all(me, size):
    barrier = pltpu.get_barrier_semaphore()
    for turn in range(1, size):
        pl.semaphore_signal(
            barrier, inc=1, device_id={"ctx": (me + turn) % size}, device_id_type=MESH
        )
    pl.semaphore_wait(barrier, size - 1)


def sum_kernel(size, x_ref, out_ref, send_ref, inbox, all_ref, send_sem, recv_sem):
    me = lax.axis_index("ctx")
    greet_all(me, size)
    columns = x_ref.shape[2]
    copies = Copies("ctx", send_sem, recv_sem)
    send_ref[:, columns:] = jnp.zeros((size, send_ref.shape[1] - columns, x_ref.shape[1]), BF16)
    for e in range(size):
        send_ref[e, :columns] = x_ref[e].astype(jnp.float32).T.astype(BF16)
    come = []
    for turn in range(1, size):
        to = (me + turn) % size
        come.append(copies.send(send_ref.at[to], inbox.at[turn - 1], to))
    total = send_ref[me].astype(jnp.float32)
    for turn in range(1, size):
        come[turn - 1].wait_recv()
        total = total + inbox[turn - 1].astype(jnp.float32)
    all_ref[me] = total.astype(BF16)
    come = [
        copies.send(all_ref.at[me], all_ref.at[me], (me + turn) % size) for turn in range(1, size)
    ]
    for copy in come:
        copy.wait_recv()
    for e in range(size):
        out_ref[e] = all_ref[e].astype(jnp.float32).T[:, :columns].astype(out_ref.dtype)
    copies.finish()


def sum_everywhere(partial, collective_id):
    ctx = lax.axis_size("ctx")
    rows, columns = partial.shape[0] // ctx, partial.shape[1]
    high = columns + -columns % 16
    sems = pltpu.SemaphoreType.DMA((2 * (ctx - 1),))
    return pl.pallas_call(
        functools.partial(sum_kernel, ctx),
        out_shape=jax.ShapeDtypeStruct((ctx, rows, columns), partial.dtype),
        in_specs=[IN_VMEM],
        out_specs=IN_VMEM,
        scratch_shapes=[
            pltpu.VMEM((ctx, high, rows), BF16),
            pltpu.VMEM((ctx - 1, high, rows), BF16),
            pltpu.VMEM((ctx, high, rows), BF16),
            sems, sems,
        ],
        compiler_params=params(collective_id),
        name="sum_everywhere",
    )(partial.reshape(ctx, rows, columns)).reshape(partial.shape)


def total_kernel(size, x_ref, out_ref, inbox, send_sem, recv_sem):
    me = lax.axis_index("ctx")
    greet_all(me, size)
    copies = Copies("ctx", send_sem, recv_sem)
    come = [
        copies.send(x_ref, inbox.at[turn - 1], (me + turn) % size) for turn in range(1, size)
    ]
    inbox_total = x_ref[...]
    for turn in range(1, size):
        come[turn - 1].wait_recv()
        inbox_total = inbox_total + inbox[turn - 1]
    out_ref[...] = inbox_total
    copies.finish()


def total_of(rows_sum, collective_id):
    ctx = lax.axis_size("ctx")
    flat = rows_sum.reshape(-1, LANES)
    sems = pltpu.SemaphoreType.DMA((ctx - 1,))
    return pl.pallas_call(
        functools.partial(total_kernel, ctx),
        out_shape=jax.ShapeDtypeStruct(flat.shape, flat.dtype),
        in_specs=[IN_VMEM],
        out_specs=IN_VMEM,
        scratch_shapes=[pltpu.VMEM((ctx - 1,) + flat.shape, flat.dtype), sems, sems],
        compiler_params=params(collective_id),
        name="total_of",
    )(flat).reshape(rows_sum.shape)


def settle_kernel(
    bits, size, count, channel_ref, gain_ref, all_ref, sums_ref,
    row_inbox, gain_inbox, line_inbox, ctx_send, ctx_recv, line_send, line_recv,
):
    me, row = lax.axis_index("ctx"), lax.axis_index("fsdp")
    barrier = pltpu.get_barrier_semaphore()
    for turn in range(1, size):
        pl.semaphore_signal(
            barrier, inc=1, device_id={"ctx": (me + turn) % size}, device_id_type=MESH
        )
    for turn in range(1, count):
        pl.semaphore_signal(
            barrier, inc=1, device_id={"fsdp": (row + turn) % count}, device_id_type=MESH
        )
    pl.semaphore_wait(barrier, size - 1 + count - 1)
    across, line = Copies("ctx", ctx_send, ctx_recv), Copies("fsdp", line_send, line_recv)
    band = channel_ref.shape[0] // count

    def band_of(index):
        return pl.ds(pl.multiple_of(index * band, 8), band)

    rows_come = []
    for turn in range(1, count):
        to = (row + turn) % count
        rows_come.append(line.send(channel_ref.at[band_of(to)], row_inbox.at[turn - 1], to))
    gains_come = [
        across.send(gain_ref, gain_inbox.at[turn - 1], (me + turn) % size)
        for turn in range(1, size)
    ]
    total = channel_ref[band_of(row)]
    for turn in range(1, count):
        rows_come[turn - 1].wait_recv()
        total = total + row_inbox[turn - 1]
    all_ref[me, band_of(row)] = total
    at = all_ref.at[me, band_of(row)]
    bands_come = [line.send(at, at, (row + turn) % count) for turn in range(1, count)]
    total = gain_ref[...]
    for turn in range(1, size):
        gains_come[turn - 1].wait_recv()
        total = total + gain_inbox[turn - 1]
    line_inbox[0] = total
    line_come = [
        line.send(line_inbox.at[0], line_inbox.at[turn], (row + turn) % count)
        for turn in range(1, count)
    ]
    for copy in bands_come:
        copy.wait_recv()
    for step in gather_steps(across, bits, all_ref):
        step()
    total = line_inbox[0]
    for turn in range(1, count):
        line_come[turn - 1].wait_recv()
        total = total + line_inbox[turn]
    sums_ref[...] = total
    across.finish()
    line.finish()


def settle_small(channel, gains, collective_id):
    ctx, fsdp, bits = lax.axis_size("ctx"), lax.axis_size("fsdp"), ctx_bits()
    ctx_sems = pltpu.SemaphoreType.DMA((ctx - 1 + gather_sems(bits),))
    line_sems = pltpu.SemaphoreType.DMA((3 * (fsdp - 1),))
    rows, columns = channel.shape
    return pl.pallas_call(
        functools.partial(settle_kernel, bits, ctx, fsdp),
        out_shape=[
            jax.ShapeDtypeStruct((ctx, rows, columns), jnp.float32),
            jax.ShapeDtypeStruct(gains.shape, jnp.float32),
        ],
        in_specs=[IN_VMEM] * 2,
        out_specs=[IN_VMEM] * 2,
        scratch_shapes=[
            pltpu.VMEM((fsdp - 1, rows // fsdp, columns), jnp.float32),
            pltpu.VMEM((ctx - 1,) + gains.shape, jnp.float32),
            pltpu.VMEM((fsdp,) + gains.shape, jnp.float32),
            ctx_sems, ctx_sems, line_sems, line_sems,
        ],
        compiler_params=params(collective_id),
        name="settle_small",
    )(channel, gains)


def plane_gather(copies, out_ref):
    me = lax.axis_index("ctx")
    parts = halves_of(out_ref.shape[1])
    held = {}

    def send(name, bit, flips, part=None):
        shard = flipped(me, flips)
        at = out_ref.at[shard] if part is None else out_ref.at[shard, part]
        held[name] = copies.send(at, at, flip(me, bit))

    def start():
        for bit in (1, 2, 0):
            send(("own", bit), bit, ())

    def forward():
        held["own", 1].wait_recv()
        send(("corner", 2), 2, (1,), parts[0])
        held["own", 2].wait_recv()
        send(("corner", 1), 1, (2,), parts[1])
        send(("core", (1,)), 0, (1,))
        send(("core", (2,)), 0, (2,))

    def corner():
        held["corner", 2].wait_recv()
        held["corner", 1].wait_recv()
        send(("core", (1, 2)), 0, (1, 2))

    def wait(flips):
        held["core", flips].wait_recv() if flips else held["own", 0].wait_recv()

    return start, forward, corner, wait


def ffn_kernel(
    x_ref, top_ref, pair_w, down_w,
    dw_ref, out_ref, grad_ref,
    all_ref, hidden_ref, pair_ref, own_ref, part_grad, *rest,
):
    bits = 3
    me = lax.axis_index("ctx")
    greet(me, bits)
    all_ref[me] = x_ref[...]
    copies = Copies("ctx", *rest[-2:])
    start, forward, corner, wait = plane_gather(copies, all_ref)
    reducer = Reducer(copies, bits, part_grad, rest[:-2], grad_ref)
    rows, model = x_ref.shape
    hid = hidden_ref.shape[2]
    core = me % 2

    def work(slot, flips):
        first = 2 * (flipped(me, flips) // 2)
        pair = pl.ds(first, 2)
        x = all_ref[pair].reshape(2 * rows, model)
        pre = product(x, pair_w[...], False)
        gate, up = pre[:, :hid], pre[:, hid:]
        logistic = jax.nn.sigmoid(gate)
        gate_silu = gate * logistic
        hidden = (gate_silu * up).astype(BF16)
        hidden_ref[pair] = hidden.reshape(2, rows, hid)
        top = top_ref[pair].reshape(2 * rows, model)
        grad_hidden = product(top, down_w[...], True)
        slope = logistic * (1.0 + gate * (1.0 - logistic))
        pair_ref[pair, :, :hid] = (grad_hidden * up * slope).astype(BF16).reshape(2, rows, hid)
        pair_ref[pair, :, hid:] = (grad_hidden * gate_silu).astype(BF16).reshape(2, rows, hid)
        grads = pair_ref[pair].reshape(2 * rows, 2 * hid)
        value = product(grads, pair_w[...], True)
        low, high = value[:rows], value[rows:]
        own_ref[slot] = jnp.where(core == 0, low, high)
        reducer.to_sibling(flips, jnp.where(core == 0, high, low))

    def project(first):
        pair = pl.ds(first, 2)
        hidden = hidden_ref[pair].reshape(2 * rows, hid)
        out_ref[pair] = product(hidden, down_w[...], False).astype(BF16).reshape(2, rows, model)

    def settle(slot, flips):
        reducer.own(flips, own_ref[slot])

    start()
    wait(())
    work(0, ())
    forward()
    wait((1,))
    work(1, (1,))
    settle(0, ())
    corner()
    wait((2,))
    work(2, (2,))
    settle(1, (1,))
    wait((1, 2))
    work(3, (1, 2))
    settle(2, (2,))
    settle(3, (1, 2))

    size, blocks = all_ref.shape[0], dw_ref.shape[0]
    high, part, wide = model // blocks, hid // blocks, 2 * hid
    pieces, tall = spill_of(part, model, wide)

    def over_tokens(left_ref, right_ref, low, count):
        left = left_ref[:, :, low : low + count].reshape(size * rows, count)
        right = right_ref[...].reshape(size * rows, right_ref.shape[2])
        return lax.dot_general(
            left, right, (((0,), (0,)), ((), ())), preferred_element_type=jnp.float32
        ).astype(BF16)

    def pair_band(f):
        dw_ref[f, :high] = over_tokens(all_ref, pair_ref, f * high, high)

    def down_band(f):
        values = over_tokens(hidden_ref, top_ref, f * part, part)
        dw_ref[f, high : high + part] = values[:, :wide]
        dw_ref[f, high + part :] = jnp.zeros((dw_ref.shape[1] - high - part, wide), BF16)
        spill = model - wide
        for k in range(pieces):
            low, up = k * tall, min(part, (k + 1) * tall)
            dw_ref[f, high + part : high + part + up - low, k * spill : (k + 1) * spill] = values[
                low:up, wide:
            ]

    work_left = [functools.partial(down_band, f) for f in range(blocks)]
    work_left += [functools.partial(pair_band, f) for f in range(blocks)]
    work_left += [functools.partial(project, first) for first in range(0, size, 2)]
    turns = reducer.turns()
    done = 0
    for i, turn in enumerate(turns):
        upto = len(work_left) * (i + 1) // len(turns)
        for item in work_left[done:upto]:
            item()
        done = upto
        turn()
    copies.finish()


def spill_of(part, model, wide):
    pieces = wide // (model - wide)
    return pieces, -(-part // pieces)


def stack_rows(model, hid, blocks):
    _, tall = spill_of(hid // blocks, model, 2 * hid)
    return model // blocks + hid // blocks + tall + -tall % 16


def ffn_both_ways(ffn_in, top, pair_full, down_full, collective_id):
    ctx, fsdp, bits = lax.axis_size("ctx"), lax.axis_size("fsdp"), ctx_bits()
    rows, model = ffn_in.shape
    hid = down_full.shape[0]
    boxes, count = reducer_boxes(ctx, bits, rows, model)
    sems = pltpu.SemaphoreType.DMA((count + 8,))
    return pl.pallas_call(
        ffn_kernel,
        out_shape=[
            jax.ShapeDtypeStruct((fsdp, stack_rows(model, hid, fsdp), 2 * hid), BF16),
            jax.ShapeDtypeStruct((ctx, rows, model), BF16),
            jax.ShapeDtypeStruct((rows, model), jnp.float32),
        ],
        in_specs=[IN_VMEM] * 4,
        out_specs=[IN_VMEM] * 3,
        scratch_shapes=[
            pltpu.VMEM((ctx, rows, model), BF16),
            pltpu.VMEM((ctx, rows, hid), BF16),
            pltpu.VMEM((ctx, rows, 2 * hid), BF16),
            pltpu.VMEM((ctx // 2, rows, model), jnp.float32),
        ]
        + boxes
        + [sems, sems],
        compiler_params=params(collective_id),
        name="ffn_both_ways",
    )(ffn_in, top.reshape(ctx, rows, model), pair_full, down_full)


def pieces_of(start, width, span):
    out = []
    at = start
    while at < start + width:
        block = at // span
        end = min(start + width, (block + 1) * span)
        out.append((block, at - start, end - start, at - block * span))
        at = end
    return out


def exchange(copies, send_ref, recv_ref, me, size):
    recv_ref[me] = send_ref[me]
    return [
        copies.send(send_ref.at[(me + turn) % size], recv_ref.at[me], (me + turn) % size)
        for turn in range(1, size)
    ]


def attention_kernel(
    size, fsdp, proj_ref, gain_ref,
    branch_ref, rows_ref, prob_ref, inverse_ref, q_ref, k_ref, v_ref,
    q_send, q_recv, kv_all, score_ref, attn_send, send_sem, recv_sem,
):
    bits = size.bit_length() - 1
    me = lax.axis_index("ctx")
    own, q_mine = q_send.shape[1], q_send.shape[2]
    kv_mine = kv_all.shape[2] // 2
    groups, keys, _ = k_ref.shape
    heads = q_ref.shape[1] // own
    queries = heads * own
    chunk = 128
    greet_all(me, size)
    copies = Copies("ctx", send_sem, recv_sem)
    for s in range(size):
        q_send[s] = proj_ref[s * own : (s + 1) * own, :q_mine]
    kv_all[me] = proj_ref[:, q_mine : q_mine + 2 * kv_mine]
    steps = gather_steps(copies, bits, kv_all)
    steps[0]()
    come = exchange(copies, q_send, q_recv, me, size)
    for step in steps[1:]:
        step()
    for copy in come:
        copy.wait_recv()

    for g in range(groups):
        for s, low, high, at in pieces_of(g * HEAD, HEAD, kv_mine):
            k_ref[g, :, low:high] = kv_all[s, :, at : at + high - low]
            v_ref[g, :, low:high] = kv_all[s, :, kv_mine + at : kv_mine + at + high - low]
        for h in range(heads):
            for s, low, high, at in pieces_of((g * heads + h) * HEAD, HEAD, q_mine):
                q_ref[g, h * own : (h + 1) * own, low:high] = q_recv[s, :, at : at + high - low]

    query_ids = me * own + lax.broadcasted_iota(jnp.int32, (chunk, queries), 1) % own
    key_ids = lax.broadcasted_iota(jnp.int32, (chunk, queries), 0)
    for g in range(groups):
        q_g = q_ref[g]

        def scores(i, top):
            at = pl.ds(pl.multiple_of(i * chunk, chunk), chunk)
            raw = product(k_ref[g, at], q_g, True) * (HEAD**-0.5)
            ids = key_ids + i * chunk
            kept = jnp.logical_and(ids <= query_ids, ids > query_ids - WINDOW)
            raw = jnp.where(kept, raw, -1e30)
            score_ref[at] = raw
            return jnp.maximum(top, jnp.max(raw, axis=0, keepdims=True))

        top = lax.fori_loop(
            0, keys // chunk, scores, jnp.full((1, queries), -1e30, jnp.float32)
        )

        def weights(i, total):
            at = pl.ds(pl.multiple_of(i * chunk, chunk), chunk)
            value = jnp.exp(score_ref[at] - top)
            prob_ref[g, at] = value.astype(BF16)
            return total + jnp.sum(value, axis=0, keepdims=True)

        total = lax.fori_loop(
            0, keys // chunk, weights, jnp.zeros((1, queries), jnp.float32)
        )
        inverse = 1.0 / total
        inverse_ref[g] = inverse
        out = lax.dot_general(
            v_ref[g], prob_ref[g], (((0,), (0,)), ((), ())), preferred_element_type=jnp.float32
        )
        out = (out * inverse).T
        for h in range(heads):
            at = (g * heads + h) * HEAD
            rows_ref[:, at : at + HEAD] = out[h * own : (h + 1) * own]

    values = rows_ref[...]
    scale = lax.rsqrt(jnp.mean(values * values, axis=-1, keepdims=True) + EPSILON)
    branch = (values * scale * gain_ref[...]).astype(BF16)
    part = values.shape[1] // fsdp
    width = part // size
    for d in range(size):
        for f in range(fsdp):
            at = f * part + d * width
            attn_send[d, :, f * width : (f + 1) * width] = branch[:, at : at + width]
    for copy in exchange(copies, attn_send, branch_ref, me, size):
        copy.wait_recv()
    copies.finish()


def attention_forward(projected, gain, kv_width, collective_id):
    ctx, fsdp, bits = lax.axis_size("ctx"), lax.axis_size("fsdp"), ctx_bits()
    length, model = projected.shape[0], gain.shape[0]
    own, q_mine, kv_mine = length // ctx, model // ctx, kv_width // ctx
    heads = model // kv_width
    sems = pltpu.SemaphoreType.DMA((2 * (ctx - 1) + gather_sems(bits),))
    shape = jax.ShapeDtypeStruct
    return pl.pallas_call(
        functools.partial(attention_kernel, ctx, fsdp),
        out_shape=[
            shape((ctx, own, q_mine), BF16),
            shape((own, model), jnp.float32),
            shape((KV_HEADS, length, heads * own), BF16),
            shape((KV_HEADS, 1, heads * own), jnp.float32),
            shape((KV_HEADS, heads * own, HEAD), BF16),
            shape((KV_HEADS, length, HEAD), BF16),
            shape((KV_HEADS, length, HEAD), BF16),
        ],
        in_specs=[IN_VMEM] * 2,
        out_specs=[IN_VMEM] * 7,
        scratch_shapes=[
            pltpu.VMEM((ctx, own, q_mine), BF16),
            pltpu.VMEM((ctx, own, q_mine), BF16),
            pltpu.VMEM((ctx, length, 2 * kv_mine), BF16),
            pltpu.VMEM((length, heads * own), jnp.float32),
            pltpu.VMEM((ctx, own, q_mine), BF16),
            sems, sems,
        ],
        compiler_params=params(collective_id),
        name="attention_forward",
    )(projected, gain[None])


def stacked_rows(rows):
    return rows + -rows % 16


def folded(model, span, high):
    out = [(0, g * high, g * span, 0, high) for g in range(model // span)]
    spill = model % span
    if spill:
        pieces = span // spill
        tall = -(-high // pieces)
        for k in range(pieces):
            low, up = k * tall, min(high, (k + 1) * tall)
            if low < up:
                out.append((k * spill, model // span * high, model - spill, low, up))
    return out


def folded_rows(model, span, high):
    return stacked_rows(max(row + up - low for _, row, _, low, up in folded(model, span, high)))


def attention_back_kernel(
    size, fsdp, attn_w, mix_w, rows_ref, gain_ref, ssm_gain_ref, gated_ref,
    parts_ref, branch_ref, ssm_ref, top_ref,
    prob_ref, inverse_ref, q_ref, k_ref, v_ref,
    early_ref, gain_grad_ref, ffn_ref, dw_ref, norm_grad_ref, dot_ref,
    grad_ref, dot_part, dot_inbox, recv_ref, heads_ref, dp_ref, dq_ref, dkv_ref, dq_send, dq_recv, kv_part, kv_sum, *rest,
):
    bits = size.bit_length() - 1
    me = lax.axis_index("ctx")
    own, model = rows_ref.shape
    q_mine = model // size
    groups, keys, queries = prob_ref.shape
    heads = queries // own
    kv_mine = groups * HEAD // size
    chunk = 128
    scale_qk = HEAD**-0.5
    boxes = (len(rest) - 2) // 2
    inbox, ffn_inbox = rest[:boxes], rest[boxes : 2 * boxes]
    greet_all(me, size)
    copies = Copies("ctx", *rest[-2:])
    for s in range(size):
        grad_ref[s] = product(top_ref[s * own : (s + 1) * own], attn_w[...], True).astype(BF16)
    come = exchange(copies, grad_ref, recv_ref, me, size)
    norm_grad_ref[...] = product(top_ref[...], mix_w[...], True)
    scaled = norm_grad_ref[...] * ssm_gain_ref[...] * gated_ref[...]
    dot_part[...] = lax.dot_general(
        jnp.ones((dot_ref.shape[0], scaled.shape[1]), jnp.float32), scaled,
        (((1,), (1,)), ((), ())),
        precision=lax.Precision.HIGHEST, preferred_element_type=jnp.float32,
    )
    dots = [
        copies.send(dot_part, dot_inbox.at[turn - 1], (me + turn) % size)
        for turn in range(1, size)
    ]
    ffn_sum = Reducer(copies, bits, None, ffn_inbox, ffn_ref)
    ffn_sum.send_parts(parts_ref)

    def add_parts():
        for flips in ffn_sum.everyone:
            ffn_sum.own(flips, parts_ref[flipped(me, flips)].astype(jnp.float32))

    beside = [add_parts] + ffn_sum.turns()
    values = rows_ref[...]
    scale = lax.rsqrt(jnp.mean(values * values, axis=-1, keepdims=True) + EPSILON)
    at, span = 0, dw_ref.shape[2]
    high = stacked_rows((ssm_ref.shape[1] + branch_ref.shape[1]) // fsdp)
    dw_ref[...] = jnp.zeros(dw_ref.shape, BF16)
    for ref in (ssm_ref, branch_ref):
        wide = ref.shape[1] // fsdp
        weights = lax.dot_general(
            ref[...], top_ref[...], (((0,), (0,)), ((), ())), preferred_element_type=jnp.float32
        ).astype(BF16)
        for f in range(fsdp):
            mine = weights[f * wide : (f + 1) * wide]
            for lane, row, first, low, up in folded(model, span, high):
                begin, end = max(low, at), min(up, at + wide)
                if begin < end:
                    lanes = min(span, model - first)
                    dw_ref[f, row + begin - low : row + end - low, lane : lane + lanes] = mine[
                        begin - at : end - at, first : first + lanes
                    ]
        at += wide
    for copy in come:
        copy.wait_recv()
    part = model // fsdp
    width = part // size
    for s in range(size):
        for f in range(fsdp):
            at = f * part + s * width
            dq_ref[:, at : at + width] = recv_ref[s, :, f * width : (f + 1) * width].astype(
                jnp.float32
            )
    grad = dq_ref[...]
    gain_grad_ref[...] = jnp.sum(grad * values * scale, axis=0, keepdims=True)
    scaled = grad * gain_ref[...]
    grad = scale * scaled - values * (scale * scale * scale) * jnp.mean(
        scaled * values, axis=-1, keepdims=True
    )
    grad = grad.astype(BF16)
    for h in range(groups * heads):
        at = (h % heads) * own
        heads_ref[h // heads, at : at + own] = grad[:, h * HEAD : (h + 1) * HEAD]

    for g in range(groups):
        q_g, do_g, inverse = q_ref[g], heads_ref[g], inverse_ref[g]
        q_t = q_g.astype(jnp.float32).T.astype(BF16)
        do_t = do_g.astype(jnp.float32).T.astype(BF16)

        def first(i, row_dot):
            at = pl.ds(pl.multiple_of(i * chunk, chunk), chunk)
            prob = prob_ref[g, at].astype(jnp.float32) * inverse
            grad_prob = product(v_ref[g, at], do_g, True)
            dp_ref[at] = grad_prob
            dkv_ref[groups + g, :, at] = product(do_t, prob.astype(BF16), True)
            return row_dot + jnp.sum(prob * grad_prob, axis=0, keepdims=True)

        row_dot = lax.fori_loop(
            0, keys // chunk, first, jnp.zeros((1, queries), jnp.float32)
        )

        def second(i, dq_t):
            at = pl.ds(pl.multiple_of(i * chunk, chunk), chunk)
            prob = prob_ref[g, at].astype(jnp.float32) * inverse
            grad_score = (prob * (dp_ref[at] - row_dot)).astype(BF16)
            dkv_ref[g, :, at] = scale_qk * product(q_t, grad_score, True)
            return dq_t + lax.dot_general(
                k_ref[g, at], grad_score, (((0,), (0,)), ((), ())),
                preferred_element_type=jnp.float32,
            )

        dq_t = lax.fori_loop(
            0, keys // chunk, second, jnp.zeros((HEAD, queries), jnp.float32)
        )
        dq_g = (scale_qk * dq_t).T
        for h in range(heads):
            at = (g * heads + h) * HEAD
            dq_ref[:, at : at + HEAD] = dq_g[h * own : (h + 1) * own]
        if beside:
            beside.pop(0)()

    for step in beside:
        step()
    for copy in dots:
        copy.wait_recv()
    total = dot_part[...]
    for turn in range(1, size):
        total = total + dot_inbox[turn - 1]
    dot_ref[...] = total
    for d in range(size):
        dq_send[d] = dq_ref[:, d * q_mine : (d + 1) * q_mine].astype(BF16)
    come = exchange(copies, dq_send, dq_recv, me, size)
    flat = dkv_ref.reshape(2 * groups * HEAD, keys)
    for d in range(size):
        kv_part[d, :kv_mine] = flat[d * kv_mine : (d + 1) * kv_mine].astype(BF16)
        at = groups * HEAD + d * kv_mine
        kv_part[d, kv_mine:] = flat[at : at + kv_mine].astype(BF16)
    reducer = Reducer(copies, bits, None, inbox, kv_sum)
    reducer.send_parts(kv_part)
    for flips in reducer.everyone:
        reducer.own(flips, kv_part[flipped(me, flips)].astype(jnp.float32))
    for copy in come:
        copy.wait_recv()
    for s in range(size):
        early_ref[s * own : (s + 1) * own, :q_mine] = dq_recv[s]
    reducer.finish()
    early_ref[:, q_mine:] = kv_sum[...].T.astype(BF16)
    copies.finish()


def attention_backward(weights, rows, gains, gated, parts, branches, top, kept, span, collective_id):
    ctx, fsdp, bits = lax.axis_size("ctx"), lax.axis_size("fsdp"), ctx_bits()
    prob = kept[0]
    own, model = rows.shape
    length = own * ctx
    q_mine, kv_mine = model // ctx, KV_HEADS * HEAD // ctx
    boxes, count = reducer_boxes(ctx, bits, 2 * kv_mine, length)
    ffn_boxes, ffn_count = reducer_boxes(ctx, bits, own, model)
    dw_rows = sum(branch.shape[1] for branch in branches) // fsdp
    sems = pltpu.SemaphoreType.DMA((3 * (ctx - 1) + count + ffn_count,))
    shape = jax.ShapeDtypeStruct
    return pl.pallas_call(
        functools.partial(attention_back_kernel, ctx, fsdp),
        out_shape=[
            shape((length, q_mine + 2 * kv_mine), BF16),
            shape((1, model), jnp.float32),
            shape((own, model), jnp.float32),
            shape((fsdp, folded_rows(model, span, stacked_rows(dw_rows)), span), BF16),
            shape(gated.shape, jnp.float32),
            shape((8, length), jnp.float32),
        ],
        in_specs=[IN_VMEM] * (10 + len(kept)),
        out_specs=[IN_VMEM] * 6,
        scratch_shapes=[
            pltpu.VMEM((ctx, own, q_mine), BF16),
            pltpu.VMEM((8, length), jnp.float32),
            pltpu.VMEM((ctx - 1, 8, length), jnp.float32),
            pltpu.VMEM((ctx, own, q_mine), BF16),
            pltpu.VMEM(kept[2].shape, BF16),
            pltpu.VMEM((length, prob.shape[2]), jnp.float32),
            pltpu.VMEM((own, model), jnp.float32),
            pltpu.VMEM((2 * KV_HEADS, HEAD, length), jnp.float32),
            pltpu.VMEM((ctx, own, q_mine), BF16),
            pltpu.VMEM((ctx, own, q_mine), BF16),
            pltpu.VMEM((ctx, 2 * kv_mine, length), BF16),
            pltpu.VMEM((2 * kv_mine, length), jnp.float32),
        ]
        + boxes[1:]
        + ffn_boxes[1:]
        + [sems, sems],
        compiler_params=params(collective_id),
        name="attention_backward",
    )(*weights, rows, *[gain.reshape(1, -1) for gain in gains], gated, parts, *branches, top, *kept)


def greet_planes(me, size, row, rows):
    barrier = pltpu.get_barrier_semaphore()
    for turn in range(1, size):
        pl.semaphore_signal(
            barrier, inc=1, device_id={"ctx": (me + turn) % size}, device_id_type=MESH
        )
    for turn in range(1, rows):
        pl.semaphore_signal(
            barrier, inc=1, device_id={"fsdp": (row + turn) % rows}, device_id_type=MESH
        )
    pl.semaphore_wait(barrier, size - 1 + rows - 1)


class SomeExchange:
    def __init__(self, copies, send_ref, recv_ref, me, size, chosen):
        self.send_ref, self.recv_ref, self.me, self.mine = send_ref, recv_ref, me, chosen(me)
        self.plans = []
        for turn in range(1, size):
            to = (me + turn) % size
            self.plans.append((chosen(to), copies.make(send_ref.at[to], recv_ref.at[me], to)))

    def start(self):
        for chosen, copy in self.plans:
            pl.when(chosen)(copy.start)

        @pl.when(self.mine)
        def _():
            self.recv_ref[self.me] = self.send_ref[self.me]

    def wait(self):
        for _, copy in self.plans:
            pl.when(self.mine)(copy.wait_recv)

    def finish(self):
        for chosen, copy in self.plans:
            pl.when(chosen)(copy.wait_send)


def back_kernel(
    size, fsdp, first_ref, second_ref, weight_ref, early_ref, head_ref, state_ref,
    sum_ref, query_out, key_out, value_out, gate_recv, attn_out, mix_out, head_sum, state_sum,
    first_w, second_w, head_inbox, state_inbox, c_send, r_send, r_recv,
    ctx_send, ctx_recv, line_send, line_recv, part_ref, *inbox,
):
    bits = size.bit_length() - 1
    me, row = lax.axis_index("ctx"), lax.axis_index("fsdp")
    greet_planes(me, size, row, fsdp)
    q_mine, kv_mine = query_out.shape[1], key_out.shape[1]
    late = q_mine + 2 * kv_mine
    rows, width = c_send.shape[1], c_send.shape[2]
    high, block = mix_out.shape[0] // size, mix_out.shape[1]
    across, line = Copies("ctx", ctx_send, ctx_recv), Copies("fsdp", line_send, line_recv)
    small = ((head_ref, head_inbox, head_sum), (state_ref, state_inbox, state_sum))

    def band_of(ref, index):
        band = ref.shape[0] // fsdp
        return pl.ds(pl.multiple_of(index * band, band), band)

    bands = []
    for turn in range(1, fsdp):
        to = (row + turn) % fsdp
        for ref, box, _ in small:
            bands.append(line.send(ref.at[band_of(ref, to)], box.at[turn - 1], to))
    span, tall = early_ref.shape[1], r_send.shape[1]
    for d in range(size):
        for lane, begin, first, low, up in folded(size * block, span, tall):
            lanes = min(span, size * block - first)
            left, right = max(d * block, first), min((d + 1) * block, first + lanes)
            if left < right:
                at = lane + left - first
                r_send[d, low:up, left - d * block : right - d * block] = early_ref[
                    rows + begin : rows + begin + up - low, at : at + right - left
                ]
        if d >= fsdp:
            at = late + (d - fsdp) * width
            c_send[d] = early_ref[:rows, at : at + width]
    gates = SomeExchange(across, c_send, gate_recv, me, size, lambda d: d >= fsdp)
    gates.start()
    moved = exchange(across, r_send, r_recv, me, size)
    cut = first_w.shape[1]
    first_w[...] = weight_ref[:, :cut]
    second_w[...] = weight_ref[:, cut:]
    reducer = Reducer(across, bits, part_ref, inbox, sum_ref)

    def partial(flips):
        shard = flipped(me, flips)
        return product(first_ref[shard], first_w[...], True) + product(
            second_ref[shard], second_w[...], True
        )

    for flips in reducer.everyone:
        reducer.to_sibling(flips, partial(flips + (0,)))
    for flips in reducer.everyone:
        reducer.own(flips, partial(flips))
    for copy in bands:
        copy.wait_recv()
    bands = []
    for ref, box, sum_of in small:
        total = ref[band_of(ref, row)].astype(jnp.float32)
        for turn in range(1, fsdp):
            total = total + box[turn - 1].astype(jnp.float32)
        sum_of[band_of(ref, row)] = total.astype(sum_of.dtype)
        at = sum_of.at[band_of(ref, row)]
        bands += [line.send(at, at, (row + turn) % fsdp) for turn in range(1, fsdp)]
    turns = reducer.turns()
    for turn in turns[:2]:
        turn()

    @pl.when(me < fsdp)
    def _():
        gate_recv[...] = jnp.zeros(gate_recv.shape, BF16)

    query_out[...] = early_ref[:rows, :q_mine].astype(jnp.float32)
    key_out[...] = early_ref[:rows, q_mine : q_mine + kv_mine].astype(jnp.float32)
    value_out[...] = early_ref[:rows, q_mine + kv_mine : late].astype(jnp.float32)
    for turn in turns[2:]:
        turn()
    for copy in moved:
        copy.wait_recv()
    count = attn_out.shape[0] // size
    for s in range(size):
        mix_out[s * high : (s + 1) * high] = r_recv[s, :high].astype(jnp.float32)
        attn_out[s * count : (s + 1) * count] = r_recv[s, high : high + count].astype(jnp.float32)
    gates.wait()
    gates.finish()
    for copy in bands:
        copy.wait_recv()
    across.finish()
    line.finish()


def reduce_and_place(first, second, weight, early, head, state, sizes, collective_id):
    ctx, fsdp, bits = lax.axis_size("ctx"), lax.axis_size("fsdp"), ctx_bits()
    q_mine, kv_mine, mix_rows, attn_rows = sizes
    own, columns = first.shape[0] // ctx, weight.shape[0]
    rows, mine = columns // fsdp, second.shape[1]
    width, block, tall = mine // fsdp, columns // ctx, stacked_rows(mix_rows + attn_rows)
    boxes, count = reducer_boxes(ctx, bits, own, columns)
    ctx_sems = pltpu.SemaphoreType.DMA((count + 2 * (ctx - 1),))
    line_sems = pltpu.SemaphoreType.DMA((4 * (fsdp - 1),))

    def shape(*sizes):
        return jax.ShapeDtypeStruct(sizes, jnp.float32)

    return pl.pallas_call(
        functools.partial(back_kernel, ctx, fsdp),
        out_shape=[
            shape(own, columns), shape(rows, q_mine), shape(rows, kv_mine), shape(rows, kv_mine),
            jax.ShapeDtypeStruct((ctx, rows, width), BF16),
            shape(ctx * attn_rows, block), shape(ctx * mix_rows, block),
            shape(*head.shape),
            jax.ShapeDtypeStruct(state.shape, BF16),
        ],
        in_specs=[IN_VMEM] * 6,
        out_specs=[IN_VMEM] * 9,
        scratch_shapes=[
            pltpu.VMEM((columns, first.shape[1]), BF16),
            pltpu.VMEM((columns, second.shape[1]), BF16),
            pltpu.VMEM((fsdp - 1, head.shape[0] // fsdp, mine), jnp.float32),
            pltpu.VMEM((fsdp - 1, state.shape[0] // fsdp, mine), BF16),
            pltpu.VMEM((ctx, rows, width), BF16),
            pltpu.VMEM((ctx, tall, block), BF16),
            pltpu.VMEM((ctx, tall, block), BF16),
            ctx_sems, ctx_sems, line_sems, line_sems,
        ]
        + boxes,
        compiler_params=params(collective_id),
        name="reduce_and_place",
    )(
        first.reshape(ctx, own, -1), second.reshape(ctx, own, -1), weight, early, head, state
    )


def finish_kernel(
    size, fsdp, src_ref, gate_ref, head_ref, state_ref, gain_ref,
    mixer_out, step_out, head_out, state_out, sums_ref,
    head_all, state_all, gain_inbox, line_inbox, c_send, c_recv, s_send, s_recv, ctx_send, ctx_recv, line_send, line_recv,
):
    me, row = lax.axis_index("ctx"), lax.axis_index("fsdp")
    greet_planes(me, size, row, fsdp)
    rows, width, low = c_send.shape[1], c_send.shape[2], step_out.shape[0]
    repeat = size // fsdp
    across, line = Copies("ctx", ctx_send, ctx_recv), Copies("fsdp", line_send, line_recv)
    head_all[me] = head_ref[...]
    state_all[me] = state_ref[...]
    lists = [gather_steps(across, size.bit_length() - 1, ref) for ref in (state_all, head_all)]
    steps = [step for pair in zip(*lists) for step in pair]
    steps[0]()
    steps[1]()
    gains = [
        across.send(gain_ref, gain_inbox.at[turn - 1], (me + turn) % size)
        for turn in range(1, size)
    ]
    for d in range(size):
        if d < fsdp:
            c_send[d] = src_ref[:rows, d * width : (d + 1) * width]
        at = d // repeat * width
        s_send[d] = src_ref[rows:, at : at + width]
    parts = SomeExchange(across, c_send, c_recv, me, size, lambda d: d < fsdp)
    parts.start()
    moved = exchange(across, s_send, s_recv, me, size)
    for step in steps[2:6]:
        step()
    total = gain_ref[...]
    for turn in range(1, size):
        gains[turn - 1].wait_recv()
        total = total + gain_inbox[turn - 1]
    line_inbox[0] = total
    gains = [
        line.send(line_inbox.at[0], line_inbox.at[turn], (row + turn) % fsdp)
        for turn in range(1, fsdp)
    ]

    @pl.when(me >= fsdp)
    def _():
        for s in range(size):
            mixer_out[:, s * width : (s + 1) * width] = gate_ref[s].astype(jnp.float32)

    for step in steps[6:-2]:
        step()
    parts.wait()

    @pl.when(me < fsdp)
    def _():
        for s in range(size):
            mixer_out[:, s * width : (s + 1) * width] = c_recv[s].astype(jnp.float32)

    steps[-2]()
    steps[-1]()
    part = head_out.shape[1] // fsdp
    for out, ref in ((state_out, state_all), (head_out, head_all)):
        for s in range(size):
            for f in range(fsdp):
                at = f * part + s * width
                out[:, at : at + width] = ref[s, :, f * width : (f + 1) * width].astype(out.dtype)

    for copy in moved:
        copy.wait_recv()
    for j in range(fsdp):
        source = fsdp * (me % repeat) + j
        step_out[:, j * width : (j + 1) * width] = s_recv[source, :low].astype(jnp.float32)
    total = line_inbox[0]
    for turn in range(1, fsdp):
        gains[turn - 1].wait_recv()
        total = total + line_inbox[turn]
    sums_ref[...] = total
    parts.finish()
    across.finish()
    line.finish()


def finish(src, gates, head, state, gains, step_rows, collective_id):
    ctx, fsdp = lax.axis_size("ctx"), lax.axis_size("fsdp")
    rows, width = gates.shape[1:]
    ctx_sems = pltpu.SemaphoreType.DMA((3 * (ctx - 1) + 2 * gather_sems(ctx_bits()),))
    line_sems = pltpu.SemaphoreType.DMA((fsdp - 1,))

    def shape(*sizes):
        return jax.ShapeDtypeStruct(sizes, jnp.float32)

    return pl.pallas_call(
        functools.partial(finish_kernel, ctx, fsdp),
        out_shape=[
            shape(rows, ctx * width), shape(step_rows, fsdp * width),
            shape(head.shape[0], ctx * head.shape[1]), shape(state.shape[0], ctx * head.shape[1]),
            shape(*gains.shape),
        ],
        in_specs=[IN_VMEM] * 5,
        out_specs=[IN_VMEM] * 5,
        scratch_shapes=[
            pltpu.VMEM((ctx,) + head.shape, jnp.float32),
            pltpu.VMEM((ctx,) + state.shape, BF16),
            pltpu.VMEM((ctx - 1,) + gains.shape, jnp.float32),
            pltpu.VMEM((fsdp,) + gains.shape, jnp.float32),
            pltpu.VMEM((ctx, rows, width), BF16),
            pltpu.VMEM((ctx, rows, width), BF16),
            pltpu.VMEM((ctx, src.shape[0] - rows, width), BF16),
            pltpu.VMEM((ctx, src.shape[0] - rows, width), BF16),
            ctx_sems, ctx_sems, line_sems, line_sems,
        ],
        compiler_params=params(collective_id),
        name="finish",
    )(src, gates, head, state, gains)


def window(start, size, total, step):
    return pl.multiple_of(jnp.minimum(start // step * step, total - size), step)


def shifted(values, offset, axis):
    size = values.shape[axis]
    return pltpu.roll(values.astype(jnp.float32), lax.rem(size - offset, size), axis)


def pack_in_begin(weights, scratch):
    mixer_ref, (inbox, sems) = weights[3], scratch
    me, size = lax.axis_index("ctx"), lax.axis_size("ctx")
    units, _, span = inbox.shape
    total = mixer_ref.shape[1]
    width = total // units // size
    copies = []
    for u in range(units):
        at = window(u * (total // units) + me * width, span, total, 128)
        copy = pltpu.make_async_copy(mixer_ref.at[:, pl.ds(at, span)], inbox.at[u], sems.at[u])
        copy.start()
        copies.append(copy)
    return copies


def pack_in(row, copies, weights, scratch, in_out, state_out, step_out):
    query_ref, key_ref, value_ref, mixer_ref, state_ref, step_ref = weights
    inbox = scratch[0]
    me, size = lax.axis_index("ctx"), lax.axis_size("ctx")
    units, _, span = inbox.shape
    total = mixer_ref.shape[1]
    width = total // units // size
    at = 0
    for ref in (query_ref, key_ref, value_ref):
        wide = ref.shape[1] // size
        in_out[row, :, at : at + wide] = shifted(ref[...], me * wide, 1)[:, :wide].astype(BF16)
        at += wide
    high = state_ref.shape[1] // size
    turned = shifted(state_ref[...], me * high, 1)[:, :128].T
    state_out[row] = turned[: state_out.shape[1]].astype(BF16)
    part = step_ref.shape[1] * 2 // units
    step_out[row] = jnp.zeros(step_out.shape[1:], BF16)
    for f in range(units // 2):
        band = shifted(step_ref[:, f * part : (f + 1) * part], me * width, 1)[:, :width]
        step_out[row, : step_ref.shape[0], f * width : (f + 1) * width] = band.astype(BF16)
    for u in range(units):
        copies[u].wait()
        start = u * (total // units) + me * width
        piece = shifted(inbox[u], start - window(start, span, total, 128), 1)[:, :width]
        to = at + (u + units // 2) % units * width
        in_out[row, :, to : to + width] = piece.astype(BF16)


def pack_in_plan(first):
    shape = jax.ShapeDtypeStruct
    if len(first) == 3:
        return {"shapes": [shape(a.shape, a.dtype) for a in first], "scratch": [], "any": ()}
    query, key, value, mixer, state, step = first
    ctx, fsdp = lax.axis_size("ctx"), lax.axis_size("fsdp")
    rows = mixer.shape[0]
    mine = mixer.shape[1] // 2 // ctx
    qkv = (query.shape[1] + key.shape[1] + value.shape[1]) // ctx
    state_rows = state.shape[1] // ctx
    return {
        "shapes": [
            shape((rows, qkv + 2 * mine), BF16),
            shape((state_rows + -state_rows % 16, state.shape[0]), BF16),
            shape((step.shape[0] + -step.shape[0] % 16, mine), BF16),
        ],
        "scratch": [
            pltpu.VMEM((2 * fsdp, rows, 256), BF16), pltpu.SemaphoreType.DMA((2 * fsdp,))
        ],
        "any": (3,),
    }


def pack_out_plan(later, hidden_units):
    if not later:
        return {"inputs": 0, "outputs": 0, "shapes": [], "scratch": [], "steps": None}
    ctx, fsdp = lax.axis_size("ctx"), lax.axis_size("fsdp")
    gate, _, down, mix, attn = later
    rows, model, total = gate.shape[0], down.shape[0], gate.shape[1]
    hid_part = total // ctx // fsdp
    pad = -hid_part % 16
    units = hidden_units // fsdp
    width = hid_part // units
    high = (hid_part + pad) + (mix.shape[0] + attn.shape[0]) // ctx
    span = 256

    def box_rows(array):
        need = array.shape[0] // ctx
        return need + 15 + -(need + 15) % 16

    def steps(me, weights, outs, scratch):
        gate_ref, up_ref, down_ref, mix_ref, attn_ref = weights
        pair_out, rows_out = outs
        inbox, down_box, tail_box, mix_box, attn_box, sems = scratch
        copies = []

        def start_copy(source, target):
            copy = pltpu.make_async_copy(source, target, sems.at[len(copies)])
            copy.start()
            copies.append(copy)

        plans = []
        half = pair_out.shape[1] // 2
        for index, ref in enumerate((gate_ref, up_ref)):
            for u in range(hidden_units):
                start = u * (total // hidden_units) + me * width
                at = window(start, span, total, 128)
                start_copy(ref.at[:, pl.ds(at, span)], inbox.at[index, u])
                to = index * half + u * width + u // units * pad
                plans.append(("columns", inbox, (index, u), start - at, to, width))
        to = 0
        down_at = to
        to += units * width + pad
        for ref, box in ((mix_ref, mix_box), (attn_ref, attn_box)):
            tall = ref.shape[0] // size
            at = window(me * tall, box.shape[1], ref.shape[0], 16)
            start_copy(ref.at[pl.ds(at, box.shape[1])], box.at[0])
            plans.append(("rows", box, (0,), me * tall - at, to, tall))
            to += tall
        start_copy(down_ref, down_box)
        full = down.shape[1] // 128
        tail = down.shape[1] % 128

        def tile_of(index):
            at = pl.multiple_of(jnp.minimum(index, full - 1) * 128, 128)
            whole = down_box[:, pl.ds(at, 128)].astype(jnp.float32)
            return jnp.where(index >= full, tail_box[...], whole) if tail else whole

        def begin_down():
            copies[-1].wait()
            if tail:
                tail_box[...] = jnp.zeros(tail_box.shape, jnp.float32)
                tail_box[:, :tail] = down_box[:, full * 128 :].astype(jnp.float32)

        def place_down(u):
            start = u * (down.shape[1] // units) + me * width
            first = start // 128
            pair = jnp.concatenate([tile_of(first), tile_of(first + 1)], 1)
            turned = shifted(pair, start - first * 128, 1)[:, :128].T
            at = down_at + u * width
            rows_out[at : at + width] = turned[:width].astype(BF16)

        def clear():
            pair_out[...] = jnp.zeros(pair_out.shape, BF16)
            rows_out[...] = jnp.zeros(rows_out.shape, BF16)

        def place(copy, kind, box, index, offset, to, extent):
            copy.wait()
            values = box[index]
            if kind == "columns":
                pair_out[:, to : to + extent] = shifted(values, offset, 1)[:, :extent].astype(BF16)
            else:
                rows_out[to : to + extent] = shifted(values, offset, 0)[:extent].astype(BF16)

        placed = [functools.partial(place, copy, *plan) for copy, plan in zip(copies, plans)]
        downs = [functools.partial(place_down, u) for u in range(units)]
        return [clear] + placed + [begin_down] + downs

    size = ctx
    shape = jax.ShapeDtypeStruct
    return {
        "inputs": 5,
        "outputs": 2,
        "shapes": [
            shape((rows, 2 * fsdp * (hid_part + pad)), BF16),
            shape((high + -high % 16, model), BF16),
        ],
        "scratch": [
            pltpu.VMEM((2, hidden_units, rows, span), BF16),
            pltpu.VMEM(down.shape, BF16),
            pltpu.VMEM((model, 128), jnp.float32),
            pltpu.VMEM((1, box_rows(mix), model), BF16),
            pltpu.VMEM((1, box_rows(attn), model), BF16),
            pltpu.SemaphoreType.DMA((2 * hidden_units + 3,)),
        ],
        "steps": steps,
    }


def weight_kernel(fsdp, count, *refs):
    lefts, rights, rest, out_ref = refs[:count], refs[count : 2 * count], refs[2 * count : -1], refs[-1]
    for f in range(fsdp):
        at = 0
        for left, right in zip(lefts, rights):
            high, wide = left.shape[1] // fsdp, right.shape[1]
            out_ref[f, at : at + high, :wide] = lax.dot_general(
                left[:, f * high : (f + 1) * high], right[...], (((0,), (0,)), ((), ())),
                preferred_element_type=jnp.float32,
            ).astype(BF16)
            if wide < out_ref.shape[2]:
                out_ref[f, at : at + high, wide:] = jnp.zeros((high, out_ref.shape[2] - wide), BF16)
            at += high
        for ref in rest:
            out_ref[f, at : at + ref.shape[1]] = ref[f]
            at += ref.shape[1]
        if at < out_ref.shape[1]:
            out_ref[f, at:] = jnp.zeros((out_ref.shape[1] - at, out_ref.shape[2]), BF16)


def weight_gradients(pairs, given, span):
    fsdp = lax.axis_size("fsdp")
    rows = sum(left.shape[1] // fsdp for left, _ in pairs) + sum(part.shape[1] for part in given)
    return pl.pallas_call(
        functools.partial(weight_kernel, fsdp, len(pairs)),
        out_shape=jax.ShapeDtypeStruct((fsdp, stacked_rows(rows), span), BF16),
        in_specs=[IN_VMEM] * (2 * len(pairs) + len(given)),
        out_specs=IN_VMEM,
        compiler_params=pltpu.CompilerParams(vmem_limit_bytes=VMEM_LIMIT),
        name="weight_gradients",
    )(*[left for left, _ in pairs], *[right for _, right in pairs], *given)


def scan_fwd_kernel(steps_ref, drive_ref, in_ref, out_ref, rate_ref, scan_ref, prev_ref, state_ref):
    tiles = steps_ref.shape[1] // LANES
    chunk = steps_ref.shape[0]

    @pl.when(pl.program_id(0) == 0)
    def _():
        state_ref[...] = jnp.zeros_like(state_ref)

    rates = [rate_ref[:, j * LANES : (j + 1) * LANES] for j in range(tiles)]

    def group(g, states):
        states = list(states)
        base = pl.multiple_of(g * 8, 8)
        for j in range(tiles):
            lanes = slice(j * LANES, (j + 1) * LANES)
            step_8 = steps_ref[pl.ds(base, 8), lanes]
            drive_8 = step_8 * drive_ref[pl.ds(base, 8), lanes]
            rows = []
            for t in range(8):
                in_t = in_ref[base + t].astype(jnp.float32)
                out_t = out_ref[base + t].astype(jnp.float32)
                decay = jnp.exp2(step_8[t : t + 1] * rates[j])
                prev_ref[base + t, :, lanes] = states[j]
                states[j] = decay * states[j] + drive_8[t : t + 1] * in_t
                rows.append(jnp.sum(states[j] * out_t, axis=0, keepdims=True))
            scan_ref[pl.ds(base, 8), lanes] = jnp.concatenate(rows, 0)
        return tuple(states)

    start = tuple(state_ref[:, j * LANES : (j + 1) * LANES] for j in range(tiles))
    final = lax.fori_loop(0, chunk // 8, group, start)
    for j in range(tiles):
        state_ref[:, j * LANES : (j + 1) * LANES] = final[j]


def scan_fwd(steps, drive, in_b, out_b, rates):
    length, width = steps.shape
    chunk = CHUNK
    row = pl.BlockSpec((chunk, width), lambda i: (i, 0))
    mat = pl.BlockSpec((chunk, STATE, LANES), lambda i: (i, 0, 0))
    rate = pl.BlockSpec((STATE, width), lambda i: (0, 0))
    return pl.pallas_call(
        scan_fwd_kernel,
        grid=(length // chunk,),
        in_specs=[row, row, mat, mat, rate],
        out_specs=[row, pl.BlockSpec((chunk, STATE, width), lambda i: (i, 0, 0))],
        out_shape=[
            jax.ShapeDtypeStruct((length, width), jnp.float32),
            jax.ShapeDtypeStruct((length, STATE, width), jnp.float32),
        ],
        scratch_shapes=[pltpu.VMEM((STATE, width), jnp.float32)],
        compiler_params=pltpu.CompilerParams(vmem_limit_bytes=48 * 1024 * 1024),
        name="scan_forward",
    )(steps, drive, in_b, out_b, rates)


def scan_bwd_kernel(
    units, steps_ref, drive_ref, grad_ref, in_ref, out_ref, rate_ref, prev_ref, *refs
):
    exchanged, refs = refs[: 1 if units else 0], refs[1 if units else 0 :]
    gstep_ref, gdrive_ref, gin_ref, gout_ref, grate_ref = refs[:5]
    received, refs = refs[5 : 8 if units else 5], refs[8 if units else 5 :]
    carry_ref, pin_ref, pout_ref = refs[:3]
    slots = refs[3:]
    tiles = steps_ref.shape[1] // LANES
    chunk = steps_ref.shape[0]
    if units:
        pl.when(pl.program_id(0) == 0)(functools.partial(relay_begin, units, *exchanged, *slots))

    @pl.when(pl.program_id(0) == 0)
    def _():
        carry_ref[...] = jnp.zeros_like(carry_ref)
        grate_ref[...] = jnp.zeros_like(grate_ref)

    for first in range(0, tiles, 4):
        tile_lanes = [slice(j * LANES, (j + 1) * LANES) for j in range(first, min(first + 4, tiles))]
        tile_rates = [rate_ref[:, lanes] for lanes in tile_lanes]

        def group(k, kept):
            carries, sums = list(kept[0]), list(kept[1])
            base = pl.multiple_of(chunk - 8 - k * 8, 8)
            rows_8 = pl.ds(base, 8)
            step_8 = [steps_ref[rows_8, lanes] for lanes in tile_lanes]
            x_8 = [drive_ref[rows_8, lanes] for lanes in tile_lanes]
            grad_8 = [grad_ref[rows_8, lanes] for lanes in tile_lanes]
            drive_8 = [step * x for step, x in zip(step_8, x_8)]
            held_rows = [[None] * 8 for _ in tile_lanes]
            dot_rows = [[None] * 8 for _ in tile_lanes]
            for t in range(7, -1, -1):
                in_t = in_ref[base + t].astype(jnp.float32)
                out_t = out_ref[base + t].astype(jnp.float32)
                part_in = part_out = None
                for n, lanes in enumerate(tile_lanes):
                    rates = tile_rates[n]
                    previous = prev_ref[base + t, :, lanes]
                    step_t = step_8[n][t : t + 1]
                    drive_t = drive_8[n][t : t + 1]
                    grad_t = grad_8[n][t : t + 1]
                    decay = jnp.exp2(step_t * rates)
                    adjoint = grad_t * out_t + carries[n]
                    carries[n] = decay * adjoint
                    held = carries[n] * previous
                    state = decay * previous + drive_t * in_t
                    sums[n] = sums[n] + held * step_t
                    held_rows[n][t] = jnp.sum(held * rates, axis=0, keepdims=True)
                    dot_rows[n][t] = jnp.sum(adjoint * in_t, axis=0, keepdims=True)
                    more_in, more_out = adjoint * drive_t, state * grad_t
                    part_in = more_in if part_in is None else part_in + more_in
                    part_out = more_out if part_out is None else part_out + more_out
                at = pl.ds(pl.multiple_of((base + t) * STATE, STATE), STATE)
                if first == 0:
                    pin_ref[at] = part_in
                    pout_ref[at] = part_out
                else:
                    pin_ref[at] += part_in
                    pout_ref[at] += part_out
            for n, lanes in enumerate(tile_lanes):
                held_8 = jnp.concatenate(held_rows[n], 0)
                dot_8 = jnp.concatenate(dot_rows[n], 0)
                gstep_ref[rows_8, lanes] = held_8 * 0.6931471805599453 + x_8[n] * dot_8
                gdrive_ref[rows_8, lanes] = step_8[n] * dot_8
            return tuple(carries), tuple(sums)

        start = (
            tuple(carry_ref[:, lanes] for lanes in tile_lanes),
            tuple(grate_ref[:, lanes] for lanes in tile_lanes),
        )
        carries, sums = lax.fori_loop(0, chunk // 8, group, start)
        for n, lanes in enumerate(tile_lanes):
            carry_ref[:, lanes] = carries[n]
            grate_ref[:, lanes] = sums[n]
    ones = jnp.ones((8, LANES), jnp.float32)
    dims = (((1,), (1,)), ((), ()))
    gin_ref[0] = lax.dot_general(ones, pin_ref[...], dims, preferred_element_type=jnp.float32)
    gout_ref[0] = lax.dot_general(ones, pout_ref[...], dims, preferred_element_type=jnp.float32)
    if units:
        last = pl.num_programs(0) - 1
        pl.when(pl.program_id(0) == last)(functools.partial(relay_end, units, *received, *slots))


def scan_bwd(steps, drive, grad, in_b, out_b, rates, previous, relay=None, units=0, hidden=0, part=0, model=0, collective_id=None):
    length, width = steps.shape
    chunk = CHUNK
    count = length // chunk
    row = pl.BlockSpec((chunk, width), lambda i: (count - 1 - i, 0))
    mat = pl.BlockSpec((chunk, STATE, LANES), lambda i: (count - 1 - i, 0, 0))
    rate = pl.BlockSpec((STATE, width), lambda i: (0, 0))
    red = pl.BlockSpec((1, 8, chunk * STATE), lambda i: (count - 1 - i, 0, 0))
    shape = jax.ShapeDtypeStruct
    relay_out, slots = [], []
    extra = [] if relay is None else [relay]
    settings = dict(vmem_limit_bytes=56 * 1024 * 1024)
    if relay is not None:
        ctx, fsdp = lax.axis_size("ctx"), lax.axis_size("fsdp")
        wide, block, high = hidden // ctx, model // ctx, model // fsdp
        relay_out = [
            shape((high, ctx * wide), jnp.float32),
            shape((high, ctx * wide), jnp.float32),
            shape((units * ctx * wide, block), jnp.float32),
        ]
        slots = [
            pltpu.VMEM((ctx, high, 2 * wide), BF16),
            pltpu.VMEM((ctx, high, 2 * wide), BF16),
            pltpu.VMEM((ctx, part, block), BF16),
            pltpu.VMEM((ctx, part, block), BF16),
            pltpu.SemaphoreType.DMA((2 * (ctx - 1),)),
            pltpu.SemaphoreType.DMA((2 * (ctx - 1),)),
        ]
        settings.update(collective_id=collective_id, has_side_effects=True)
    gstep, gdrive, gin, gout, grate, *relayed = pl.pallas_call(
        functools.partial(scan_bwd_kernel, units),
        grid=(count,),
        in_specs=[row, row, row, mat, mat, rate,
                  pl.BlockSpec((chunk, STATE, width), lambda i: (count - 1 - i, 0, 0))]
        + [pl.BlockSpec(a.shape, lambda i: (0, 0)) for a in extra],
        out_specs=[row, row, red, red, rate]
        + [pl.BlockSpec(a.shape, lambda i: (0, 0)) for a in relay_out],
        out_shape=[
            shape((length, width), jnp.float32),
            shape((length, width), jnp.float32),
            shape((count, 8, chunk * STATE), jnp.float32),
            shape((count, 8, chunk * STATE), jnp.float32),
            shape((STATE, width), jnp.float32),
        ]
        + relay_out,
        scratch_shapes=[
            pltpu.VMEM((STATE, width), jnp.float32),
            pltpu.VMEM((chunk * STATE, LANES), jnp.float32),
            pltpu.VMEM((chunk * STATE, LANES), jnp.float32),
        ]
        + slots,
        compiler_params=pltpu.CompilerParams(**settings),
        name="scan_backward",
    )(steps, drive, grad, in_b, out_b, rates, previous, *extra)
    return (
        gstep, gdrive, gin[:, 0].reshape(length, STATE), gout[:, 0].reshape(length, STATE), grate,
        relayed,
    )


def matmul(left, right):
    return jnp.dot(left, right, preferred_element_type=jnp.float32)


def left_trans(left, right):
    return lax.dot_general(
        left, right, (((0,), (0,)), ((), ())), preferred_element_type=jnp.float32
    )


def right_trans(left, right):
    return lax.dot_general(
        left, right, (((1,), (1,)), ((), ())), preferred_element_type=jnp.float32
    )


def rms_scale(values):
    return lax.rsqrt(jnp.mean(values * values, axis=-1, keepdims=True) + EPSILON)


def norm_back(grad_out, values, scale_in, gain_in):
    scaled = grad_out * gain_in
    grad_in = scale_in * scaled - values * scale_in**3 * jnp.mean(
        scaled * values, axis=-1, keepdims=True
    )
    return (grad_in, jnp.sum(grad_out * values * scale_in, axis=0))


def silu_slope(values):
    logistic = jax.nn.sigmoid(values)
    return logistic * (1.0 + values * (1.0 - logistic))


def unit_count(width, ctx, fsdp):
    return ctx if width % (ctx * ctx) == 0 and ctx % fsdp == 0 else fsdp


def my_columns(array, units):
    span = array.shape[1] // units
    width = span // lax.axis_size("ctx")
    start = lax.axis_index("ctx") * width
    return [
        lax.dynamic_slice_in_dim(array, unit * span + start, width, 1) for unit in range(units)
    ]


def my_rows(array, units):
    span = array.shape[0] // units
    width = span // lax.axis_size("ctx")
    start = lax.axis_index("ctx") * width
    return [
        lax.dynamic_slice_in_dim(array, unit * span + start, width, 0) for unit in range(units)
    ]


def block_columns(array):
    width = array.shape[1] // lax.axis_size("ctx")
    return lax.dynamic_slice_in_dim(array, lax.axis_index("ctx") * width, width, 1)


def over_fsdp(array):
    return lax.all_gather(array, "fsdp", axis=0, tiled=True)


def to_slots(array, units):
    repeat = lax.axis_size("ctx") // units
    rows, width = array.shape[0], array.shape[1] // units
    pieces = array.reshape(rows, units, width).transpose(1, 0, 2)
    return jnp.repeat(pieces, repeat, axis=0) if repeat > 1 else pieces


def from_slots(got, units):
    repeat = lax.axis_size("ctx") // units
    if repeat > 1:
        first = units * lax.rem(lax.axis_index("ctx"), repeat)
        got = lax.dynamic_slice_in_dim(got, first, units, 0)
    rows, width = got.shape[1:]
    return got.transpose(1, 0, 2).reshape(rows, units * width).astype(jnp.float32)


def to_blocks(array, units):
    got = lax.all_to_all(to_slots(array, units), "ctx", 0, 0, tiled=True)
    return from_slots(got, units)


def rows_to_slots(array):
    ctx = lax.axis_size("ctx")
    rows, columns = array.shape
    return array.reshape(rows, ctx, columns // ctx).transpose(1, 0, 2)


def rows_from_slots(got, units):
    ctx, rows, columns = got.shape
    got = got.reshape(ctx, units, rows // units, columns).transpose(1, 0, 2, 3)
    return got.reshape(ctx * rows, columns).astype(jnp.float32)


def rows_to_blocks(array, units):
    got = lax.all_to_all(rows_to_slots(array), "ctx", 0, 0, tiled=True)
    return rows_from_slots(got, units)


def scatter_fsdp(*gradients):
    fsdp = lax.axis_size("fsdp")
    parts = [g.astype(BF16).reshape(fsdp, -1, g.shape[1]) for g in gradients]
    pad = -sum(part.shape[1] for part in parts) % 16
    if pad:
        parts.append(jnp.zeros((fsdp, pad, gradients[0].shape[1]), BF16))
    joined = jnp.concatenate(parts, 1) if len(parts) > 1 else parts[0]
    joined = joined.reshape(-1, joined.shape[2])
    return lax.psum_scatter(joined, "fsdp", scatter_dimension=0, tiled=True)


def body(
    inputs,
    cotangent,
    norm_gain,
    query_proj,
    key_proj,
    value_proj,
    attn_proj,
    attn_gain,
    mixer_in,
    conv_taps,
    conv_bias,
    state_proj,
    step_proj,
    step_bias,
    decay_rate,
    skip_gain,
    mixer_out,
    ssm_gain,
    ffn_gain,
    gate_proj,
    up_proj,
    down_proj,
):
    ctx, fsdp = lax.axis_size("ctx"), lax.axis_size("fsdp")
    place = lax.axis_index("ctx")
    tokens = inputs[0].astype(jnp.float32)
    own, model = tokens.shape
    length = own * ctx
    inner = conv_bias.shape[0]
    mine = inner // ctx
    kv_mine = key_proj.shape[1] // ctx
    q_mine = query_proj.shape[1] // ctx
    hidden_units = unit_count(gate_proj.shape[1], ctx, fsdp)
    hidden_rows = hidden_units // fsdp
    hid = gate_proj.shape[1] // ctx
    group_size = query_proj.shape[1] // key_proj.shape[1]
    score_scale = HEAD ** (-0.5)

    hid_part = hid // fsdp
    hid_pad = -hid_part % 16
    hid_all = hid + fsdp * hid_pad
    attn_pad = -attn_proj.shape[0] % ctx
    attn_rows_mine = (attn_proj.shape[0] + attn_pad) // ctx
    state_rows, step_rows = state_proj.shape[0] // ctx, step_proj.shape[0]
    if ctx == 8:
        first = (query_proj, key_proj, value_proj, mixer_in, state_proj.T, step_proj)
        later = (gate_proj, up_proj, down_proj.T, mixer_out, attn_proj)
        x_in, top_in = inputs[0].T, cotangent[0].T
    else:
        in_part = jnp.concatenate(
            [block_columns(array) for array in (query_proj, key_proj, value_proj)]
            + my_columns(mixer_in[:, inner:], fsdp)
            + my_columns(mixer_in[:, :inner], fsdp),
            1,
        )
        later = ()
        x_in, top_in = inputs[0], cotangent[0]
        state_part = jnp.pad(my_rows(state_proj, 1)[0], ((0, -state_rows % 16), (0, 0)))
        step_part = jnp.pad(
            jnp.concatenate(my_columns(step_proj, fsdp), 1), ((0, -step_rows % 16), (0, 0))
        )

        first = (in_part, state_part, step_part)

        def hidden_columns(array):
            pieces = my_columns(array, hidden_units)
            if hid_pad:
                for f in range(fsdp, 0, -1):
                    pieces.insert(f * hidden_rows, jnp.zeros((array.shape[0], hid_pad), BF16))
            return pieces

        ffn_part = jnp.concatenate(hidden_columns(gate_proj) + hidden_columns(up_proj), 1)
        rows_part = jnp.concatenate(
            my_rows(down_proj, hidden_rows)
            + [jnp.zeros((hid_pad, model), BF16)]
            + my_rows(mixer_out, 1)
            + my_rows(jnp.pad(attn_proj, ((0, attn_pad), (0, 0))), 1),
            0,
        )
    mix_rows = mixer_out.shape[0] // ctx
    normed_all, grad_top, in_full, state_full, step_full, *parts = front(
        x_in, norm_gain[None], top_in, first, later, hidden_units, 0
    )
    if parts:
        ffn_part, rows_part = parts
    normed_all = normed_all.reshape(length, model)
    grad_top = grad_top.reshape(length, model)
    in_full = in_full.reshape(model, -1)
    state_full = state_full[:, :state_rows].reshape(-1, state_proj.shape[1])
    step_full = step_full[:, :step_rows].reshape(-1, mine)
    norm_scale = rms_scale(tokens)
    rows_full = lax.all_gather(rows_part, "fsdp", axis=0)
    ffn_full = over_fsdp(ffn_part)
    down_at = hid_part + hid_pad
    down_full = rows_full[:, :down_at].reshape(-1, model)
    mixout_full = rows_full[:, down_at : down_at + mix_rows].reshape(-1, model)
    attn_at = down_at + mix_rows
    attn_full = rows_full[:, attn_at : attn_at + attn_rows_mine].reshape(-1, model)
    attn_width = attn_full.shape[0]

    def mine_of(vector):
        return jnp.concatenate(my_columns(vector.reshape(-1, inner), fsdp), 1)

    taps, bias, skip, gain_ssm, bias_step = (
        mine_of(conv_taps),
        mine_of(conv_bias),
        mine_of(skip_gain),
        mine_of(ssm_gain),
        mine_of(step_bias),
    )
    rates = jnp.concatenate(
        [
            lax.dynamic_slice_in_dim(
                decay_rate, unit * (inner // fsdp) + place * (mine // fsdp), mine // fsdp, 0
            )
            for unit in range(fsdp)
        ],
        0,
    ).T
    pad = -mine % LANES

    def padded(values):
        return jnp.pad(values, ((0, 0), (0, pad)))

    projected_in = matmul(normed_all, in_full).astype(BF16)
    conv_src = projected_in[:, q_mine + 2 * kv_mine + mine :]

    padded_src = jnp.concatenate(
        [jnp.zeros((CONV - 1, mine), jnp.float32), conv_src.astype(jnp.float32)], 0
    )
    conv_pre = bias + sum(taps[tap][None] * padded_src[tap : tap + length] for tap in range(CONV))
    conv_act = jax.nn.silu(conv_pre).astype(BF16)
    conv_vals = conv_act.astype(jnp.float32)
    projected = sum_everywhere(matmul(conv_act, state_full).astype(BF16), 2).astype(jnp.float32)
    step_low = projected[:, :DT_RANK].astype(BF16)
    input_mat = projected[:, DT_RANK : DT_RANK + STATE]
    output_mat = projected[:, DT_RANK + STATE :]
    step_pre = matmul(step_low, step_full) + bias_step
    steps_dt = jax.nn.softplus(step_pre)
    in_b = jnp.broadcast_to(input_mat.astype(BF16)[:, :, None], (length, STATE, LANES))
    out_b = jnp.broadcast_to(output_mat.astype(BF16)[:, :, None], (length, STATE, LANES))
    rates_log2 = padded(-LOG2_E * rates)
    steps_pad, vals_pad = padded(steps_dt), padded(conv_vals)
    scan_out, states = scan_fwd(steps_pad, vals_pad, in_b, out_b, rates_log2)
    scan_out = scan_out[:, :mine]

    gate_z = projected_in[:, q_mine + 2 * kv_mine : q_mine + 2 * kv_mine + mine].astype(jnp.float32)
    def attn_to_channels(values):
        parts = jnp.pad(values.reshape(own, fsdp, -1), ((0, 0), (0, 0), (0, attn_pad)))
        parts = parts.reshape(own, fsdp, ctx, -1).transpose(2, 0, 1, 3).reshape(ctx, own, -1)
        return lax.all_to_all(parts, "ctx", 0, 0, tiled=True).reshape(length, -1)

    def attn_to_tokens(values):
        parts = values.reshape(ctx, own, -1)
        got = lax.all_to_all(parts, "ctx", 0, 0, tiled=True)
        got = got.reshape(ctx, own, fsdp, -1).transpose(1, 2, 0, 3).reshape(own, fsdp, -1)
        return got[:, :, : attn_proj.shape[0]].reshape(own, -1)

    if ctx == 8:
        branch_attn_c, attn_rows, *attn_kept = attention_forward(
            projected_in, attn_gain, key_proj.shape[1], 1
        )
        branch_attn_c = branch_attn_c.reshape(length, -1)
    else:
        queries = lax.all_to_all(projected_in[:, :q_mine], "ctx", 0, 1, tiled=True)
        keyvals = gather_shards(projected_in[:, q_mine : q_mine + 2 * kv_mine], 1)
        keys_all = keyvals[:, :, :kv_mine].transpose(1, 0, 2).reshape(length, KV_HEADS, HEAD)
        vals_all = keyvals[:, :, kv_mine:].transpose(1, 0, 2).reshape(length, KV_HEADS, HEAD)
        heads_q = queries.reshape(own, KV_HEADS, group_size, HEAD)
        row_ids = place * own + lax.broadcasted_iota(jnp.int32, (own, length), 0)
        col_ids = lax.broadcasted_iota(jnp.int32, (own, length), 1)
        allowed = (col_ids <= row_ids) & (col_ids > row_ids - WINDOW)

        def scores_of():
            raw = jnp.einsum("qhgd,khd->hgqk", heads_q, keys_all, preferred_element_type=jnp.float32)
            return jnp.where(allowed, raw * score_scale, -1e30)

        scores = scores_of()
        row_top = jnp.max(scores, axis=-1, keepdims=True)
        log_total = row_top + jnp.log(jnp.sum(jnp.exp(scores - row_top), axis=-1, keepdims=True))
        probs = jnp.exp(scores - log_total)
        probs_bf = probs.astype(BF16)
        attn_rows = jnp.einsum(
            "hgqk,khd->qhgd", probs_bf, vals_all, preferred_element_type=jnp.float32
        ).reshape(own, -1)
        attn_scale = rms_scale(attn_rows)
        branch_attn = (attn_rows * attn_scale * attn_gain).astype(BF16)
        branch_attn_c = attn_to_channels(branch_attn)

    ssm_raw = scan_out + skip * conv_vals
    gate_act = jax.nn.silu(gate_z)
    ssm_gated = ssm_raw * gate_act
    square = total_of(jnp.sum(ssm_gated * ssm_gated, axis=-1), 3)
    ssm_scale = lax.rsqrt(square / inner + EPSILON)[:, None]
    branch_ssm = (ssm_gated * ssm_scale * gain_ssm).astype(BF16)
    middle = tokens + 0.5 * reduce_products(
        [branch_attn_c, branch_ssm], [attn_full, mixout_full], False, 4
    )
    ffn_scale = rms_scale(middle)
    ffn_in = (middle * ffn_scale * ffn_gain).astype(BF16)
    if ctx == 8:
        ffn_dw, ffn_out, grad_ffn_in = ffn_both_ways(ffn_in, grad_top, ffn_full, down_full, 5)
        ffn_dw = [ffn_dw.reshape(-1, 2 * hid_all)]
    else:
        ffn_all = gather_tokens(ffn_in, 5)
        pre = matmul(ffn_all, ffn_full)
        gate_pre, up_pre = pre[:, :hid_all], pre[:, hid_all:]
        gate_silu = jax.nn.silu(gate_pre)
        hidden = (gate_silu * up_pre).astype(BF16)
        ffn_out = reduce_products([hidden], [down_full], False, 6)
        grad_hidden = right_trans(grad_top, down_full)
        grad_gate = (grad_hidden * up_pre * silu_slope(gate_pre)).astype(BF16)
        grad_up = (grad_hidden * gate_silu).astype(BF16)
        grad_pair = jnp.concatenate([grad_gate, grad_up], 1)
        grad_ffn_in = reduce_products([grad_pair], [ffn_full], True, 7)
        down_dw = left_trans(hidden, grad_top).astype(BF16)
        pair_dw = left_trans(ffn_all, grad_pair).astype(BF16)
        ffn_dw = [pair_dw, down_dw]
    grad_ffn_in, ffn_dw = lax.optimization_barrier((grad_ffn_in, ffn_dw))
    ffn_grad = [scatter_fsdp(dw) for dw in ffn_dw]
    grad_middle, grad_ffn_gain = norm_back(grad_ffn_in, middle, ffn_scale, ffn_gain)
    grad_middle = grad_middle + cotangent[0].astype(jnp.float32)
    grad_branch = (0.5 * grad_middle).astype(BF16)
    branch_all = gather_tokens(grad_branch, 8)
    placing = ctx == 8 and ctx == 2 * fsdp and not attn_pad
    early_wide = q_mine + 2 * kv_mine + mine
    early_span = early_wide + -early_wide % LANES
    if ctx == 8:
        grad_early, grad_attn_gain, ffn_out, out_dw, grad_norm, dots = attention_backward(
            (attn_full, mixout_full), attn_rows, (attn_gain, gain_ssm), ssm_gated, ffn_out,
            (branch_attn_c, branch_ssm), branch_all, attn_kept, early_span, 13,
        )
        dots = dots[0]
        grad_attn_gain = grad_attn_gain[0]
    else:
        grad_attn_c = right_trans(branch_all, attn_full).astype(BF16)
        grad_norm = right_trans(branch_all, mixout_full)
        dots = total_of(jnp.sum(grad_norm * gain_ssm * ssm_gated, axis=-1), 9)
        grad_attn = attn_to_tokens(grad_attn_c).astype(jnp.float32)
        grad_attn_raw, grad_attn_gain = norm_back(grad_attn, attn_rows, attn_scale, attn_gain)
        grad_heads = grad_attn_raw.astype(BF16).reshape(own, KV_HEADS, group_size, HEAD)
        grad_probs = jnp.einsum(
            "qhgd,khd->hgqk", grad_heads, vals_all, preferred_element_type=jnp.float32
        )
        row_dot = jnp.sum(probs * grad_probs, axis=-1, keepdims=True)
        grad_scores = (probs * (grad_probs - row_dot)).astype(BF16)
        grad_queries = score_scale * jnp.einsum(
            "hgqk,khd->qhgd", grad_scores, keys_all, preferred_element_type=jnp.float32
        ).reshape(own, -1)
        grad_keys = score_scale * jnp.einsum(
            "hgqk,qhgd->khd", grad_scores, heads_q, preferred_element_type=jnp.float32
        )
        grad_vals = jnp.einsum(
            "hgqk,qhgd->khd", probs_bf, grad_heads, preferred_element_type=jnp.float32
        )
        grad_queries = lax.all_to_all(
            grad_queries.astype(BF16).reshape(own, ctx, -1).transpose(1, 0, 2), "ctx", 0, 0, tiled=True
        ).reshape(length, -1)
        grad_kv = jnp.concatenate(
            [
                grad_keys.reshape(length, ctx, kv_mine).transpose(1, 0, 2),
                grad_vals.reshape(length, ctx, kv_mine).transpose(1, 0, 2),
            ],
            2,
        ).astype(BF16)
        grad_kv = jnp.sum(
            lax.all_to_all(grad_kv, "ctx", 0, 0, tiled=True).astype(jnp.float32), axis=0
        ).astype(BF16)
        grad_early = jnp.concatenate([grad_queries, grad_kv], 1)
        out_dw = [
            left_trans(branch_ssm, branch_all).astype(BF16),
            left_trans(branch_attn_c, branch_all).astype(BF16),
        ]

    grad_early, out_dw = lax.optimization_barrier((grad_early, out_dw))
    if not placing:
        out_grad = scatter_fsdp(*out_dw)

    output = middle + ffn_out

    grad_ssm_gain = jnp.sum(grad_norm * ssm_gated * ssm_scale, axis=0)
    scaled = grad_norm * gain_ssm
    mean_dot = dots[:, None] / inner
    grad_gated = ssm_scale * scaled - ssm_gated * ssm_scale**3 * mean_dot
    grad_scan = grad_gated * gate_act
    grad_gate_z = grad_gated * ssm_raw * silu_slope(gate_z)
    grad_skip = jnp.sum(grad_scan * conv_vals, axis=0)
    grad_gate_bf = grad_gate_z.astype(BF16)
    grad_early = jnp.concatenate([grad_early, grad_gate_bf], 1)
    if placing:
        early_dw = weight_gradients([(normed_all, grad_early)], [out_dw], early_span)
        early_dw = early_dw.reshape(-1, early_span)
    else:
        early_dw = left_trans(normed_all, grad_early)
    early_grad = scatter_fsdp(early_dw)
    with_relay = ctx == 8
    grad_steps, grad_drive, grad_input_mat, grad_output_mat, grad_rate, relayed = scan_bwd(
        steps_pad, vals_pad, padded(grad_scan), in_b, out_b, rates_log2, states,
        *((ffn_grad[0], hidden_rows, hid, down_at, model, 14) if with_relay else ()),
    )
    grad_steps, grad_drive, grad_rate = (
        grad_steps[:, :mine],
        grad_drive[:, :mine],
        -grad_rate[:, :mine],
    )
    grad_pre_full = grad_steps * jax.nn.sigmoid(step_pre)
    grad_step_bias = jnp.sum(grad_pre_full, axis=0)
    grad_pre = grad_pre_full.astype(BF16)
    grad_projected = sum_everywhere(
        jnp.concatenate(
            [right_trans(grad_pre, step_full), grad_input_mat, grad_output_mat], 1
        ).astype(BF16),
        10,
    )
    grad_state_proj = left_trans(conv_act, grad_projected)
    grad_conv_act = (
        right_trans(grad_projected, state_full) + grad_scan * skip + grad_drive
    ).astype(BF16)
    grad_conv = grad_conv_act.astype(jnp.float32) * silu_slope(conv_pre)
    grad_conv_bias = jnp.sum(grad_conv, axis=0)
    grad_taps = jnp.stack(
        [jnp.sum(grad_conv * padded_src[tap : tap + length], axis=0) for tap in range(CONV)]
    )
    conv_tail = jnp.concatenate([grad_conv, jnp.zeros((CONV - 1, mine), jnp.float32)], 0)
    grad_src = sum(
        taps[tap][None] * conv_tail[CONV - 1 - tap : CONV - 1 - tap + length]
        for tap in range(CONV)
    )
    grad_src = grad_src.astype(BF16)
    if placing:
        src_dw = weight_gradients([(normed_all, grad_src), (step_low, grad_pre)], [], mine)
        src_dw, early_grad = lax.optimization_barrier((src_dw, early_grad))
        src_grad = scatter_fsdp(src_dw.reshape(-1, mine))
    else:
        src_grad = scatter_fsdp(left_trans(normed_all, grad_src), left_trans(step_low, grad_pre))
    state_rows_all = grad_state_proj.shape[1]
    state_cut = state_rows_all // (16 * fsdp) * 16 * fsdp
    grad_state = grad_state_proj.T
    head = jnp.concatenate(
        [
            grad_taps,
            jnp.stack([grad_conv_bias, grad_step_bias, grad_skip, grad_ssm_gain]),
            grad_rate,
            grad_state[state_cut:],
        ],
        0,
    )
    head = jnp.pad(head, ((0, -head.shape[0] % (8 * fsdp)), (0, 0)))
    grad_state = grad_state[:state_cut].astype(BF16)
    if placing:
        (
            grad_normed, query_grad, key_grad, value_grad, gates, attn_grad, mixout_grad, head,
            grad_state,
        ) = reduce_and_place(
            grad_early, grad_src, in_full, early_grad, head, grad_state,
            (q_mine, kv_mine, mix_rows, attn_rows_mine), 11,
        )
    else:
        grad_normed = reduce_products([grad_early, grad_src], [in_full], True, 11)
    if with_relay:
        gate_blocks, up_blocks, down_blocks = relayed
    else:
        pair_grad, down_grad = ffn_grad
        pair_grad = pair_grad.reshape(-1, 2, fsdp, down_at)[..., :hid_part]
        gate_blocks = to_blocks(pair_grad[:, 0].reshape(-1, hid), hidden_units)
        up_blocks = to_blocks(pair_grad[:, 1].reshape(-1, hid), hidden_units)
        down_blocks = rows_to_blocks(down_grad[:hid_part], hidden_rows)
    grad_tokens, grad_norm_gain = norm_back(grad_normed, tokens, norm_scale, norm_gain)
    grad_tokens = grad_tokens + grad_middle

    gains = jnp.stack([grad_norm_gain, grad_attn_gain, grad_ffn_gain])
    gains = jnp.pad(gains, ((0, 5), (0, 0)))
    if placing:
        mixer_grad, step_grad, head, grad_state, gains = finish(
            src_grad, gates, head, grad_state, gains, step_rows, 12
        )
    else:
        channel = jnp.concatenate([head, grad_state.astype(jnp.float32)], 0)
        channel, gains = settle_small(channel, gains, 12)
        channel = channel.reshape(ctx, -1, fsdp, mine // fsdp).transpose(1, 2, 0, 3)
        channel = channel.reshape(-1, inner)
        head, grad_state = channel[: head.shape[0]], channel[head.shape[0] :]
        late_at = q_mine + 2 * kv_mine
        step_grad = src_grad[early_grad.shape[0] :][:step_rows]
        src_grad = src_grad[: early_grad.shape[0]]
        mixout_grad = out_grad[:mix_rows]
        attn_grad = out_grad[mix_rows : mix_rows + attn_rows_mine]
        query_grad = early_grad[:, :q_mine].astype(jnp.float32)
        key_grad = early_grad[:, q_mine : q_mine + kv_mine].astype(jnp.float32)
        value_grad = early_grad[:, q_mine + kv_mine : late_at].astype(jnp.float32)
        mixer_grad = to_blocks(
            jnp.concatenate([src_grad, early_grad[:, late_at:]], 1), 2 * fsdp
        )
        step_grad = to_blocks(step_grad, fsdp)
        attn_grad = rows_to_blocks(attn_grad, 1)[: attn_proj.shape[0]]
        mixout_grad = rows_to_blocks(mixout_grad, 1)
    sum_norm_gain, sum_attn_gain, sum_ffn_gain = gains[0], gains[1], gains[2]
    return (
        output[None],
        grad_tokens[None],
        sum_norm_gain,
        query_grad,
        key_grad,
        value_grad,
        attn_grad,
        sum_attn_gain,
        mixer_grad,
        head[:CONV],
        head[CONV],
        jnp.concatenate(
            [grad_state, head[CONV + 4 + STATE :][: state_rows_all - state_cut]], 0
        ).T,
        step_grad,
        head[CONV + 1],
        head[CONV + 4 : CONV + 4 + STATE].T,
        head[CONV + 2],
        mixout_grad,
        head[CONV + 3],
        sum_ffn_gain,
        gate_blocks,
        up_blocks,
        down_blocks,
    )


def solution(mesh):
    rows, whole = P("fsdp", None), P()
    blocks, sequence = P("fsdp", "ctx"), P("fsdp", "ctx", None)
    return jax.shard_map(
        body,
        mesh=mesh,
        in_specs=(
            sequence, sequence, whole, rows, rows, rows, rows, whole, rows, whole, whole,
            rows, rows, whole, whole, whole, rows, whole, whole, rows, rows, rows,
        ),
        out_specs=(
            sequence, sequence, whole, blocks, blocks, blocks, blocks, whole, blocks, whole, whole,
            whole, blocks, whole, whole, whole, blocks, whole, whole, blocks, blocks, blocks,
        ),
        check_vma=False,
    )
```
